32 devices in a mesh: groups: 2 (over x), bulk: 16 (over z, y, core).
Axes of the slice: x: 2, y: 2, z: 4, core: 2. Of those that a mesh axis runs over, the one named last changes fastest.
Arguments:
- grid_in: bfloat16 [65536, 474], P(('groups', 'bulk')), parts along dimension 0, may hold values from -6 to 6
- grid_first: bfloat16 [474, 512], replicated, may hold values from -0.25 to 0.25
- grid_bias: float32 [512], replicated, may hold values from -4 to 4
- grid_second: bfloat16 [512, 512], replicated, may hold values from -0.25 to 0.25
- send_weight: bfloat16 [512, 512], replicated, may hold values from -0.25 to 0.25
- edge_bias: float32 [512], replicated, may hold values from -4 to 4
- feat_weight: bfloat16 [4, 512], replicated, may hold values from -3 to 3
- edge_out: bfloat16 [512, 512], replicated, may hold values from -0.0625 to 0.0625
- node_input: bfloat16 [1024, 512], replicated, may hold values from -0.1875 to 0.1875
- node_bias: float32 [512], replicated, may hold values from -4 to 4
- node_out: bfloat16 [512, 512], replicated, may hold values from -0.25 to 0.25
- node_gain: float32 [512], replicated, may hold values from 0.1 to 1.9
- mesh_sender: bfloat16 [512, 512], replicated, may hold values from -0.25 to 0.25
- mesh_receiver: bfloat16 [512, 512], replicated, may hold values from -0.25 to 0.25
- message_bias: float32 [512], replicated, may hold values from -4 to 4
- message_out: bfloat16 [512, 512], replicated, may hold values from -0.09375 to 0.09375
- update_input: bfloat16 [1024, 512], replicated, may hold values from -0.1875 to 0.1875
- update_bias: float32 [512], replicated, may hold values from -4 to 4
- update_out: bfloat16 [512, 512], replicated, may hold values from -0.25 to 0.25
- update_gain: float32 [512], replicated, may hold values from 0.1 to 1.9
- mesh_latent: bfloat16 [1024, 512], P('bulk'), may hold values from -6 to 6
- g2m_send: int32 [384, 128], P('bulk'), may hold values from 0 to 2047
- g2m_recv: int32 [384, 128], P('bulk'), may hold values from 0 to 1023, as said below
- g2m_feat: float32 [384, 4, 128], P('bulk'), may hold values from -6 to 6
- g2m_count: int32 [16], P('bulk'), may hold values from 1 to 24, as said below
- mesh_slot: int32 [1024], replicated, may hold values from 0 to 1023, as said below
- mesh_send: int32 [64, 128], P('bulk'), may hold values from 0 to 1023, as said below
- mesh_recv: int32 [64, 128], P('bulk'), may hold values from 0 to 1023, as said below
Outputs:
- mesh_out: bfloat16 [2048, 512], P(('groups', 'bulk')), parts along dimension 0
The draws below stay inside these ranges and needn't reach their ends.
There are 2 independent parts, one for each index of `groups`. The reference program is written for one: setup_inputs(seed, part) draws one part's arguments, and reference() takes and returns one part's arrays. A program takes and returns all parts, laid end to end along the dimension named above; an argument that names none is the same for every part. Nothing has to cross between parts.
Inputs may be any that keep to these rules, and one draw needn't show every extreme that they name: `mesh_slot`: A permutation: mesh node id to storage row; row r belongs to bulk device r // 64. `g2m_recv`: in every block, used or not, mesh_slot[id] // 64 differs by at most 1 from the bulk index of the device holding the block. `g2m_count`: blocks past the count are padding; some device is full and some device uses one block. `mesh_send`: among the edges of one device's blocks, the senders owned by any one bulk device (mesh_slot[id] // 64) are at most 16 distinct nodes; every device reaches 16 for some owner. `mesh_recv`: mesh_slot[id] // 64 equals the bulk index of the device holding the block.
All inputs are finite; a program needn't handle non-finite values.
Results may differ from the reference program's by a relative error of at most 0.015.
Values may be sent and summed in bfloat16 or wider, within the bound.
No kernel may reach another device: no remote copies, remote signals or barrier semaphores. Data moves between devices by JAX's collectives and lax.ppermute only.
A program may use at most 64 MiB of HBM per device.

```python
import jax
import jax.numpy as jnp
from jax import lax

CHANNELS = 474
LATENT = 512
EDGE_F = 4
EB = 128
SEND_CAP = 16
G_DEV = 2048
M_DEV = 64
G2M_BLK = 24
MESH_BLK = 4
GRID = 32768
MESH = 1024
GBLK = 384
N_BULK = 16


def slot_tables(key):
    slots = jax.random.permutation(key, MESH).astype(jnp.int32)
    node_of_row = jnp.argsort(slots).astype(jnp.int32)
    return (slots, node_of_row)


def draw_mesh_slot(key, part):
    slots, node_of_row = slot_tables(key)
    return slots


def draw_g2m_recv(key, part):
    slots, node_of_row = slot_tables(key)
    key = jax.random.fold_in(key, 11)
    first_key, second_key = jax.random.split(key)
    blocks = G2M_BLK * N_BULK
    holder = (jnp.arange(blocks, dtype=jnp.int32) // G2M_BLK)[:, None]
    offset = jax.random.randint(first_key, (blocks, EB), -1, 2).astype(jnp.int32)
    leading = (jnp.arange(blocks, dtype=jnp.int32) % G2M_BLK == 0)[:, None]
    column = jnp.arange(EB, dtype=jnp.int32)[None, :]
    offset = jnp.where(leading & (column == 0), -1, offset)
    offset = jnp.where(leading & (column == 1), 1, offset)
    owner = jnp.clip(holder + offset, 0, N_BULK - 1)
    row = owner * M_DEV + jax.random.randint(second_key, (blocks, EB), 0, M_DEV).astype(jnp.int32)
    return node_of_row[row].astype(jnp.int32)


def draw_g2m_count(key, part):
    key = jax.random.fold_in(key, 12)
    first_key, second_key = jax.random.split(key)
    shifts = jax.random.randint(first_key, (N_BULK,), 0, 4).astype(jnp.int32)
    counts = jnp.maximum(jnp.right_shift(jnp.full((N_BULK,), G2M_BLK, jnp.int32), shifts), 1)
    chosen = jax.random.randint(second_key, (), 0, N_BULK).astype(jnp.int32)
    index = jnp.arange(N_BULK, dtype=jnp.int32)
    counts = jnp.where(index == (chosen + 1) % N_BULK, 1, counts)
    return jnp.where(index == chosen, G2M_BLK, counts).astype(jnp.int32)


def draw_mesh_send(key, part):
    slots, node_of_row = slot_tables(key)
    key = jax.random.fold_in(key, 14)
    first_key, second_key, third_key = jax.random.split(key, 3)
    edges = MESH_BLK * EB
    scores = jax.random.randint(first_key, (N_BULK, N_BULK, M_DEV), 0, 65536).astype(jnp.int32) * M_DEV + jnp.arange(M_DEV, dtype=jnp.int32)
    orders = jnp.argsort(scores, axis=-1).astype(jnp.int32)
    owner = jax.random.randint(second_key, (N_BULK, edges), 0, N_BULK).astype(jnp.int32)
    picked = jax.random.randint(third_key, (N_BULK, edges), 0, SEND_CAP).astype(jnp.int32)
    column = jnp.arange(edges, dtype=jnp.int32)[None, :]
    holder = jnp.arange(N_BULK, dtype=jnp.int32)[:, None]
    forced = column < SEND_CAP
    owner = jnp.where(forced, (holder + 1) % N_BULK, owner)
    picked = jnp.where(forced, column, picked)
    local = orders[holder, owner, picked]
    return node_of_row[owner * M_DEV + local].reshape(MESH_BLK * N_BULK, EB).astype(jnp.int32)


def draw_mesh_recv(key, part):
    slots, node_of_row = slot_tables(key)
    key = jax.random.fold_in(key, 13)
    blocks = MESH_BLK * N_BULK
    holder = (jnp.arange(blocks, dtype=jnp.int32) // MESH_BLK)[:, None]
    row = holder * M_DEV + jax.random.randint(key, (blocks, EB), 0, M_DEV).astype(jnp.int32)
    return node_of_row[row].astype(jnp.int32)


def place_ends(array, own_key, smallest, high):
    shape = array.shape
    spot = [jax.random.randint(jax.random.fold_in(own_key, axis), (), 0, shape[axis]) for axis in range(len(shape))]
    array = array.at[tuple(spot)].set(smallest)
    longest = shape.index(max(shape))
    spot[longest] = (spot[longest] + 1) % shape[longest]
    return array.at[tuple(spot)].set(high)


def levels(stream_key, shape, cuts, least, largest):
    gain, own = 1.0, jax.random.fold_in(stream_key, 6)
    for dim, blocks in cuts:
        steps = jnp.exp(jax.random.uniform(jax.random.fold_in(own, dim), (blocks,), jnp.float32, least / len(cuts), largest / len(cuts)))
        gain = gain * jnp.repeat(steps, shape[dim] // blocks).reshape([-1 if axis == dim else 1 for axis in range(len(shape))])
    return gain


def scatter_about(rng, extent, scale, limit, cuts=(), kind=jnp.bfloat16):
    factor_of = levels(rng, extent, cuts, -0.22, 0.18) if cuts else 1.0
    drawn = jax.random.normal(rng, extent, jnp.float32) * scale * factor_of
    return jnp.minimum(jnp.maximum(drawn, -limit), limit).astype(kind)


def setup_inputs(seed: int = 0, part: int = 0) -> dict:
    streams_of = jax.random.split(jax.random.key(seed), 29)
    part_splits = jax.random.split(jax.random.fold_in(streams_of[28], part), 29)
    grid_in = scatter_about(part_splits[0], (GRID, CHANNELS), 1.0, 6.0, ((0, 16),))
    grid_first = scatter_about(streams_of[1], (CHANNELS, LATENT), CHANNELS ** -0.5, 0.25)
    grid_bias = scatter_about(streams_of[2], (LATENT,), 1.0, 4.0, (), jnp.float32)
    grid_second = scatter_about(streams_of[3], (LATENT, LATENT), LATENT ** -0.5, 0.25)
    send_weight = scatter_about(streams_of[4], (LATENT, LATENT), LATENT ** -0.5, 0.25)
    edge_bias = scatter_about(streams_of[5], (LATENT,), 1.0, 4.0, (), jnp.float32)
    feat_weight = scatter_about(streams_of[6], (EDGE_F, LATENT), EDGE_F ** -0.5, 3.0)
    edge_out = scatter_about(streams_of[7], (LATENT, LATENT), (LATENT * 16) ** -0.5, 0.0625)
    node_input = scatter_about(streams_of[8], (2 * LATENT, LATENT), (2 * LATENT) ** -0.5, 0.1875)
    node_bias = scatter_about(streams_of[9], (LATENT,), 1.0, 4.0, (), jnp.float32)
    node_out = scatter_about(streams_of[10], (LATENT, LATENT), LATENT ** -0.5, 0.25)
    node_gain = jnp.clip(1.0 + 0.18 * jax.random.normal(streams_of[11], (LATENT,), jnp.float32), 0.1, 1.9)
    mesh_sender = scatter_about(streams_of[12], (LATENT, LATENT), LATENT ** -0.5, 0.25)
    mesh_receiver = scatter_about(streams_of[13], (LATENT, LATENT), LATENT ** -0.5, 0.25)
    message_bias = scatter_about(streams_of[14], (LATENT,), 1.0, 4.0, (), jnp.float32)
    message_out = scatter_about(streams_of[15], (LATENT, LATENT), (LATENT * 8) ** -0.5, 0.09375)
    update_input = scatter_about(streams_of[16], (2 * LATENT, LATENT), (2 * LATENT) ** -0.5, 0.1875)
    update_bias = scatter_about(streams_of[17], (LATENT,), 1.0, 4.0, (), jnp.float32)
    update_out = scatter_about(streams_of[18], (LATENT, LATENT), LATENT ** -0.5, 0.25)
    update_gain = jnp.clip(1.0 + 0.18 * jax.random.normal(streams_of[19], (LATENT,), jnp.float32), 0.1, 1.9)
    mesh_latent = scatter_about(streams_of[20], (MESH, LATENT), 1.0, 6.0, ((0, 16),))
    g2m_send = place_ends(jax.random.randint(streams_of[21], (GBLK, EB), 0, G_DEV), jax.random.fold_in(streams_of[21], 1), 0, G_DEV - 1).astype(jnp.int32)
    g2m_recv = draw_g2m_recv(jax.random.fold_in(streams_of[28], 71), part)
    g2m_feat = scatter_about(streams_of[23], (GBLK, EDGE_F, EB), 1.0, 6.0, ((0, 16),), jnp.float32)
    g2m_count = draw_g2m_count(jax.random.fold_in(streams_of[28], 71), part)
    mesh_slot = draw_mesh_slot(jax.random.fold_in(streams_of[28], 71), part)
    mesh_send = draw_mesh_send(jax.random.fold_in(streams_of[28], 71), part)
    mesh_recv = draw_mesh_recv(jax.random.fold_in(streams_of[28], 71), part)
    return dict(grid_in=grid_in, grid_first=grid_first, grid_bias=grid_bias, grid_second=grid_second, send_weight=send_weight, edge_bias=edge_bias, feat_weight=feat_weight, edge_out=edge_out, node_input=node_input, node_bias=node_bias, node_out=node_out, node_gain=node_gain, mesh_sender=mesh_sender, mesh_receiver=mesh_receiver, message_bias=message_bias, message_out=message_out, update_input=update_input, update_bias=update_bias, update_out=update_out, update_gain=update_gain, mesh_latent=mesh_latent, g2m_send=g2m_send, g2m_recv=g2m_recv, g2m_feat=g2m_feat, g2m_count=g2m_count, mesh_slot=mesh_slot, mesh_send=mesh_send, mesh_recv=mesh_recv)


def layer_norm(value):
    center = value - lax.optimization_barrier(jnp.mean(value, axis=-1, keepdims=True))
    spread = lax.optimization_barrier(jnp.mean(center * center, axis=-1, keepdims=True))
    return center * lax.rsqrt(spread + 1e-05)

def reference(grid_in, grid_first, grid_bias, grid_second, send_weight, edge_bias, feat_weight, edge_out, node_input, node_bias, node_out, node_gain, mesh_sender, mesh_receiver, message_bias, message_out, update_input, update_bias, update_out, update_gain, mesh_latent, g2m_send, g2m_recv, g2m_feat, g2m_count, mesh_slot, mesh_send, mesh_recv):
    f32 = jnp.float32
    bf16 = jnp.bfloat16
    grid_hidden = jax.nn.silu(jnp.dot(grid_in, grid_first, preferred_element_type=f32) + grid_bias).astype(bf16)
    grid_code = layer_norm(jnp.dot(grid_hidden, grid_second, preferred_element_type=f32)).astype(bf16)
    sender_part = (jnp.dot(grid_code, send_weight, preferred_element_type=f32) + edge_bias).astype(bf16)
    width = sender_part.shape[1]

    def one_device(index, total):
        start = (index * G2M_BLK).astype(jnp.int32)
        senders = lax.dynamic_slice_in_dim(g2m_send, start, G2M_BLK, 0).reshape(-1)
        receivers = lax.dynamic_slice_in_dim(g2m_recv, start, G2M_BLK, 0).reshape(-1)
        feats = lax.dynamic_slice_in_dim(g2m_feat, start, G2M_BLK, 0)
        rows = lax.dynamic_slice_in_dim(sender_part, (index * G_DEV).astype(jnp.int32), G_DEV, 0)
        extra = jnp.einsum('bfe,fl->bel', feats.astype(f32), feat_weight.astype(f32)).reshape(-1, width)
        hidden = jax.nn.silu(rows[senders].astype(f32) + extra).astype(bf16)
        keep = (jnp.arange(G2M_BLK, dtype=jnp.int32) < g2m_count[index]).astype(f32)
        weights = jnp.repeat(keep, EB)[:, None]
        return total.at[mesh_slot[receivers]].add(hidden.astype(f32) * weights)
    node_total = lax.fori_loop(0, N_BULK, one_device, jnp.zeros((MESH, width), f32))
    node_sum = node_total.astype(bf16)
    aggregate = jnp.dot(node_sum, edge_out, preferred_element_type=f32).astype(bf16)
    joined = jnp.concatenate([mesh_latent, aggregate], axis=1)
    node_hidden = jax.nn.silu(jnp.dot(joined, node_input, preferred_element_type=f32) + node_bias).astype(bf16)
    encoded = (mesh_latent.astype(f32) + layer_norm(jnp.dot(node_hidden, node_out, preferred_element_type=f32)) * node_gain).astype(bf16)
    sender_code = jnp.dot(encoded, mesh_sender, preferred_element_type=f32).astype(bf16)
    receiver_code = jnp.dot(encoded, mesh_receiver, preferred_element_type=f32) + message_bias
    send_rows = mesh_slot[mesh_send.reshape(-1)]
    recv_rows = mesh_slot[mesh_recv.reshape(-1)]
    message = jax.nn.silu(sender_code[send_rows].astype(f32) + receiver_code[recv_rows]).astype(bf16)
    message_total = jax.ops.segment_sum(message.astype(f32), recv_rows, num_segments=MESH)
    message_sum = message_total.astype(bf16)
    update = jnp.dot(message_sum, message_out, preferred_element_type=f32).astype(bf16)
    joined_two = jnp.concatenate([encoded, update], axis=1)
    update_hidden = jax.nn.silu(jnp.dot(joined_two, update_input, preferred_element_type=f32) + update_bias).astype(bf16)
    mesh_out = encoded.astype(f32) + layer_norm(jnp.dot(update_hidden, update_out, preferred_element_type=f32)) * update_gain
    return mesh_out.astype(bf16)
```

```python
import functools
import math

import jax
import jax.numpy as jnp
from jax import lax
from jax.experimental import pallas as pl
from jax.experimental.pallas import tpu as pltpu
from jax.sharding import PartitionSpec as P

F32 = jnp.float32
BF16 = jnp.bfloat16
I32 = jnp.int32
SEND_CAP = 16
LANES = 128
VMEM = pltpu.VMEM
SMEM = pltpu.SMEM
PARAMS = pltpu.CompilerParams(vmem_limit_bytes=40 * 1024 * 1024)


def mm(left, right):
    return jnp.dot(left, right, preferred_element_type=F32)


def mm_nt(left, right):
    return lax.dot_general(left, right, (((1,), (1,)), ((), ())), preferred_element_type=F32)


def silu_half(half):
    return half + half * jnp.tanh(half)


def silu(value):
    return silu_half(0.5 * value)


def layer_norm(value):
    center = value - jnp.mean(value, axis=-1, keepdims=True)
    spread = jnp.mean(center * center, axis=-1, keepdims=True)
    return center * lax.rsqrt(spread + 1e-05)


def iota(shape, dim):
    return lax.broadcasted_iota(I32, shape, dim)


def ids_of_rows(slot, first, count):
    nodes = slot.shape[1]
    rows = iota((count, nodes), 0) + first
    return jnp.max(jnp.where(slot == rows, iota((count, nodes), 1), -1), axis=1, keepdims=True)


def edge_kernel(
    place_ref,
    count_ref,
    grid_ref,
    first_ref,
    grid_bias_ref,
    second_ref,
    send_weight_ref,
    edge_bias_ref,
    feat_weight_ref,
    slot_ref,
    send_ref,
    recv_ref,
    feat_ref,
    below_ref,
    own_ref,
    above_ref,
    table,
    weight_t,
    bias_t,
    feat_weight_t,
    total,
):
    grid_rows = grid_ref.shape[0]
    width = second_ref.shape[1]
    blocks, block_edges = send_ref.shape
    owned = own_ref.shape[0]
    step_rows = 256
    weight_t[...] = (0.5 * send_weight_ref[...].astype(F32)).T.astype(BF16)
    bias_t[...] = jnp.broadcast_to(0.5 * edge_bias_ref[...], (LANES, width)).T
    feat_weight_t[...] = jnp.concatenate(
        [0.5 * feat_weight_ref[...].astype(F32), jnp.zeros((LANES - feat_weight_ref.shape[0], width), F32)],
        axis=0,
    ).T.astype(BF16)
    total[...] = jnp.zeros_like(total)

    def grid_step(step, carry):
        start = pl.multiple_of(step * step_rows, step_rows)
        value = grid_ref[pl.ds(start, step_rows), :]
        hidden = silu(mm(value, first_ref[...]) + grid_bias_ref[...]).astype(BF16)
        code = layer_norm(mm(hidden, second_ref[...])).astype(BF16)
        bias = jnp.concatenate([bias_t[...]] * (step_rows // LANES), axis=1)
        table[:, pl.ds(start, step_rows)] = (mm_nt(weight_t[...], code) + bias).astype(BF16)
        return carry

    lax.fori_loop(0, grid_rows // step_rows, grid_step, 0)

    ids = ids_of_rows(slot_ref[...], (place_ref[0] - 1) * owned, 3 * owned)
    used = count_ref[0]
    group = math.gcd(blocks, 2)
    feats = feat_ref.shape[1]

    def edge_step(step, carry):
        first = step * group
        senders = jnp.concatenate([send_ref[pl.ds(first + b, 1), :] for b in range(group)], axis=1)
        picker = (senders == iota((grid_rows, group * block_edges), 0)).astype(F32).astype(BF16)
        feat = jnp.concatenate([feat_ref[first + b] for b in range(group)], axis=1)
        half = mm(table[...], picker) + mm(feat_weight_t[:, :feats], feat.astype(BF16))
        hidden = silu_half(half).astype(BF16)
        spread = jnp.concatenate(
            [
                (ids == jnp.where(first + b < used, recv_ref[pl.ds(first + b, 1), :], -2))
                for b in range(group)
            ],
            axis=1,
        )
        total[...] += mm_nt(spread.astype(F32).astype(BF16), hidden)
        return carry

    lax.fori_loop(0, blocks // group, edge_step, 0)
    below_ref[...] = total[:owned].astype(BF16)
    own_ref[...] = total[owned : 2 * owned]
    above_ref[...] = total[2 * owned :].astype(BF16)


def wanted_kernel(owned, slot_ref, send_ref, wanted_ref):
    nodes = slot_ref.shape[1]
    blocks, block_edges = send_ref.shape
    places = wanted_ref.shape[1]
    chunk = LANES
    per_chunk = chunk // owned * SEND_CAP
    row, column = iota((chunk, chunk), 0), iota((chunk, chunk), 1)
    before = ((row > column) & (row // owned == column // owned)).astype(F32).astype(BF16)
    local_owner = (iota((chunk, LANES), 0) // owned * SEND_CAP).astype(F32)

    def find(index, best):
        ids = ids_of_rows(slot_ref[...], index * chunk, chunk)
        hit = jnp.zeros((chunk, block_edges), F32)
        for b in range(blocks):
            hit = jnp.maximum(hit, (ids == send_ref[b : b + 1, :]).astype(F32))
        hit = jnp.broadcast_to(jnp.max(hit, axis=1, keepdims=True), (chunk, LANES))
        rank = mm(before, hit.astype(BF16)) + local_owner
        spot = jnp.where(hit > 0, rank.astype(I32) + index * per_chunk, -1)
        spot = jnp.concatenate([spot] * (places // LANES), axis=1)
        found = jnp.where(spot == iota((chunk, places), 1), ids, -1)
        return jnp.maximum(best, jnp.max(found, axis=0, keepdims=True))

    best = lax.fori_loop(0, nodes // chunk, find, jnp.full((1, places), -1, I32))
    best = best.astype(F32)
    for b in range(blocks):
        senders = jnp.broadcast_to(send_ref[b : b + 1, :].astype(F32), (block_edges, block_edges)).T
        senders = jnp.concatenate([senders] * (places // LANES), axis=1)
        wanted_ref[b * block_edges : (b + 1) * block_edges, :] = (
            (senders == best).astype(F32).astype(BF16)
        )


def supply_kernel(place_ref, slot_ref, request_ref, supply_ref):
    owned = supply_ref.shape[1]
    devices = supply_ref.shape[0] // SEND_CAP
    per_device = request_ref.shape[0] // devices
    ids = ids_of_rows(slot_ref[...], place_ref[0] * owned, owned)
    lane = iota((owned, LANES), 1)
    used = jnp.zeros((owned, LANES), F32)
    for d in range(devices):
        hit = jnp.zeros((owned, request_ref.shape[1]), F32)
        for b in range(per_device):
            at = d * per_device + b
            hit = jnp.maximum(hit, (ids == request_ref[at : at + 1, :]).astype(F32))
        used = jnp.where(lane == d, jnp.max(hit, axis=1, keepdims=True), used)
    before = (iota((owned, owned), 0) > iota((owned, owned), 1)).astype(F32).astype(BF16)
    rank = jnp.where(used > 0, mm(before, used.astype(BF16)), -1.0)
    rank = jnp.concatenate([rank, jnp.full((LANES - owned, LANES), -1.0, F32)], axis=0).T
    slots = iota((SEND_CAP, owned), 0).astype(F32)
    for d in range(devices):
        supply_ref[d * SEND_CAP : (d + 1) * SEND_CAP, :] = (
            (rank[d : d + 1, :owned] == slots).astype(F32).astype(BF16)
        )


def node_kernel(
    own_ref,
    from_below_ref,
    from_above_ref,
    latent_ref,
    edge_out_ref,
    node_input_ref,
    node_bias_ref,
    node_out_ref,
    node_gain_ref,
    mesh_sender_ref,
    mesh_receiver_ref,
    message_bias_ref,
    supply_ref,
    rows_ref,
    encoded_ref,
    receiver_ref,
):
    width = latent_ref.shape[1]
    latent = latent_ref[...]
    node_sum = own_ref[...] + from_below_ref[...].astype(F32) + from_above_ref[...].astype(F32)
    aggregate = mm(node_sum.astype(BF16), edge_out_ref[...]).astype(BF16)
    hidden = mm(latent, node_input_ref[:width]) + mm(aggregate, node_input_ref[width:])
    hidden = silu(hidden + node_bias_ref[...]).astype(BF16)
    encoded = latent.astype(F32) + layer_norm(mm(hidden, node_out_ref[...])) * node_gain_ref[...]
    encoded = encoded.astype(BF16)
    encoded_ref[...] = encoded
    sender_code = mm(encoded, mesh_sender_ref[...]).astype(BF16)
    rows_ref[...] = mm(supply_ref[...], sender_code).astype(BF16)
    receiver_ref[...] = mm(encoded, mesh_receiver_ref[...]) + message_bias_ref[...]


def message_kernel(
    place_ref,
    slot_ref,
    recv_ref,
    wanted_ref,
    piece_ref,
    encoded_ref,
    receiver_ref,
    message_out_ref,
    update_input_ref,
    update_bias_ref,
    update_out_ref,
    update_gain_ref,
    out_ref,
):
    owned, width = encoded_ref.shape
    blocks = recv_ref.shape[0]
    ids = ids_of_rows(slot_ref[...], place_ref[0] * owned, owned)
    incoming = jnp.concatenate(
        [(ids == recv_ref[b : b + 1, :]).astype(F32) for b in range(blocks)], axis=1
    )
    pick = incoming.T.astype(BF16)
    incoming = incoming.astype(BF16)
    receiver = receiver_ref[...]
    high = receiver.astype(BF16)
    low = (receiver - high.astype(F32)).astype(BF16)
    encoded = encoded_ref[...]
    value = mm(wanted_ref[...], piece_ref[...]) + (mm(pick, high) + mm(pick, low))
    message = silu(value).astype(BF16)
    message_sum = mm(incoming, message).astype(BF16)
    update = mm(message_sum, message_out_ref[...]).astype(BF16)
    hidden = mm(encoded, update_input_ref[:width]) + mm(update, update_input_ref[width:])
    hidden = silu(hidden + update_bias_ref[...]).astype(BF16)
    out = encoded.astype(F32) + layer_norm(mm(hidden, update_out_ref[...])) * update_gain_ref[...]
    out_ref[...] = out.astype(BF16)


def call(kernel, out_shape, spaces, scratch=(), flops=0, moved=0):
    return pl.pallas_call(
        kernel,
        out_shape=out_shape,
        in_specs=[pl.BlockSpec(memory_space=space) for space in spaces],
        out_specs=jax.tree.map(lambda _: pl.BlockSpec(memory_space=VMEM), out_shape),
        scratch_shapes=scratch,
        compiler_params=PARAMS,
        cost_estimate=pl.CostEstimate(flops=flops, bytes_accessed=moved, transcendentals=0),
    )


def shape(*sizes, kind=BF16):
    return jax.ShapeDtypeStruct(sizes, kind)


def per_device(
    grid_in,
    grid_first,
    grid_bias,
    grid_second,
    send_weight,
    edge_bias,
    feat_weight,
    edge_out,
    node_input,
    node_bias,
    node_out,
    node_gain,
    mesh_sender,
    mesh_receiver,
    message_bias,
    message_out,
    update_input,
    update_bias,
    update_out,
    update_gain,
    mesh_latent,
    g2m_send,
    g2m_recv,
    g2m_feat,
    g2m_count,
    mesh_slot,
    mesh_send,
    mesh_recv,
):
    devices = lax.axis_size("bulk")
    position = lax.axis_index("bulk")
    place = position.astype(I32).reshape(1)
    owned, width = mesh_latent.shape
    grid_rows = grid_in.shape[0]
    places = devices * SEND_CAP
    edges = mesh_send.size
    slot = mesh_slot.reshape(1, -1)
    row = lambda vector: vector.reshape(1, -1)

    requests = lax.all_gather(mesh_send, "bulk", axis=0, tiled=True)

    below, own, above = call(
        edge_kernel,
        (shape(owned, width), shape(owned, width, kind=F32), shape(owned, width)),
        [SMEM, SMEM] + [VMEM] * 11,
        scratch=[
            pltpu.VMEM((width, grid_rows), BF16),
            pltpu.VMEM((width, width), BF16),
            pltpu.VMEM((width, LANES), F32),
            pltpu.VMEM((width, LANES), BF16),
            pltpu.VMEM((3 * owned, width), F32),
        ],
        flops=10_000_000_000,
        moved=4_000_000,
    )(
        place,
        g2m_count,
        grid_in,
        grid_first,
        row(grid_bias),
        grid_second,
        send_weight,
        row(edge_bias),
        feat_weight,
        slot,
        g2m_send,
        g2m_recv,
        g2m_feat,
    )
    from_below = lax.ppermute(above, "bulk", [(d, d + 1) for d in range(devices - 1)])
    from_above = lax.ppermute(below, "bulk", [(d + 1, d) for d in range(devices - 1)])
    wanted = call(
        functools.partial(wanted_kernel, owned),
        shape(edges, places),
        [VMEM] * 2,
        flops=1_000_000_000,
        moved=500_000,
    )(slot, mesh_send)
    supply = call(
        supply_kernel,
        shape(places, owned),
        [SMEM] + [VMEM] * 2,
        flops=500_000_000,
        moved=500_000,
    )(place, slot, requests)
    rows, encoded, receiver = call(
        node_kernel,
        (shape(places, width), shape(owned, width), shape(owned, width, kind=F32)),
        [VMEM] * 13,
        flops=500_000_000,
        moved=4_000_000,
    )(
        own,
        from_below,
        from_above,
        mesh_latent,
        edge_out,
        node_input,
        row(node_bias),
        node_out,
        row(node_gain),
        mesh_sender,
        mesh_receiver,
        row(message_bias),
        supply,
    )
    piece = lax.all_to_all(rows, "bulk", 0, 0, tiled=True)
    return call(
        message_kernel,
        shape(owned, width),
        [SMEM] + [VMEM] * 11,
        flops=1_000_000_000,
        moved=4_000_000,
    )(
        place,
        slot,
        mesh_recv,
        wanted,
        piece,
        encoded,
        receiver,
        message_out,
        update_input,
        row(update_bias),
        update_out,
        row(update_gain),
    )


def solution(mesh):
    split = {0: ("groups", "bulk"), 20: "bulk", 21: "bulk", 22: "bulk", 23: "bulk", 24: "bulk"}
    split.update({26: "bulk", 27: "bulk"})
    placed = tuple(P(split[at]) if at in split else P() for at in range(28))
    return jax.shard_map(
        per_device,
        mesh=mesh,
        in_specs=placed,
        out_specs=P(("groups", "bulk"), None),
        check_vma=False,
    )
```

```python
import functools
import math

import jax
import jax.numpy as jnp
from jax import lax
from jax.experimental import pallas as pl
from jax.experimental.pallas import tpu as pltpu
from jax.sharding import PartitionSpec as P

F32 = jnp.float32
BF16 = jnp.bfloat16
I32 = jnp.int32
SEND_CAP = 16
LANES = 128
VMEM = pltpu.VMEM
SMEM = pltpu.SMEM
PARAMS = pltpu.CompilerParams(vmem_limit_bytes=40 * 1024 * 1024)


def mm(left, right):
    return jnp.dot(left, right, preferred_element_type=F32)


def mm_nt(left, right):
    return lax.dot_general(left, right, (((1,), (1,)), ((), ())), preferred_element_type=F32)


def silu_half(half):
    return half + half * jnp.tanh(half)


def silu(value):
    return silu_half(0.5 * value)


def layer_norm(value):
    center = value - jnp.mean(value, axis=-1, keepdims=True)
    spread = jnp.mean(center * center, axis=-1, keepdims=True)
    return center * lax.rsqrt(spread + 1e-05)


def iota(shape, dim):
    return lax.broadcasted_iota(I32, shape, dim)


def one_hot(columns, rows):
    hit = columns.astype(jnp.int16) == lax.broadcasted_iota(jnp.int16, (rows, columns.shape[1]), 0)
    return jnp.where(hit, jnp.ones((), BF16), jnp.zeros((), BF16))


def ids_of_rows(slot, first, count):
    nodes = slot.shape[1]
    rows = iota((count, nodes), 0) + first
    return jnp.max(jnp.where(slot == rows, iota((count, nodes), 1), -1), axis=1, keepdims=True)


def grid_kernel(
    grid_ref,
    first_ref,
    grid_bias_ref,
    second_ref,
    send_weight_ref,
    edge_bias_ref,
    table_ref,
):
    channels, grid_rows = grid_ref.shape
    width = second_ref.shape[1]
    step_rows = 512
    first_t = (0.5 * first_ref[...].astype(F32)).T.astype(BF16)
    second_t = second_ref[...].T
    weight_t = (0.5 * send_weight_ref[...].astype(F32)).T.astype(BF16)
    grid_bias = jnp.broadcast_to(0.5 * grid_bias_ref[...], (LANES, width)).T
    edge_bias = jnp.broadcast_to(0.5 * edge_bias_ref[...], (LANES, width)).T
    wide = lambda column: jnp.concatenate([column] * (step_rows // LANES), axis=1)
    for start in range(0, grid_rows, step_rows):
        half = mm(first_t, grid_ref[:, start : start + step_rows]) + wide(grid_bias)
        value = mm(second_t, silu_half(half).astype(BF16))
        center = value - jnp.mean(value, axis=0, keepdims=True)
        spread = jnp.mean(center * center, axis=0, keepdims=True)
        code = (center * lax.rsqrt(spread + 1e-05)).astype(BF16)
        part = mm(weight_t, code) + wide(edge_bias)
        table_ref[:, start : start + step_rows] = part.astype(BF16)


def edge_kernel(
    place_ref,
    count_ref,
    table_ref,
    feat_weight_ref,
    slot_ref,
    send_ref,
    recv_ref,
    feat_ref,
    own_ref,
    cross_ref,
    chip_ref,
    total,
):
    grid_rows = table_ref.shape[1]
    width = table_ref.shape[0]
    blocks, block_edges = send_ref.shape
    owned = own_ref.shape[0]
    feats = feat_ref.shape[1]
    place = place_ref[0]
    used = count_ref[0]
    feat_weight = jnp.concatenate(
        [0.5 * feat_weight_ref[...].astype(F32), jnp.zeros((LANES - feats, width), F32)], axis=0
    )
    feat_weight = feat_weight.T.astype(BF16)[:, :feats]
    ids = ids_of_rows(slot_ref[...], (place - 1) * owned, 3 * owned)
    group = math.gcd(blocks, 4)
    total[...] = jnp.zeros_like(total)

    def edge_step(step, carry):
        first = step * group
        senders = jnp.concatenate([send_ref[pl.ds(first + b, 1), :] for b in range(group)], axis=1)
        picker = one_hot(senders, grid_rows)
        feat = jnp.concatenate([feat_ref[first + b] for b in range(group)], axis=1)
        half = mm(table_ref[...], picker) + mm(feat_weight, feat.astype(BF16))
        hidden = silu_half(half).astype(BF16)
        receivers = jnp.concatenate(
            [
                jnp.where(first + b < used, recv_ref[pl.ds(first + b, 1), :], -2)
                for b in range(group)
            ],
            axis=1,
        )
        spread = (ids == receivers).astype(F32).astype(BF16)
        total[...] += mm_nt(hidden, spread)
        return carry

    lax.fori_loop(0, blocks // group, edge_step, 0)
    pad = -3 * owned % LANES
    sums = jnp.concatenate([total[...], jnp.zeros((width, pad), F32)], axis=1).T
    below, above = sums[:owned].astype(BF16), sums[2 * owned : 3 * owned].astype(BF16)
    own_ref[...] = sums[owned : 2 * owned]
    odd = place % 2 == 1
    cross_ref[...] = jnp.where(odd, above, below)
    chip_ref[...] = jnp.where(odd, below, above)


def wanted_kernel(owned, slot_ref, send_ref, wanted_ref):
    nodes = slot_ref.shape[1]
    blocks, block_edges = send_ref.shape
    places = wanted_ref.shape[1]
    chunk = LANES
    per_chunk = chunk // owned * SEND_CAP
    row, column = iota((chunk, chunk), 0), iota((chunk, chunk), 1)
    before = ((row > column) & (row // owned == column // owned)).astype(F32).astype(BF16)
    local_owner = (iota((chunk, LANES), 0) // owned * SEND_CAP).astype(F32)

    def find(index, best):
        ids = ids_of_rows(slot_ref[...], index * chunk, chunk)
        hit = jnp.zeros((chunk, block_edges), F32)
        for b in range(blocks):
            hit = jnp.maximum(hit, (ids == send_ref[b : b + 1, :]).astype(F32))
        hit = jnp.broadcast_to(jnp.max(hit, axis=1, keepdims=True), (chunk, LANES))
        rank = mm(before, hit.astype(BF16)) + local_owner
        spot = jnp.where(hit > 0, rank.astype(I32) + index * per_chunk, -1)
        spot = jnp.concatenate([spot] * (places // LANES), axis=1)
        found = jnp.where(spot == iota((chunk, places), 1), ids, -1)
        return jnp.maximum(best, jnp.max(found, axis=0, keepdims=True))

    best = lax.fori_loop(0, nodes // chunk, find, jnp.full((1, places), -1, I32))
    best = best.astype(F32)
    for b in range(blocks):
        senders = jnp.broadcast_to(send_ref[b : b + 1, :].astype(F32), (block_edges, block_edges)).T
        senders = jnp.concatenate([senders] * (places // LANES), axis=1)
        wanted_ref[b * block_edges : (b + 1) * block_edges, :] = (
            (senders == best).astype(F32).astype(BF16)
        )


def supply_kernel(place_ref, slot_ref, request_ref, code_ref, rows_ref):
    owned = code_ref.shape[0]
    devices = rows_ref.shape[0] // SEND_CAP
    per_device = request_ref.shape[0] // devices
    ids = ids_of_rows(slot_ref[...], place_ref[0] * owned, owned)
    lane = iota((owned, LANES), 1)
    used = jnp.zeros((owned, LANES), F32)
    for d in range(devices):
        hit = jnp.zeros((owned, request_ref.shape[1]), F32)
        for b in range(per_device):
            at = d * per_device + b
            hit = jnp.maximum(hit, (ids == request_ref[at : at + 1, :]).astype(F32))
        used = jnp.where(lane == d, jnp.max(hit, axis=1, keepdims=True), used)
    before = (iota((owned, owned), 0) > iota((owned, owned), 1)).astype(F32).astype(BF16)
    rank = jnp.where(used > 0, mm(before, used.astype(BF16)), -1.0)
    rank = jnp.concatenate([rank, jnp.full((LANES - owned, LANES), -1.0, F32)], axis=0).T
    slots = iota((SEND_CAP, owned), 0).astype(F32)
    supply = jnp.concatenate(
        [(rank[d : d + 1, :owned] == slots).astype(F32) for d in range(devices)], axis=0
    )
    rows_ref[...] = mm(supply.astype(BF16), code_ref[...]).astype(BF16)


def node_kernel(
    own_ref,
    from_cross_ref,
    from_chip_ref,
    latent_ref,
    edge_out_ref,
    node_input_ref,
    node_bias_ref,
    node_out_ref,
    node_gain_ref,
    mesh_sender_ref,
    encoded_ref,
    code_ref,
):
    width = latent_ref.shape[1]
    latent = latent_ref[...]
    node_sum = own_ref[...] + from_cross_ref[...].astype(F32) + from_chip_ref[...].astype(F32)
    aggregate = mm(node_sum.astype(BF16), edge_out_ref[...]).astype(BF16)
    hidden = mm(latent, node_input_ref[:width]) + mm(aggregate, node_input_ref[width:])
    hidden = silu(hidden + node_bias_ref[...]).astype(BF16)
    encoded = latent.astype(F32) + layer_norm(mm(hidden, node_out_ref[...])) * node_gain_ref[...]
    encoded = encoded.astype(BF16)
    encoded_ref[...] = encoded
    code_ref[...] = mm(encoded, mesh_sender_ref[...]).astype(BF16)


def receiver_kernel(
    place_ref,
    slot_ref,
    recv_ref,
    encoded_ref,
    mesh_receiver_ref,
    message_bias_ref,
    update_input_ref,
    update_bias_ref,
    incoming_ref,
    receiver_ref,
    upper_ref,
):
    owned, width = encoded_ref.shape
    blocks = recv_ref.shape[0]
    ids = ids_of_rows(slot_ref[...], place_ref[0] * owned, owned)
    incoming = jnp.concatenate(
        [(ids == recv_ref[b : b + 1, :]).astype(F32) for b in range(blocks)], axis=1
    )
    pick = incoming.T.astype(BF16)
    incoming_ref[...] = incoming.astype(BF16)
    encoded = encoded_ref[...]
    receiver = mm(encoded, mesh_receiver_ref[...]) + message_bias_ref[...]
    high = receiver.astype(BF16)
    low = (receiver - high.astype(F32)).astype(BF16)
    receiver_ref[...] = mm(pick, high) + mm(pick, low)
    upper_ref[...] = mm(encoded, update_input_ref[:width]) + update_bias_ref[...]


def message_kernel(
    wanted_ref,
    piece_ref,
    incoming_ref,
    receiver_ref,
    upper_ref,
    encoded_ref,
    message_out_ref,
    update_input_ref,
    update_out_ref,
    update_gain_ref,
    out_ref,
):
    width = encoded_ref.shape[1]
    message = silu(mm(wanted_ref[...], piece_ref[...]) + receiver_ref[...]).astype(BF16)
    message_sum = mm(incoming_ref[...], message).astype(BF16)
    update = mm(message_sum, message_out_ref[...]).astype(BF16)
    hidden = silu(upper_ref[...] + mm(update, update_input_ref[width:])).astype(BF16)
    out = layer_norm(mm(hidden, update_out_ref[...])) * update_gain_ref[...]
    out_ref[...] = (encoded_ref[...].astype(F32) + out).astype(BF16)


def call(kernel, out_shape, spaces, scratch=(), flops=0, moved=0):
    return pl.pallas_call(
        kernel,
        out_shape=out_shape,
        in_specs=[pl.BlockSpec(memory_space=space) for space in spaces],
        out_specs=jax.tree.map(lambda _: pl.BlockSpec(memory_space=VMEM), out_shape),
        scratch_shapes=scratch,
        compiler_params=PARAMS,
        cost_estimate=pl.CostEstimate(flops=flops, bytes_accessed=moved, transcendentals=0),
    )


def shape(*sizes, kind=BF16):
    return jax.ShapeDtypeStruct(sizes, kind)


def per_device(
    grid_in,
    grid_first,
    grid_bias,
    grid_second,
    send_weight,
    edge_bias,
    feat_weight,
    edge_out,
    node_input,
    node_bias,
    node_out,
    node_gain,
    mesh_sender,
    mesh_receiver,
    message_bias,
    message_out,
    update_input,
    update_bias,
    update_out,
    update_gain,
    mesh_latent,
    g2m_send,
    g2m_recv,
    g2m_feat,
    g2m_count,
    mesh_slot,
    mesh_send,
    mesh_recv,
):
    devices = lax.axis_size("bulk")
    position = lax.axis_index("bulk")
    place = position.astype(I32).reshape(1)
    owned, width = mesh_latent.shape
    grid_rows = grid_in.shape[0]
    places = devices * SEND_CAP
    edges = mesh_send.size
    slot = mesh_slot.reshape(1, -1)
    row = lambda vector: vector.reshape(1, -1)

    table = call(
        grid_kernel,
        shape(width, grid_rows),
        [VMEM] * 6,
        flops=3_000_000_000,
        moved=4_000_000,
    )(grid_in.T, grid_first, row(grid_bias), grid_second, send_weight, row(edge_bias))
    own, cross, chip = call(
        edge_kernel,
        (shape(owned, width, kind=F32), shape(owned, width), shape(owned, width)),
        [SMEM, SMEM] + [VMEM] * 6,
        scratch=[pltpu.VMEM((width, 3 * owned), F32)],
        flops=7_000_000_000,
        moved=4_000_000,
    )(place, g2m_count, table, feat_weight, slot, g2m_send, g2m_recv, g2m_feat)
    crossing = [(d, d + 1) for d in range(1, devices - 1, 2)]
    within = [(d, d + 1) for d in range(0, devices, 2)]
    both = lambda pairs: pairs + [(b, a) for a, b in pairs]
    from_cross = lax.ppermute(cross, "bulk", both(crossing))
    from_chip = lax.ppermute(chip, "bulk", both(within))
    asked = jnp.tile(mesh_send, (devices, 1))
    asked, _ = lax.optimization_barrier((asked, chip))
    requests = lax.all_to_all(asked, "bulk", 0, 0, tiled=True)
    encoded, code = call(
        node_kernel,
        (shape(owned, width), shape(owned, width)),
        [VMEM] * 10,
        flops=500_000_000,
        moved=4_000_000,
    )(
        own,
        from_cross,
        from_chip,
        mesh_latent,
        edge_out,
        node_input,
        row(node_bias),
        node_out,
        row(node_gain),
        mesh_sender,
    )
    rows = call(
        supply_kernel,
        shape(places, width),
        [SMEM] + [VMEM] * 3,
        flops=500_000_000,
        moved=500_000,
    )(place, slot, requests, code)
    piece = lax.all_to_all(rows, "bulk", 0, 0, tiled=True)
    wanted = call(
        functools.partial(wanted_kernel, owned),
        shape(edges, places),
        [VMEM] * 2,
        flops=1_000_000_000,
        moved=500_000,
    )(slot, mesh_send)
    incoming, receiver, upper = call(
        receiver_kernel,
        (shape(owned, edges), shape(edges, width, kind=F32), shape(owned, width, kind=F32)),
        [SMEM] + [VMEM] * 7,
        flops=1_000_000_000,
        moved=4_000_000,
    )(
        place,
        slot,
        mesh_recv,
        encoded,
        mesh_receiver,
        row(message_bias),
        update_input,
        row(update_bias),
    )
    return call(
        message_kernel,
        shape(owned, width),
        [VMEM] * 10,
        flops=1_000_000_000,
        moved=4_000_000,
    )(
        wanted,
        piece,
        incoming,
        receiver,
        upper,
        encoded,
        message_out,
        update_input,
        update_out,
        row(update_gain),
    )


def solution(mesh):
    split = {0: ("groups", "bulk"), 20: "bulk", 21: "bulk", 22: "bulk", 23: "bulk", 24: "bulk"}
    split.update({26: "bulk", 27: "bulk"})
    placed = tuple(P(split[at]) if at in split else P() for at in range(28))
    return jax.shard_map(
        per_device,
        mesh=mesh,
        in_specs=placed,
        out_specs=P(("groups", "bulk"), None),
        check_vma=False,
    )
```

```python
import functools
import math

import jax
import jax.numpy as jnp
from jax import lax
from jax.experimental import pallas as pl
from jax.experimental.pallas import tpu as pltpu
from jax.sharding import PartitionSpec as P

F32 = jnp.float32
BF16 = jnp.bfloat16
I32 = jnp.int32
SEND_CAP = 16
LANES = 128
VMEM = pltpu.VMEM
SMEM = pltpu.SMEM
HBM = pltpu.HBM
GRID_STEPS = 4
MEBI = 1024 * 1024


def mm(left, right):
    return jnp.dot(left, right, preferred_element_type=F32)


def mm_nt(left, right):
    return lax.dot_general(left, right, (((1,), (1,)), ((), ())), preferred_element_type=F32)


def silu_half(half):
    return half + half * jnp.tanh(half)


def silu(value):
    return silu_half(0.5 * value)


def layer_norm(value):
    center = value - jnp.mean(value, axis=-1, keepdims=True)
    spread = jnp.mean(center * center, axis=-1, keepdims=True)
    return center * lax.rsqrt(spread + 1e-05)


def iota(shape, dim):
    return lax.broadcasted_iota(I32, shape, dim)


def one_hot(columns, rows):
    hit = columns.astype(jnp.int16) == lax.broadcasted_iota(jnp.int16, (rows, columns.shape[1]), 0)
    return jnp.where(hit, jnp.ones((), BF16), jnp.zeros((), BF16))


def ids_of_rows(slot, first, count):
    nodes = slot.shape[1]
    rows = iota((count, nodes), 0) + first
    return jnp.max(jnp.where(slot == rows, iota((count, nodes), 1), -1), axis=1, keepdims=True)


def grid_kernel(
    grid_hbm,
    first_hbm,
    grid_bias_hbm,
    second_hbm,
    send_weight_hbm,
    edge_bias_hbm,
    table_ref,
    grid_ref,
    first_ref,
    grid_bias_ref,
    second_ref,
    send_weight_ref,
    edge_bias_ref,
    sems,
):
    channels, grid_rows = grid_ref.shape
    width = second_ref.shape[1]
    step_rows = grid_rows // GRID_STEPS
    columns = [pl.ds(step * step_rows, step_rows) for step in range(GRID_STEPS)]
    pairs = [
        (first_hbm, first_ref),
        (grid_bias_hbm, grid_bias_ref),
        (grid_hbm.at[:, columns[0]], grid_ref.at[:, columns[0]]),
        (second_hbm, second_ref),
        (send_weight_hbm, send_weight_ref),
        (edge_bias_hbm, edge_bias_ref),
    ] + [(grid_hbm.at[:, part], grid_ref.at[:, part]) for part in columns[1:]]
    copies = [
        pltpu.make_async_copy(source, target, sems.at[at])
        for at, (source, target) in enumerate(pairs)
    ]
    for copy in copies:
        copy.start()
    column = lambda ref: jnp.broadcast_to(0.5 * ref[...], (LANES, width)).T
    wide = lambda value: jnp.concatenate([value] * (step_rows // LANES), axis=1)
    for copy in copies[:2]:
        copy.wait()
    first_t = (0.5 * first_ref[...].astype(F32)).T.astype(BF16)
    grid_bias = column(grid_bias_ref)
    for step, part in enumerate(columns):
        copies[2 if step == 0 else 5 + step].wait()
        half = mm(first_t, grid_ref[:, part]) + wide(grid_bias)
        hidden = silu_half(half).astype(BF16)
        if step == 0:
            for copy in copies[3:6]:
                copy.wait()
            second_t = second_ref[...].T
            weight_t = (0.5 * send_weight_ref[...].astype(F32)).T.astype(BF16)
            edge_bias = column(edge_bias_ref)
        value = mm(second_t, hidden)
        center = value - jnp.mean(value, axis=0, keepdims=True)
        spread = jnp.mean(center * center, axis=0, keepdims=True)
        code = (center * lax.rsqrt(spread + 1e-05)).astype(BF16)
        table_ref[:, part] = (mm(weight_t, code) + wide(edge_bias)).astype(BF16)


def edge_kernel(
    place_ref,
    count_ref,
    table_ref,
    feat_weight_ref,
    slot_ref,
    send_ref,
    recv_ref,
    feat_ref,
    own_ref,
    cross_ref,
    chip_ref,
    total,
):
    grid_rows = table_ref.shape[1]
    width = table_ref.shape[0]
    blocks, block_edges = send_ref.shape
    owned = own_ref.shape[0]
    feats = feat_ref.shape[1]
    place = place_ref[0]
    used = count_ref[0]
    feat_weight = jnp.concatenate(
        [0.5 * feat_weight_ref[...].astype(F32), jnp.zeros((LANES - feats, width), F32)], axis=0
    )
    feat_weight = feat_weight.T.astype(BF16)[:, :feats]
    ids = ids_of_rows(slot_ref[...], (place - 1) * owned, 3 * owned)
    group = math.gcd(blocks, 4)
    total[...] = jnp.zeros_like(total)

    def edge_step(step, carry):
        first = step * group
        senders = jnp.concatenate([send_ref[pl.ds(first + b, 1), :] for b in range(group)], axis=1)
        picker = one_hot(senders, grid_rows)
        feat = jnp.concatenate([feat_ref[first + b] for b in range(group)], axis=1)
        half = mm(table_ref[...], picker) + mm(feat_weight, feat.astype(BF16))
        hidden = silu_half(half).astype(BF16)
        receivers = jnp.concatenate(
            [
                jnp.where(first + b < used, recv_ref[pl.ds(first + b, 1), :], -2)
                for b in range(group)
            ],
            axis=1,
        )
        spread = (ids == receivers).astype(F32).astype(BF16)
        total[...] += mm_nt(hidden, spread)
        return carry

    lax.fori_loop(0, blocks // group, edge_step, 0)
    pad = -3 * owned % LANES
    sums = jnp.concatenate([total[...], jnp.zeros((width, pad), F32)], axis=1).T
    below, above = sums[:owned].astype(BF16), sums[2 * owned : 3 * owned].astype(BF16)
    own_ref[...] = sums[owned : 2 * owned]
    odd = place % 2 == 1
    cross_ref[...] = jnp.where(odd, above, below)
    chip_ref[...] = jnp.where(odd, below, above)


def wanted_kernel(owned, slot_ref, send_ref, wanted_ref):
    nodes = slot_ref.shape[1]
    blocks, block_edges = send_ref.shape
    places = wanted_ref.shape[1]
    chunk = LANES
    per_chunk = chunk // owned * SEND_CAP
    row, column = iota((chunk, chunk), 0), iota((chunk, chunk), 1)
    before = ((row > column) & (row // owned == column // owned)).astype(F32).astype(BF16)
    local_owner = (iota((chunk, LANES), 0) // owned * SEND_CAP).astype(F32)

    def find(index, best):
        ids = ids_of_rows(slot_ref[...], index * chunk, chunk)
        hit = jnp.zeros((chunk, block_edges), F32)
        for b in range(blocks):
            hit = jnp.maximum(hit, (ids == send_ref[b : b + 1, :]).astype(F32))
        hit = jnp.broadcast_to(jnp.max(hit, axis=1, keepdims=True), (chunk, LANES))
        rank = mm(before, hit.astype(BF16)) + local_owner
        spot = jnp.where(hit > 0, rank.astype(I32) + index * per_chunk, -1)
        spot = jnp.concatenate([spot] * (places // LANES), axis=1)
        found = jnp.where(spot == iota((chunk, places), 1), ids, -1)
        return jnp.maximum(best, jnp.max(found, axis=0, keepdims=True))

    best = lax.fori_loop(0, nodes // chunk, find, jnp.full((1, places), -1, I32))
    best = best.astype(F32)
    for b in range(blocks):
        senders = jnp.broadcast_to(send_ref[b : b + 1, :].astype(F32), (block_edges, block_edges)).T
        senders = jnp.concatenate([senders] * (places // LANES), axis=1)
        wanted_ref[b * block_edges : (b + 1) * block_edges, :] = (
            (senders == best).astype(F32).astype(BF16)
        )


def supply_kernel(place_ref, slot_ref, request_ref, supply_ref):
    owned = supply_ref.shape[1]
    devices = supply_ref.shape[0] // SEND_CAP
    per_device = request_ref.shape[0] // devices
    ids = ids_of_rows(slot_ref[...], place_ref[0] * owned, owned)
    lane = iota((owned, LANES), 1)
    used = jnp.zeros((owned, LANES), F32)
    for d in range(devices):
        hit = jnp.zeros((owned, request_ref.shape[1]), F32)
        for b in range(per_device):
            at = d * per_device + b
            hit = jnp.maximum(hit, (ids == request_ref[at : at + 1, :]).astype(F32))
        used = jnp.where(lane == d, jnp.max(hit, axis=1, keepdims=True), used)
    before = (iota((owned, owned), 0) > iota((owned, owned), 1)).astype(F32).astype(BF16)
    rank = jnp.where(used > 0, mm(before, used.astype(BF16)), -1.0)
    rank = jnp.concatenate([rank, jnp.full((LANES - owned, LANES), -1.0, F32)], axis=0).T
    slots = iota((SEND_CAP, owned), 0).astype(F32)
    supply = jnp.concatenate(
        [(rank[d : d + 1, :owned] == slots).astype(F32) for d in range(devices)], axis=0
    )
    supply_ref[...] = supply.astype(BF16)


def node_kernel(
    own_ref,
    from_cross_ref,
    from_chip_ref,
    latent_ref,
    edge_out_ref,
    node_input_ref,
    node_bias_ref,
    node_out_ref,
    node_gain_ref,
    mesh_sender_ref,
    supply_ref,
    encoded_ref,
    rows_ref,
):
    width = latent_ref.shape[1]
    latent = latent_ref[...]
    node_sum = own_ref[...] + from_cross_ref[...].astype(F32) + from_chip_ref[...].astype(F32)
    aggregate = mm(node_sum.astype(BF16), edge_out_ref[...]).astype(BF16)
    hidden = mm(latent, node_input_ref[:width]) + mm(aggregate, node_input_ref[width:])
    hidden = silu(hidden + node_bias_ref[...]).astype(BF16)
    encoded = latent.astype(F32) + layer_norm(mm(hidden, node_out_ref[...])) * node_gain_ref[...]
    encoded = encoded.astype(BF16)
    encoded_ref[...] = encoded
    sender_code = mm(encoded, mesh_sender_ref[...]).astype(BF16)
    rows_ref[...] = mm(supply_ref[...], sender_code).astype(BF16)


def receiver_kernel(
    place_ref,
    slot_ref,
    recv_ref,
    encoded_ref,
    mesh_receiver_ref,
    message_bias_ref,
    update_input_ref,
    update_bias_ref,
    incoming_ref,
    receiver_ref,
    upper_ref,
):
    owned, width = encoded_ref.shape
    blocks = recv_ref.shape[0]
    ids = ids_of_rows(slot_ref[...], place_ref[0] * owned, owned)
    incoming = jnp.concatenate(
        [(ids == recv_ref[b : b + 1, :]).astype(F32) for b in range(blocks)], axis=1
    )
    pick = incoming.T.astype(BF16)
    incoming_ref[...] = incoming.astype(BF16)
    encoded = encoded_ref[...]
    receiver = mm(encoded, mesh_receiver_ref[...]) + message_bias_ref[...]
    high = receiver.astype(BF16)
    low = (receiver - high.astype(F32)).astype(BF16)
    receiver_ref[...] = mm(pick, high) + mm(pick, low)
    upper_ref[...] = mm(encoded, update_input_ref[:width]) + update_bias_ref[...]


def message_kernel(
    wanted_ref,
    piece_ref,
    incoming_ref,
    receiver_ref,
    upper_ref,
    encoded_ref,
    message_out_ref,
    update_input_ref,
    update_out_ref,
    update_gain_ref,
    out_ref,
):
    width = encoded_ref.shape[1]
    message = silu(mm(wanted_ref[...], piece_ref[...]) + receiver_ref[...]).astype(BF16)
    message_sum = mm(incoming_ref[...], message).astype(BF16)
    update = mm(message_sum, message_out_ref[...]).astype(BF16)
    hidden = silu(upper_ref[...] + mm(update, update_input_ref[width:])).astype(BF16)
    out = layer_norm(mm(hidden, update_out_ref[...])) * update_gain_ref[...]
    out_ref[...] = (encoded_ref[...].astype(F32) + out).astype(BF16)


def call(kernel, out_shape, spaces, scratch=(), flops=0, moved=0, vmem=8):
    return pl.pallas_call(
        kernel,
        out_shape=out_shape,
        in_specs=[pl.BlockSpec(memory_space=space) for space in spaces],
        out_specs=jax.tree.map(lambda _: pl.BlockSpec(memory_space=VMEM), out_shape),
        scratch_shapes=scratch,
        compiler_params=pltpu.CompilerParams(vmem_limit_bytes=vmem * MEBI),
        cost_estimate=pl.CostEstimate(flops=flops, bytes_accessed=moved, transcendentals=0),
    )


def shape(*sizes, kind=BF16):
    return jax.ShapeDtypeStruct(sizes, kind)


def per_device(
    grid_in,
    grid_first,
    grid_bias,
    grid_second,
    send_weight,
    edge_bias,
    feat_weight,
    edge_out,
    node_input,
    node_bias,
    node_out,
    node_gain,
    mesh_sender,
    mesh_receiver,
    message_bias,
    message_out,
    update_input,
    update_bias,
    update_out,
    update_gain,
    mesh_latent,
    g2m_send,
    g2m_recv,
    g2m_feat,
    g2m_count,
    mesh_slot,
    mesh_send,
    mesh_recv,
):
    devices = lax.axis_size("bulk")
    position = lax.axis_index("bulk")
    place = position.astype(I32).reshape(1)
    owned, width = mesh_latent.shape
    grid_rows = grid_in.shape[0]
    places = devices * SEND_CAP
    edges = mesh_send.size
    slot = mesh_slot.reshape(1, -1)
    row = lambda vector: vector.reshape(1, -1)

    requests = lax.all_to_all(jnp.tile(mesh_send, (devices, 1)), "bulk", 0, 0, tiled=True)
    table = call(
        grid_kernel,
        shape(width, grid_rows),
        [HBM] * 6,
        scratch=[
            pltpu.VMEM(grid_in.shape[::-1], BF16),
            pltpu.VMEM(grid_first.shape, BF16),
            pltpu.VMEM((1, width), F32),
            pltpu.VMEM(grid_second.shape, BF16),
            pltpu.VMEM(send_weight.shape, BF16),
            pltpu.VMEM((1, width), F32),
            pltpu.SemaphoreType.DMA((5 + GRID_STEPS,)),
        ],
        flops=3_000_000_000,
        moved=4_000_000,
        vmem=56,
    )(grid_in.T, grid_first, row(grid_bias), grid_second, send_weight, row(edge_bias))
    table, requests = lax.optimization_barrier((table, requests))
    own, cross, chip = call(
        edge_kernel,
        (shape(owned, width, kind=F32), shape(owned, width), shape(owned, width)),
        [SMEM, SMEM] + [VMEM] * 6,
        scratch=[pltpu.VMEM((width, 3 * owned), F32)],
        flops=7_000_000_000,
        moved=4_000_000,
        vmem=16,
    )(place, g2m_count, table, feat_weight, slot, g2m_send, g2m_recv, g2m_feat)
    crossing = [(d, d + 1) for d in range(1, devices - 1, 2)]
    within = [(d, d + 1) for d in range(0, devices, 2)]
    both = lambda pairs: pairs + [(b, a) for a, b in pairs]
    from_cross = lax.ppermute(cross, "bulk", both(crossing))
    from_chip = lax.ppermute(chip, "bulk", both(within))
    requests, _ = lax.optimization_barrier((requests, own))
    supply = call(
        supply_kernel,
        shape(places, owned),
        [SMEM] + [VMEM] * 2,
        flops=500_000_000,
        moved=500_000,
    )(place, slot, requests)
    encoded, rows = call(
        node_kernel,
        (shape(owned, width), shape(places, width)),
        [VMEM] * 11,
        flops=500_000_000,
        moved=4_000_000,
    )(
        own,
        from_cross,
        from_chip,
        mesh_latent,
        edge_out,
        node_input,
        row(node_bias),
        node_out,
        row(node_gain),
        mesh_sender,
        supply,
    )
    piece = lax.all_to_all(rows, "bulk", 0, 0, tiled=True)
    mesh_send, _ = lax.optimization_barrier((mesh_send, encoded))
    wanted = call(
        functools.partial(wanted_kernel, owned),
        shape(edges, places),
        [VMEM] * 2,
        flops=1_000_000_000,
        moved=500_000,
    )(slot, mesh_send)
    incoming, receiver, upper = call(
        receiver_kernel,
        (shape(owned, edges), shape(edges, width, kind=F32), shape(owned, width, kind=F32)),
        [SMEM] + [VMEM] * 7,
        flops=1_000_000_000,
        moved=4_000_000,
    )(
        place,
        slot,
        mesh_recv,
        encoded,
        mesh_receiver,
        row(message_bias),
        update_input,
        row(update_bias),
    )
    return call(
        message_kernel,
        shape(owned, width),
        [VMEM] * 10,
        flops=1_000_000_000,
        moved=4_000_000,
    )(
        wanted,
        piece,
        incoming,
        receiver,
        upper,
        encoded,
        message_out,
        update_input,
        update_out,
        row(update_gain),
    )


def solution(mesh):
    split = {0: ("groups", "bulk"), 20: "bulk", 21: "bulk", 22: "bulk", 23: "bulk", 24: "bulk"}
    split.update({26: "bulk", 27: "bulk"})
    placed = tuple(P(split[at]) if at in split else P() for at in range(28))
    return jax.shard_map(
        per_device,
        mesh=mesh,
        in_specs=placed,
        out_specs=P(("groups", "bulk"), None),
        check_vma=False,
    )
```

```python
import functools
import math

import jax
import jax.numpy as jnp
from jax import lax
from jax.experimental import pallas as pl
from jax.experimental.pallas import tpu as pltpu
from jax.sharding import PartitionSpec as P

F32 = jnp.float32
BF16 = jnp.bfloat16
I32 = jnp.int32
SEND_CAP = 16
LANES = 128
VMEM = pltpu.VMEM
SMEM = pltpu.SMEM
HBM = pltpu.HBM
GRID_STEPS = 4
MEBI = 1024 * 1024


def mm(left, right):
    return jnp.dot(left, right, preferred_element_type=F32)


def mm_nt(left, right):
    return lax.dot_general(left, right, (((1,), (1,)), ((), ())), preferred_element_type=F32)


def silu_half(half):
    return half + half * jnp.tanh(half)


def silu(value):
    return silu_half(0.5 * value)


def layer_norm(value):
    center = value - jnp.mean(value, axis=-1, keepdims=True)
    spread = jnp.mean(center * center, axis=-1, keepdims=True)
    return center * lax.rsqrt(spread + 1e-05)


def iota(shape, dim):
    return lax.broadcasted_iota(I32, shape, dim)


def one_hot(columns, rows):
    hit = columns.astype(jnp.int16) == lax.broadcasted_iota(jnp.int16, (rows, columns.shape[1]), 0)
    return jnp.where(hit, jnp.ones((), BF16), jnp.zeros((), BF16))


def ids_of_rows(slot, first, count):
    nodes = slot.shape[1]
    rows = iota((count, nodes), 0) + first
    return jnp.max(jnp.where(slot == rows, iota((count, nodes), 1), -1), axis=1, keepdims=True)


def edge_kernel(
    place_ref,
    first_hbm,
    grid_bias_hbm,
    grid_hbm,
    second_hbm,
    send_weight_hbm,
    edge_bias_hbm,
    count_hbm,
    slot_hbm,
    feat_weight_hbm,
    send_hbm,
    recv_hbm,
    feat_hbm,
    mesh_send_hbm,
    own_ref,
    cross_ref,
    chip_ref,
    asked_ref,
    first_ref,
    grid_bias_ref,
    grid_ref,
    second_ref,
    send_weight_ref,
    edge_bias_ref,
    count_ref,
    slot_ref,
    feat_weight_ref,
    send_ref,
    recv_ref,
    feat_ref,
    mesh_send_ref,
    table,
    total,
    sems,
):
    channels, grid_rows = grid_ref.shape
    width = second_ref.shape[1]
    blocks, block_edges = send_ref.shape
    owned = own_ref.shape[0]
    feats = feat_ref.shape[1]
    step_rows = grid_rows // GRID_STEPS
    columns = [pl.ds(step * step_rows, step_rows) for step in range(GRID_STEPS)]
    pairs = [
        (first_hbm, first_ref),
        (grid_bias_hbm, grid_bias_ref),
        (grid_hbm.at[:, columns[0]], grid_ref.at[:, columns[0]]),
        (second_hbm, second_ref),
        (send_weight_hbm, send_weight_ref),
        (edge_bias_hbm, edge_bias_ref),
    ]
    pairs += [(grid_hbm.at[:, part], grid_ref.at[:, part]) for part in columns[1:]]
    pairs += [
        (slot_hbm, slot_ref),
        (feat_weight_hbm, feat_weight_ref),
        (send_hbm, send_ref),
        (recv_hbm, recv_ref),
        (feat_hbm, feat_ref),
        (mesh_send_hbm, mesh_send_ref),
        (count_hbm, count_ref),
    ]
    copies = [
        pltpu.make_async_copy(source, target, sems.at[at])
        for at, (source, target) in enumerate(pairs)
    ]
    for copy in copies[:3]:
        copy.start()
    column = lambda ref: jnp.broadcast_to(0.5 * ref[...], (LANES, width)).T
    wide = lambda value: jnp.concatenate([value] * (step_rows // LANES), axis=1)
    for copy in copies[:2]:
        copy.wait()
    for copy in copies[3:]:
        copy.start()
    first_t = (0.5 * first_ref[...].astype(F32)).T.astype(BF16)
    grid_bias = column(grid_bias_ref)
    for step, part in enumerate(columns):
        copies[2 if step == 0 else 5 + step].wait()
        half = mm(first_t, grid_ref[:, part]) + wide(grid_bias)
        hidden = silu_half(half).astype(BF16)
        if step == 0:
            for copy in copies[3:6]:
                copy.wait()
            second_t = second_ref[...].T
            weight_t = (0.5 * send_weight_ref[...].astype(F32)).T.astype(BF16)
            edge_bias = column(edge_bias_ref)
        value = mm(second_t, hidden)
        center = value - jnp.mean(value, axis=0, keepdims=True)
        spread = jnp.mean(center * center, axis=0, keepdims=True)
        code = (center * lax.rsqrt(spread + 1e-05)).astype(BF16)
        table[:, part] = (mm(weight_t, code) + wide(edge_bias)).astype(BF16)

    for copy in copies[5 + GRID_STEPS :]:
        copy.wait()
    asked = mesh_send_ref[...]
    for at in range(asked_ref.shape[0] // asked.shape[0]):
        asked_ref[at * asked.shape[0] : (at + 1) * asked.shape[0], :] = asked
    place = place_ref[0]
    used = count_ref[...]
    feat_weight = jnp.concatenate(
        [0.5 * feat_weight_ref[...].astype(F32), jnp.zeros((LANES - feats, width), F32)], axis=0
    )
    feat_weight = feat_weight.T.astype(BF16)[:, :feats]
    ids = ids_of_rows(slot_ref[...], (place - 1) * owned, 3 * owned)
    group = math.gcd(blocks, 4)
    for first in range(0, blocks, group):
        senders = jnp.concatenate([send_ref[b : b + 1, :] for b in range(first, first + group)], axis=1)
        picker = one_hot(senders, grid_rows)
        feat = jnp.concatenate([feat_ref[b] for b in range(first, first + group)], axis=1)
        half = mm(table[...], picker) + mm(feat_weight, feat.astype(BF16))
        hidden = silu_half(half).astype(BF16)
        receivers = jnp.concatenate(
            [jnp.where(b < used, recv_ref[b : b + 1, :], -2) for b in range(first, first + group)],
            axis=1,
        )
        spread = (ids == receivers).astype(F32).astype(BF16)
        sums = mm_nt(hidden, spread)
        total[...] = sums if first == 0 else total[...] + sums
    pad = -3 * owned % LANES
    sums = jnp.concatenate([total[...], jnp.zeros((width, pad), F32)], axis=1).T
    below, above = sums[:owned].astype(BF16), sums[2 * owned : 3 * owned].astype(BF16)
    own_ref[...] = sums[owned : 2 * owned]
    odd = place % 2 == 1
    cross_ref[...] = jnp.where(odd, above, below)
    chip_ref[...] = jnp.where(odd, below, above)


def wanted_kernel(owned, slot_ref, send_ref, wanted_ref):
    nodes = slot_ref.shape[1]
    blocks, block_edges = send_ref.shape
    places = wanted_ref.shape[1]
    chunk = LANES
    per_chunk = chunk // owned * SEND_CAP
    row, column = iota((chunk, chunk), 0), iota((chunk, chunk), 1)
    before = ((row > column) & (row // owned == column // owned)).astype(F32).astype(BF16)
    local_owner = (iota((chunk, LANES), 0) // owned * SEND_CAP).astype(F32)

    def find(index, best):
        ids = ids_of_rows(slot_ref[...], index * chunk, chunk)
        hit = jnp.zeros((chunk, block_edges), F32)
        for b in range(blocks):
            hit = jnp.maximum(hit, (ids == send_ref[b : b + 1, :]).astype(F32))
        hit = jnp.broadcast_to(jnp.max(hit, axis=1, keepdims=True), (chunk, LANES))
        rank = mm(before, hit.astype(BF16)) + local_owner
        spot = jnp.where(hit > 0, rank.astype(I32) + index * per_chunk, -1)
        spot = jnp.concatenate([spot] * (places // LANES), axis=1)
        found = jnp.where(spot == iota((chunk, places), 1), ids, -1)
        return jnp.maximum(best, jnp.max(found, axis=0, keepdims=True))

    best = lax.fori_loop(0, nodes // chunk, find, jnp.full((1, places), -1, I32), unroll=2)
    best = best.astype(F32)
    for b in range(blocks):
        senders = jnp.broadcast_to(send_ref[b : b + 1, :].astype(F32), (block_edges, block_edges)).T
        senders = jnp.concatenate([senders] * (places // LANES), axis=1)
        wanted_ref[b * block_edges : (b + 1) * block_edges, :] = (
            (senders == best).astype(F32).astype(BF16)
        )


def supply_kernel(place_ref, slot_ref, request_ref, supply_ref):
    owned = supply_ref.shape[1]
    devices = supply_ref.shape[0] // SEND_CAP
    per_device = request_ref.shape[0] // devices
    ids = ids_of_rows(slot_ref[...], place_ref[0] * owned, owned)
    lane = iota((owned, LANES), 1)
    used = jnp.zeros((owned, LANES), F32)
    for d in range(devices):
        hit = jnp.zeros((owned, request_ref.shape[1]), F32)
        for b in range(per_device):
            at = d * per_device + b
            hit = jnp.maximum(hit, (ids == request_ref[at : at + 1, :]).astype(F32))
        used = jnp.where(lane == d, jnp.max(hit, axis=1, keepdims=True), used)
    before = (iota((owned, owned), 0) > iota((owned, owned), 1)).astype(F32).astype(BF16)
    rank = jnp.where(used > 0, mm(before, used.astype(BF16)), -1.0)
    rank = jnp.concatenate([rank, jnp.full((LANES - owned, LANES), -1.0, F32)], axis=0).T
    slots = iota((SEND_CAP, owned), 0).astype(F32)
    supply = jnp.concatenate(
        [(rank[d : d + 1, :owned] == slots).astype(F32) for d in range(devices)], axis=0
    )
    supply_ref[...] = supply.astype(BF16)


def node_kernel(
    own_ref,
    from_cross_ref,
    from_chip_ref,
    latent_ref,
    edge_out_ref,
    node_input_ref,
    node_bias_ref,
    node_out_ref,
    node_gain_ref,
    mesh_sender_ref,
    supply_ref,
    encoded_ref,
    rows_ref,
):
    width = latent_ref.shape[1]
    latent = latent_ref[...]
    node_sum = own_ref[...] + from_cross_ref[...].astype(F32) + from_chip_ref[...].astype(F32)
    aggregate = mm(node_sum.astype(BF16), edge_out_ref[...]).astype(BF16)
    hidden = mm(latent, node_input_ref[:width]) + mm(aggregate, node_input_ref[width:])
    hidden = silu(hidden + node_bias_ref[...]).astype(BF16)
    encoded = latent.astype(F32) + layer_norm(mm(hidden, node_out_ref[...])) * node_gain_ref[...]
    encoded = encoded.astype(BF16)
    encoded_ref[...] = encoded
    sender_code = mm(encoded, mesh_sender_ref[...]).astype(BF16)
    rows_ref[...] = mm(supply_ref[...], sender_code).astype(BF16)


def receiver_kernel(
    place_ref,
    slot_ref,
    recv_ref,
    encoded_ref,
    mesh_receiver_ref,
    message_bias_ref,
    update_input_ref,
    update_bias_ref,
    incoming_ref,
    pick_ref,
    high_ref,
    low_ref,
    upper_ref,
):
    owned, width = encoded_ref.shape
    blocks = recv_ref.shape[0]
    ids = ids_of_rows(slot_ref[...], place_ref[0] * owned, owned)
    incoming = jnp.concatenate(
        [(ids == recv_ref[b : b + 1, :]).astype(F32) for b in range(blocks)], axis=1
    )
    pick_ref[...] = incoming.T.astype(BF16)
    incoming_ref[...] = incoming.astype(BF16)
    encoded = encoded_ref[...]
    receiver = mm(encoded, mesh_receiver_ref[...]) + message_bias_ref[...]
    high = receiver.astype(BF16)
    high_ref[...] = high
    low_ref[...] = (receiver - high.astype(F32)).astype(BF16)
    upper_ref[...] = mm(encoded, update_input_ref[:width]) + update_bias_ref[...]


def message_kernel(
    wanted_ref,
    piece_ref,
    incoming_ref,
    pick_ref,
    high_ref,
    low_ref,
    upper_ref,
    encoded_ref,
    message_out_ref,
    update_input_ref,
    update_out_ref,
    update_gain_ref,
    out_ref,
):
    width = encoded_ref.shape[1]
    receiver = mm(pick_ref[...], high_ref[...]) + mm(pick_ref[...], low_ref[...])
    message = silu(mm(wanted_ref[...], piece_ref[...]) + receiver).astype(BF16)
    message_sum = mm(incoming_ref[...], message).astype(BF16)
    update = mm(message_sum, message_out_ref[...]).astype(BF16)
    hidden = silu(upper_ref[...] + mm(update, update_input_ref[width:])).astype(BF16)
    out = layer_norm(mm(hidden, update_out_ref[...])) * update_gain_ref[...]
    out_ref[...] = (encoded_ref[...].astype(F32) + out).astype(BF16)


def call(kernel, out_shape, spaces, scratch=(), flops=0, moved=0, vmem=8):
    return pl.pallas_call(
        kernel,
        out_shape=out_shape,
        in_specs=[pl.BlockSpec(memory_space=space) for space in spaces],
        out_specs=jax.tree.map(lambda _: pl.BlockSpec(memory_space=VMEM), out_shape),
        scratch_shapes=scratch,
        compiler_params=pltpu.CompilerParams(vmem_limit_bytes=vmem * MEBI),
        cost_estimate=pl.CostEstimate(flops=flops, bytes_accessed=moved, transcendentals=0),
    )


def shape(*sizes, kind=BF16):
    return jax.ShapeDtypeStruct(sizes, kind)


def per_device(
    grid_in,
    grid_first,
    grid_bias,
    grid_second,
    send_weight,
    edge_bias,
    feat_weight,
    edge_out,
    node_input,
    node_bias,
    node_out,
    node_gain,
    mesh_sender,
    mesh_receiver,
    message_bias,
    message_out,
    update_input,
    update_bias,
    update_out,
    update_gain,
    mesh_latent,
    g2m_send,
    g2m_recv,
    g2m_feat,
    g2m_count,
    mesh_slot,
    mesh_send,
    mesh_recv,
):
    devices = lax.axis_size("bulk")
    position = lax.axis_index("bulk")
    place = position.astype(I32).reshape(1)
    owned, width = mesh_latent.shape
    grid_rows = grid_in.shape[0]
    places = devices * SEND_CAP
    edges = mesh_send.size
    slot = mesh_slot.reshape(1, -1)
    row = lambda vector: vector.reshape(1, -1)

    operands = (
        grid_first,
        row(grid_bias),
        grid_in.T,
        grid_second,
        send_weight,
        row(edge_bias),
        g2m_count.reshape(1, 1),
        slot,
        feat_weight,
        g2m_send,
        g2m_recv,
        g2m_feat,
        mesh_send,
    )
    own, cross, chip, asked = call(
        edge_kernel,
        (
            shape(owned, width, kind=F32),
            shape(owned, width),
            shape(owned, width),
            shape(devices * mesh_send.shape[0], mesh_send.shape[1], kind=I32),
        ),
        [SMEM] + [HBM] * len(operands),
        scratch=[VMEM(value.shape, value.dtype) for value in operands]
        + [
            pltpu.VMEM((width, grid_rows), BF16),
            pltpu.VMEM((width, 3 * owned), F32),
            pltpu.SemaphoreType.DMA((len(operands) - 1 + GRID_STEPS,)),
        ],
        flops=10_000_000_000,
        moved=4_000_000,
        vmem=56,
    )(place, *operands)
    requests = lax.all_to_all(asked, "bulk", 0, 0, tiled=True)
    crossing = [(d, d + 1) for d in range(1, devices - 1, 2)]
    within = [(d, d + 1) for d in range(0, devices, 2)]
    both = lambda pairs: pairs + [(b, a) for a, b in pairs]
    from_cross = lax.ppermute(cross, "bulk", both(crossing))
    from_chip = lax.ppermute(chip, "bulk", both(within))
    supply = call(
        supply_kernel,
        shape(places, owned),
        [SMEM] + [VMEM] * 2,
        flops=500_000_000,
        moved=500_000,
    )(place, slot, requests)
    encoded, rows = call(
        node_kernel,
        (shape(owned, width), shape(places, width)),
        [VMEM] * 11,
        flops=500_000_000,
        moved=4_000_000,
    )(
        own,
        from_cross,
        from_chip,
        mesh_latent,
        edge_out,
        node_input,
        row(node_bias),
        node_out,
        row(node_gain),
        mesh_sender,
        supply,
    )
    piece = lax.all_to_all(rows, "bulk", 0, 0, tiled=True)
    mesh_send, _ = lax.optimization_barrier((mesh_send, encoded))
    wanted = call(
        functools.partial(wanted_kernel, owned),
        shape(edges, places),
        [VMEM] * 2,
        flops=1_000_000_000,
        moved=500_000,
    )(slot, mesh_send)
    incoming, pick, high, low, upper = call(
        receiver_kernel,
        (
            shape(owned, edges),
            shape(edges, owned),
            shape(owned, width),
            shape(owned, width),
            shape(owned, width, kind=F32),
        ),
        [SMEM] + [VMEM] * 7,
        flops=1_000_000_000,
        moved=4_000_000,
    )(
        place,
        slot,
        mesh_recv,
        encoded,
        mesh_receiver,
        row(message_bias),
        update_input,
        row(update_bias),
    )
    return call(
        message_kernel,
        shape(owned, width),
        [VMEM] * 12,
        flops=1_000_000_000,
        moved=4_000_000,
    )(
        wanted,
        piece,
        incoming,
        pick,
        high,
        low,
        upper,
        encoded,
        message_out,
        update_input,
        update_out,
        row(update_gain),
    )


def solution(mesh):
    split = {0: ("groups", "bulk"), 20: "bulk", 21: "bulk", 22: "bulk", 23: "bulk", 24: "bulk"}
    split.update({26: "bulk", 27: "bulk"})
    placed = tuple(P(split[at]) if at in split else P() for at in range(28))
    return jax.shard_map(
        per_device,
        mesh=mesh,
        in_specs=placed,
        out_specs=P(("groups", "bulk"), None),
        check_vma=False,
    )
```

```python
import functools
import math

import jax
import jax.numpy as jnp
from jax import lax
from jax.experimental import pallas as pl
from jax.experimental.pallas import tpu as pltpu
from jax.sharding import PartitionSpec as P

F32 = jnp.float32
BF16 = jnp.bfloat16
I32 = jnp.int32
SEND_CAP = 16
LANES = 128
VMEM = pltpu.VMEM
SMEM = pltpu.SMEM
HBM = pltpu.HBM
GRID_STEPS = 4
MEBI = 1024 * 1024


def mm(left, right):
    return jnp.dot(left, right, preferred_element_type=F32)


def mm_nt(left, right):
    return lax.dot_general(left, right, (((1,), (1,)), ((), ())), preferred_element_type=F32)


def silu_half(half):
    return half + half * jnp.tanh(half)


def silu(value):
    return silu_half(0.5 * value)


def layer_norm(value):
    center = value - jnp.mean(value, axis=-1, keepdims=True)
    spread = jnp.mean(center * center, axis=-1, keepdims=True)
    return center * lax.rsqrt(spread + 1e-05)


def iota(shape, dim):
    return lax.broadcasted_iota(I32, shape, dim)


def one_hot(columns, rows):
    hit = columns.astype(jnp.int16) == lax.broadcasted_iota(jnp.int16, (rows, columns.shape[1]), 0)
    return jnp.where(hit, jnp.ones((), BF16), jnp.zeros((), BF16))


def ids_of_rows(slot, first, count):
    nodes = slot.shape[1]
    rows = iota((count, nodes), 0) + first
    return jnp.max(jnp.where(slot == rows, iota((count, nodes), 1), -1), axis=1, keepdims=True)


def edge_kernel(
    place_ref,
    first_hbm,
    grid_bias_hbm,
    grid_hbm,
    second_hbm,
    send_weight_hbm,
    edge_bias_hbm,
    count_hbm,
    slot_hbm,
    feat_weight_hbm,
    send_hbm,
    recv_hbm,
    feat_hbm,
    own_ref,
    cross_ref,
    chip_ref,
    first_ref,
    grid_bias_ref,
    grid_ref,
    second_ref,
    send_weight_ref,
    edge_bias_ref,
    count_ref,
    slot_ref,
    feat_weight_ref,
    send_ref,
    recv_ref,
    feat_ref,
    table,
    total,
    sems,
):
    channels, grid_rows = grid_ref.shape
    width = second_ref.shape[1]
    blocks, block_edges = send_ref.shape
    owned = own_ref.shape[0]
    feats = feat_ref.shape[1]
    step_rows = grid_rows // GRID_STEPS
    columns = [pl.ds(step * step_rows, step_rows) for step in range(GRID_STEPS)]
    pairs = [
        (first_hbm, first_ref),
        (grid_bias_hbm, grid_bias_ref),
        (grid_hbm.at[:, columns[0]], grid_ref.at[:, columns[0]]),
        (second_hbm, second_ref),
        (send_weight_hbm, send_weight_ref),
        (edge_bias_hbm, edge_bias_ref),
    ]
    pairs += [(grid_hbm.at[:, part], grid_ref.at[:, part]) for part in columns[1:]]
    pairs += [
        (slot_hbm, slot_ref),
        (feat_weight_hbm, feat_weight_ref),
        (send_hbm, send_ref),
        (recv_hbm, recv_ref),
        (feat_hbm, feat_ref),
        (count_hbm, count_ref),
    ]
    copies = [
        pltpu.make_async_copy(source, target, sems.at[at])
        for at, (source, target) in enumerate(pairs)
    ]
    for copy in copies[:3]:
        copy.start()
    column = lambda ref: jnp.broadcast_to(0.5 * ref[...], (LANES, width)).T
    wide = lambda value: jnp.concatenate([value] * (step_rows // LANES), axis=1)
    for copy in copies[:2]:
        copy.wait()
    for copy in copies[3:]:
        copy.start()
    first_t = (0.5 * first_ref[...].astype(F32)).T.astype(BF16)
    grid_bias = column(grid_bias_ref)
    for step, part in enumerate(columns):
        copies[2 if step == 0 else 5 + step].wait()
        half = mm(first_t, grid_ref[:, part]) + wide(grid_bias)
        hidden = silu_half(half).astype(BF16)
        if step == 0:
            for copy in copies[3:6]:
                copy.wait()
            second_t = second_ref[...].T
            weight_t = (0.5 * send_weight_ref[...].astype(F32)).T.astype(BF16)
            edge_bias = column(edge_bias_ref)
        value = mm(second_t, hidden)
        center = value - jnp.mean(value, axis=0, keepdims=True)
        spread = jnp.mean(center * center, axis=0, keepdims=True)
        code = (center * lax.rsqrt(spread + 1e-05)).astype(BF16)
        table[:, part] = (mm(weight_t, code) + wide(edge_bias)).astype(BF16)

    for copy in copies[5 + GRID_STEPS :]:
        copy.wait()
    place = place_ref[0]
    used = count_ref[...]
    feat_weight = jnp.concatenate(
        [0.5 * feat_weight_ref[...].astype(F32), jnp.zeros((LANES - feats, width), F32)], axis=0
    )
    feat_weight = feat_weight.T.astype(BF16)[:, :feats]
    ids = ids_of_rows(slot_ref[...], (place - 1) * owned, 3 * owned)
    group = math.gcd(blocks, 4)
    total[...] = jnp.zeros_like(total)

    def edge_step(step, carry):
        here = [step * group + b for b in range(group)]
        senders = jnp.concatenate([send_ref[pl.ds(b, 1), :] for b in here], axis=1)
        picker = one_hot(senders, grid_rows)
        feat = jnp.concatenate([feat_ref[b] for b in here], axis=1)
        half = mm(table[...], picker) + mm(feat_weight, feat.astype(BF16))
        hidden = silu_half(half).astype(BF16)
        receivers = [jnp.where(b < used, recv_ref[pl.ds(b, 1), :], -2) for b in here]
        spread = (ids == jnp.concatenate(receivers, axis=1)).astype(F32).astype(BF16)
        total[...] += mm_nt(hidden, spread)
        return carry

    lax.fori_loop(0, blocks // group, edge_step, 0)
    pad = -3 * owned % LANES
    sums = jnp.concatenate([total[...], jnp.zeros((width, pad), F32)], axis=1).T
    below, above = sums[:owned].astype(BF16), sums[2 * owned : 3 * owned].astype(BF16)
    own_ref[...] = sums[owned : 2 * owned]
    odd = place % 2 == 1
    cross_ref[...] = jnp.where(odd, above, below)
    chip_ref[...] = jnp.where(odd, below, above)


def wanted_kernel(owned, slot_ref, send_ref, wanted_ref):
    nodes = slot_ref.shape[1]
    blocks, block_edges = send_ref.shape
    places = wanted_ref.shape[1]
    chunk = LANES
    per_chunk = chunk // owned * SEND_CAP
    row, column = iota((chunk, chunk), 0), iota((chunk, chunk), 1)
    before = ((row > column) & (row // owned == column // owned)).astype(F32).astype(BF16)
    local_owner = (iota((chunk, LANES), 0) // owned * SEND_CAP).astype(F32)

    def find(index, best):
        ids = ids_of_rows(slot_ref[...], index * chunk, chunk)
        hit = jnp.zeros((chunk, block_edges), F32)
        for b in range(blocks):
            hit = jnp.maximum(hit, (ids == send_ref[b : b + 1, :]).astype(F32))
        hit = jnp.broadcast_to(jnp.max(hit, axis=1, keepdims=True), (chunk, LANES))
        rank = mm(before, hit.astype(BF16)) + local_owner
        spot = jnp.where(hit > 0, rank.astype(I32) + index * per_chunk, -1)
        spot = jnp.concatenate([spot] * (places // LANES), axis=1)
        found = jnp.where(spot == iota((chunk, places), 1), ids, -1)
        return jnp.maximum(best, jnp.max(found, axis=0, keepdims=True))

    best = lax.fori_loop(0, nodes // chunk, find, jnp.full((1, places), -1, I32), unroll=2)
    best = best.astype(F32)
    for b in range(blocks):
        senders = jnp.broadcast_to(send_ref[b : b + 1, :].astype(F32), (block_edges, block_edges)).T
        senders = jnp.concatenate([senders] * (places // LANES), axis=1)
        wanted_ref[b * block_edges : (b + 1) * block_edges, :] = (
            (senders == best).astype(F32).astype(BF16)
        )


def supply_kernel(place_ref, slot_ref, request_ref, supply_ref):
    owned = supply_ref.shape[1]
    devices = supply_ref.shape[0] // SEND_CAP
    per_device = request_ref.shape[0] // devices
    ids = ids_of_rows(slot_ref[...], place_ref[0] * owned, owned)
    lane = iota((owned, LANES), 1)
    used = jnp.zeros((owned, LANES), F32)
    for d in range(devices):
        hit = jnp.zeros((owned, request_ref.shape[1]), F32)
        for b in range(per_device):
            at = d * per_device + b
            hit = jnp.maximum(hit, (ids == request_ref[at : at + 1, :]).astype(F32))
        used = jnp.where(lane == d, jnp.max(hit, axis=1, keepdims=True), used)
    before = (iota((owned, owned), 0) > iota((owned, owned), 1)).astype(F32).astype(BF16)
    rank = jnp.where(used > 0, mm(before, used.astype(BF16)), -1.0)
    rank = jnp.concatenate([rank, jnp.full((LANES - owned, LANES), -1.0, F32)], axis=0).T
    slots = iota((SEND_CAP, owned), 0).astype(F32)
    supply = jnp.concatenate(
        [(rank[d : d + 1, :owned] == slots).astype(F32) for d in range(devices)], axis=0
    )
    supply_ref[...] = supply.astype(BF16)


def node_kernel(
    own_ref,
    from_cross_ref,
    from_chip_ref,
    latent_ref,
    edge_out_ref,
    node_input_ref,
    node_bias_ref,
    node_out_ref,
    node_gain_ref,
    mesh_sender_ref,
    supply_ref,
    encoded_ref,
    rows_ref,
):
    width = latent_ref.shape[1]
    latent = latent_ref[...]
    node_sum = own_ref[...] + from_cross_ref[...].astype(F32) + from_chip_ref[...].astype(F32)
    aggregate = mm(node_sum.astype(BF16), edge_out_ref[...]).astype(BF16)
    hidden = mm(latent, node_input_ref[:width]) + mm(aggregate, node_input_ref[width:])
    hidden = silu(hidden + node_bias_ref[...]).astype(BF16)
    encoded = latent.astype(F32) + layer_norm(mm(hidden, node_out_ref[...])) * node_gain_ref[...]
    encoded = encoded.astype(BF16)
    encoded_ref[...] = encoded
    sender_code = mm(encoded, mesh_sender_ref[...]).astype(BF16)
    rows_ref[...] = mm(supply_ref[...], sender_code).astype(BF16)


def receiver_kernel(
    place_ref,
    slot_ref,
    recv_ref,
    encoded_ref,
    mesh_receiver_ref,
    message_bias_ref,
    update_input_ref,
    update_bias_ref,
    incoming_ref,
    pick_ref,
    high_ref,
    low_ref,
    upper_ref,
):
    owned, width = encoded_ref.shape
    blocks = recv_ref.shape[0]
    ids = ids_of_rows(slot_ref[...], place_ref[0] * owned, owned)
    incoming = jnp.concatenate(
        [(ids == recv_ref[b : b + 1, :]).astype(F32) for b in range(blocks)], axis=1
    )
    pick_ref[...] = incoming.T.astype(BF16)
    incoming_ref[...] = incoming.astype(BF16)
    encoded = encoded_ref[...]
    receiver = mm(encoded, mesh_receiver_ref[...]) + message_bias_ref[...]
    high = receiver.astype(BF16)
    high_ref[...] = high
    low_ref[...] = (receiver - high.astype(F32)).astype(BF16)
    upper_ref[...] = mm(encoded, update_input_ref[:width]) + update_bias_ref[...]


def message_kernel(
    wanted_ref,
    piece_ref,
    incoming_ref,
    pick_ref,
    high_ref,
    low_ref,
    upper_ref,
    encoded_ref,
    message_out_ref,
    update_input_ref,
    update_out_ref,
    update_gain_ref,
    out_ref,
):
    width = encoded_ref.shape[1]
    receiver = mm(pick_ref[...], high_ref[...]) + mm(pick_ref[...], low_ref[...])
    message = silu(mm(wanted_ref[...], piece_ref[...]) + receiver).astype(BF16)
    message_sum = mm(incoming_ref[...], message).astype(BF16)
    update = mm(message_sum, message_out_ref[...]).astype(BF16)
    hidden = silu(upper_ref[...] + mm(update, update_input_ref[width:])).astype(BF16)
    out = layer_norm(mm(hidden, update_out_ref[...])) * update_gain_ref[...]
    out_ref[...] = (encoded_ref[...].astype(F32) + out).astype(BF16)


def call(kernel, out_shape, spaces, scratch=(), flops=0, moved=0, vmem=8):
    return pl.pallas_call(
        kernel,
        out_shape=out_shape,
        in_specs=[pl.BlockSpec(memory_space=space) for space in spaces],
        out_specs=jax.tree.map(lambda _: pl.BlockSpec(memory_space=VMEM), out_shape),
        scratch_shapes=scratch,
        compiler_params=pltpu.CompilerParams(vmem_limit_bytes=vmem * MEBI),
        cost_estimate=pl.CostEstimate(flops=flops, bytes_accessed=moved, transcendentals=0),
    )


def shape(*sizes, kind=BF16):
    return jax.ShapeDtypeStruct(sizes, kind)


def per_device(
    grid_in,
    grid_first,
    grid_bias,
    grid_second,
    send_weight,
    edge_bias,
    feat_weight,
    edge_out,
    node_input,
    node_bias,
    node_out,
    node_gain,
    mesh_sender,
    mesh_receiver,
    message_bias,
    message_out,
    update_input,
    update_bias,
    update_out,
    update_gain,
    mesh_latent,
    g2m_send,
    g2m_recv,
    g2m_feat,
    g2m_count,
    mesh_slot,
    mesh_send,
    mesh_recv,
):
    devices = lax.axis_size("bulk")
    position = lax.axis_index("bulk")
    place = position.astype(I32).reshape(1)
    owned, width = mesh_latent.shape
    grid_rows = grid_in.shape[0]
    places = devices * SEND_CAP
    edges = mesh_send.size
    slot = mesh_slot.reshape(1, -1)
    row = lambda vector: vector.reshape(1, -1)

    requests = lax.all_to_all(jnp.tile(mesh_send, (devices, 1)), "bulk", 0, 0, tiled=True)
    operands = (
        grid_first,
        row(grid_bias),
        grid_in.T,
        grid_second,
        send_weight,
        row(edge_bias),
        g2m_count.reshape(1, 1),
        slot,
        feat_weight,
        g2m_send,
        g2m_recv,
        g2m_feat,
    )
    own, cross, chip = call(
        edge_kernel,
        (
            shape(owned, width, kind=F32),
            shape(owned, width),
            shape(owned, width),
        ),
        [SMEM] + [HBM] * len(operands),
        scratch=[VMEM(value.shape, value.dtype) for value in operands]
        + [
            pltpu.VMEM((width, grid_rows), BF16),
            pltpu.VMEM((width, 3 * owned), F32),
            pltpu.SemaphoreType.DMA((len(operands) - 1 + GRID_STEPS,)),
        ],
        flops=10_000_000_000,
        moved=4_000_000,
        vmem=56,
    )(place, *operands)
    requests, _ = lax.optimization_barrier((requests, own))
    crossing = [(d, d + 1) for d in range(1, devices - 1, 2)]
    within = [(d, d + 1) for d in range(0, devices, 2)]
    both = lambda pairs: pairs + [(b, a) for a, b in pairs]
    from_cross = lax.ppermute(cross, "bulk", both(crossing))
    from_chip = lax.ppermute(chip, "bulk", both(within))
    supply = call(
        supply_kernel,
        shape(places, owned),
        [SMEM] + [VMEM] * 2,
        flops=500_000_000,
        moved=500_000,
    )(place, slot, requests)
    encoded, rows = call(
        node_kernel,
        (shape(owned, width), shape(places, width)),
        [VMEM] * 11,
        flops=500_000_000,
        moved=4_000_000,
    )(
        own,
        from_cross,
        from_chip,
        mesh_latent,
        edge_out,
        node_input,
        row(node_bias),
        node_out,
        row(node_gain),
        mesh_sender,
        supply,
    )
    piece = lax.all_to_all(rows, "bulk", 0, 0, tiled=True)
    mesh_send, _ = lax.optimization_barrier((mesh_send, encoded))
    wanted = call(
        functools.partial(wanted_kernel, owned),
        shape(edges, places),
        [VMEM] * 2,
        flops=1_000_000_000,
        moved=500_000,
    )(slot, mesh_send)
    incoming, pick, high, low, upper = call(
        receiver_kernel,
        (
            shape(owned, edges),
            shape(edges, owned),
            shape(owned, width),
            shape(owned, width),
            shape(owned, width, kind=F32),
        ),
        [SMEM] + [VMEM] * 7,
        flops=1_000_000_000,
        moved=4_000_000,
    )(
        place,
        slot,
        mesh_recv,
        encoded,
        mesh_receiver,
        row(message_bias),
        update_input,
        row(update_bias),
    )
    return call(
        message_kernel,
        shape(owned, width),
        [VMEM] * 12,
        flops=1_000_000_000,
        moved=4_000_000,
    )(
        wanted,
        piece,
        incoming,
        pick,
        high,
        low,
        upper,
        encoded,
        message_out,
        update_input,
        update_out,
        row(update_gain),
    )


def solution(mesh):
    split = {0: ("groups", "bulk"), 20: "bulk", 21: "bulk", 22: "bulk", 23: "bulk", 24: "bulk"}
    split.update({26: "bulk", 27: "bulk"})
    placed = tuple(P(split[at]) if at in split else P() for at in range(28))
    return jax.shard_map(
        per_device,
        mesh=mesh,
        in_specs=placed,
        out_specs=P(("groups", "bulk"), None),
        check_vma=False,
    )
```

```python
import functools
import math

import jax
import jax.numpy as jnp
from jax import lax
from jax.experimental import pallas as pl
from jax.experimental.pallas import tpu as pltpu
from jax.sharding import PartitionSpec as P

F32 = jnp.float32
BF16 = jnp.bfloat16
I32 = jnp.int32
SEND_CAP = 16
LANES = 128
VMEM = pltpu.VMEM
SMEM = pltpu.SMEM
HBM = pltpu.HBM
GRID_STEPS = 4
MEBI = 1024 * 1024


def mm(left, right):
    return jnp.dot(left, right, preferred_element_type=F32)


def mm_nt(left, right):
    return lax.dot_general(left, right, (((1,), (1,)), ((), ())), preferred_element_type=F32)


def silu_half(half):
    return half + half * jnp.tanh(half)


def silu(value):
    return silu_half(0.5 * value)


def layer_norm(value):
    center = value - jnp.mean(value, axis=-1, keepdims=True)
    spread = jnp.mean(center * center, axis=-1, keepdims=True)
    return center * lax.rsqrt(spread + 1e-05)


def iota(shape, dim):
    return lax.broadcasted_iota(I32, shape, dim)


def one_hot(columns, rows):
    hit = columns.astype(jnp.int16) == lax.broadcasted_iota(jnp.int16, (rows, columns.shape[1]), 0)
    return jnp.where(hit, jnp.ones((), BF16), jnp.zeros((), BF16))


def ids_of_rows(slot, first, count):
    nodes = slot.shape[1]
    rows = iota((count, nodes), 0) + first
    return jnp.max(jnp.where(slot == rows, iota((count, nodes), 1), -1), axis=1, keepdims=True)


def edge_kernel(
    place_ref,
    first_hbm,
    grid_hbm,
    second_hbm,
    send_weight_hbm,
    grid_bias_hbm,
    edge_bias_hbm,
    slot_hbm,
    feat_weight_hbm,
    send_hbm,
    recv_hbm,
    feat_hbm,
    count_hbm,
    own_ref,
    cross_ref,
    chip_ref,
    first_ref,
    grid_ref,
    second_ref,
    send_weight_ref,
    grid_bias_ref,
    edge_bias_ref,
    slot_ref,
    feat_weight_ref,
    send_ref,
    recv_ref,
    feat_ref,
    count_ref,
    table,
    first_t,
    second_t,
    weight_t,
    grid_column,
    edge_column,
    total,
    sems,
):
    channels, grid_rows = grid_ref.shape
    width = second_ref.shape[1]
    blocks, block_edges = send_ref.shape
    owned = own_ref.shape[0]
    feats = feat_ref.shape[1]
    step_rows = grid_rows // GRID_STEPS

    def grid_copy(step):
        part = pl.ds(pl.multiple_of(step * step_rows, step_rows), step_rows)
        return pltpu.make_async_copy(grid_hbm.at[:, part], grid_ref.at[:, part], sems.at[step])

    pairs = [
        (first_hbm, first_ref),
        (second_hbm, second_ref),
        (send_weight_hbm, send_weight_ref),
        (grid_bias_hbm, grid_bias_ref),
        (edge_bias_hbm, edge_bias_ref),
        (slot_hbm, slot_ref),
        (feat_weight_hbm, feat_weight_ref),
        (send_hbm, send_ref),
        (recv_hbm, recv_ref),
        (feat_hbm, feat_ref),
        (count_hbm, count_ref),
    ]
    copies = [
        pltpu.make_async_copy(source, target, sems.at[GRID_STEPS + at])
        for at, (source, target) in enumerate(pairs)
    ]
    for copy in copies[:5]:
        copy.start()
    for step in range(GRID_STEPS):
        grid_copy(step).start()
    for copy in copies[5:]:
        copy.start()
    copies[0].wait()
    first_t[...] = (0.5 * first_ref[...].astype(F32)).T.astype(BF16)
    copies[1].wait()
    second_t[...] = second_ref[...].T
    copies[2].wait()
    weight_t[...] = (0.5 * send_weight_ref[...].astype(F32)).T.astype(BF16)
    copies[3].wait()
    grid_column[...] = jnp.broadcast_to(0.5 * grid_bias_ref[...], (LANES, width)).T
    copies[4].wait()
    edge_column[...] = jnp.broadcast_to(0.5 * edge_bias_ref[...], (LANES, width)).T
    wide = lambda ref: jnp.concatenate([ref[...]] * (step_rows // LANES), axis=1)

    def grid_step(step, carry):
        part = pl.ds(pl.multiple_of(step * step_rows, step_rows), step_rows)
        grid_copy(step).wait()
        hidden = silu_half(mm(first_t[...], grid_ref[:, part]) + wide(grid_column)).astype(BF16)
        value = mm(second_t[...], hidden)
        center = value - jnp.mean(value, axis=0, keepdims=True)
        spread = jnp.mean(center * center, axis=0, keepdims=True)
        code = (center * lax.rsqrt(spread + 1e-05)).astype(BF16)
        table[:, part] = (mm(weight_t[...], code) + wide(edge_column)).astype(BF16)
        return carry

    lax.fori_loop(0, GRID_STEPS, grid_step, 0)
    for copy in copies[5:]:
        copy.wait()
    place = place_ref[0]
    used = count_ref[...]
    feat_weight = jnp.concatenate(
        [0.5 * feat_weight_ref[...].astype(F32), jnp.zeros((LANES - feats, width), F32)], axis=0
    )
    table[:, grid_rows:] = feat_weight.T.astype(BF16)
    ids = ids_of_rows(slot_ref[...], (place - 1) * owned, 3 * owned)
    group = math.gcd(blocks, 4)
    blank = jnp.zeros((LANES - feats, group * block_edges), F32)
    total[...] = jnp.zeros_like(total)

    def edge_step(step, carry):
        here = [step * group + b for b in range(group)]
        senders = jnp.concatenate([send_ref[pl.ds(b, 1), :] for b in here], axis=1)
        feat = jnp.concatenate([feat_ref[b] for b in here], axis=1)
        feat = jnp.concatenate([feat, blank], axis=0).astype(BF16)
        picker = jnp.concatenate([one_hot(senders, grid_rows), feat], axis=0)
        hidden = silu_half(mm(table[...], picker)).astype(BF16)
        receivers = [jnp.where(b < used, recv_ref[pl.ds(b, 1), :], -2) for b in here]
        spread = (ids == jnp.concatenate(receivers, axis=1)).astype(F32).astype(BF16)
        total[...] += mm_nt(hidden, spread)
        return carry

    lax.fori_loop(0, blocks // group, edge_step, 0)
    pad = -3 * owned % LANES
    sums = jnp.concatenate([total[...], jnp.zeros((width, pad), F32)], axis=1).T
    below, above = sums[:owned].astype(BF16), sums[2 * owned : 3 * owned].astype(BF16)
    own_ref[...] = sums[owned : 2 * owned]
    odd = place % 2 == 1
    cross_ref[...] = jnp.where(odd, above, below)
    chip_ref[...] = jnp.where(odd, below, above)


def wanted_kernel(owned, slot_ref, send_ref, wanted_ref):
    nodes = slot_ref.shape[1]
    blocks, block_edges = send_ref.shape
    places = wanted_ref.shape[1]
    chunk = LANES
    per_chunk = chunk // owned * SEND_CAP
    row, column = iota((chunk, chunk), 0), iota((chunk, chunk), 1)
    before = ((row > column) & (row // owned == column // owned)).astype(F32).astype(BF16)
    local_owner = (iota((chunk, LANES), 0) // owned * SEND_CAP).astype(F32)

    def find(index, best):
        ids = ids_of_rows(slot_ref[...], index * chunk, chunk)
        hit = jnp.zeros((chunk, block_edges), F32)
        for b in range(blocks):
            hit = jnp.maximum(hit, (ids == send_ref[b : b + 1, :]).astype(F32))
        hit = jnp.broadcast_to(jnp.max(hit, axis=1, keepdims=True), (chunk, LANES))
        rank = mm(before, hit.astype(BF16)) + local_owner
        spot = jnp.where(hit > 0, rank.astype(I32) + index * per_chunk, -1)
        spot = jnp.concatenate([spot] * (places // LANES), axis=1)
        found = jnp.where(spot == iota((chunk, places), 1), ids, -1)
        return jnp.maximum(best, jnp.max(found, axis=0, keepdims=True))

    best = lax.fori_loop(0, nodes // chunk, find, jnp.full((1, places), -1, I32), unroll=2)
    best = best.astype(F32)
    for b in range(blocks):
        senders = jnp.broadcast_to(send_ref[b : b + 1, :].astype(F32), (block_edges, block_edges)).T
        senders = jnp.concatenate([senders] * (places // LANES), axis=1)
        wanted_ref[b * block_edges : (b + 1) * block_edges, :] = (
            (senders == best).astype(F32).astype(BF16)
        )


def supply_kernel(blocks, place_ref, slot_ref, request_ref, supply_ref):
    owned = supply_ref.shape[1]
    devices = supply_ref.shape[0] // SEND_CAP
    per_device = request_ref.shape[0] // devices
    ids = ids_of_rows(slot_ref[...], place_ref[0] * owned, owned)
    lane = iota((owned, LANES), 1)
    used = jnp.zeros((owned, LANES), F32)
    for d in range(devices):
        hit = jnp.zeros((owned, request_ref.shape[1]), F32)
        for b in range(blocks):
            at = d * per_device + b
            hit = jnp.maximum(hit, (ids == request_ref[at : at + 1, :]).astype(F32))
        used = jnp.where(lane == d, jnp.max(hit, axis=1, keepdims=True), used)
    before = (iota((owned, owned), 0) > iota((owned, owned), 1)).astype(F32).astype(BF16)
    rank = jnp.where(used > 0, mm(before, used.astype(BF16)), -1.0)
    rank = jnp.concatenate([rank, jnp.full((LANES - owned, LANES), -1.0, F32)], axis=0).T
    slots = iota((SEND_CAP, owned), 0).astype(F32)
    supply = jnp.concatenate(
        [(rank[d : d + 1, :owned] == slots).astype(F32) for d in range(devices)], axis=0
    )
    supply_ref[...] = supply.astype(BF16)


def node_kernel(
    own_ref,
    from_cross_ref,
    from_chip_ref,
    latent_ref,
    edge_out_ref,
    node_input_ref,
    node_bias_ref,
    node_out_ref,
    node_gain_ref,
    mesh_sender_ref,
    supply_ref,
    encoded_ref,
    rows_ref,
):
    width = latent_ref.shape[1]
    latent = latent_ref[...]
    node_sum = own_ref[...] + from_cross_ref[...].astype(F32) + from_chip_ref[...].astype(F32)
    aggregate = mm(node_sum.astype(BF16), edge_out_ref[...]).astype(BF16)
    hidden = mm(latent, node_input_ref[:width]) + mm(aggregate, node_input_ref[width:])
    hidden = silu(hidden + node_bias_ref[...]).astype(BF16)
    encoded = latent.astype(F32) + layer_norm(mm(hidden, node_out_ref[...])) * node_gain_ref[...]
    encoded = encoded.astype(BF16)
    encoded_ref[...] = encoded
    sender_code = mm(encoded, mesh_sender_ref[...]).astype(BF16)
    rows_ref[...] = mm(supply_ref[...], sender_code).astype(BF16)


def receiver_kernel(
    place_ref,
    slot_ref,
    recv_ref,
    encoded_ref,
    mesh_receiver_ref,
    message_bias_ref,
    update_input_ref,
    update_bias_ref,
    incoming_ref,
    pick_ref,
    high_ref,
    low_ref,
    upper_ref,
):
    owned, width = encoded_ref.shape
    blocks = recv_ref.shape[0]
    ids = ids_of_rows(slot_ref[...], place_ref[0] * owned, owned)
    incoming = jnp.concatenate(
        [(ids == recv_ref[b : b + 1, :]).astype(F32) for b in range(blocks)], axis=1
    )
    pick_ref[...] = incoming.T.astype(BF16)
    incoming_ref[...] = incoming.astype(BF16)
    encoded = encoded_ref[...]
    receiver = mm(encoded, mesh_receiver_ref[...]) + message_bias_ref[...]
    high = receiver.astype(BF16)
    high_ref[...] = high
    low_ref[...] = (receiver - high.astype(F32)).astype(BF16)
    upper_ref[...] = mm(encoded, update_input_ref[:width]) + update_bias_ref[...]


def message_kernel(
    wanted_ref,
    piece_ref,
    incoming_ref,
    pick_ref,
    high_ref,
    low_ref,
    upper_ref,
    encoded_ref,
    message_out_ref,
    update_input_ref,
    update_out_ref,
    update_gain_ref,
    out_ref,
):
    width = encoded_ref.shape[1]
    receiver = mm(pick_ref[...], high_ref[...]) + mm(pick_ref[...], low_ref[...])
    message = silu(mm(wanted_ref[...], piece_ref[...]) + receiver).astype(BF16)
    message_sum = mm(incoming_ref[...], message).astype(BF16)
    update = mm(message_sum, message_out_ref[...]).astype(BF16)
    hidden = silu(upper_ref[...] + mm(update, update_input_ref[width:])).astype(BF16)
    out = layer_norm(mm(hidden, update_out_ref[...])) * update_gain_ref[...]
    out_ref[...] = (encoded_ref[...].astype(F32) + out).astype(BF16)


def call(kernel, out_shape, spaces, scratch=(), flops=0, moved=0, vmem=8):
    return pl.pallas_call(
        kernel,
        out_shape=out_shape,
        in_specs=[pl.BlockSpec(memory_space=space) for space in spaces],
        out_specs=jax.tree.map(lambda _: pl.BlockSpec(memory_space=VMEM), out_shape),
        scratch_shapes=scratch,
        compiler_params=pltpu.CompilerParams(vmem_limit_bytes=vmem * MEBI),
        cost_estimate=pl.CostEstimate(flops=flops, bytes_accessed=moved, transcendentals=0),
    )


def hold(value):
    return value if value.size == 1 else pltpu.with_memory_space_constraint(value, HBM)


def shape(*sizes, kind=BF16):
    return jax.ShapeDtypeStruct(sizes, kind)


def per_device(
    grid_in,
    grid_first,
    grid_bias,
    grid_second,
    send_weight,
    edge_bias,
    feat_weight,
    edge_out,
    node_input,
    node_bias,
    node_out,
    node_gain,
    mesh_sender,
    mesh_receiver,
    message_bias,
    message_out,
    update_input,
    update_bias,
    update_out,
    update_gain,
    mesh_latent,
    g2m_send,
    g2m_recv,
    g2m_feat,
    g2m_count,
    mesh_slot,
    mesh_send,
    mesh_recv,
):
    devices = lax.axis_size("bulk")
    position = lax.axis_index("bulk")
    place = position.astype(I32).reshape(1)
    owned, width = mesh_latent.shape
    grid_rows = grid_in.shape[0]
    places = devices * SEND_CAP
    edges = mesh_send.size
    slot = mesh_slot.reshape(1, -1)
    row = lambda vector: vector.reshape(1, -1)

    requests = lax.all_to_all(jnp.tile(mesh_send, (devices, 1)), "bulk", 0, 0, tiled=True)
    operands = (
        grid_first,
        grid_in.T,
        grid_second,
        send_weight,
        row(grid_bias),
        row(edge_bias),
        slot,
        feat_weight,
        g2m_send,
        g2m_recv,
        g2m_feat,
        g2m_count.reshape(1, 1),
    )
    own, cross, chip = call(
        edge_kernel,
        (shape(owned, width, kind=F32), shape(owned, width), shape(owned, width)),
        [SMEM] + [HBM] * len(operands),
        scratch=[VMEM(value.shape, value.dtype) for value in operands]
        + [
            pltpu.VMEM((width, grid_rows + LANES), BF16),
            pltpu.VMEM((width, grid_first.shape[0]), BF16),
            pltpu.VMEM((width, width), BF16),
            pltpu.VMEM((width, width), BF16),
            pltpu.VMEM((width, LANES), F32),
            pltpu.VMEM((width, LANES), F32),
            pltpu.VMEM((width, 3 * owned), F32),
            pltpu.SemaphoreType.DMA((len(operands) - 1 + GRID_STEPS,)),
        ],
        flops=10_000_000_000,
        moved=4_000_000,
        vmem=32,
    )(place, *[hold(value) for value in operands])
    requests, _ = lax.optimization_barrier((requests, own))
    crossing = [(d, d + 1) for d in range(1, devices - 1, 2)]
    within = [(d, d + 1) for d in range(0, devices, 2)]
    both = lambda pairs: pairs + [(b, a) for a, b in pairs]
    from_cross = lax.ppermute(cross, "bulk", both(crossing))
    from_chip = lax.ppermute(chip, "bulk", both(within))
    supply = call(
        functools.partial(supply_kernel, mesh_send.shape[0]),
        shape(places, owned),
        [SMEM] + [VMEM] * 2,
        flops=500_000_000,
        moved=500_000,
    )(place, slot, requests)
    encoded, rows = call(
        node_kernel,
        (shape(owned, width), shape(places, width)),
        [VMEM] * 11,
        flops=500_000_000,
        moved=4_000_000,
    )(
        own,
        from_cross,
        from_chip,
        mesh_latent,
        edge_out,
        node_input,
        row(node_bias),
        node_out,
        row(node_gain),
        mesh_sender,
        supply,
    )
    piece = lax.all_to_all(rows, "bulk", 0, 0, tiled=True)
    mesh_send, _ = lax.optimization_barrier((mesh_send, encoded))
    wanted = call(
        functools.partial(wanted_kernel, owned),
        shape(edges, places),
        [VMEM] * 2,
        flops=1_000_000_000,
        moved=500_000,
    )(slot, mesh_send)
    incoming, pick, high, low, upper = call(
        receiver_kernel,
        (
            shape(owned, edges),
            shape(edges, owned),
            shape(owned, width),
            shape(owned, width),
            shape(owned, width, kind=F32),
        ),
        [SMEM] + [VMEM] * 7,
        flops=1_000_000_000,
        moved=4_000_000,
    )(
        place,
        slot,
        mesh_recv,
        encoded,
        mesh_receiver,
        row(message_bias),
        update_input,
        row(update_bias),
    )
    return call(
        message_kernel,
        shape(owned, width),
        [VMEM] * 12,
        flops=1_000_000_000,
        moved=4_000_000,
    )(
        wanted,
        piece,
        incoming,
        pick,
        high,
        low,
        upper,
        encoded,
        message_out,
        update_input,
        update_out,
        row(update_gain),
    )


def solution(mesh):
    split = {0: ("groups", "bulk"), 20: "bulk", 21: "bulk", 22: "bulk", 23: "bulk", 24: "bulk"}
    split.update({26: "bulk", 27: "bulk"})
    placed = tuple(P(split[at]) if at in split else P() for at in range(28))
    return jax.shard_map(
        per_device,
        mesh=mesh,
        in_specs=placed,
        out_specs=P(("groups", "bulk"), None),
        check_vma=False,
    )
```

```python
import functools
import math

import jax
import jax.numpy as jnp
from jax import lax
from jax.experimental import pallas as pl
from jax.experimental.pallas import tpu as pltpu
from jax.sharding import PartitionSpec as P

F32 = jnp.float32
BF16 = jnp.bfloat16
I32 = jnp.int32
SEND_CAP = 16
LANES = 128
VMEM = pltpu.VMEM
SMEM = pltpu.SMEM
HBM = pltpu.HBM
GRID_STEPS = 4
MEBI = 1024 * 1024


def mm(left, right):
    return jnp.dot(left, right, preferred_element_type=F32)


def mm_nt(left, right):
    return lax.dot_general(left, right, (((1,), (1,)), ((), ())), preferred_element_type=F32)


def silu_half(half):
    return half + half * jnp.tanh(half)


def silu(value):
    return silu_half(0.5 * value)


def layer_norm(value):
    center = value - jnp.mean(value, axis=-1, keepdims=True)
    spread = jnp.mean(center * center, axis=-1, keepdims=True)
    return center * lax.rsqrt(spread + 1e-05)


def iota(shape, dim):
    return lax.broadcasted_iota(I32, shape, dim)


def one_hot(columns, rows):
    hit = columns.astype(jnp.int16) == lax.broadcasted_iota(jnp.int16, (rows, columns.shape[1]), 0)
    return jnp.where(hit, jnp.ones((), BF16), jnp.zeros((), BF16))


def ids_of_rows(slot, first, count):
    nodes = slot.shape[1]
    rows = iota((count, nodes), 0) + first
    return jnp.max(jnp.where(slot == rows, iota((count, nodes), 1), -1), axis=1, keepdims=True)


def edge_kernel(
    place_ref,
    first_hbm,
    grid_hbm,
    second_hbm,
    send_weight_hbm,
    grid_bias_hbm,
    edge_bias_hbm,
    slot_hbm,
    feat_weight_hbm,
    send_hbm,
    recv_hbm,
    feat_hbm,
    count_hbm,
    own_ref,
    cross_ref,
    chip_ref,
    first_ref,
    grid_ref,
    second_ref,
    send_weight_ref,
    grid_bias_ref,
    edge_bias_ref,
    slot_ref,
    feat_weight_ref,
    send_ref,
    recv_ref,
    feat_ref,
    count_ref,
    starts,
    table,
    even_rows,
    odd_rows,
    hidden_ref,
    total,
    sems,
):
    channels, grid_rows = grid_ref.shape
    width = second_ref.shape[1]
    pieces = width // LANES
    blocks, block_edges = send_ref.shape
    owned = own_ref.shape[0]
    feats = feat_ref.shape[1]
    step_rows = grid_rows // GRID_STEPS

    def grid_copy(step):
        part = pl.ds(pl.multiple_of(step * step_rows, step_rows), step_rows)
        return pltpu.make_async_copy(grid_hbm.at[:, part], grid_ref.at[:, part], sems.at[step])

    pairs = [
        (first_hbm, first_ref),
        (second_hbm, second_ref),
        (send_weight_hbm, send_weight_ref),
        (grid_bias_hbm, grid_bias_ref),
        (edge_bias_hbm, edge_bias_ref),
        (send_hbm, send_ref),
        (slot_hbm, slot_ref),
        (feat_weight_hbm, feat_weight_ref),
        (recv_hbm, recv_ref),
        (feat_hbm, feat_ref),
        (count_hbm, count_ref),
        (send_ref, starts),
    ]
    copies = [
        pltpu.make_async_copy(source, target, sems.at[GRID_STEPS + at])
        for at, (source, target) in enumerate(pairs)
    ]
    copies[0].start()
    grid_copy(0).start()
    for copy in copies[1:6]:
        copy.start()
    for step in range(1, GRID_STEPS):
        grid_copy(step).start()
    for copy in copies[6:-1]:
        copy.start()
    copies[0].wait()
    first_ref[...] = first_ref[...] * 0.5
    for copy in copies[1:6]:
        copy.wait()
    send_weight_ref[...] = send_weight_ref[...] * 0.5
    grid_bias = 0.5 * grid_bias_ref[...]
    edge_bias = 0.5 * edge_bias_ref[...]
    senders = send_ref[...]
    send_ref[...] = (senders // 8) * (8 * pieces) + senders % 8
    copies[-1].start()

    def grid_step(step, carry):
        part = pl.ds(pl.multiple_of(step * step_rows, step_rows), step_rows)
        grid_copy(step).wait()
        value = grid_ref[:, part].T
        hidden = silu_half(mm(value, first_ref[...]) + grid_bias).astype(BF16)
        code = layer_norm(mm(hidden, second_ref[...])).astype(BF16)
        row = (mm(code, send_weight_ref[...]) + edge_bias).astype(BF16).astype(F32)
        first = pl.multiple_of(step * (step_rows * pieces), step_rows * pieces)
        for group in range(step_rows // 8):
            for piece in range(pieces):
                at = (group * pieces + piece) * 8
                table[pl.ds(first + at, 8), :] = row[
                    group * 8 : group * 8 + 8, piece * LANES : (piece + 1) * LANES
                ]
        return carry

    lax.fori_loop(0, GRID_STEPS, grid_step, 0)
    for copy in copies[6:]:
        copy.wait()
    place = place_ref[0]
    used = count_ref[...]
    feat_weight = 0.5 * feat_weight_ref[...].astype(F32)
    feat_weight = jnp.concatenate([feat_weight, jnp.zeros((8 - feats, width), F32)], axis=0)
    feat_weight = feat_weight.astype(BF16)
    ids = ids_of_rows(slot_ref[...], (place - 1) * owned, 3 * owned)
    group = 2 if blocks % 4 == 0 else 1
    chunks = blocks // group
    part_rows = 64
    total[...] = jnp.zeros_like(total)

    def gather(chunk, edges, target):
        for edge in edges:
            start = starts[chunk * group + edge // block_edges, edge % block_edges]
            target[pl.ds(edge // 8 * (8 * pieces) + edge % 8, pieces, stride=8), :] = table[
                pl.ds(start, pieces, stride=8), :
            ]

    def rows_of(source, first, count):
        return jnp.concatenate(
            [
                jnp.concatenate(
                    [
                        source[pl.ds((at * pieces + piece) * 8, 8), :]
                        for at in range(first // 8, (first + count) // 8)
                    ],
                    axis=0,
                )
                for piece in range(pieces)
            ],
            axis=1,
        )

    def work(chunk, source, target):
        here = [chunk * group + b for b in range(group)]
        feat = jnp.concatenate([feat_ref[b] for b in here], axis=1)
        feat = jnp.concatenate([feat, jnp.zeros((8 - feats, feat.shape[1]), F32)], axis=0)
        extra = mm(feat.T.astype(BF16), feat_weight)
        after = jnp.minimum(chunk + 1, chunks - 1)
        for first in range(0, group * block_edges, part_rows):
            gather(after, range(first, first + part_rows), target)
            half = rows_of(source, first, part_rows) + extra[first : first + part_rows]
            hidden_ref[first : first + part_rows, :] = silu_half(half).astype(BF16)
        receivers = [jnp.where(b < used, recv_ref[pl.ds(b, 1), :], -2) for b in here]
        spread = (ids == jnp.concatenate(receivers, axis=1)).astype(F32).astype(BF16)
        total[...] += mm(spread, hidden_ref[...])

    def edge_step(step, carry):
        work(2 * step, even_rows, odd_rows)
        work(2 * step + 1, odd_rows, even_rows)
        return carry

    gather(0, range(group * block_edges), even_rows)
    lax.fori_loop(0, chunks // 2, edge_step, 0)
    odd = place % 2 == 1
    below, above = total[:owned].astype(BF16), total[2 * owned :].astype(BF16)
    own_ref[...] = total[owned : 2 * owned]
    cross_ref[...] = jnp.where(odd, above, below)
    chip_ref[...] = jnp.where(odd, below, above)


def wanted_kernel(owned, slot_ref, send_ref, wanted_ref):
    nodes = slot_ref.shape[1]
    blocks, block_edges = send_ref.shape
    places = wanted_ref.shape[1]
    chunk = LANES
    per_chunk = chunk // owned * SEND_CAP
    row, column = iota((chunk, chunk), 0), iota((chunk, chunk), 1)
    before = ((row > column) & (row // owned == column // owned)).astype(F32).astype(BF16)
    local_owner = (iota((chunk, LANES), 0) // owned * SEND_CAP).astype(F32)

    def find(index, best):
        ids = ids_of_rows(slot_ref[...], index * chunk, chunk)
        hit = jnp.zeros((chunk, block_edges), F32)
        for b in range(blocks):
            hit = jnp.maximum(hit, (ids == send_ref[b : b + 1, :]).astype(F32))
        hit = jnp.broadcast_to(jnp.max(hit, axis=1, keepdims=True), (chunk, LANES))
        rank = mm(before, hit.astype(BF16)) + local_owner
        spot = jnp.where(hit > 0, rank.astype(I32) + index * per_chunk, -1)
        spot = jnp.concatenate([spot] * (places // LANES), axis=1)
        found = jnp.where(spot == iota((chunk, places), 1), ids, -1)
        return jnp.maximum(best, jnp.max(found, axis=0, keepdims=True))

    best = lax.fori_loop(0, nodes // chunk, find, jnp.full((1, places), -1, I32), unroll=2)
    best = best.astype(F32)
    for b in range(blocks):
        senders = jnp.broadcast_to(send_ref[b : b + 1, :].astype(F32), (block_edges, block_edges)).T
        senders = jnp.concatenate([senders] * (places // LANES), axis=1)
        wanted_ref[b * block_edges : (b + 1) * block_edges, :] = (
            (senders == best).astype(F32).astype(BF16)
        )


def supply_kernel(blocks, place_ref, slot_ref, request_ref, supply_ref):
    owned = supply_ref.shape[1]
    devices = supply_ref.shape[0] // SEND_CAP
    per_device = request_ref.shape[0] // devices
    ids = ids_of_rows(slot_ref[...], place_ref[0] * owned, owned)
    lane = iota((owned, LANES), 1)
    used = jnp.zeros((owned, LANES), F32)
    for d in range(devices):
        hit = jnp.zeros((owned, request_ref.shape[1]), F32)
        for b in range(blocks):
            at = d * per_device + b
            hit = jnp.maximum(hit, (ids == request_ref[at : at + 1, :]).astype(F32))
        used = jnp.where(lane == d, jnp.max(hit, axis=1, keepdims=True), used)
    before = (iota((owned, owned), 0) > iota((owned, owned), 1)).astype(F32).astype(BF16)
    rank = jnp.where(used > 0, mm(before, used.astype(BF16)), -1.0)
    rank = jnp.concatenate([rank, jnp.full((LANES - owned, LANES), -1.0, F32)], axis=0).T
    slots = iota((SEND_CAP, owned), 0).astype(F32)
    supply = jnp.concatenate(
        [(rank[d : d + 1, :owned] == slots).astype(F32) for d in range(devices)], axis=0
    )
    supply_ref[...] = supply.astype(BF16)


def node_kernel(
    own_ref,
    from_cross_ref,
    from_chip_ref,
    latent_ref,
    edge_out_ref,
    node_input_ref,
    node_bias_ref,
    node_out_ref,
    node_gain_ref,
    mesh_sender_ref,
    supply_ref,
    encoded_ref,
    rows_ref,
):
    width = latent_ref.shape[1]
    latent = latent_ref[...]
    node_sum = own_ref[...] + from_cross_ref[...].astype(F32) + from_chip_ref[...].astype(F32)
    aggregate = mm(node_sum.astype(BF16), edge_out_ref[...]).astype(BF16)
    hidden = mm(latent, node_input_ref[:width]) + mm(aggregate, node_input_ref[width:])
    hidden = silu(hidden + node_bias_ref[...]).astype(BF16)
    encoded = latent.astype(F32) + layer_norm(mm(hidden, node_out_ref[...])) * node_gain_ref[...]
    encoded = encoded.astype(BF16)
    encoded_ref[...] = encoded
    sender_code = mm(encoded, mesh_sender_ref[...]).astype(BF16)
    rows_ref[...] = mm(supply_ref[...], sender_code).astype(BF16)


def receiver_kernel(
    place_ref,
    slot_ref,
    recv_ref,
    encoded_ref,
    mesh_receiver_ref,
    message_bias_ref,
    update_input_ref,
    update_bias_ref,
    incoming_ref,
    pick_ref,
    high_ref,
    low_ref,
    upper_ref,
):
    owned, width = encoded_ref.shape
    blocks = recv_ref.shape[0]
    ids = ids_of_rows(slot_ref[...], place_ref[0] * owned, owned)
    incoming = jnp.concatenate(
        [(ids == recv_ref[b : b + 1, :]).astype(F32) for b in range(blocks)], axis=1
    )
    pick_ref[...] = incoming.T.astype(BF16)
    incoming_ref[...] = incoming.astype(BF16)
    encoded = encoded_ref[...]
    receiver = mm(encoded, mesh_receiver_ref[...]) + message_bias_ref[...]
    high = receiver.astype(BF16)
    high_ref[...] = high
    low_ref[...] = (receiver - high.astype(F32)).astype(BF16)
    upper_ref[...] = mm(encoded, update_input_ref[:width]) + update_bias_ref[...]


def message_kernel(
    wanted_ref,
    piece_ref,
    incoming_ref,
    pick_ref,
    high_ref,
    low_ref,
    upper_ref,
    encoded_ref,
    message_out_ref,
    update_input_ref,
    update_out_ref,
    update_gain_ref,
    out_ref,
):
    width = encoded_ref.shape[1]
    receiver = mm(pick_ref[...], high_ref[...]) + mm(pick_ref[...], low_ref[...])
    message = silu(mm(wanted_ref[...], piece_ref[...]) + receiver).astype(BF16)
    message_sum = mm(incoming_ref[...], message).astype(BF16)
    update = mm(message_sum, message_out_ref[...]).astype(BF16)
    hidden = silu(upper_ref[...] + mm(update, update_input_ref[width:])).astype(BF16)
    out = layer_norm(mm(hidden, update_out_ref[...])) * update_gain_ref[...]
    out_ref[...] = (encoded_ref[...].astype(F32) + out).astype(BF16)


def call(kernel, out_shape, spaces, scratch=(), flops=0, moved=0, vmem=8):
    return pl.pallas_call(
        kernel,
        out_shape=out_shape,
        in_specs=[pl.BlockSpec(memory_space=space) for space in spaces],
        out_specs=jax.tree.map(lambda _: pl.BlockSpec(memory_space=VMEM), out_shape),
        scratch_shapes=scratch,
        compiler_params=pltpu.CompilerParams(vmem_limit_bytes=vmem * MEBI),
        cost_estimate=pl.CostEstimate(flops=flops, bytes_accessed=moved, transcendentals=0),
    )


def hold(value):
    return value if value.size == 1 else pltpu.with_memory_space_constraint(value, HBM)


def shape(*sizes, kind=BF16):
    return jax.ShapeDtypeStruct(sizes, kind)


def per_device(
    grid_in,
    grid_first,
    grid_bias,
    grid_second,
    send_weight,
    edge_bias,
    feat_weight,
    edge_out,
    node_input,
    node_bias,
    node_out,
    node_gain,
    mesh_sender,
    mesh_receiver,
    message_bias,
    message_out,
    update_input,
    update_bias,
    update_out,
    update_gain,
    mesh_latent,
    g2m_send,
    g2m_recv,
    g2m_feat,
    g2m_count,
    mesh_slot,
    mesh_send,
    mesh_recv,
):
    devices = lax.axis_size("bulk")
    position = lax.axis_index("bulk")
    place = position.astype(I32).reshape(1)
    owned, width = mesh_latent.shape
    grid_rows = grid_in.shape[0]
    places = devices * SEND_CAP
    edges = mesh_send.size
    slot = mesh_slot.reshape(1, -1)
    row = lambda vector: vector.reshape(1, -1)

    requests = lax.all_to_all(jnp.tile(mesh_send, (devices, 1)), "bulk", 0, 0, tiled=True)
    operands = (
        grid_first,
        grid_in.T,
        grid_second,
        send_weight,
        row(grid_bias),
        row(edge_bias),
        slot,
        feat_weight,
        g2m_send,
        g2m_recv,
        g2m_feat,
        g2m_count.reshape(1, 1),
    )
    own, cross, chip = call(
        edge_kernel,
        (shape(owned, width, kind=F32), shape(owned, width), shape(owned, width)),
        [SMEM] + [HBM] * len(operands),
        scratch=[VMEM(value.shape, value.dtype) for value in operands]
        + [
            SMEM(g2m_send.shape, I32),
            VMEM((grid_rows * (width // LANES), LANES), F32),
            VMEM((2 * g2m_send.shape[1] * (width // LANES), LANES), F32),
            VMEM((2 * g2m_send.shape[1] * (width // LANES), LANES), F32),
            VMEM((2 * g2m_send.shape[1], width), BF16),
            VMEM((3 * owned, width), F32),
            pltpu.SemaphoreType.DMA((len(operands) + GRID_STEPS,)),
        ],
        flops=10_000_000_000,
        moved=4_000_000,
        vmem=32,
    )(place, *[hold(value) for value in operands])
    requests, _ = lax.optimization_barrier((requests, own))
    crossing = [(d, d + 1) for d in range(1, devices - 1, 2)]
    within = [(d, d + 1) for d in range(0, devices, 2)]
    both = lambda pairs: pairs + [(b, a) for a, b in pairs]
    from_cross = lax.ppermute(cross, "bulk", both(crossing))
    from_chip = lax.ppermute(chip, "bulk", both(within))
    supply = call(
        functools.partial(supply_kernel, mesh_send.shape[0]),
        shape(places, owned),
        [SMEM] + [VMEM] * 2,
        flops=500_000_000,
        moved=500_000,
    )(place, slot, requests)
    encoded, rows = call(
        node_kernel,
        (shape(owned, width), shape(places, width)),
        [VMEM] * 11,
        flops=500_000_000,
        moved=4_000_000,
    )(
        own,
        from_cross,
        from_chip,
        mesh_latent,
        edge_out,
        node_input,
        row(node_bias),
        node_out,
        row(node_gain),
        mesh_sender,
        supply,
    )
    piece = lax.all_to_all(rows, "bulk", 0, 0, tiled=True)
    mesh_send, _ = lax.optimization_barrier((mesh_send, encoded))
    wanted = call(
        functools.partial(wanted_kernel, owned),
        shape(edges, places),
        [VMEM] * 2,
        flops=1_000_000_000,
        moved=500_000,
    )(slot, mesh_send)
    incoming, pick, high, low, upper = call(
        receiver_kernel,
        (
            shape(owned, edges),
            shape(edges, owned),
            shape(owned, width),
            shape(owned, width),
            shape(owned, width, kind=F32),
        ),
        [SMEM] + [VMEM] * 7,
        flops=1_000_000_000,
        moved=4_000_000,
    )(
        place,
        slot,
        mesh_recv,
        encoded,
        mesh_receiver,
        row(message_bias),
        update_input,
        row(update_bias),
    )
    return call(
        message_kernel,
        shape(owned, width),
        [VMEM] * 12,
        flops=1_000_000_000,
        moved=4_000_000,
    )(
        wanted,
        piece,
        incoming,
        pick,
        high,
        low,
        upper,
        encoded,
        message_out,
        update_input,
        update_out,
        row(update_gain),
    )


def solution(mesh):
    split = {0: ("groups", "bulk"), 20: "bulk", 21: "bulk", 22: "bulk", 23: "bulk", 24: "bulk"}
    split.update({26: "bulk", 27: "bulk"})
    placed = tuple(P(split[at]) if at in split else P() for at in range(28))
    return jax.shard_map(
        per_device,
        mesh=mesh,
        in_specs=placed,
        out_specs=P(("groups", "bulk"), None),
        check_vma=False,
    )
```

```python
import functools
import math

import jax
import jax.numpy as jnp
from jax import lax
from jax.experimental import pallas as pl
from jax.experimental.pallas import tpu as pltpu
from jax.sharding import PartitionSpec as P

F32 = jnp.float32
BF16 = jnp.bfloat16
I32 = jnp.int32
SEND_CAP = 16
LANES = 128
VMEM = pltpu.VMEM
SMEM = pltpu.SMEM
HBM = pltpu.HBM
GRID_STEPS = 4
MEBI = 1024 * 1024


def mm(left, right):
    return jnp.dot(left, right, preferred_element_type=F32)


def mm_nt(left, right):
    return lax.dot_general(left, right, (((1,), (1,)), ((), ())), preferred_element_type=F32)


def silu_half(half):
    return half + half * jnp.tanh(half)


def silu(value):
    return silu_half(0.5 * value)


def layer_norm(value):
    center = value - jnp.mean(value, axis=-1, keepdims=True)
    spread = jnp.mean(center * center, axis=-1, keepdims=True)
    return center * lax.rsqrt(spread + 1e-05)


def iota(shape, dim):
    return lax.broadcasted_iota(I32, shape, dim)


def one_hot(columns, rows):
    hit = columns.astype(jnp.int16) == lax.broadcasted_iota(jnp.int16, (rows, columns.shape[1]), 0)
    return jnp.where(hit, jnp.ones((), BF16), jnp.zeros((), BF16))


def ids_of_rows(slot, first, count):
    nodes = slot.shape[1]
    rows = iota((count, nodes), 0) + first
    return jnp.max(jnp.where(slot == rows, iota((count, nodes), 1), -1), axis=1, keepdims=True)


def edge_kernel(
    place_ref,
    first_hbm,
    grid_hbm,
    second_hbm,
    send_weight_hbm,
    grid_bias_hbm,
    edge_bias_hbm,
    slot_hbm,
    feat_weight_hbm,
    send_hbm,
    recv_hbm,
    feat_hbm,
    count_hbm,
    own_ref,
    cross_ref,
    chip_ref,
    first_ref,
    grid_ref,
    second_ref,
    send_weight_ref,
    grid_bias_ref,
    edge_bias_ref,
    slot_ref,
    feat_weight_ref,
    send_ref,
    recv_ref,
    feat_ref,
    count_ref,
    starts,
    table,
    even_rows,
    odd_rows,
    hidden_ref,
    ids_ref,
    total,
    sems,
):
    channels, grid_rows = grid_ref.shape
    width = second_ref.shape[1]
    pieces = width // LANES
    blocks, block_edges = send_ref.shape
    owned = own_ref.shape[0]
    feats = feat_ref.shape[1]
    step_rows = grid_rows // GRID_STEPS

    def grid_copy(step):
        part = pl.ds(pl.multiple_of(step * step_rows, step_rows), step_rows)
        return pltpu.make_async_copy(grid_hbm.at[:, part], grid_ref.at[:, part], sems.at[step])

    pairs = [
        (first_hbm, first_ref),
        (second_hbm, second_ref),
        (send_weight_hbm, send_weight_ref),
        (grid_bias_hbm, grid_bias_ref),
        (edge_bias_hbm, edge_bias_ref),
        (send_hbm, send_ref),
        (slot_hbm, slot_ref),
        (feat_weight_hbm, feat_weight_ref),
        (recv_hbm, recv_ref),
        (feat_hbm, feat_ref),
        (count_hbm, count_ref),
        (send_ref, starts),
    ]
    copies = [
        pltpu.make_async_copy(source, target, sems.at[GRID_STEPS + at])
        for at, (source, target) in enumerate(pairs)
    ]
    first_copy, second_copy, send_weight_copy, grid_bias_copy, edge_bias_copy, send_copy = copies[:6]
    slot_copy, starts_copy = copies[6], copies[-1]
    first_copy.start()
    grid_copy(0).start()
    for copy in copies[1:-1]:
        copy.start()
    for step in range(1, GRID_STEPS):
        grid_copy(step).start()
    send_copy.wait()
    senders = send_ref[...]
    send_ref[...] = (senders // 8) * (8 * pieces) + senders % 8
    starts_copy.start()
    slot_copy.wait()
    place = place_ref[0]
    ids_ref[...] = jnp.broadcast_to(
        ids_of_rows(slot_ref[...], (place - 1) * owned, 3 * owned), ids_ref.shape
    )
    total[...] = jnp.zeros_like(total)
    first_copy.wait()
    first_ref[...] = first_ref[...] * 0.5
    second_copy.wait()
    send_weight_copy.wait()
    send_weight_ref[...] = send_weight_ref[...] * 0.5
    grid_bias_copy.wait()
    edge_bias_copy.wait()
    grid_bias = 0.5 * grid_bias_ref[...]
    edge_bias = 0.5 * edge_bias_ref[...]
    half_rows = step_rows // 2

    def grid_step(step, carry):
        grid_copy(step).wait()
        first = pl.multiple_of(step * step_rows, step_rows)
        values = [
            mm(grid_ref[:, pl.ds(first + at, half_rows)].T, first_ref[...])
            for at in (0, half_rows)
        ]
        values = [silu_half(value + grid_bias).astype(BF16) for value in values]
        values = [mm(value, second_ref[...]) for value in values]
        values = [layer_norm(value).astype(BF16) for value in values]
        values = [mm(value, send_weight_ref[...]) for value in values]
        for half, value in enumerate(values):
            row = (value + edge_bias).astype(BF16).astype(F32)
            base = pl.multiple_of((first + half * half_rows) * pieces, half_rows * pieces)
            for group in range(half_rows // 8):
                for piece in range(pieces):
                    at = (group * pieces + piece) * 8
                    table[pl.ds(base + at, 8), :] = row[
                        group * 8 : group * 8 + 8, piece * LANES : (piece + 1) * LANES
                    ]
        return carry

    lax.fori_loop(0, GRID_STEPS, grid_step, 0)
    for copy in copies[7:]:
        copy.wait()
    used = count_ref[...]
    feat_weight = 0.5 * feat_weight_ref[...].astype(F32)
    feat_weight = jnp.concatenate([feat_weight, jnp.zeros((8 - feats, width), F32)], axis=0)
    feat_weight = feat_weight.astype(BF16)
    group = 2 if blocks % 4 == 0 else 1
    chunks = blocks // group
    part_rows = 64

    def gather(chunk, edges, target):
        for edge in edges:
            start = starts[chunk * group + edge // block_edges, edge % block_edges]
            target[pl.ds(edge // 8 * (8 * pieces) + edge % 8, pieces, stride=8), :] = table[
                pl.ds(start, pieces, stride=8), :
            ]

    def rows_of(source, first, count):
        return jnp.concatenate(
            [
                jnp.concatenate(
                    [
                        source[pl.ds((at * pieces + piece) * 8, 8), :]
                        for at in range(first // 8, (first + count) // 8)
                    ],
                    axis=0,
                )
                for piece in range(pieces)
            ],
            axis=1,
        )

    def work(chunk, source, target):
        here = [chunk * group + b for b in range(group)]
        feat = jnp.concatenate([feat_ref[b] for b in here], axis=1)
        feat = jnp.concatenate([feat, jnp.zeros((8 - feats, feat.shape[1]), F32)], axis=0)
        extra = mm(feat.T.astype(BF16), feat_weight)
        after = jnp.minimum(chunk + 1, chunks - 1)
        for first in range(0, group * block_edges, part_rows):
            gather(after, range(first, first + part_rows), target)
            half = rows_of(source, first, part_rows) + extra[first : first + part_rows]
            hidden_ref[first : first + part_rows, :] = silu_half(half).astype(BF16)
        receivers = [jnp.where(b < used, recv_ref[pl.ds(b, 1), :], -2) for b in here]
        spread = jnp.concatenate([(ids_ref[...] == row).astype(F32) for row in receivers], axis=1)
        spread = spread.astype(BF16)
        total[...] += mm(spread, hidden_ref[...])

    def edge_step(step, carry):
        work(2 * step, even_rows, odd_rows)
        work(2 * step + 1, odd_rows, even_rows)
        return carry

    gather(0, range(group * block_edges), even_rows)
    lax.fori_loop(0, chunks // 2, edge_step, 0)
    odd = place % 2 == 1
    below, above = total[:owned].astype(BF16), total[2 * owned :].astype(BF16)
    own_ref[...] = total[owned : 2 * owned]
    cross_ref[...] = jnp.where(odd, above, below)
    chip_ref[...] = jnp.where(odd, below, above)


def wanted_kernel(owned, slot_ref, send_ref, wanted_ref):
    nodes = slot_ref.shape[1]
    blocks, block_edges = send_ref.shape
    places = wanted_ref.shape[1]
    chunk = LANES
    per_chunk = chunk // owned * SEND_CAP
    row, column = iota((chunk, chunk), 0), iota((chunk, chunk), 1)
    before = ((row > column) & (row // owned == column // owned)).astype(F32).astype(BF16)
    local_owner = (iota((chunk, LANES), 0) // owned * SEND_CAP).astype(F32)

    def find(index, best):
        ids = ids_of_rows(slot_ref[...], index * chunk, chunk)
        hit = jnp.zeros((chunk, block_edges), F32)
        for b in range(blocks):
            hit = jnp.maximum(hit, (ids == send_ref[b : b + 1, :]).astype(F32))
        hit = jnp.broadcast_to(jnp.max(hit, axis=1, keepdims=True), (chunk, LANES))
        rank = mm(before, hit.astype(BF16)) + local_owner
        spot = jnp.where(hit > 0, rank.astype(I32) + index * per_chunk, -1)
        spot = jnp.concatenate([spot] * (places // LANES), axis=1)
        found = jnp.where(spot == iota((chunk, places), 1), ids, -1)
        return jnp.maximum(best, jnp.max(found, axis=0, keepdims=True))

    best = lax.fori_loop(0, nodes // chunk, find, jnp.full((1, places), -1, I32), unroll=2)
    best = best.astype(F32)
    for b in range(blocks):
        senders = jnp.broadcast_to(send_ref[b : b + 1, :].astype(F32), (block_edges, block_edges)).T
        senders = jnp.concatenate([senders] * (places // LANES), axis=1)
        wanted_ref[b * block_edges : (b + 1) * block_edges, :] = (
            (senders == best).astype(F32).astype(BF16)
        )


def supply_kernel(blocks, place_ref, slot_ref, request_ref, supply_ref):
    owned = supply_ref.shape[1]
    devices = supply_ref.shape[0] // SEND_CAP
    per_device = request_ref.shape[0] // devices
    ids = ids_of_rows(slot_ref[...], place_ref[0] * owned, owned)
    lane = iota((owned, LANES), 1)
    used = jnp.zeros((owned, LANES), F32)
    for d in range(devices):
        hit = jnp.zeros((owned, request_ref.shape[1]), F32)
        for b in range(blocks):
            at = d * per_device + b
            hit = jnp.maximum(hit, (ids == request_ref[at : at + 1, :]).astype(F32))
        used = jnp.where(lane == d, jnp.max(hit, axis=1, keepdims=True), used)
    before = (iota((owned, owned), 0) > iota((owned, owned), 1)).astype(F32).astype(BF16)
    rank = jnp.where(used > 0, mm(before, used.astype(BF16)), -1.0)
    rank = jnp.concatenate([rank, jnp.full((LANES - owned, LANES), -1.0, F32)], axis=0).T
    slots = iota((SEND_CAP, owned), 0).astype(F32)
    supply = jnp.concatenate(
        [(rank[d : d + 1, :owned] == slots).astype(F32) for d in range(devices)], axis=0
    )
    supply_ref[...] = supply.astype(BF16)


def node_kernel(
    own_ref,
    from_cross_ref,
    from_chip_ref,
    latent_ref,
    edge_out_ref,
    node_input_ref,
    node_bias_ref,
    node_out_ref,
    node_gain_ref,
    mesh_sender_ref,
    supply_ref,
    encoded_ref,
    rows_ref,
):
    width = latent_ref.shape[1]
    latent = latent_ref[...]
    node_sum = own_ref[...] + from_cross_ref[...].astype(F32) + from_chip_ref[...].astype(F32)
    aggregate = mm(node_sum.astype(BF16), edge_out_ref[...]).astype(BF16)
    hidden = mm(latent, node_input_ref[:width]) + mm(aggregate, node_input_ref[width:])
    hidden = silu(hidden + node_bias_ref[...]).astype(BF16)
    encoded = latent.astype(F32) + layer_norm(mm(hidden, node_out_ref[...])) * node_gain_ref[...]
    encoded = encoded.astype(BF16)
    encoded_ref[...] = encoded
    sender_code = mm(encoded, mesh_sender_ref[...]).astype(BF16)
    rows_ref[...] = mm(supply_ref[...], sender_code).astype(BF16)


def receiver_kernel(
    place_ref,
    slot_ref,
    recv_ref,
    encoded_ref,
    mesh_receiver_ref,
    message_bias_ref,
    update_input_ref,
    update_bias_ref,
    incoming_ref,
    pick_ref,
    parts_ref,
    upper_ref,
):
    owned, width = encoded_ref.shape
    blocks = recv_ref.shape[0]
    ids = ids_of_rows(slot_ref[...], place_ref[0] * owned, owned)
    incoming = jnp.concatenate(
        [(ids == recv_ref[b : b + 1, :]).astype(F32) for b in range(blocks)], axis=1
    )
    pick = incoming.T.astype(BF16)
    pick_ref[...] = jnp.concatenate([pick, pick], axis=1)
    incoming_ref[...] = incoming.astype(BF16)
    encoded = encoded_ref[...]
    receiver = mm(encoded, mesh_receiver_ref[...]) + message_bias_ref[...]
    high = receiver.astype(BF16)
    parts_ref[:owned, :] = high
    parts_ref[owned:, :] = (receiver - high.astype(F32)).astype(BF16)
    upper_ref[...] = mm(encoded, update_input_ref[:width]) + update_bias_ref[...]


def message_kernel(
    wanted_ref,
    piece_ref,
    incoming_ref,
    pick_ref,
    parts_ref,
    upper_ref,
    encoded_ref,
    message_out_ref,
    update_input_ref,
    update_out_ref,
    update_gain_ref,
    out_ref,
):
    width = encoded_ref.shape[1]
    chosen = jnp.concatenate([wanted_ref[...], pick_ref[...]], axis=1)
    codes = jnp.concatenate([piece_ref[...], parts_ref[...]], axis=0)
    message = silu(mm(chosen, codes)).astype(BF16)
    message_sum = mm(incoming_ref[...], message).astype(BF16)
    update = mm(message_sum, message_out_ref[...]).astype(BF16)
    hidden = silu(upper_ref[...] + mm(update, update_input_ref[width:])).astype(BF16)
    out = layer_norm(mm(hidden, update_out_ref[...])) * update_gain_ref[...]
    out_ref[...] = (encoded_ref[...].astype(F32) + out).astype(BF16)


def call(kernel, out_shape, spaces, scratch=(), flops=0, moved=0, vmem=8):
    return pl.pallas_call(
        kernel,
        out_shape=out_shape,
        in_specs=[pl.BlockSpec(memory_space=space) for space in spaces],
        out_specs=jax.tree.map(lambda _: pl.BlockSpec(memory_space=VMEM), out_shape),
        scratch_shapes=scratch,
        compiler_params=pltpu.CompilerParams(vmem_limit_bytes=vmem * MEBI),
        cost_estimate=pl.CostEstimate(flops=flops, bytes_accessed=moved, transcendentals=0),
    )


def hold(value):
    return value if value.size == 1 else pltpu.with_memory_space_constraint(value, HBM)


def shape(*sizes, kind=BF16):
    return jax.ShapeDtypeStruct(sizes, kind)


def per_device(
    grid_in,
    grid_first,
    grid_bias,
    grid_second,
    send_weight,
    edge_bias,
    feat_weight,
    edge_out,
    node_input,
    node_bias,
    node_out,
    node_gain,
    mesh_sender,
    mesh_receiver,
    message_bias,
    message_out,
    update_input,
    update_bias,
    update_out,
    update_gain,
    mesh_latent,
    g2m_send,
    g2m_recv,
    g2m_feat,
    g2m_count,
    mesh_slot,
    mesh_send,
    mesh_recv,
):
    devices = lax.axis_size("bulk")
    position = lax.axis_index("bulk")
    place = position.astype(I32).reshape(1)
    owned, width = mesh_latent.shape
    grid_rows = grid_in.shape[0]
    places = devices * SEND_CAP
    edges = mesh_send.size
    slot = mesh_slot.reshape(1, -1)
    row = lambda vector: vector.reshape(1, -1)

    requests = lax.all_to_all(jnp.tile(mesh_send, (devices, 1)), "bulk", 0, 0, tiled=True)
    operands = (
        grid_first,
        grid_in.T,
        grid_second,
        send_weight,
        row(grid_bias),
        row(edge_bias),
        slot,
        feat_weight,
        g2m_send,
        g2m_recv,
        g2m_feat,
        g2m_count.reshape(1, 1),
    )
    own, cross, chip = call(
        edge_kernel,
        (shape(owned, width, kind=F32), shape(owned, width), shape(owned, width)),
        [SMEM] + [HBM] * len(operands),
        scratch=[VMEM(value.shape, value.dtype) for value in operands]
        + [
            SMEM(g2m_send.shape, I32),
            VMEM((grid_rows * (width // LANES), LANES), F32),
            VMEM((2 * g2m_send.shape[1] * (width // LANES), LANES), F32),
            VMEM((2 * g2m_send.shape[1] * (width // LANES), LANES), F32),
            VMEM((2 * g2m_send.shape[1], width), BF16),
            VMEM((3 * owned, LANES), I32),
            VMEM((3 * owned, width), F32),
            pltpu.SemaphoreType.DMA((len(operands) + GRID_STEPS,)),
        ],
        flops=10_000_000_000,
        moved=4_000_000,
        vmem=32,
    )(place, *[hold(value) for value in operands])
    requests, _ = lax.optimization_barrier((requests, own))
    crossing = [(d, d + 1) for d in range(1, devices - 1, 2)]
    within = [(d, d + 1) for d in range(0, devices, 2)]
    both = lambda pairs: pairs + [(b, a) for a, b in pairs]
    from_cross = lax.ppermute(cross, "bulk", both(crossing))
    from_chip = lax.ppermute(chip, "bulk", both(within))
    supply = call(
        functools.partial(supply_kernel, mesh_send.shape[0]),
        shape(places, owned),
        [SMEM] + [VMEM] * 2,
        flops=500_000_000,
        moved=500_000,
    )(place, slot, requests)
    encoded, rows = call(
        node_kernel,
        (shape(owned, width), shape(places, width)),
        [VMEM] * 11,
        flops=500_000_000,
        moved=4_000_000,
    )(
        own,
        from_cross,
        from_chip,
        mesh_latent,
        edge_out,
        node_input,
        row(node_bias),
        node_out,
        row(node_gain),
        mesh_sender,
        supply,
    )
    rows = pltpu.with_memory_space_constraint(rows, VMEM)
    piece = lax.all_to_all(rows, "bulk", 0, 0, tiled=True)
    mesh_send, _ = lax.optimization_barrier((mesh_send, encoded))
    wanted = call(
        functools.partial(wanted_kernel, owned),
        shape(edges, places),
        [VMEM] * 2,
        flops=1_000_000_000,
        moved=500_000,
    )(slot, mesh_send)
    incoming, pick, parts, upper = call(
        receiver_kernel,
        (
            shape(owned, edges),
            shape(edges, 2 * owned),
            shape(2 * owned, width),
            shape(owned, width, kind=F32),
        ),
        [SMEM] + [VMEM] * 7,
        flops=1_000_000_000,
        moved=4_000_000,
    )(
        place,
        slot,
        mesh_recv,
        encoded,
        mesh_receiver,
        row(message_bias),
        update_input,
        row(update_bias),
    )
    return call(
        message_kernel,
        shape(owned, width),
        [VMEM] * 11,
        flops=1_000_000_000,
        moved=4_000_000,
    )(
        wanted,
        piece,
        incoming,
        pick,
        parts,
        upper,
        encoded,
        message_out,
        update_input,
        update_out,
        row(update_gain),
    )


def solution(mesh):
    split = {0: ("groups", "bulk"), 20: "bulk", 21: "bulk", 22: "bulk", 23: "bulk", 24: "bulk"}
    split.update({26: "bulk", 27: "bulk"})
    placed = tuple(P(split[at]) if at in split else P() for at in range(28))
    return jax.shard_map(
        per_device,
        mesh=mesh,
        in_specs=placed,
        out_specs=P(("groups", "bulk"), None),
        check_vma=False,
    )
```

```python
import functools
import math

import jax
import jax.numpy as jnp
from jax import lax
from jax.experimental import pallas as pl
from jax.experimental.pallas import tpu as pltpu
from jax.sharding import PartitionSpec as P

F32 = jnp.float32
BF16 = jnp.bfloat16
I32 = jnp.int32
SEND_CAP = 16
LANES = 128
VMEM = pltpu.VMEM
SMEM = pltpu.SMEM
HBM = pltpu.HBM
GRID_STEPS = 4
MEBI = 1024 * 1024


def mm(left, right):
    return jnp.dot(left, right, preferred_element_type=F32)


def mm_nt(left, right):
    return lax.dot_general(left, right, (((1,), (1,)), ((), ())), preferred_element_type=F32)


def silu_half(half):
    return half + half * jnp.tanh(half)


def silu(value):
    return silu_half(0.5 * value)


def layer_norm(value, axis=-1):
    center = value - jnp.mean(value, axis=axis, keepdims=True)
    spread = jnp.mean(center * center, axis=axis, keepdims=True)
    return center * lax.rsqrt(spread + 1e-05)


def iota(shape, dim):
    return lax.broadcasted_iota(I32, shape, dim)


def one_hot(columns, rows):
    hit = columns.astype(jnp.int16) == lax.broadcasted_iota(jnp.int16, (rows, columns.shape[1]), 0)
    return jnp.where(hit, jnp.ones((), BF16), jnp.zeros((), BF16))


def ids_of_rows(slot, first, count):
    nodes = slot.shape[1]
    rows = iota((count, nodes), 0) + first
    return jnp.max(jnp.where(slot == rows, iota((count, nodes), 1), -1), axis=1, keepdims=True)


def edge_kernel(
    place_ref,
    first_hbm,
    grid_hbm,
    second_hbm,
    send_weight_hbm,
    grid_bias_hbm,
    edge_bias_hbm,
    slot_hbm,
    feat_weight_hbm,
    send_hbm,
    recv_hbm,
    feat_hbm,
    count_hbm,
    own_ref,
    cross_ref,
    chip_ref,
    first_ref,
    grid_ref,
    second_ref,
    send_weight_ref,
    grid_bias_ref,
    edge_bias_ref,
    slot_ref,
    feat_weight_ref,
    send_ref,
    recv_ref,
    feat_ref,
    count_ref,
    starts,
    first_t,
    second_t,
    grid_column,
    table,
    even_rows,
    odd_rows,
    hidden_ref,
    ids_ref,
    total,
    sems,
):
    channels, grid_rows = grid_ref.shape
    width = second_ref.shape[1]
    pieces = width // LANES
    blocks, block_edges = send_ref.shape
    owned = own_ref.shape[0]
    feats = feat_ref.shape[1]
    step_rows = grid_rows // GRID_STEPS

    def grid_copy(step):
        part = pl.ds(pl.multiple_of(step * step_rows, step_rows), step_rows)
        return pltpu.make_async_copy(grid_hbm.at[:, part], grid_ref.at[:, part], sems.at[step])

    pairs = [
        (first_hbm, first_ref),
        (second_hbm, second_ref),
        (send_weight_hbm, send_weight_ref),
        (grid_bias_hbm, grid_bias_ref),
        (edge_bias_hbm, edge_bias_ref),
        (send_hbm, send_ref),
        (slot_hbm, slot_ref),
        (feat_weight_hbm, feat_weight_ref),
        (recv_hbm, recv_ref),
        (feat_hbm, feat_ref),
        (count_hbm, count_ref),
        (send_ref, starts),
    ]
    copies = [
        pltpu.make_async_copy(source, target, sems.at[GRID_STEPS + at])
        for at, (source, target) in enumerate(pairs)
    ]
    first_copy, second_copy, send_weight_copy, grid_bias_copy, edge_bias_copy, send_copy = copies[:6]
    slot_copy, starts_copy = copies[6], copies[-1]
    first_copy.start()
    grid_copy(0).start()
    for copy in copies[1:-1]:
        copy.start()
    for step in range(1, GRID_STEPS):
        grid_copy(step).start()
    send_copy.wait()
    senders = send_ref[...]
    send_ref[...] = (senders // 8) * (8 * pieces) + senders % 8
    starts_copy.start()
    slot_copy.wait()
    place = place_ref[0]
    ids_ref[...] = jnp.broadcast_to(
        ids_of_rows(slot_ref[...], (place - 1) * owned, 3 * owned), ids_ref.shape
    )
    total[...] = jnp.zeros_like(total)
    first_copy.wait()
    first_t[...] = (first_ref[...] * 0.5).T
    second_copy.wait()
    second_t[...] = second_ref[...].T
    grid_bias_copy.wait()
    grid_column[...] = jnp.broadcast_to(0.5 * grid_bias_ref[...], (LANES, width)).T
    send_weight_copy.wait()
    send_weight_ref[...] = send_weight_ref[...] * 0.5
    edge_bias_copy.wait()
    edge_bias = 0.5 * edge_bias_ref[...]
    half_rows = step_rows // 2

    def grid_step(step, carry):
        grid_copy(step).wait()
        first = pl.multiple_of(step * step_rows, step_rows)
        bias = jnp.concatenate([grid_column[...]] * (half_rows // LANES), axis=1)
        values = [
            mm(first_t[...], grid_ref[:, pl.ds(first + at, half_rows)]) for at in (0, half_rows)
        ]
        values = [silu_half(value + bias).astype(BF16) for value in values]
        values = [mm(second_t[...], value) for value in values]
        values = [layer_norm(value, 0).astype(BF16).T for value in values]
        values = [mm(value, send_weight_ref[...]) for value in values]
        for half, value in enumerate(values):
            row = (value + edge_bias).astype(BF16).astype(F32)
            base = pl.multiple_of((first + half * half_rows) * pieces, half_rows * pieces)
            for group in range(half_rows // 8):
                for piece in range(pieces):
                    at = (group * pieces + piece) * 8
                    table[pl.ds(base + at, 8), :] = row[
                        group * 8 : group * 8 + 8, piece * LANES : (piece + 1) * LANES
                    ]
        return carry

    lax.fori_loop(0, GRID_STEPS, grid_step, 0)
    for copy in copies[7:]:
        copy.wait()
    used = count_ref[...]
    feat_weight = 0.5 * feat_weight_ref[...].astype(F32)
    feat_weight = jnp.concatenate([feat_weight, jnp.zeros((8 - feats, width), F32)], axis=0)
    feat_weight = feat_weight.astype(BF16)
    group = 2 if blocks % 4 == 0 else 1
    chunks = blocks // group
    part_rows = 64

    def gather(chunk, edges, target):
        for edge in edges:
            start = starts[chunk * group + edge // block_edges, edge % block_edges]
            target[pl.ds(edge // 8 * (8 * pieces) + edge % 8, pieces, stride=8), :] = table[
                pl.ds(start, pieces, stride=8), :
            ]

    def rows_of(source, first, count):
        return jnp.concatenate(
            [
                jnp.concatenate(
                    [
                        source[pl.ds((at * pieces + piece) * 8, 8), :]
                        for at in range(first // 8, (first + count) // 8)
                    ],
                    axis=0,
                )
                for piece in range(pieces)
            ],
            axis=1,
        )

    def work(chunk, source, target):
        here = [chunk * group + b for b in range(group)]
        feat = jnp.concatenate([feat_ref[b] for b in here], axis=1)
        feat = jnp.concatenate([feat, jnp.zeros((8 - feats, feat.shape[1]), F32)], axis=0)
        extra = mm(feat.T.astype(BF16), feat_weight)
        after = jnp.minimum(chunk + 1, chunks - 1)
        for first in range(0, group * block_edges, part_rows):
            gather(after, range(first, first + part_rows), target)
            half = rows_of(source, first, part_rows) + extra[first : first + part_rows]
            hidden_ref[first : first + part_rows, :] = silu_half(half).astype(BF16)
        receivers = [jnp.where(b < used, recv_ref[pl.ds(b, 1), :], -2) for b in here]
        spread = jnp.concatenate([(ids_ref[...] == row).astype(F32) for row in receivers], axis=1)
        spread = spread.astype(BF16)
        total[...] += mm(spread, hidden_ref[...])

    def edge_step(step, carry):
        work(2 * step, even_rows, odd_rows)
        work(2 * step + 1, odd_rows, even_rows)
        return carry

    gather(0, range(group * block_edges), even_rows)
    lax.fori_loop(0, chunks // 2, edge_step, 0)
    odd = place % 2 == 1
    below, above = total[:owned].astype(BF16), total[2 * owned :].astype(BF16)
    own_ref[...] = total[owned : 2 * owned]
    cross_ref[...] = jnp.where(odd, above, below)
    chip_ref[...] = jnp.where(odd, below, above)


def wanted_kernel(owned, slot_ref, send_ref, wanted_ref):
    nodes = slot_ref.shape[1]
    blocks, block_edges = send_ref.shape
    places = wanted_ref.shape[1]
    chunk = LANES
    per_chunk = chunk // owned * SEND_CAP
    row, column = iota((chunk, chunk), 0), iota((chunk, chunk), 1)
    before = ((row > column) & (row // owned == column // owned)).astype(F32).astype(BF16)
    local_owner = (iota((chunk, LANES), 0) // owned * SEND_CAP).astype(F32)

    def find(index, best):
        ids = ids_of_rows(slot_ref[...], index * chunk, chunk)
        hit = jnp.zeros((chunk, block_edges), F32)
        for b in range(blocks):
            hit = jnp.maximum(hit, (ids == send_ref[b : b + 1, :]).astype(F32))
        hit = jnp.broadcast_to(jnp.max(hit, axis=1, keepdims=True), (chunk, LANES))
        rank = mm(before, hit.astype(BF16)) + local_owner
        spot = jnp.where(hit > 0, rank.astype(I32) + index * per_chunk, -1)
        spot = jnp.concatenate([spot] * (places // LANES), axis=1)
        found = jnp.where(spot == iota((chunk, places), 1), ids, -1)
        return jnp.maximum(best, jnp.max(found, axis=0, keepdims=True))

    best = lax.fori_loop(0, nodes // chunk, find, jnp.full((1, places), -1, I32), unroll=2)
    best = best.astype(F32)
    for b in range(blocks):
        senders = jnp.broadcast_to(send_ref[b : b + 1, :].astype(F32), (block_edges, block_edges)).T
        senders = jnp.concatenate([senders] * (places // LANES), axis=1)
        wanted_ref[b * block_edges : (b + 1) * block_edges, :] = (
            (senders == best).astype(F32).astype(BF16)
        )


def supply_kernel(blocks, place_ref, slot_ref, request_ref, supply_ref):
    owned = supply_ref.shape[1]
    devices = supply_ref.shape[0] // SEND_CAP
    per_device = request_ref.shape[0] // devices
    ids = ids_of_rows(slot_ref[...], place_ref[0] * owned, owned)
    lane = iota((owned, LANES), 1)
    used = jnp.zeros((owned, LANES), F32)
    for d in range(devices):
        hit = jnp.zeros((owned, request_ref.shape[1]), F32)
        for b in range(blocks):
            at = d * per_device + b
            hit = jnp.maximum(hit, (ids == request_ref[at : at + 1, :]).astype(F32))
        used = jnp.where(lane == d, jnp.max(hit, axis=1, keepdims=True), used)
    before = (iota((owned, owned), 0) > iota((owned, owned), 1)).astype(F32).astype(BF16)
    rank = jnp.where(used > 0, mm(before, used.astype(BF16)), -1.0)
    rank = jnp.concatenate([rank, jnp.full((LANES - owned, LANES), -1.0, F32)], axis=0).T
    slots = iota((SEND_CAP, owned), 0).astype(F32)
    supply = jnp.concatenate(
        [(rank[d : d + 1, :owned] == slots).astype(F32) for d in range(devices)], axis=0
    )
    supply_ref[...] = supply.astype(BF16)


def node_kernel(
    own_ref,
    from_cross_ref,
    from_chip_ref,
    latent_ref,
    edge_out_ref,
    node_input_ref,
    node_bias_ref,
    node_out_ref,
    node_gain_ref,
    mesh_sender_ref,
    supply_ref,
    encoded_ref,
    rows_ref,
):
    width = latent_ref.shape[1]
    latent = latent_ref[...]
    node_sum = own_ref[...] + from_cross_ref[...].astype(F32) + from_chip_ref[...].astype(F32)
    aggregate = mm(node_sum.astype(BF16), edge_out_ref[...]).astype(BF16)
    hidden = mm(latent, node_input_ref[:width]) + mm(aggregate, node_input_ref[width:])
    hidden = silu(hidden + node_bias_ref[...]).astype(BF16)
    encoded = latent.astype(F32) + layer_norm(mm(hidden, node_out_ref[...])) * node_gain_ref[...]
    encoded = encoded.astype(BF16)
    encoded_ref[...] = encoded
    sender_code = mm(encoded, mesh_sender_ref[...]).astype(BF16)
    rows_ref[...] = mm(supply_ref[...], sender_code).astype(BF16)


def receiver_kernel(
    place_ref,
    slot_ref,
    recv_ref,
    encoded_ref,
    mesh_receiver_ref,
    message_bias_ref,
    update_input_ref,
    update_bias_ref,
    incoming_ref,
    pick_ref,
    parts_ref,
    upper_ref,
):
    owned, width = encoded_ref.shape
    blocks = recv_ref.shape[0]
    ids = ids_of_rows(slot_ref[...], place_ref[0] * owned, owned)
    incoming = jnp.concatenate(
        [(ids == recv_ref[b : b + 1, :]).astype(F32) for b in range(blocks)], axis=1
    )
    pick = incoming.T.astype(BF16)
    pick_ref[...] = jnp.concatenate([pick, pick], axis=1)
    incoming_ref[...] = incoming.astype(BF16)
    encoded = encoded_ref[...]
    receiver = mm(encoded, mesh_receiver_ref[...]) + message_bias_ref[...]
    high = receiver.astype(BF16)
    parts_ref[:owned, :] = high
    parts_ref[owned:, :] = (receiver - high.astype(F32)).astype(BF16)
    upper_ref[...] = mm(encoded, update_input_ref[:width]) + update_bias_ref[...]


def message_kernel(
    wanted_ref,
    piece_ref,
    incoming_ref,
    pick_ref,
    parts_ref,
    upper_ref,
    encoded_ref,
    message_out_ref,
    update_input_ref,
    update_out_ref,
    update_gain_ref,
    out_ref,
):
    width = encoded_ref.shape[1]
    chosen = jnp.concatenate([wanted_ref[...], pick_ref[...]], axis=1)
    codes = jnp.concatenate([piece_ref[...], parts_ref[...]], axis=0)
    message = silu(mm(chosen, codes)).astype(BF16)
    message_sum = mm(incoming_ref[...], message).astype(BF16)
    update = mm(message_sum, message_out_ref[...]).astype(BF16)
    hidden = silu(upper_ref[...] + mm(update, update_input_ref[width:])).astype(BF16)
    out = layer_norm(mm(hidden, update_out_ref[...])) * update_gain_ref[...]
    out_ref[...] = (encoded_ref[...].astype(F32) + out).astype(BF16)


def call(kernel, out_shape, spaces, scratch=(), flops=0, moved=0, vmem=8):
    return pl.pallas_call(
        kernel,
        out_shape=out_shape,
        in_specs=[pl.BlockSpec(memory_space=space) for space in spaces],
        out_specs=jax.tree.map(lambda _: pl.BlockSpec(memory_space=VMEM), out_shape),
        scratch_shapes=scratch,
        compiler_params=pltpu.CompilerParams(vmem_limit_bytes=vmem * MEBI),
        cost_estimate=pl.CostEstimate(flops=flops, bytes_accessed=moved, transcendentals=0),
    )


def hold(value):
    return value if value.size == 1 else pltpu.with_memory_space_constraint(value, HBM)


def shape(*sizes, kind=BF16):
    return jax.ShapeDtypeStruct(sizes, kind)


def per_device(
    grid_in,
    grid_first,
    grid_bias,
    grid_second,
    send_weight,
    edge_bias,
    feat_weight,
    edge_out,
    node_input,
    node_bias,
    node_out,
    node_gain,
    mesh_sender,
    mesh_receiver,
    message_bias,
    message_out,
    update_input,
    update_bias,
    update_out,
    update_gain,
    mesh_latent,
    g2m_send,
    g2m_recv,
    g2m_feat,
    g2m_count,
    mesh_slot,
    mesh_send,
    mesh_recv,
):
    devices = lax.axis_size("bulk")
    position = lax.axis_index("bulk")
    place = position.astype(I32).reshape(1)
    owned, width = mesh_latent.shape
    grid_rows = grid_in.shape[0]
    places = devices * SEND_CAP
    edges = mesh_send.size
    slot = mesh_slot.reshape(1, -1)
    row = lambda vector: vector.reshape(1, -1)

    requests = lax.all_to_all(jnp.tile(mesh_send, (devices, 1)), "bulk", 0, 0, tiled=True)
    operands = (
        grid_first,
        grid_in.T,
        grid_second,
        send_weight,
        row(grid_bias),
        row(edge_bias),
        slot,
        feat_weight,
        g2m_send,
        g2m_recv,
        g2m_feat,
        g2m_count.reshape(1, 1),
    )
    own, cross, chip = call(
        edge_kernel,
        (shape(owned, width, kind=F32), shape(owned, width), shape(owned, width)),
        [SMEM] + [HBM] * len(operands),
        scratch=[VMEM(value.shape, value.dtype) for value in operands]
        + [
            SMEM(g2m_send.shape, I32),
            VMEM(grid_first.shape[::-1], BF16),
            VMEM(grid_second.shape, BF16),
            VMEM((width, LANES), F32),
            VMEM((grid_rows * (width // LANES), LANES), F32),
            VMEM((2 * g2m_send.shape[1] * (width // LANES), LANES), F32),
            VMEM((2 * g2m_send.shape[1] * (width // LANES), LANES), F32),
            VMEM((2 * g2m_send.shape[1], width), BF16),
            VMEM((3 * owned, LANES), I32),
            VMEM((3 * owned, width), F32),
            pltpu.SemaphoreType.DMA((len(operands) + GRID_STEPS,)),
        ],
        flops=10_000_000_000,
        moved=4_000_000,
        vmem=32,
    )(place, *[hold(value) for value in operands])
    requests, _ = lax.optimization_barrier((requests, own))
    crossing = [(d, d + 1) for d in range(1, devices - 1, 2)]
    within = [(d, d + 1) for d in range(0, devices, 2)]
    both = lambda pairs: pairs + [(b, a) for a, b in pairs]
    from_cross = lax.ppermute(cross, "bulk", both(crossing))
    from_chip = lax.ppermute(chip, "bulk", both(within))
    supply = call(
        functools.partial(supply_kernel, mesh_send.shape[0]),
        shape(places, owned),
        [SMEM] + [VMEM] * 2,
        flops=500_000_000,
        moved=500_000,
    )(place, slot, requests)
    encoded, rows = call(
        node_kernel,
        (shape(owned, width), shape(places, width)),
        [VMEM] * 11,
        flops=500_000_000,
        moved=4_000_000,
    )(
        own,
        from_cross,
        from_chip,
        mesh_latent,
        edge_out,
        node_input,
        row(node_bias),
        node_out,
        row(node_gain),
        mesh_sender,
        supply,
    )
    rows = pltpu.with_memory_space_constraint(rows, VMEM)
    piece = lax.all_to_all(rows, "bulk", 0, 0, tiled=True)
    mesh_send, _ = lax.optimization_barrier((mesh_send, encoded))
    wanted = call(
        functools.partial(wanted_kernel, owned),
        shape(edges, places),
        [VMEM] * 2,
        flops=1_000_000_000,
        moved=500_000,
    )(slot, mesh_send)
    incoming, pick, parts, upper = call(
        receiver_kernel,
        (
            shape(owned, edges),
            shape(edges, 2 * owned),
            shape(2 * owned, width),
            shape(owned, width, kind=F32),
        ),
        [SMEM] + [VMEM] * 7,
        flops=1_000_000_000,
        moved=4_000_000,
    )(
        place,
        slot,
        mesh_recv,
        encoded,
        mesh_receiver,
        row(message_bias),
        update_input,
        row(update_bias),
    )
    return call(
        message_kernel,
        shape(owned, width),
        [VMEM] * 11,
        flops=1_000_000_000,
        moved=4_000_000,
    )(
        wanted,
        piece,
        incoming,
        pick,
        parts,
        upper,
        encoded,
        message_out,
        update_input,
        update_out,
        row(update_gain),
    )


def solution(mesh):
    split = {0: ("groups", "bulk"), 20: "bulk", 21: "bulk", 22: "bulk", 23: "bulk", 24: "bulk"}
    split.update({26: "bulk", 27: "bulk"})
    placed = tuple(P(split[at]) if at in split else P() for at in range(28))
    return jax.shard_map(
        per_device,
        mesh=mesh,
        in_specs=placed,
        out_specs=P(("groups", "bulk"), None),
        check_vma=False,
    )
```

```python
import functools
import math

import jax
import jax.numpy as jnp
from jax import lax
from jax.experimental import pallas as pl
from jax.experimental.pallas import tpu as pltpu
from jax.sharding import PartitionSpec as P

F32 = jnp.float32
BF16 = jnp.bfloat16
I32 = jnp.int32
SEND_CAP = 16
LANES = 128
VMEM = pltpu.VMEM
SMEM = pltpu.SMEM
HBM = pltpu.HBM
GRID_STEPS = 4
MEBI = 1024 * 1024


def mm(left, right):
    return jnp.dot(left, right, preferred_element_type=F32)


def mm_nt(left, right):
    return lax.dot_general(left, right, (((1,), (1,)), ((), ())), preferred_element_type=F32)


def silu_half(half):
    return half + half * jnp.tanh(half)


def silu(value):
    return silu_half(0.5 * value)


def layer_norm(value):
    center = value - jnp.mean(value, axis=-1, keepdims=True)
    spread = jnp.mean(center * center, axis=-1, keepdims=True)
    return center * lax.rsqrt(spread + 1e-05)


def iota(shape, dim):
    return lax.broadcasted_iota(I32, shape, dim)


def one_hot(columns, rows):
    hit = columns.astype(jnp.int16) == lax.broadcasted_iota(jnp.int16, (rows, columns.shape[1]), 0)
    return jnp.where(hit, jnp.ones((), BF16), jnp.zeros((), BF16))


def sending_order(devices):
    quarter = devices // 4
    members = list(range(devices))
    return members[: 2 * quarter] + members[3 * quarter :] + members[2 * quarter : 3 * quarter]


def ids_of_rows(slot, first, count):
    nodes = slot.shape[1]
    rows = iota((count, nodes), 0) + first
    return jnp.max(jnp.where(slot == rows, iota((count, nodes), 1), -1), axis=1, keepdims=True)


def opening_kernel(
    mesh_send_hbm,
    first_hbm,
    grid_hbm,
    second_hbm,
    send_weight_hbm,
    asked_ref,
    first_ref,
    grid_ref,
    second_ref,
    send_weight_ref,
    mesh_send_ref,
    sems,
):
    pairs = [
        (mesh_send_hbm, mesh_send_ref),
        (first_hbm, first_ref),
        (send_weight_hbm, send_weight_ref),
        (second_hbm, second_ref),
        (grid_hbm.at[:, : grid_ref.shape[1]], grid_ref),
    ]
    copies = [
        pltpu.make_async_copy(source, target, sems.at[at])
        for at, (source, target) in enumerate(pairs)
    ]
    for copy in copies:
        copy.start()
    copies[0].wait()
    rows = mesh_send_ref.shape[0]
    for at in range(asked_ref.shape[0] // rows):
        asked_ref[at * rows : (at + 1) * rows, :] = mesh_send_ref[...]
    for copy, ref in zip(copies[1:3], (first_ref, send_weight_ref)):
        copy.wait()
        ref[...] = ref[...] * 0.5
    for copy in copies[3:]:
        copy.wait()


def edge_kernel(
    place_ref,
    first_ref,
    opening_ref,
    second_ref,
    send_weight_ref,
    grid_hbm,
    grid_bias_hbm,
    edge_bias_hbm,
    slot_hbm,
    feat_weight_hbm,
    send_hbm,
    recv_hbm,
    feat_hbm,
    count_hbm,
    own_ref,
    cross_ref,
    chip_ref,
    grid_ref,
    grid_bias_ref,
    edge_bias_ref,
    slot_ref,
    feat_weight_ref,
    send_ref,
    recv_ref,
    feat_ref,
    count_ref,
    starts,
    table,
    even_rows,
    odd_rows,
    hidden_ref,
    ids_ref,
    total,
    sems,
):
    channels, grid_rows = grid_ref.shape
    width = second_ref.shape[1]
    pieces = width // LANES
    blocks, block_edges = send_ref.shape
    owned = own_ref.shape[0]
    feats = feat_ref.shape[1]
    step_rows = grid_rows // GRID_STEPS

    def grid_copy(step):
        part = pl.ds(pl.multiple_of(step * step_rows, step_rows), step_rows)
        return pltpu.make_async_copy(grid_hbm.at[:, part], grid_ref.at[:, part], sems.at[step])

    pairs = [
        (grid_bias_hbm, grid_bias_ref),
        (edge_bias_hbm, edge_bias_ref),
        (send_hbm, send_ref),
        (slot_hbm, slot_ref),
        (feat_weight_hbm, feat_weight_ref),
        (recv_hbm, recv_ref),
        (feat_hbm, feat_ref),
        (count_hbm, count_ref),
        (send_ref, starts),
    ]
    copies = [
        pltpu.make_async_copy(source, target, sems.at[GRID_STEPS + at])
        for at, (source, target) in enumerate(pairs)
    ]
    grid_bias_copy, edge_bias_copy, send_copy, slot_copy = copies[:4]
    starts_copy = copies[-1]
    for copy in copies[:-1]:
        copy.start()
    for step in range(1, GRID_STEPS):
        grid_copy(step).start()
    grid_ref[:, :step_rows] = opening_ref[...]
    send_copy.wait()
    senders = send_ref[...]
    send_ref[...] = (senders // 8) * (8 * pieces) + senders % 8
    starts_copy.start()
    slot_copy.wait()
    place = place_ref[0]
    ids_ref[...] = jnp.broadcast_to(
        ids_of_rows(slot_ref[...], (place - 1) * owned, 3 * owned), ids_ref.shape
    )
    total[...] = jnp.zeros_like(total)
    grid_bias_copy.wait()
    edge_bias_copy.wait()
    grid_bias = 0.5 * grid_bias_ref[...]
    edge_bias = 0.5 * edge_bias_ref[...]
    half_rows = step_rows // 2

    def grid_step(step, carry):
        @pl.when(step > 0)
        def _():
            grid_copy(step).wait()

        first = pl.multiple_of(step * step_rows, step_rows)
        values = [
            mm(grid_ref[:, pl.ds(first + at, half_rows)].T, first_ref[...])
            for at in (0, half_rows)
        ]
        values = [silu_half(value + grid_bias).astype(BF16) for value in values]
        values = [mm(value, second_ref[...]) for value in values]
        values = [layer_norm(value).astype(BF16) for value in values]
        values = [mm(value, send_weight_ref[...]) for value in values]
        for half, value in enumerate(values):
            row = (value + edge_bias).astype(BF16).astype(F32)
            base = pl.multiple_of((first + half * half_rows) * pieces, half_rows * pieces)
            for group in range(half_rows // 8):
                for piece in range(pieces):
                    at = (group * pieces + piece) * 8
                    table[pl.ds(base + at, 8), :] = row[
                        group * 8 : group * 8 + 8, piece * LANES : (piece + 1) * LANES
                    ]
        return carry

    lax.fori_loop(0, GRID_STEPS, grid_step, 0)
    for copy in copies[4:]:
        copy.wait()
    used = count_ref[...]
    feat_weight = 0.5 * feat_weight_ref[...].astype(F32)
    feat_weight = jnp.concatenate([feat_weight, jnp.zeros((8 - feats, width), F32)], axis=0)
    feat_weight = feat_weight.astype(BF16)
    group = 2 if blocks % 4 == 0 else 1
    chunks = blocks // group
    part_rows = 64

    def gather(chunk, edges, target):
        for edge in edges:
            start = starts[chunk * group + edge // block_edges, edge % block_edges]
            target[pl.ds(edge // 8 * (8 * pieces) + edge % 8, pieces, stride=8), :] = table[
                pl.ds(start, pieces, stride=8), :
            ]

    def rows_of(source, first, count):
        return jnp.concatenate(
            [
                jnp.concatenate(
                    [
                        source[pl.ds((at * pieces + piece) * 8, 8), :]
                        for at in range(first // 8, (first + count) // 8)
                    ],
                    axis=0,
                )
                for piece in range(pieces)
            ],
            axis=1,
        )

    def work(chunk, source, target):
        here = [chunk * group + b for b in range(group)]
        feat = jnp.concatenate([feat_ref[b] for b in here], axis=1)
        feat = jnp.concatenate([feat, jnp.zeros((8 - feats, feat.shape[1]), F32)], axis=0)
        extra = mm(feat.T.astype(BF16), feat_weight)
        after = jnp.minimum(chunk + 1, chunks - 1)
        for first in range(0, group * block_edges, part_rows):
            gather(after, range(first, first + part_rows), target)
            half = rows_of(source, first, part_rows) + extra[first : first + part_rows]
            hidden_ref[first : first + part_rows, :] = silu_half(half).astype(BF16)
        receivers = [jnp.where(b < used, recv_ref[pl.ds(b, 1), :], -2) for b in here]
        spread = jnp.concatenate([(ids_ref[...] == row).astype(F32) for row in receivers], axis=1)
        spread = spread.astype(BF16)
        total[...] += mm(spread, hidden_ref[...])

    def edge_step(step, carry):
        work(2 * step, even_rows, odd_rows)
        work(2 * step + 1, odd_rows, even_rows)
        return carry

    gather(0, range(group * block_edges), even_rows)
    lax.fori_loop(0, chunks // 2, edge_step, 0)
    odd = place % 2 == 1
    below, above = total[:owned].astype(BF16), total[2 * owned :].astype(BF16)
    own_ref[...] = total[owned : 2 * owned]
    cross_ref[...] = jnp.where(odd, above, below)
    chip_ref[...] = jnp.where(odd, below, above)


def wanted_kernel(owned, slot_ref, send_ref, wanted_ref):
    nodes = slot_ref.shape[1]
    blocks, block_edges = send_ref.shape
    places = wanted_ref.shape[1]
    chunk = LANES
    per_chunk = chunk // owned * SEND_CAP
    row, column = iota((chunk, chunk), 0), iota((chunk, chunk), 1)
    before = ((row > column) & (row // owned == column // owned)).astype(F32).astype(BF16)
    local_owner = (iota((chunk, LANES), 0) // owned * SEND_CAP).astype(F32)

    def find(index, best):
        ids = ids_of_rows(slot_ref[...], index * chunk, chunk)
        hit = jnp.zeros((chunk, block_edges), F32)
        for b in range(blocks):
            hit = jnp.maximum(hit, (ids == send_ref[b : b + 1, :]).astype(F32))
        hit = jnp.broadcast_to(jnp.max(hit, axis=1, keepdims=True), (chunk, LANES))
        rank = mm(before, hit.astype(BF16)) + local_owner
        spot = jnp.where(hit > 0, rank.astype(I32) + index * per_chunk, -1)
        spot = jnp.concatenate([spot] * (places // LANES), axis=1)
        found = jnp.where(spot == iota((chunk, places), 1), ids, -1)
        return jnp.maximum(best, jnp.max(found, axis=0, keepdims=True))

    best = lax.fori_loop(0, nodes // chunk, find, jnp.full((1, places), -1, I32), unroll=2)
    best = best.astype(F32)
    best = jnp.concatenate(
        [
            best[:, owner * SEND_CAP : (owner + 1) * SEND_CAP]
            for owner in sending_order(places // SEND_CAP)
        ],
        axis=1,
    )
    for b in range(blocks):
        senders = jnp.broadcast_to(send_ref[b : b + 1, :].astype(F32), (block_edges, block_edges)).T
        senders = jnp.concatenate([senders] * (places // LANES), axis=1)
        wanted_ref[b * block_edges : (b + 1) * block_edges, :] = (
            (senders == best).astype(F32).astype(BF16)
        )


def supply_kernel(blocks, place_ref, slot_ref, request_ref, supply_ref):
    owned = supply_ref.shape[1]
    devices = supply_ref.shape[0] // SEND_CAP
    per_device = request_ref.shape[0] // devices
    ids = ids_of_rows(slot_ref[...], place_ref[0] * owned, owned)
    lane = iota((owned, LANES), 1)
    used = jnp.zeros((owned, LANES), F32)
    for d in range(devices):
        hit = jnp.zeros((owned, request_ref.shape[1]), F32)
        for b in range(blocks):
            at = d * per_device + b
            hit = jnp.maximum(hit, (ids == request_ref[at : at + 1, :]).astype(F32))
        used = jnp.where(lane == d, jnp.max(hit, axis=1, keepdims=True), used)
    before = (iota((owned, owned), 0) > iota((owned, owned), 1)).astype(F32).astype(BF16)
    rank = jnp.where(used > 0, mm(before, used.astype(BF16)), -1.0)
    rank = jnp.concatenate([rank, jnp.full((LANES - owned, LANES), -1.0, F32)], axis=0).T
    slots = iota((SEND_CAP, owned), 0).astype(F32)
    supply = jnp.concatenate(
        [(rank[d : d + 1, :owned] == slots).astype(F32) for d in sending_order(devices)], axis=0
    )
    supply_ref[...] = supply.astype(BF16)


def node_kernel(
    own_ref,
    from_cross_ref,
    from_chip_ref,
    latent_ref,
    edge_out_ref,
    node_input_ref,
    node_bias_ref,
    node_out_ref,
    node_gain_ref,
    mesh_sender_ref,
    supply_ref,
    encoded_ref,
    rows_ref,
):
    width = latent_ref.shape[1]
    latent = latent_ref[...]
    node_sum = own_ref[...] + from_cross_ref[...].astype(F32) + from_chip_ref[...].astype(F32)
    aggregate = mm(node_sum.astype(BF16), edge_out_ref[...]).astype(BF16)
    hidden = mm(latent, node_input_ref[:width]) + mm(aggregate, node_input_ref[width:])
    hidden = silu(hidden + node_bias_ref[...]).astype(BF16)
    encoded = latent.astype(F32) + layer_norm(mm(hidden, node_out_ref[...])) * node_gain_ref[...]
    encoded = encoded.astype(BF16)
    encoded_ref[...] = encoded
    sender_code = mm(encoded, mesh_sender_ref[...]).astype(BF16)
    rows_ref[...] = mm(supply_ref[...], sender_code).astype(BF16)


def receiver_kernel(
    place_ref,
    slot_ref,
    recv_ref,
    encoded_ref,
    mesh_receiver_ref,
    message_bias_ref,
    update_input_ref,
    update_bias_ref,
    incoming_ref,
    pick_ref,
    parts_ref,
    upper_ref,
):
    owned, width = encoded_ref.shape
    blocks = recv_ref.shape[0]
    ids = ids_of_rows(slot_ref[...], place_ref[0] * owned, owned)
    incoming = jnp.concatenate(
        [(ids == recv_ref[b : b + 1, :]).astype(F32) for b in range(blocks)], axis=1
    )
    pick = incoming.T.astype(BF16)
    pick_ref[...] = jnp.concatenate([pick, pick], axis=1)
    incoming_ref[...] = incoming.astype(BF16)
    encoded = encoded_ref[...]
    receiver = mm(encoded, mesh_receiver_ref[...]) + message_bias_ref[...]
    high = receiver.astype(BF16)
    parts_ref[:owned, :] = high
    parts_ref[owned:, :] = (receiver - high.astype(F32)).astype(BF16)
    upper_ref[...] = mm(encoded, update_input_ref[:width]) + update_bias_ref[...]


def message_kernel(
    wanted_ref,
    piece_ref,
    incoming_ref,
    pick_ref,
    parts_ref,
    upper_ref,
    encoded_ref,
    message_out_ref,
    update_input_ref,
    update_out_ref,
    update_gain_ref,
    out_ref,
):
    width = encoded_ref.shape[1]
    chosen = jnp.concatenate([wanted_ref[...], pick_ref[...]], axis=1)
    codes = jnp.concatenate([piece_ref[...], parts_ref[...]], axis=0)
    message = silu(mm(chosen, codes)).astype(BF16)
    message_sum = mm(incoming_ref[...], message).astype(BF16)
    update = mm(message_sum, message_out_ref[...]).astype(BF16)
    hidden = silu(upper_ref[...] + mm(update, update_input_ref[width:])).astype(BF16)
    out = layer_norm(mm(hidden, update_out_ref[...])) * update_gain_ref[...]
    out_ref[...] = (encoded_ref[...].astype(F32) + out).astype(BF16)


def call(kernel, out_shape, spaces, scratch=(), flops=0, moved=0, vmem=8):
    return pl.pallas_call(
        kernel,
        out_shape=out_shape,
        in_specs=[pl.BlockSpec(memory_space=space) for space in spaces],
        out_specs=jax.tree.map(lambda _: pl.BlockSpec(memory_space=VMEM), out_shape),
        scratch_shapes=scratch,
        compiler_params=pltpu.CompilerParams(vmem_limit_bytes=vmem * MEBI),
        cost_estimate=pl.CostEstimate(flops=flops, bytes_accessed=moved, transcendentals=0),
    )


def hold(value):
    return value if value.size == 1 else pltpu.with_memory_space_constraint(value, HBM)


def shape(*sizes, kind=BF16):
    return jax.ShapeDtypeStruct(sizes, kind)


def per_device(
    grid_in,
    grid_first,
    grid_bias,
    grid_second,
    send_weight,
    edge_bias,
    feat_weight,
    edge_out,
    node_input,
    node_bias,
    node_out,
    node_gain,
    mesh_sender,
    mesh_receiver,
    message_bias,
    message_out,
    update_input,
    update_bias,
    update_out,
    update_gain,
    mesh_latent,
    g2m_send,
    g2m_recv,
    g2m_feat,
    g2m_count,
    mesh_slot,
    mesh_send,
    mesh_recv,
):
    devices = lax.axis_size("bulk")
    position = lax.axis_index("bulk")
    place = position.astype(I32).reshape(1)
    owned, width = mesh_latent.shape
    grid_rows = grid_in.shape[0]
    places = devices * SEND_CAP
    edges = mesh_send.size
    slot = mesh_slot.reshape(1, -1)
    row = lambda vector: vector.reshape(1, -1)

    grid_turned = pltpu.with_memory_space_constraint(grid_in.T, HBM)
    asked, *opened = call(
        opening_kernel,
        (
            shape(devices * mesh_send.shape[0], mesh_send.shape[1], kind=I32),
            shape(*grid_first.shape),
            shape(grid_in.shape[1], grid_rows // GRID_STEPS),
            shape(*grid_second.shape),
            shape(*send_weight.shape),
        ),
        [HBM] * 5,
        scratch=[VMEM(mesh_send.shape, I32), pltpu.SemaphoreType.DMA((5,))],
        flops=1_000_000,
        moved=3_000_000,
    )(
        hold(mesh_send),
        hold(grid_first),
        grid_turned,
        hold(grid_second),
        hold(send_weight),
    )
    requests = lax.all_to_all(asked, "bulk", 0, 0, tiled=True)
    opened = [pltpu.with_memory_space_constraint(value, VMEM) for value in opened]
    operands = (
        grid_turned,
        row(grid_bias),
        row(edge_bias),
        slot,
        feat_weight,
        g2m_send,
        g2m_recv,
        g2m_feat,
        g2m_count.reshape(1, 1),
    )
    own, cross, chip = call(
        edge_kernel,
        (shape(owned, width, kind=F32), shape(owned, width), shape(owned, width)),
        [SMEM] + [VMEM] * 4 + [HBM] * len(operands),
        scratch=[VMEM(value.shape, value.dtype) for value in operands]
        + [
            SMEM(g2m_send.shape, I32),
            VMEM((grid_rows * (width // LANES), LANES), F32),
            VMEM((2 * g2m_send.shape[1] * (width // LANES), LANES), F32),
            VMEM((2 * g2m_send.shape[1] * (width // LANES), LANES), F32),
            VMEM((2 * g2m_send.shape[1], width), BF16),
            VMEM((3 * owned, LANES), I32),
            VMEM((3 * owned, width), F32),
            pltpu.SemaphoreType.DMA((len(operands) + GRID_STEPS,)),
        ],
        flops=10_000_000_000,
        moved=4_000_000,
        vmem=32,
    )(place, *opened, grid_turned, *[hold(value) for value in operands[1:]])
    requests, _ = lax.optimization_barrier((requests, own))
    crossing = [(d, d + 1) for d in range(1, devices - 1, 2)]
    within = [(d, d + 1) for d in range(0, devices, 2)]
    both = lambda pairs: pairs + [(b, a) for a, b in pairs]
    from_cross = lax.ppermute(cross, "bulk", both(crossing))
    from_chip = lax.ppermute(chip, "bulk", both(within))
    supply = call(
        functools.partial(supply_kernel, mesh_send.shape[0]),
        shape(places, owned),
        [SMEM] + [VMEM] * 2,
        flops=500_000_000,
        moved=500_000,
    )(place, slot, requests)
    encoded, rows = call(
        node_kernel,
        (shape(owned, width), shape(places, width)),
        [VMEM] * 11,
        flops=500_000_000,
        moved=4_000_000,
    )(
        own,
        from_cross,
        from_chip,
        mesh_latent,
        edge_out,
        node_input,
        row(node_bias),
        node_out,
        row(node_gain),
        mesh_sender,
        supply,
    )
    members = [sending_order(devices)]
    piece = lax.all_to_all(rows, "bulk", 0, 0, axis_index_groups=members, tiled=True)
    mesh_send, _ = lax.optimization_barrier((mesh_send, encoded))
    wanted = call(
        functools.partial(wanted_kernel, owned),
        shape(edges, places),
        [VMEM] * 2,
        flops=1_000_000_000,
        moved=500_000,
    )(slot, mesh_send)
    incoming, pick, parts, upper = call(
        receiver_kernel,
        (
            shape(owned, edges),
            shape(edges, 2 * owned),
            shape(2 * owned, width),
            shape(owned, width, kind=F32),
        ),
        [SMEM] + [VMEM] * 7,
        flops=1_000_000_000,
        moved=4_000_000,
    )(
        place,
        slot,
        mesh_recv,
        encoded,
        mesh_receiver,
        row(message_bias),
        update_input,
        row(update_bias),
    )
    return call(
        message_kernel,
        shape(owned, width),
        [VMEM] * 11,
        flops=1_000_000_000,
        moved=4_000_000,
    )(
        wanted,
        piece,
        incoming,
        pick,
        parts,
        upper,
        encoded,
        message_out,
        update_input,
        update_out,
        row(update_gain),
    )


def solution(mesh):
    split = {0: ("groups", "bulk"), 20: "bulk", 21: "bulk", 22: "bulk", 23: "bulk", 24: "bulk"}
    split.update({26: "bulk", 27: "bulk"})
    placed = tuple(P(split[at]) if at in split else P() for at in range(28))
    return jax.shard_map(
        per_device,
        mesh=mesh,
        in_specs=placed,
        out_specs=P(("groups", "bulk"), None),
        check_vma=False,
    )
```

```python
import functools
import math

import jax
import jax.numpy as jnp
from jax import lax
from jax.experimental import pallas as pl
from jax.experimental.pallas import tpu as pltpu
from jax.sharding import PartitionSpec as P

F32 = jnp.float32
BF16 = jnp.bfloat16
I32 = jnp.int32
SEND_CAP = 16
LANES = 128
VMEM = pltpu.VMEM
SMEM = pltpu.SMEM
HBM = pltpu.HBM
GRID_STEPS = 4
STEP_ROWS = 256
BATCH = 16
MEBI = 1024 * 1024


def mm(left, right):
    return jnp.dot(left, right, preferred_element_type=F32)


def mm_nt(left, right):
    return lax.dot_general(left, right, (((1,), (1,)), ((), ())), preferred_element_type=F32)


def silu_half(half):
    return half + half * jnp.tanh(half)


def silu(value):
    return silu_half(0.5 * value)


def layer_norm(value):
    center = value - jnp.mean(value, axis=-1, keepdims=True)
    spread = jnp.mean(center * center, axis=-1, keepdims=True)
    return center * lax.rsqrt(spread + 1e-05)


def iota(shape, dim):
    return lax.broadcasted_iota(I32, shape, dim)


def one_hot(columns, rows):
    hit = columns.astype(jnp.int16) == lax.broadcasted_iota(jnp.int16, (rows, columns.shape[1]), 0)
    return jnp.where(hit, jnp.ones((), BF16), jnp.zeros((), BF16))


def ids_of_rows(slot, first, count):
    nodes = slot.shape[1]
    rows = iota((count, nodes), 0) + first
    return jnp.max(jnp.where(slot == rows, iota((count, nodes), 1), -1), axis=1, keepdims=True)


def edge_kernel(
    place_ref,
    first_hbm,
    grid_hbm,
    second_hbm,
    send_weight_hbm,
    grid_bias_hbm,
    edge_bias_hbm,
    slot_hbm,
    feat_weight_hbm,
    send_hbm,
    recv_hbm,
    feat_hbm,
    count_hbm,
    own_ref,
    cross_ref,
    chip_ref,
    first_ref,
    grid_ref,
    second_ref,
    send_weight_ref,
    grid_bias_ref,
    edge_bias_ref,
    slot_ref,
    feat_weight_ref,
    send_ref,
    recv_ref,
    feat_ref,
    count_ref,
    starts,
    table,
    even_rows,
    odd_rows,
    hidden_ref,
    ids_ref,
    total,
    sems,
):
    channels, grid_rows = grid_ref.shape
    width = second_ref.shape[1]
    pieces = width // LANES
    blocks, block_edges = send_ref.shape
    owned = own_ref.shape[0]
    feats = feat_ref.shape[1]
    step_rows = grid_rows // GRID_STEPS

    def grid_copy(step):
        part = pl.ds(pl.multiple_of(step * step_rows, step_rows), step_rows)
        return pltpu.make_async_copy(grid_hbm.at[:, part], grid_ref.at[:, part], sems.at[step])

    pairs = [
        (first_hbm, first_ref),
        (second_hbm, second_ref),
        (send_weight_hbm, send_weight_ref),
        (grid_bias_hbm, grid_bias_ref),
        (edge_bias_hbm, edge_bias_ref),
        (send_hbm, send_ref),
        (slot_hbm, slot_ref),
        (feat_weight_hbm, feat_weight_ref),
        (recv_hbm, recv_ref),
        (feat_hbm, feat_ref),
        (count_hbm, count_ref),
        (send_ref, starts),
    ]
    copies = [
        pltpu.make_async_copy(source, target, sems.at[GRID_STEPS + at])
        for at, (source, target) in enumerate(pairs)
    ]
    first_copy, second_copy, send_weight_copy, grid_bias_copy, edge_bias_copy, send_copy = copies[:6]
    slot_copy, starts_copy = copies[6], copies[-1]
    first_copy.start()
    grid_copy(0).start()
    for copy in copies[1:-1]:
        copy.start()
    for step in range(1, GRID_STEPS):
        grid_copy(step).start()
    send_copy.wait()
    senders = send_ref[...]
    send_ref[...] = (senders // 8) * (8 * pieces) + senders % 8
    starts_copy.start()
    slot_copy.wait()
    place = place_ref[0]
    ids_ref[...] = jnp.broadcast_to(
        ids_of_rows(slot_ref[...], (place - 1) * owned, 3 * owned), ids_ref.shape
    )
    total[...] = jnp.zeros_like(total)
    first_copy.wait()
    first_ref[...] = first_ref[...] * 0.5
    second_copy.wait()
    send_weight_copy.wait()
    send_weight_ref[...] = send_weight_ref[...] * 0.5
    grid_bias_copy.wait()
    edge_bias_copy.wait()
    grid_bias = 0.5 * grid_bias_ref[...]
    edge_bias = 0.5 * edge_bias_ref[...]
    def grid_step(step, carry):
        first = pl.multiple_of(step * STEP_ROWS, STEP_ROWS)
        per_copy = step_rows // STEP_ROWS

        @pl.when(step % per_copy == 0)
        def _():
            grid_copy(step // per_copy).wait()

        value = mm(grid_ref[:, pl.ds(first, STEP_ROWS)].T, first_ref[...])
        value = silu_half(value + grid_bias).astype(BF16)
        value = layer_norm(mm(value, second_ref[...])).astype(BF16)
        row = mm(value, send_weight_ref[...]) + edge_bias
        row = row.astype(BF16).astype(F32)
        base = pl.multiple_of(first * pieces, STEP_ROWS * pieces)
        for group in range(STEP_ROWS // 8):
            for piece in range(pieces):
                at = (group * pieces + piece) * 8
                table[pl.ds(base + at, 8), :] = row[
                    group * 8 : group * 8 + 8, piece * LANES : (piece + 1) * LANES
                ]
        return carry

    lax.fori_loop(0, grid_rows // STEP_ROWS, grid_step, 0)
    for copy in copies[7:]:
        copy.wait()
    used = count_ref[...]
    feat_weight = 0.5 * feat_weight_ref[...].astype(F32)
    feat_weight = jnp.concatenate([feat_weight, jnp.zeros((8 - feats, width), F32)], axis=0)
    feat_weight = feat_weight.astype(BF16)
    group = 1
    chunks = blocks // group
    part_rows = 64

    def gather(chunk, edges, target):
        for batch in range(0, len(edges), BATCH):
            some = edges[batch : batch + BATCH]
            places = [starts[chunk * group + e // block_edges, e % block_edges] for e in some]
            rows = [table[pl.ds(place, pieces, stride=8), :] for place in places]
            for e, row in zip(some, rows):
                target[pl.ds(e // 8 * (8 * pieces) + e % 8, pieces, stride=8), :] = row

    def rows_of(source, first, count):
        return jnp.concatenate(
            [
                jnp.concatenate(
                    [
                        source[pl.ds((at * pieces + piece) * 8, 8), :]
                        for at in range(first // 8, (first + count) // 8)
                    ],
                    axis=0,
                )
                for piece in range(pieces)
            ],
            axis=1,
        )

    def work(chunk, source, target):
        here = [chunk * group + b for b in range(group)]
        feat = jnp.concatenate([feat_ref[b] for b in here], axis=1)
        feat = jnp.concatenate([feat, jnp.zeros((8 - feats, feat.shape[1]), F32)], axis=0)
        extra = mm(feat.T.astype(BF16), feat_weight)
        after = jnp.minimum(chunk + 1, chunks - 1)
        for first in range(0, group * block_edges, part_rows):
            gather(after, range(first, first + part_rows), target)
            half = rows_of(source, first, part_rows) + extra[first : first + part_rows]
            hidden_ref[first : first + part_rows, :] = silu_half(half).astype(BF16)
        receivers = [jnp.where(b < used, recv_ref[pl.ds(b, 1), :], -2) for b in here]
        spread = jnp.concatenate([(ids_ref[...] == row).astype(F32) for row in receivers], axis=1)
        spread = spread.astype(BF16)
        total[...] += mm(spread, hidden_ref[...])

    def edge_step(step, carry):
        work(2 * step, even_rows, odd_rows)
        work(2 * step + 1, odd_rows, even_rows)
        return carry

    gather(0, range(group * block_edges), even_rows)
    lax.fori_loop(0, chunks // 2, edge_step, 0)
    odd = place % 2 == 1
    below, above = total[:owned].astype(BF16), total[2 * owned :].astype(BF16)
    own_ref[...] = total[owned : 2 * owned]
    cross_ref[...] = jnp.where(odd, above, below)
    chip_ref[...] = jnp.where(odd, below, above)


def wanted_kernel(owned, slot_ref, send_ref, wanted_ref):
    nodes = slot_ref.shape[1]
    blocks, block_edges = send_ref.shape
    places = wanted_ref.shape[1]
    chunk = LANES
    per_chunk = chunk // owned * SEND_CAP
    row, column = iota((chunk, chunk), 0), iota((chunk, chunk), 1)
    before = ((row > column) & (row // owned == column // owned)).astype(F32).astype(BF16)
    local_owner = (iota((chunk, LANES), 0) // owned * SEND_CAP).astype(F32)

    def find(index, best):
        ids = ids_of_rows(slot_ref[...], index * chunk, chunk)
        hit = jnp.zeros((chunk, block_edges), F32)
        for b in range(blocks):
            hit = jnp.maximum(hit, (ids == send_ref[b : b + 1, :]).astype(F32))
        hit = jnp.broadcast_to(jnp.max(hit, axis=1, keepdims=True), (chunk, LANES))
        rank = mm(before, hit.astype(BF16)) + local_owner
        spot = jnp.where(hit > 0, rank.astype(I32) + index * per_chunk, -1)
        spot = jnp.concatenate([spot] * (places // LANES), axis=1)
        found = jnp.where(spot == iota((chunk, places), 1), ids, -1)
        return jnp.maximum(best, jnp.max(found, axis=0, keepdims=True))

    best = lax.fori_loop(0, nodes // chunk, find, jnp.full((1, places), -1, I32), unroll=2)
    best = best.astype(F32)
    for b in range(blocks):
        senders = jnp.broadcast_to(send_ref[b : b + 1, :].astype(F32), (block_edges, block_edges)).T
        senders = jnp.concatenate([senders] * (places // LANES), axis=1)
        wanted_ref[b * block_edges : (b + 1) * block_edges, :] = (
            (senders == best).astype(F32).astype(BF16)
        )


def supply_kernel(blocks, place_ref, slot_ref, request_ref, supply_ref):
    owned = supply_ref.shape[1]
    devices = supply_ref.shape[0] // SEND_CAP
    per_device = request_ref.shape[0] // devices
    ids = ids_of_rows(slot_ref[...], place_ref[0] * owned, owned)
    lane = iota((owned, LANES), 1)
    used = jnp.zeros((owned, LANES), F32)
    for d in range(devices):
        hit = jnp.zeros((owned, request_ref.shape[1]), F32)
        for b in range(blocks):
            at = d * per_device + b
            hit = jnp.maximum(hit, (ids == request_ref[at : at + 1, :]).astype(F32))
        used = jnp.where(lane == d, jnp.max(hit, axis=1, keepdims=True), used)
    before = (iota((owned, owned), 0) > iota((owned, owned), 1)).astype(F32).astype(BF16)
    rank = jnp.where(used > 0, mm(before, used.astype(BF16)), -1.0)
    rank = jnp.concatenate([rank, jnp.full((LANES - owned, LANES), -1.0, F32)], axis=0).T
    slots = iota((SEND_CAP, owned), 0).astype(F32)
    supply = jnp.concatenate(
        [(rank[d : d + 1, :owned] == slots).astype(F32) for d in range(devices)], axis=0
    )
    supply_ref[...] = supply.astype(BF16)


def node_kernel(
    own_ref,
    from_cross_ref,
    from_chip_ref,
    latent_ref,
    edge_out_ref,
    node_input_ref,
    node_bias_ref,
    node_out_ref,
    node_gain_ref,
    mesh_sender_ref,
    supply_ref,
    encoded_ref,
    rows_ref,
):
    width = latent_ref.shape[1]
    latent = latent_ref[...]
    node_sum = own_ref[...] + from_cross_ref[...].astype(F32) + from_chip_ref[...].astype(F32)
    aggregate = mm(node_sum.astype(BF16), edge_out_ref[...]).astype(BF16)
    hidden = mm(latent, node_input_ref[:width]) + mm(aggregate, node_input_ref[width:])
    hidden = silu(hidden + node_bias_ref[...]).astype(BF16)
    encoded = latent.astype(F32) + layer_norm(mm(hidden, node_out_ref[...])) * node_gain_ref[...]
    encoded = encoded.astype(BF16)
    encoded_ref[...] = encoded
    sender_code = mm(encoded, mesh_sender_ref[...]).astype(BF16)
    rows_ref[...] = mm(supply_ref[...], sender_code).astype(BF16)


def receiver_kernel(
    place_ref,
    slot_ref,
    recv_ref,
    encoded_ref,
    mesh_receiver_ref,
    message_bias_ref,
    update_input_ref,
    update_bias_ref,
    incoming_ref,
    pick_ref,
    parts_ref,
    upper_ref,
):
    owned, width = encoded_ref.shape
    blocks = recv_ref.shape[0]
    ids = ids_of_rows(slot_ref[...], place_ref[0] * owned, owned)
    incoming = jnp.concatenate(
        [(ids == recv_ref[b : b + 1, :]).astype(F32) for b in range(blocks)], axis=1
    )
    pick = incoming.T.astype(BF16)
    pick_ref[...] = jnp.concatenate([pick, pick], axis=1)
    incoming_ref[...] = incoming.astype(BF16)
    encoded = encoded_ref[...]
    receiver = mm(encoded, mesh_receiver_ref[...]) + message_bias_ref[...]
    high = receiver.astype(BF16)
    parts_ref[:owned, :] = high
    parts_ref[owned:, :] = (receiver - high.astype(F32)).astype(BF16)
    upper_ref[...] = mm(encoded, update_input_ref[:width]) + update_bias_ref[...]


def message_kernel(
    wanted_ref,
    piece_ref,
    incoming_ref,
    pick_ref,
    parts_ref,
    upper_ref,
    encoded_ref,
    message_out_ref,
    update_input_ref,
    update_out_ref,
    update_gain_ref,
    out_ref,
):
    width = encoded_ref.shape[1]
    chosen = jnp.concatenate([wanted_ref[...], pick_ref[...]], axis=1)
    codes = jnp.concatenate([piece_ref[...], parts_ref[...]], axis=0)
    message = silu(mm(chosen, codes)).astype(BF16)
    message_sum = mm(incoming_ref[...], message).astype(BF16)
    update = mm(message_sum, message_out_ref[...]).astype(BF16)
    hidden = silu(upper_ref[...] + mm(update, update_input_ref[width:])).astype(BF16)
    out = layer_norm(mm(hidden, update_out_ref[...])) * update_gain_ref[...]
    out_ref[...] = (encoded_ref[...].astype(F32) + out).astype(BF16)


def call(kernel, out_shape, spaces, scratch=(), flops=0, moved=0, vmem=8):
    return pl.pallas_call(
        kernel,
        out_shape=out_shape,
        in_specs=[pl.BlockSpec(memory_space=space) for space in spaces],
        out_specs=jax.tree.map(lambda _: pl.BlockSpec(memory_space=VMEM), out_shape),
        scratch_shapes=scratch,
        compiler_params=pltpu.CompilerParams(vmem_limit_bytes=vmem * MEBI),
        cost_estimate=pl.CostEstimate(flops=flops, bytes_accessed=moved, transcendentals=0),
    )


def hold(value):
    return value if value.size == 1 else pltpu.with_memory_space_constraint(value, HBM)


def shape(*sizes, kind=BF16):
    return jax.ShapeDtypeStruct(sizes, kind)


def per_device(
    grid_in,
    grid_first,
    grid_bias,
    grid_second,
    send_weight,
    edge_bias,
    feat_weight,
    edge_out,
    node_input,
    node_bias,
    node_out,
    node_gain,
    mesh_sender,
    mesh_receiver,
    message_bias,
    message_out,
    update_input,
    update_bias,
    update_out,
    update_gain,
    mesh_latent,
    g2m_send,
    g2m_recv,
    g2m_feat,
    g2m_count,
    mesh_slot,
    mesh_send,
    mesh_recv,
):
    devices = lax.axis_size("bulk")
    position = lax.axis_index("bulk")
    place = position.astype(I32).reshape(1)
    owned, width = mesh_latent.shape
    grid_rows = grid_in.shape[0]
    places = devices * SEND_CAP
    edges = mesh_send.size
    slot = mesh_slot.reshape(1, -1)
    row = lambda vector: vector.reshape(1, -1)

    requests = lax.all_to_all(jnp.tile(mesh_send, (devices, 1)), "bulk", 0, 0, tiled=True)
    operands = (
        grid_first,
        grid_in.T,
        grid_second,
        send_weight,
        row(grid_bias),
        row(edge_bias),
        slot,
        feat_weight,
        g2m_send,
        g2m_recv,
        g2m_feat,
        g2m_count.reshape(1, 1),
    )
    own, cross, chip = call(
        edge_kernel,
        (shape(owned, width, kind=F32), shape(owned, width), shape(owned, width)),
        [SMEM] + [HBM] * len(operands),
        scratch=[VMEM(value.shape, value.dtype) for value in operands]
        + [
            SMEM(g2m_send.shape, I32),
            VMEM((grid_rows * (width // LANES), LANES), F32),
            VMEM((g2m_send.shape[1] * (width // LANES), LANES), F32),
            VMEM((g2m_send.shape[1] * (width // LANES), LANES), F32),
            VMEM((g2m_send.shape[1], width), BF16),
            VMEM((3 * owned, LANES), I32),
            VMEM((3 * owned, width), F32),
            pltpu.SemaphoreType.DMA((len(operands) + GRID_STEPS,)),
        ],
        flops=10_000_000_000,
        moved=4_000_000,
        vmem=32,
    )(place, *[hold(value) for value in operands])
    requests, _ = lax.optimization_barrier((requests, own))
    crossing = [(d, d + 1) for d in range(1, devices - 1, 2)]
    within = [(d, d + 1) for d in range(0, devices, 2)]
    both = lambda pairs: pairs + [(b, a) for a, b in pairs]
    from_cross = lax.ppermute(cross, "bulk", both(crossing))
    from_chip = lax.ppermute(chip, "bulk", both(within))
    supply = call(
        functools.partial(supply_kernel, mesh_send.shape[0]),
        shape(places, owned),
        [SMEM] + [VMEM] * 2,
        flops=500_000_000,
        moved=500_000,
    )(place, slot, requests)
    encoded, rows = call(
        node_kernel,
        (shape(owned, width), shape(places, width)),
        [VMEM] * 11,
        flops=500_000_000,
        moved=4_000_000,
    )(
        own,
        from_cross,
        from_chip,
        mesh_latent,
        edge_out,
        node_input,
        row(node_bias),
        node_out,
        row(node_gain),
        mesh_sender,
        supply,
    )
    piece = lax.all_to_all(rows, "bulk", 0, 0, tiled=True)
    mesh_send, _ = lax.optimization_barrier((mesh_send, encoded))
    wanted = call(
        functools.partial(wanted_kernel, owned),
        shape(edges, places),
        [VMEM] * 2,
        flops=1_000_000_000,
        moved=500_000,
    )(slot, mesh_send)
    incoming, pick, parts, upper = call(
        receiver_kernel,
        (
            shape(owned, edges),
            shape(edges, 2 * owned),
            shape(2 * owned, width),
            shape(owned, width, kind=F32),
        ),
        [SMEM] + [VMEM] * 7,
        flops=1_000_000_000,
        moved=4_000_000,
    )(
        place,
        slot,
        mesh_recv,
        encoded,
        mesh_receiver,
        row(message_bias),
        update_input,
        row(update_bias),
    )
    return call(
        message_kernel,
        shape(owned, width),
        [VMEM] * 11,
        flops=1_000_000_000,
        moved=4_000_000,
    )(
        wanted,
        piece,
        incoming,
        pick,
        parts,
        upper,
        encoded,
        message_out,
        update_input,
        update_out,
        row(update_gain),
    )


def solution(mesh):
    split = {0: ("groups", "bulk"), 20: "bulk", 21: "bulk", 22: "bulk", 23: "bulk", 24: "bulk"}
    split.update({26: "bulk", 27: "bulk"})
    placed = tuple(P(split[at]) if at in split else P() for at in range(28))
    return jax.shard_map(
        per_device,
        mesh=mesh,
        in_specs=placed,
        out_specs=P(("groups", "bulk"), None),
        check_vma=False,
    )
```

```python
import functools
import math

import jax
import jax.numpy as jnp
from jax import lax
from jax.experimental import pallas as pl
from jax.experimental.pallas import tpu as pltpu
from jax.sharding import PartitionSpec as P

F32 = jnp.float32
BF16 = jnp.bfloat16
I32 = jnp.int32
SEND_CAP = 16
LANES = 128
VMEM = pltpu.VMEM
SMEM = pltpu.SMEM
HBM = pltpu.HBM
GRID_STEPS = 2
CHUNK_BLOCKS = 4
MEBI = 1024 * 1024


def mm(left, right):
    return jnp.dot(left, right, preferred_element_type=F32)


def mm_nt(left, right):
    return lax.dot_general(left, right, (((1,), (1,)), ((), ())), preferred_element_type=F32)


def silu_half(half):
    return half + half * jnp.tanh(half)


def silu(value):
    return silu_half(0.5 * value)


def layer_norm(value):
    center = value - jnp.mean(value, axis=-1, keepdims=True)
    spread = jnp.mean(center * center, axis=-1, keepdims=True)
    return center * lax.rsqrt(spread + 1e-05)


def iota(shape, dim):
    return lax.broadcasted_iota(I32, shape, dim)


def one_hot(columns, rows):
    hit = columns.astype(jnp.int16) == lax.broadcasted_iota(jnp.int16, (rows, columns.shape[1]), 0)
    return jnp.where(hit, jnp.ones((), BF16), jnp.zeros((), BF16))


def ids_of_rows(slot, first, count):
    nodes = slot.shape[1]
    rows = iota((count, nodes), 0) + first
    return jnp.max(jnp.where(slot == rows, iota((count, nodes), 1), -1), axis=1, keepdims=True)


def edge_kernel(
    place_ref,
    first_hbm,
    grid_hbm,
    second_hbm,
    send_weight_hbm,
    grid_bias_hbm,
    edge_bias_hbm,
    slot_hbm,
    feat_weight_hbm,
    send_hbm,
    recv_hbm,
    feat_hbm,
    count_hbm,
    own_ref,
    cross_ref,
    chip_ref,
    first_ref,
    grid_ref,
    second_ref,
    send_weight_ref,
    grid_bias_ref,
    edge_bias_ref,
    slot_ref,
    feat_weight_ref,
    send_ref,
    recv_ref,
    feat_ref,
    count_ref,
    starts,
    table,
    even_rows,
    odd_rows,
    hidden_ref,
    ids_ref,
    total,
    sems,
):
    channels, grid_rows = grid_ref.shape
    width = second_ref.shape[1]
    pieces = width // LANES
    blocks, block_edges = send_ref.shape
    owned = own_ref.shape[0]
    feats = feat_ref.shape[1]
    step_rows = grid_rows // GRID_STEPS

    def grid_copy(step):
        part = pl.ds(pl.multiple_of(step * step_rows, step_rows), step_rows)
        return pltpu.make_async_copy(grid_hbm.at[:, part], grid_ref.at[:, part], sems.at[step])

    pairs = [
        (first_hbm, first_ref),
        (second_hbm, second_ref),
        (send_weight_hbm, send_weight_ref),
        (grid_bias_hbm, grid_bias_ref),
        (edge_bias_hbm, edge_bias_ref),
        (send_hbm, send_ref),
        (slot_hbm, slot_ref),
        (feat_weight_hbm, feat_weight_ref),
        (recv_hbm, recv_ref),
        (feat_hbm, feat_ref),
        (count_hbm, count_ref),
        (send_ref, starts),
    ]
    copies = [
        pltpu.make_async_copy(source, target, sems.at[GRID_STEPS + at])
        for at, (source, target) in enumerate(pairs)
    ]
    first_copy, second_copy, send_weight_copy, grid_bias_copy, edge_bias_copy, send_copy = copies[:6]
    slot_copy, starts_copy = copies[6], copies[-1]
    first_copy.start()
    grid_copy(0).start()
    for copy in copies[1:-1]:
        copy.start()
    for step in range(1, GRID_STEPS):
        grid_copy(step).start()
    send_copy.wait()
    senders = send_ref[...]
    send_ref[...] = (senders // 8) * (8 * pieces) + senders % 8
    starts_copy.start()
    slot_copy.wait()
    place = place_ref[0]
    ids_ref[...] = jnp.broadcast_to(
        ids_of_rows(slot_ref[...], (place - 1) * owned, 3 * owned), ids_ref.shape
    )
    total[...] = jnp.zeros_like(total)
    first_copy.wait()
    first_ref[...] = first_ref[...] * 0.5
    second_copy.wait()
    send_weight_copy.wait()
    send_weight_ref[...] = send_weight_ref[...] * 0.5
    grid_bias_copy.wait()
    edge_bias_copy.wait()
    grid_bias = 0.5 * grid_bias_ref[...]
    edge_bias = 0.5 * edge_bias_ref[...]
    half_rows = step_rows // 2

    def grid_step(step, carry):
        grid_copy(step).wait()
        first = pl.multiple_of(step * step_rows, step_rows)
        values = [
            mm(grid_ref[:, pl.ds(first + at, half_rows)].T, first_ref[...])
            for at in (0, half_rows)
        ]
        values = [silu_half(value + grid_bias).astype(BF16) for value in values]
        values = [mm(value, second_ref[...]) for value in values]
        values = [layer_norm(value).astype(BF16) for value in values]
        values = [mm(value, send_weight_ref[...]) for value in values]
        for half, value in enumerate(values):
            row = (value + edge_bias).astype(BF16).astype(F32)
            base = pl.multiple_of((first + half * half_rows) * pieces, half_rows * pieces)
            for group in range(half_rows // 8):
                for piece in range(pieces):
                    at = (group * pieces + piece) * 8
                    table[pl.ds(base + at, 8), :] = row[
                        group * 8 : group * 8 + 8, piece * LANES : (piece + 1) * LANES
                    ]
        return carry

    lax.fori_loop(0, GRID_STEPS, grid_step, 0)
    for copy in copies[7:]:
        copy.wait()
    used = count_ref[...]
    feat_weight = 0.5 * feat_weight_ref[...].astype(F32)
    feat_weight = jnp.concatenate([feat_weight, jnp.zeros((8 - feats, width), F32)], axis=0)
    feat_weight = feat_weight.astype(BF16)
    group = CHUNK_BLOCKS
    chunks = blocks // group
    part_rows = 64

    def gather(chunk, edges, target):
        for edge in edges:
            start = starts[chunk * group + edge // block_edges, edge % block_edges]
            target[pl.ds(edge // 8 * (8 * pieces) + edge % 8, pieces, stride=8), :] = table[
                pl.ds(start, pieces, stride=8), :
            ]

    def rows_of(source, first, count):
        return jnp.concatenate(
            [
                jnp.concatenate(
                    [
                        source[pl.ds((at * pieces + piece) * 8, 8), :]
                        for at in range(first // 8, (first + count) // 8)
                    ],
                    axis=0,
                )
                for piece in range(pieces)
            ],
            axis=1,
        )

    def work(chunk, source, target):
        here = [chunk * group + b for b in range(group)]
        feat = jnp.concatenate([feat_ref[b] for b in here], axis=1)
        feat = jnp.concatenate([feat, jnp.zeros((8 - feats, feat.shape[1]), F32)], axis=0)
        extra = mm(feat.T.astype(BF16), feat_weight)
        after = jnp.minimum(chunk + 1, chunks - 1)
        for first in range(0, group * block_edges, part_rows):
            gather(after, range(first, first + part_rows), target)
            half = rows_of(source, first, part_rows) + extra[first : first + part_rows]
            hidden_ref[first : first + part_rows, :] = silu_half(half).astype(BF16)
        receivers = [jnp.where(b < used, recv_ref[pl.ds(b, 1), :], -2) for b in here]
        spread = jnp.concatenate([(ids_ref[...] == row).astype(F32) for row in receivers], axis=1)
        spread = spread.astype(BF16)
        total[...] += mm(spread, hidden_ref[...])

    def edge_step(step, carry):
        work(2 * step, even_rows, odd_rows)
        work(2 * step + 1, odd_rows, even_rows)
        return carry

    gather(0, range(group * block_edges), even_rows)
    lax.fori_loop(0, chunks // 2, edge_step, 0)
    odd = place % 2 == 1
    below, above = total[:owned].astype(BF16), total[2 * owned :].astype(BF16)
    own_ref[...] = total[owned : 2 * owned]
    cross_ref[...] = jnp.where(odd, above, below)
    chip_ref[...] = jnp.where(odd, below, above)


def wanted_kernel(owned, slot_ref, send_ref, wanted_ref):
    nodes = slot_ref.shape[1]
    blocks, block_edges = send_ref.shape
    places = wanted_ref.shape[1]
    chunk = LANES
    per_chunk = chunk // owned * SEND_CAP
    row, column = iota((chunk, chunk), 0), iota((chunk, chunk), 1)
    before = ((row > column) & (row // owned == column // owned)).astype(F32).astype(BF16)
    local_owner = (iota((chunk, LANES), 0) // owned * SEND_CAP).astype(F32)

    def find(index, best):
        ids = ids_of_rows(slot_ref[...], index * chunk, chunk)
        hit = jnp.zeros((chunk, block_edges), F32)
        for b in range(blocks):
            hit = jnp.maximum(hit, (ids == send_ref[b : b + 1, :]).astype(F32))
        hit = jnp.broadcast_to(jnp.max(hit, axis=1, keepdims=True), (chunk, LANES))
        rank = mm(before, hit.astype(BF16)) + local_owner
        spot = jnp.where(hit > 0, rank.astype(I32) + index * per_chunk, -1)
        spot = jnp.concatenate([spot] * (places // LANES), axis=1)
        found = jnp.where(spot == iota((chunk, places), 1), ids, -1)
        return jnp.maximum(best, jnp.max(found, axis=0, keepdims=True))

    best = lax.fori_loop(0, nodes // chunk, find, jnp.full((1, places), -1, I32), unroll=2)
    best = best.astype(F32)
    for b in range(blocks):
        senders = jnp.broadcast_to(send_ref[b : b + 1, :].astype(F32), (block_edges, block_edges)).T
        senders = jnp.concatenate([senders] * (places // LANES), axis=1)
        wanted_ref[b * block_edges : (b + 1) * block_edges, :] = (
            (senders == best).astype(F32).astype(BF16)
        )


def supply_kernel(blocks, place_ref, slot_ref, request_ref, supply_ref):
    owned = supply_ref.shape[1]
    devices = supply_ref.shape[0] // SEND_CAP
    per_device = request_ref.shape[0] // devices
    ids = ids_of_rows(slot_ref[...], place_ref[0] * owned, owned)
    lane = iota((owned, LANES), 1)
    used = jnp.zeros((owned, LANES), F32)
    for d in range(devices):
        hit = jnp.zeros((owned, request_ref.shape[1]), F32)
        for b in range(blocks):
            at = d * per_device + b
            hit = jnp.maximum(hit, (ids == request_ref[at : at + 1, :]).astype(F32))
        used = jnp.where(lane == d, jnp.max(hit, axis=1, keepdims=True), used)
    before = (iota((owned, owned), 0) > iota((owned, owned), 1)).astype(F32).astype(BF16)
    rank = jnp.where(used > 0, mm(before, used.astype(BF16)), -1.0)
    rank = jnp.concatenate([rank, jnp.full((LANES - owned, LANES), -1.0, F32)], axis=0).T
    slots = iota((SEND_CAP, owned), 0).astype(F32)
    supply = jnp.concatenate(
        [(rank[d : d + 1, :owned] == slots).astype(F32) for d in range(devices)], axis=0
    )
    supply_ref[...] = supply.astype(BF16)


def node_kernel(
    own_ref,
    from_cross_ref,
    from_chip_ref,
    latent_ref,
    edge_out_ref,
    node_input_ref,
    node_bias_ref,
    node_out_ref,
    node_gain_ref,
    mesh_sender_ref,
    supply_ref,
    encoded_ref,
    rows_ref,
):
    width = latent_ref.shape[1]
    latent = latent_ref[...]
    node_sum = own_ref[...] + from_cross_ref[...].astype(F32) + from_chip_ref[...].astype(F32)
    aggregate = mm(node_sum.astype(BF16), edge_out_ref[...]).astype(BF16)
    hidden = mm(latent, node_input_ref[:width]) + mm(aggregate, node_input_ref[width:])
    hidden = silu(hidden + node_bias_ref[...]).astype(BF16)
    encoded = latent.astype(F32) + layer_norm(mm(hidden, node_out_ref[...])) * node_gain_ref[...]
    encoded = encoded.astype(BF16)
    encoded_ref[...] = encoded
    sender_code = mm(encoded, mesh_sender_ref[...]).astype(BF16)
    rows_ref[...] = mm(supply_ref[...], sender_code).astype(BF16)


def receiver_kernel(
    place_ref,
    slot_ref,
    recv_ref,
    encoded_ref,
    mesh_receiver_ref,
    message_bias_ref,
    update_input_ref,
    update_bias_ref,
    incoming_ref,
    pick_ref,
    parts_ref,
    upper_ref,
):
    owned, width = encoded_ref.shape
    blocks = recv_ref.shape[0]
    ids = ids_of_rows(slot_ref[...], place_ref[0] * owned, owned)
    incoming = jnp.concatenate(
        [(ids == recv_ref[b : b + 1, :]).astype(F32) for b in range(blocks)], axis=1
    )
    pick = incoming.T.astype(BF16)
    pick_ref[...] = jnp.concatenate([pick, pick], axis=1)
    incoming_ref[...] = incoming.astype(BF16)
    encoded = encoded_ref[...]
    receiver = mm(encoded, mesh_receiver_ref[...]) + message_bias_ref[...]
    high = receiver.astype(BF16)
    parts_ref[:owned, :] = high
    parts_ref[owned:, :] = (receiver - high.astype(F32)).astype(BF16)
    upper_ref[...] = mm(encoded, update_input_ref[:width]) + update_bias_ref[...]


def message_kernel(
    wanted_ref,
    piece_ref,
    incoming_ref,
    pick_ref,
    parts_ref,
    upper_ref,
    encoded_ref,
    message_out_ref,
    update_input_ref,
    update_out_ref,
    update_gain_ref,
    out_ref,
):
    width = encoded_ref.shape[1]
    chosen = jnp.concatenate([wanted_ref[...], pick_ref[...]], axis=1)
    codes = jnp.concatenate([piece_ref[...], parts_ref[...]], axis=0)
    message = silu(mm(chosen, codes)).astype(BF16)
    message_sum = mm(incoming_ref[...], message).astype(BF16)
    update = mm(message_sum, message_out_ref[...]).astype(BF16)
    hidden = silu(upper_ref[...] + mm(update, update_input_ref[width:])).astype(BF16)
    out = layer_norm(mm(hidden, update_out_ref[...])) * update_gain_ref[...]
    out_ref[...] = (encoded_ref[...].astype(F32) + out).astype(BF16)


def call(kernel, out_shape, spaces, scratch=(), flops=0, moved=0, vmem=8):
    return pl.pallas_call(
        kernel,
        out_shape=out_shape,
        in_specs=[pl.BlockSpec(memory_space=space) for space in spaces],
        out_specs=jax.tree.map(lambda _: pl.BlockSpec(memory_space=VMEM), out_shape),
        scratch_shapes=scratch,
        compiler_params=pltpu.CompilerParams(vmem_limit_bytes=vmem * MEBI),
        cost_estimate=pl.CostEstimate(flops=flops, bytes_accessed=moved, transcendentals=0),
    )


def hold(value):
    return value if value.size == 1 else pltpu.with_memory_space_constraint(value, HBM)


def shape(*sizes, kind=BF16):
    return jax.ShapeDtypeStruct(sizes, kind)


def per_device(
    grid_in,
    grid_first,
    grid_bias,
    grid_second,
    send_weight,
    edge_bias,
    feat_weight,
    edge_out,
    node_input,
    node_bias,
    node_out,
    node_gain,
    mesh_sender,
    mesh_receiver,
    message_bias,
    message_out,
    update_input,
    update_bias,
    update_out,
    update_gain,
    mesh_latent,
    g2m_send,
    g2m_recv,
    g2m_feat,
    g2m_count,
    mesh_slot,
    mesh_send,
    mesh_recv,
):
    devices = lax.axis_size("bulk")
    position = lax.axis_index("bulk")
    place = position.astype(I32).reshape(1)
    owned, width = mesh_latent.shape
    grid_rows = grid_in.shape[0]
    places = devices * SEND_CAP
    edges = mesh_send.size
    slot = mesh_slot.reshape(1, -1)
    row = lambda vector: vector.reshape(1, -1)

    requests = lax.all_to_all(jnp.tile(mesh_send, (devices, 1)), "bulk", 0, 0, tiled=True)
    operands = (
        grid_first,
        grid_in.T,
        grid_second,
        send_weight,
        row(grid_bias),
        row(edge_bias),
        slot,
        feat_weight,
        g2m_send,
        g2m_recv,
        g2m_feat,
        g2m_count.reshape(1, 1),
    )
    own, cross, chip = call(
        edge_kernel,
        (shape(owned, width, kind=F32), shape(owned, width), shape(owned, width)),
        [SMEM] + [HBM] * len(operands),
        scratch=[VMEM(value.shape, value.dtype) for value in operands]
        + [
            SMEM(g2m_send.shape, I32),
            VMEM((grid_rows * (width // LANES), LANES), F32),
            VMEM((CHUNK_BLOCKS * g2m_send.shape[1] * (width // LANES), LANES), F32),
            VMEM((CHUNK_BLOCKS * g2m_send.shape[1] * (width // LANES), LANES), F32),
            VMEM((CHUNK_BLOCKS * g2m_send.shape[1], width), BF16),
            VMEM((3 * owned, LANES), I32),
            VMEM((3 * owned, width), F32),
            pltpu.SemaphoreType.DMA((len(operands) + GRID_STEPS,)),
        ],
        flops=10_000_000_000,
        moved=4_000_000,
        vmem=32,
    )(place, *[hold(value) for value in operands])
    requests, _ = lax.optimization_barrier((requests, own))
    crossing = [(d, d + 1) for d in range(1, devices - 1, 2)]
    within = [(d, d + 1) for d in range(0, devices, 2)]
    both = lambda pairs: pairs + [(b, a) for a, b in pairs]
    from_cross = lax.ppermute(cross, "bulk", both(crossing))
    from_chip = lax.ppermute(chip, "bulk", both(within))
    supply = call(
        functools.partial(supply_kernel, mesh_send.shape[0]),
        shape(places, owned),
        [SMEM] + [VMEM] * 2,
        flops=500_000_000,
        moved=500_000,
    )(place, slot, requests)
    encoded, rows = call(
        node_kernel,
        (shape(owned, width), shape(places, width)),
        [VMEM] * 11,
        flops=500_000_000,
        moved=4_000_000,
    )(
        own,
        from_cross,
        from_chip,
        mesh_latent,
        edge_out,
        node_input,
        row(node_bias),
        node_out,
        row(node_gain),
        mesh_sender,
        supply,
    )
    piece = lax.all_to_all(rows, "bulk", 0, 0, tiled=True)
    mesh_send, _ = lax.optimization_barrier((mesh_send, encoded))
    wanted = call(
        functools.partial(wanted_kernel, owned),
        shape(edges, places),
        [VMEM] * 2,
        flops=1_000_000_000,
        moved=500_000,
    )(slot, mesh_send)
    incoming, pick, parts, upper = call(
        receiver_kernel,
        (
            shape(owned, edges),
            shape(edges, 2 * owned),
            shape(2 * owned, width),
            shape(owned, width, kind=F32),
        ),
        [SMEM] + [VMEM] * 7,
        flops=1_000_000_000,
        moved=4_000_000,
    )(
        place,
        slot,
        mesh_recv,
        encoded,
        mesh_receiver,
        row(message_bias),
        update_input,
        row(update_bias),
    )
    return call(
        message_kernel,
        shape(owned, width),
        [VMEM] * 11,
        flops=1_000_000_000,
        moved=4_000_000,
    )(
        wanted,
        piece,
        incoming,
        pick,
        parts,
        upper,
        encoded,
        message_out,
        update_input,
        update_out,
        row(update_gain),
    )


def solution(mesh):
    split = {0: ("groups", "bulk"), 20: "bulk", 21: "bulk", 22: "bulk", 23: "bulk", 24: "bulk"}
    split.update({26: "bulk", 27: "bulk"})
    placed = tuple(P(split[at]) if at in split else P() for at in range(28))
    return jax.shard_map(
        per_device,
        mesh=mesh,
        in_specs=placed,
        out_specs=P(("groups", "bulk"), None),
        check_vma=False,
    )
```

```python
import functools
import math

import jax
import jax.numpy as jnp
from jax import lax
from jax.experimental import pallas as pl
from jax.experimental.pallas import tpu as pltpu
from jax.sharding import PartitionSpec as P

F32 = jnp.float32
BF16 = jnp.bfloat16
I32 = jnp.int32
SEND_CAP = 16
LANES = 128
VMEM = pltpu.VMEM
SMEM = pltpu.SMEM
HBM = pltpu.HBM
GRID_STEPS = 2
CHUNK_BLOCKS = 4
MEBI = 1024 * 1024


def mm(left, right):
    return jnp.dot(left, right, preferred_element_type=F32)


def mm_nt(left, right):
    return lax.dot_general(left, right, (((1,), (1,)), ((), ())), preferred_element_type=F32)


def silu_half(half):
    return half + half * jnp.tanh(half)


def silu(value):
    return silu_half(0.5 * value)


def layer_norm(value):
    center = value - jnp.mean(value, axis=-1, keepdims=True)
    spread = jnp.mean(center * center, axis=-1, keepdims=True)
    return center * lax.rsqrt(spread + 1e-05)


def iota(shape, dim):
    return lax.broadcasted_iota(I32, shape, dim)


def one_hot(columns, rows):
    hit = columns.astype(jnp.int16) == lax.broadcasted_iota(jnp.int16, (rows, columns.shape[1]), 0)
    return jnp.where(hit, jnp.ones((), BF16), jnp.zeros((), BF16))


def ids_of_rows(slot, first, count):
    nodes = slot.shape[1]
    rows = iota((count, nodes), 0) + first
    return jnp.max(jnp.where(slot == rows, iota((count, nodes), 1), -1), axis=1, keepdims=True)


def edge_kernel(
    place_ref,
    first_hbm,
    grid_hbm,
    second_hbm,
    send_weight_hbm,
    grid_bias_hbm,
    edge_bias_hbm,
    slot_hbm,
    feat_weight_hbm,
    send_hbm,
    recv_hbm,
    feat_hbm,
    count_hbm,
    own_ref,
    cross_ref,
    chip_ref,
    first_ref,
    grid_ref,
    second_ref,
    send_weight_ref,
    grid_bias_ref,
    edge_bias_ref,
    slot_ref,
    feat_weight_ref,
    send_ref,
    recv_ref,
    feat_ref,
    count_ref,
    starts,
    table,
    even_rows,
    odd_rows,
    even_hidden,
    odd_hidden,
    ids_ref,
    total,
    sems,
):
    channels, grid_rows = grid_ref.shape
    width = second_ref.shape[1]
    pieces = width // LANES
    blocks, block_edges = send_ref.shape
    owned = own_ref.shape[0]
    feats = feat_ref.shape[1]
    step_rows = grid_rows // GRID_STEPS

    def grid_copy(step):
        part = pl.ds(pl.multiple_of(step * step_rows, step_rows), step_rows)
        return pltpu.make_async_copy(grid_hbm.at[:, part], grid_ref.at[:, part], sems.at[step])

    pairs = [
        (first_hbm, first_ref),
        (second_hbm, second_ref),
        (send_weight_hbm, send_weight_ref),
        (grid_bias_hbm, grid_bias_ref),
        (edge_bias_hbm, edge_bias_ref),
        (send_hbm, send_ref),
        (slot_hbm, slot_ref),
        (feat_weight_hbm, feat_weight_ref),
        (recv_hbm, recv_ref),
        (feat_hbm, feat_ref),
        (count_hbm, count_ref),
        (send_ref, starts),
    ]
    copies = [
        pltpu.make_async_copy(source, target, sems.at[GRID_STEPS + at])
        for at, (source, target) in enumerate(pairs)
    ]
    first_copy, second_copy, send_weight_copy, grid_bias_copy, edge_bias_copy, send_copy = copies[:6]
    slot_copy, starts_copy = copies[6], copies[-1]
    first_copy.start()
    grid_copy(0).start()
    for copy in copies[1:-1]:
        copy.start()
    for step in range(1, GRID_STEPS):
        grid_copy(step).start()
    send_copy.wait()
    senders = send_ref[...]
    send_ref[...] = (senders // 8) * (8 * pieces) + senders % 8
    starts_copy.start()
    slot_copy.wait()
    place = place_ref[0]
    ids_ref[...] = jnp.broadcast_to(
        ids_of_rows(slot_ref[...], (place - 1) * owned, 3 * owned), ids_ref.shape
    )
    total[...] = jnp.zeros_like(total)
    first_copy.wait()
    first_ref[...] = first_ref[...] * 0.5
    second_copy.wait()
    send_weight_copy.wait()
    send_weight_ref[...] = send_weight_ref[...] * 0.5
    grid_bias_copy.wait()
    edge_bias_copy.wait()
    grid_bias = 0.5 * grid_bias_ref[...]
    edge_bias = 0.5 * edge_bias_ref[...]
    half_rows = step_rows // 2

    def grid_step(step, carry):
        grid_copy(step).wait()
        first = pl.multiple_of(step * step_rows, step_rows)
        values = [
            mm(grid_ref[:, pl.ds(first + at, half_rows)].T, first_ref[...])
            for at in (0, half_rows)
        ]
        values = [silu_half(value + grid_bias).astype(BF16) for value in values]
        values = [mm(value, second_ref[...]) for value in values]
        values = [layer_norm(value).astype(BF16) for value in values]
        values = [mm(value, send_weight_ref[...]) for value in values]
        for half, value in enumerate(values):
            row = (value + edge_bias).astype(BF16).astype(F32)
            base = pl.multiple_of((first + half * half_rows) * pieces, half_rows * pieces)
            for group in range(half_rows // 8):
                for piece in range(pieces):
                    at = (group * pieces + piece) * 8
                    table[pl.ds(base + at, 8), :] = row[
                        group * 8 : group * 8 + 8, piece * LANES : (piece + 1) * LANES
                    ]
        return carry

    lax.fori_loop(0, GRID_STEPS, grid_step, 0)
    for copy in copies[7:]:
        copy.wait()
    used = count_ref[...]
    feat_weight = 0.5 * feat_weight_ref[...].astype(F32)
    feat_weight = jnp.concatenate([feat_weight, jnp.zeros((8 - feats, width), F32)], axis=0)
    feat_weight = feat_weight.astype(BF16)
    group = CHUNK_BLOCKS
    chunks = blocks // group
    part_rows = 64

    def gather(chunk, edges, target):
        for edge in edges:
            start = starts[chunk * group + edge // block_edges, edge % block_edges]
            target[pl.ds(edge // 8 * (8 * pieces) + edge % 8, pieces, stride=8), :] = table[
                pl.ds(start, pieces, stride=8), :
            ]

    def rows_of(source, first, count):
        return jnp.concatenate(
            [
                jnp.concatenate(
                    [
                        source[pl.ds((at * pieces + piece) * 8, 8), :]
                        for at in range(first // 8, (first + count) // 8)
                    ],
                    axis=0,
                )
                for piece in range(pieces)
            ],
            axis=1,
        )

    def add_sums(chunk, hidden):
        here = [chunk * group + b for b in range(group)]
        receivers = [jnp.where(b < used, recv_ref[pl.ds(b, 1), :], -2) for b in here]
        spread = jnp.concatenate([(ids_ref[...] == row).astype(F32) for row in receivers], axis=1)
        total[...] += mm(spread.astype(BF16), hidden[...])

    def work(chunk, source, target, hidden, hidden_before):
        here = [chunk * group + b for b in range(group)]
        feat = jnp.concatenate([feat_ref[b] for b in here], axis=1)
        feat = jnp.concatenate([feat, jnp.zeros((8 - feats, feat.shape[1]), F32)], axis=0)
        extra = mm(feat.T.astype(BF16), feat_weight)
        add_sums(jnp.maximum(chunk - 1, 0), hidden_before)
        after = jnp.minimum(chunk + 1, chunks - 1)
        for first in range(0, group * block_edges, part_rows):
            gather(after, range(first, first + part_rows), target)
            half = rows_of(source, first, part_rows) + extra[first : first + part_rows]
            hidden[first : first + part_rows, :] = silu_half(half).astype(BF16)

    def edge_step(step, carry):
        work(2 * step, even_rows, odd_rows, even_hidden, odd_hidden)
        work(2 * step + 1, odd_rows, even_rows, odd_hidden, even_hidden)
        return carry

    odd_hidden[...] = jnp.zeros_like(odd_hidden)
    gather(0, range(group * block_edges), even_rows)
    lax.fori_loop(0, chunks // 2, edge_step, 0)
    add_sums(chunks - 1, odd_hidden)
    odd = place % 2 == 1
    below, above = total[:owned].astype(BF16), total[2 * owned :].astype(BF16)
    own_ref[...] = total[owned : 2 * owned]
    cross_ref[...] = jnp.where(odd, above, below)
    chip_ref[...] = jnp.where(odd, below, above)


def wanted_kernel(owned, slot_ref, send_ref, wanted_ref):
    nodes = slot_ref.shape[1]
    blocks, block_edges = send_ref.shape
    places = wanted_ref.shape[1]
    chunk = LANES
    per_chunk = chunk // owned * SEND_CAP
    row, column = iota((chunk, chunk), 0), iota((chunk, chunk), 1)
    before = ((row > column) & (row // owned == column // owned)).astype(F32).astype(BF16)
    local_owner = (iota((chunk, LANES), 0) // owned * SEND_CAP).astype(F32)

    def find(index, best):
        ids = ids_of_rows(slot_ref[...], index * chunk, chunk)
        hit = jnp.zeros((chunk, block_edges), F32)
        for b in range(blocks):
            hit = jnp.maximum(hit, (ids == send_ref[b : b + 1, :]).astype(F32))
        hit = jnp.broadcast_to(jnp.max(hit, axis=1, keepdims=True), (chunk, LANES))
        rank = mm(before, hit.astype(BF16)) + local_owner
        spot = jnp.where(hit > 0, rank.astype(I32) + index * per_chunk, -1)
        spot = jnp.concatenate([spot] * (places // LANES), axis=1)
        found = jnp.where(spot == iota((chunk, places), 1), ids, -1)
        return jnp.maximum(best, jnp.max(found, axis=0, keepdims=True))

    best = lax.fori_loop(0, nodes // chunk, find, jnp.full((1, places), -1, I32), unroll=2)
    best = best.astype(F32)
    for b in range(blocks):
        senders = jnp.broadcast_to(send_ref[b : b + 1, :].astype(F32), (block_edges, block_edges)).T
        senders = jnp.concatenate([senders] * (places // LANES), axis=1)
        wanted_ref[b * block_edges : (b + 1) * block_edges, :] = (
            (senders == best).astype(F32).astype(BF16)
        )


def supply_kernel(blocks, place_ref, slot_ref, request_ref, supply_ref):
    owned = supply_ref.shape[1]
    devices = supply_ref.shape[0] // SEND_CAP
    per_device = request_ref.shape[0] // devices
    ids = ids_of_rows(slot_ref[...], place_ref[0] * owned, owned)
    lane = iota((owned, LANES), 1)
    used = jnp.zeros((owned, LANES), F32)
    for d in range(devices):
        hit = jnp.zeros((owned, request_ref.shape[1]), F32)
        for b in range(blocks):
            at = d * per_device + b
            hit = jnp.maximum(hit, (ids == request_ref[at : at + 1, :]).astype(F32))
        used = jnp.where(lane == d, jnp.max(hit, axis=1, keepdims=True), used)
    before = (iota((owned, owned), 0) > iota((owned, owned), 1)).astype(F32).astype(BF16)
    rank = jnp.where(used > 0, mm(before, used.astype(BF16)), -1.0)
    rank = jnp.concatenate([rank, jnp.full((LANES - owned, LANES), -1.0, F32)], axis=0).T
    slots = iota((SEND_CAP, owned), 0).astype(F32)
    supply = jnp.concatenate(
        [(rank[d : d + 1, :owned] == slots).astype(F32) for d in range(devices)], axis=0
    )
    supply_ref[...] = supply.astype(BF16)


def node_kernel(
    own_ref,
    from_cross_ref,
    from_chip_ref,
    latent_ref,
    edge_out_ref,
    node_input_ref,
    node_bias_ref,
    node_out_ref,
    node_gain_ref,
    mesh_sender_ref,
    supply_ref,
    encoded_ref,
    rows_ref,
):
    width = latent_ref.shape[1]
    latent = latent_ref[...]
    node_sum = own_ref[...] + from_cross_ref[...].astype(F32) + from_chip_ref[...].astype(F32)
    aggregate = mm(node_sum.astype(BF16), edge_out_ref[...]).astype(BF16)
    hidden = mm(latent, node_input_ref[:width]) + mm(aggregate, node_input_ref[width:])
    hidden = silu(hidden + node_bias_ref[...]).astype(BF16)
    encoded = latent.astype(F32) + layer_norm(mm(hidden, node_out_ref[...])) * node_gain_ref[...]
    encoded = encoded.astype(BF16)
    encoded_ref[...] = encoded
    sender_code = mm(encoded, mesh_sender_ref[...]).astype(BF16)
    rows_ref[...] = mm(supply_ref[...], sender_code).astype(BF16)


def receiver_kernel(
    place_ref,
    slot_ref,
    recv_ref,
    encoded_ref,
    mesh_receiver_ref,
    message_bias_ref,
    update_input_ref,
    update_bias_ref,
    incoming_ref,
    pick_ref,
    parts_ref,
    upper_ref,
):
    owned, width = encoded_ref.shape
    blocks = recv_ref.shape[0]
    ids = ids_of_rows(slot_ref[...], place_ref[0] * owned, owned)
    incoming = jnp.concatenate(
        [(ids == recv_ref[b : b + 1, :]).astype(F32) for b in range(blocks)], axis=1
    )
    pick = incoming.T.astype(BF16)
    pick_ref[...] = jnp.concatenate([pick, pick], axis=1)
    incoming_ref[...] = incoming.astype(BF16)
    encoded = encoded_ref[...]
    receiver = mm(encoded, mesh_receiver_ref[...]) + message_bias_ref[...]
    high = receiver.astype(BF16)
    parts_ref[:owned, :] = high
    parts_ref[owned:, :] = (receiver - high.astype(F32)).astype(BF16)
    upper_ref[...] = mm(encoded, update_input_ref[:width]) + update_bias_ref[...]


def message_kernel(
    wanted_ref,
    piece_ref,
    incoming_ref,
    pick_ref,
    parts_ref,
    upper_ref,
    encoded_ref,
    message_out_ref,
    update_input_ref,
    update_out_ref,
    update_gain_ref,
    out_ref,
):
    width = encoded_ref.shape[1]
    chosen = jnp.concatenate([wanted_ref[...], pick_ref[...]], axis=1)
    codes = jnp.concatenate([piece_ref[...], parts_ref[...]], axis=0)
    message = silu(mm(chosen, codes)).astype(BF16)
    message_sum = mm(incoming_ref[...], message).astype(BF16)
    update = mm(message_sum, message_out_ref[...]).astype(BF16)
    hidden = silu(upper_ref[...] + mm(update, update_input_ref[width:])).astype(BF16)
    out = layer_norm(mm(hidden, update_out_ref[...])) * update_gain_ref[...]
    out_ref[...] = (encoded_ref[...].astype(F32) + out).astype(BF16)


def call(kernel, out_shape, spaces, scratch=(), flops=0, moved=0, vmem=8):
    return pl.pallas_call(
        kernel,
        out_shape=out_shape,
        in_specs=[pl.BlockSpec(memory_space=space) for space in spaces],
        out_specs=jax.tree.map(lambda _: pl.BlockSpec(memory_space=VMEM), out_shape),
        scratch_shapes=scratch,
        compiler_params=pltpu.CompilerParams(vmem_limit_bytes=vmem * MEBI),
        cost_estimate=pl.CostEstimate(flops=flops, bytes_accessed=moved, transcendentals=0),
    )


def hold(value):
    return value if value.size == 1 else pltpu.with_memory_space_constraint(value, HBM)


def shape(*sizes, kind=BF16):
    return jax.ShapeDtypeStruct(sizes, kind)


def per_device(
    grid_in,
    grid_first,
    grid_bias,
    grid_second,
    send_weight,
    edge_bias,
    feat_weight,
    edge_out,
    node_input,
    node_bias,
    node_out,
    node_gain,
    mesh_sender,
    mesh_receiver,
    message_bias,
    message_out,
    update_input,
    update_bias,
    update_out,
    update_gain,
    mesh_latent,
    g2m_send,
    g2m_recv,
    g2m_feat,
    g2m_count,
    mesh_slot,
    mesh_send,
    mesh_recv,
):
    devices = lax.axis_size("bulk")
    position = lax.axis_index("bulk")
    place = position.astype(I32).reshape(1)
    owned, width = mesh_latent.shape
    grid_rows = grid_in.shape[0]
    places = devices * SEND_CAP
    edges = mesh_send.size
    slot = mesh_slot.reshape(1, -1)
    row = lambda vector: vector.reshape(1, -1)

    requests = lax.all_to_all(jnp.tile(mesh_send, (devices, 1)), "bulk", 0, 0, tiled=True)
    operands = (
        grid_first,
        grid_in.T,
        grid_second,
        send_weight,
        row(grid_bias),
        row(edge_bias),
        slot,
        feat_weight,
        g2m_send,
        g2m_recv,
        g2m_feat,
        g2m_count.reshape(1, 1),
    )
    own, cross, chip = call(
        edge_kernel,
        (shape(owned, width, kind=F32), shape(owned, width), shape(owned, width)),
        [SMEM] + [HBM] * len(operands),
        scratch=[VMEM(value.shape, value.dtype) for value in operands]
        + [
            SMEM(g2m_send.shape, I32),
            VMEM((grid_rows * (width // LANES), LANES), F32),
            VMEM((CHUNK_BLOCKS * g2m_send.shape[1] * (width // LANES), LANES), F32),
            VMEM((CHUNK_BLOCKS * g2m_send.shape[1] * (width // LANES), LANES), F32),
            VMEM((CHUNK_BLOCKS * g2m_send.shape[1], width), BF16),
            VMEM((CHUNK_BLOCKS * g2m_send.shape[1], width), BF16),
            VMEM((3 * owned, LANES), I32),
            VMEM((3 * owned, width), F32),
            pltpu.SemaphoreType.DMA((len(operands) + GRID_STEPS,)),
        ],
        flops=10_000_000_000,
        moved=4_000_000,
        vmem=32,
    )(place, *[hold(value) for value in operands])
    requests, _ = lax.optimization_barrier((requests, own))
    crossing = [(d, d + 1) for d in range(1, devices - 1, 2)]
    within = [(d, d + 1) for d in range(0, devices, 2)]
    both = lambda pairs: pairs + [(b, a) for a, b in pairs]
    from_cross = lax.ppermute(cross, "bulk", both(crossing))
    from_chip = lax.ppermute(chip, "bulk", both(within))
    supply = call(
        functools.partial(supply_kernel, mesh_send.shape[0]),
        shape(places, owned),
        [SMEM] + [VMEM] * 2,
        flops=500_000_000,
        moved=500_000,
    )(place, slot, requests)
    encoded, rows = call(
        node_kernel,
        (shape(owned, width), shape(places, width)),
        [VMEM] * 11,
        flops=500_000_000,
        moved=4_000_000,
    )(
        own,
        from_cross,
        from_chip,
        mesh_latent,
        edge_out,
        node_input,
        row(node_bias),
        node_out,
        row(node_gain),
        mesh_sender,
        supply,
    )
    piece = lax.all_to_all(rows, "bulk", 0, 0, tiled=True)
    mesh_send, _ = lax.optimization_barrier((mesh_send, encoded))
    wanted = call(
        functools.partial(wanted_kernel, owned),
        shape(edges, places),
        [VMEM] * 2,
        flops=1_000_000_000,
        moved=500_000,
    )(slot, mesh_send)
    incoming, pick, parts, upper = call(
        receiver_kernel,
        (
            shape(owned, edges),
            shape(edges, 2 * owned),
            shape(2 * owned, width),
            shape(owned, width, kind=F32),
        ),
        [SMEM] + [VMEM] * 7,
        flops=1_000_000_000,
        moved=4_000_000,
    )(
        place,
        slot,
        mesh_recv,
        encoded,
        mesh_receiver,
        row(message_bias),
        update_input,
        row(update_bias),
    )
    return call(
        message_kernel,
        shape(owned, width),
        [VMEM] * 11,
        flops=1_000_000_000,
        moved=4_000_000,
    )(
        wanted,
        piece,
        incoming,
        pick,
        parts,
        upper,
        encoded,
        message_out,
        update_input,
        update_out,
        row(update_gain),
    )


def solution(mesh):
    split = {0: ("groups", "bulk"), 20: "bulk", 21: "bulk", 22: "bulk", 23: "bulk", 24: "bulk"}
    split.update({26: "bulk", 27: "bulk"})
    placed = tuple(P(split[at]) if at in split else P() for at in range(28))
    return jax.shard_map(
        per_device,
        mesh=mesh,
        in_specs=placed,
        out_specs=P(("groups", "bulk"), None),
        check_vma=False,
    )
```

```python
import functools
import math

import jax
import jax.numpy as jnp
from jax import lax
from jax.experimental import pallas as pl
from jax.experimental.pallas import tpu as pltpu
from jax.sharding import PartitionSpec as P

F32 = jnp.float32
BF16 = jnp.bfloat16
I32 = jnp.int32
SEND_CAP = 16
LANES = 128
VMEM = pltpu.VMEM
SMEM = pltpu.SMEM
HBM = pltpu.HBM
GRID_STEPS = 2
CHUNK_BLOCKS = 4
MEBI = 1024 * 1024


def mm(left, right):
    return jnp.dot(left, right, preferred_element_type=F32)


def mm_nt(left, right):
    return lax.dot_general(left, right, (((1,), (1,)), ((), ())), preferred_element_type=F32)


def silu_half(half):
    return half + half * jnp.tanh(half)


def silu(value):
    return silu_half(0.5 * value)


def layer_norm(value):
    center = value - jnp.mean(value, axis=-1, keepdims=True)
    spread = jnp.mean(center * center, axis=-1, keepdims=True)
    return center * lax.rsqrt(spread + 1e-05)


def iota(shape, dim):
    return lax.broadcasted_iota(I32, shape, dim)


def one_hot(columns, rows):
    hit = columns.astype(jnp.int16) == lax.broadcasted_iota(jnp.int16, (rows, columns.shape[1]), 0)
    return jnp.where(hit, jnp.ones((), BF16), jnp.zeros((), BF16))


def ids_of_rows(slot, first, count):
    nodes = slot.shape[1]
    rows = iota((count, nodes), 0) + first
    return jnp.max(jnp.where(slot == rows, iota((count, nodes), 1), -1), axis=1, keepdims=True)


def asking_kernel(mesh_send_hbm, asked_hbm, sems):
    rows = mesh_send_hbm.shape[0]
    copies = [
        pltpu.make_async_copy(mesh_send_hbm, asked_hbm.at[pl.ds(at * rows, rows), :], sems.at[at])
        for at in range(asked_hbm.shape[0] // rows)
    ]
    for copy in copies:
        copy.start()
    for copy in copies:
        copy.wait()


def edge_kernel(
    place_ref,
    first_hbm,
    grid_hbm,
    second_hbm,
    send_weight_hbm,
    grid_bias_hbm,
    edge_bias_hbm,
    slot_hbm,
    feat_weight_hbm,
    send_hbm,
    recv_hbm,
    feat_hbm,
    count_hbm,
    own_ref,
    cross_ref,
    chip_ref,
    first_ref,
    grid_ref,
    second_ref,
    send_weight_ref,
    grid_bias_ref,
    edge_bias_ref,
    slot_ref,
    feat_weight_ref,
    send_ref,
    recv_ref,
    feat_ref,
    count_ref,
    starts,
    table,
    even_rows,
    odd_rows,
    even_hidden,
    odd_hidden,
    ids_ref,
    total,
    sems,
):
    channels, grid_rows = grid_ref.shape
    width = second_ref.shape[1]
    pieces = width // LANES
    blocks, block_edges = send_ref.shape
    owned = own_ref.shape[0]
    feats = feat_ref.shape[1]
    step_rows = grid_rows // GRID_STEPS

    def grid_copy(step):
        part = pl.ds(pl.multiple_of(step * step_rows, step_rows), step_rows)
        return pltpu.make_async_copy(grid_hbm.at[:, part], grid_ref.at[:, part], sems.at[step])

    pairs = [
        (first_hbm, first_ref),
        (second_hbm, second_ref),
        (send_weight_hbm, send_weight_ref),
        (grid_bias_hbm, grid_bias_ref),
        (edge_bias_hbm, edge_bias_ref),
        (send_hbm, send_ref),
        (slot_hbm, slot_ref),
        (feat_weight_hbm, feat_weight_ref),
        (recv_hbm, recv_ref),
        (feat_hbm, feat_ref),
        (count_hbm, count_ref),
        (send_ref, starts),
    ]
    copies = [
        pltpu.make_async_copy(source, target, sems.at[GRID_STEPS + at])
        for at, (source, target) in enumerate(pairs)
    ]
    first_copy, second_copy, send_weight_copy, grid_bias_copy, edge_bias_copy, send_copy = copies[:6]
    slot_copy, starts_copy = copies[6], copies[-1]
    first_copy.start()
    grid_copy(0).start()
    for copy in copies[1:-1]:
        copy.start()
    for step in range(1, GRID_STEPS):
        grid_copy(step).start()
    send_copy.wait()
    senders = send_ref[...]
    send_ref[...] = (senders // 8) * (8 * pieces) + senders % 8
    starts_copy.start()
    slot_copy.wait()
    place = place_ref[0]
    ids_ref[...] = jnp.broadcast_to(
        ids_of_rows(slot_ref[...], (place - 1) * owned, 3 * owned), ids_ref.shape
    )
    total[...] = jnp.zeros_like(total)
    first_copy.wait()
    first_ref[...] = first_ref[...] * 0.5
    second_copy.wait()
    send_weight_copy.wait()
    send_weight_ref[...] = send_weight_ref[...] * 0.5
    grid_bias_copy.wait()
    edge_bias_copy.wait()
    grid_bias = 0.5 * grid_bias_ref[...]
    edge_bias = 0.5 * edge_bias_ref[...]
    values = []
    for step in range(GRID_STEPS):
        grid_copy(step).wait()
        value = grid_ref[:, step * step_rows : (step + 1) * step_rows].T
        values.append(mm(value, first_ref[...]))
    values = [silu_half(value + grid_bias).astype(BF16) for value in values]
    values = [mm(value, second_ref[...]) for value in values]
    values = [layer_norm(value).astype(BF16) for value in values]
    values = [mm(value, send_weight_ref[...]) for value in values]
    for step, value in enumerate(values):
        row = (value + edge_bias).astype(BF16).astype(F32)
        for group in range(step_rows // 8):
            for piece in range(pieces):
                at = ((step * step_rows // 8 + group) * pieces + piece) * 8
                table[at : at + 8, :] = row[
                    group * 8 : group * 8 + 8, piece * LANES : (piece + 1) * LANES
                ]
    for copy in copies[7:]:
        copy.wait()
    used = count_ref[...]
    feat_weight = 0.5 * feat_weight_ref[...].astype(F32)
    feat_weight = jnp.concatenate([feat_weight, jnp.zeros((8 - feats, width), F32)], axis=0)
    feat_weight = feat_weight.astype(BF16)
    group = CHUNK_BLOCKS
    chunks = blocks // group
    part_rows = 64

    def gather(chunk, edges, target):
        for edge in edges:
            start = starts[chunk * group + edge // block_edges, edge % block_edges]
            target[pl.ds(edge // 8 * (8 * pieces) + edge % 8, pieces, stride=8), :] = table[
                pl.ds(start, pieces, stride=8), :
            ]

    def rows_of(source, first, count):
        return jnp.concatenate(
            [
                jnp.concatenate(
                    [
                        source[pl.ds((at * pieces + piece) * 8, 8), :]
                        for at in range(first // 8, (first + count) // 8)
                    ],
                    axis=0,
                )
                for piece in range(pieces)
            ],
            axis=1,
        )

    def add_sums(chunk, hidden):
        here = [chunk * group + b for b in range(group)]
        receivers = [jnp.where(b < used, recv_ref[pl.ds(b, 1), :], -2) for b in here]
        spread = jnp.concatenate([(ids_ref[...] == row).astype(F32) for row in receivers], axis=1)
        total[...] += mm(spread.astype(BF16), hidden[...])

    def work(chunk, source, target, hidden, hidden_before):
        here = [chunk * group + b for b in range(group)]
        feat = jnp.concatenate([feat_ref[b] for b in here], axis=1)
        feat = jnp.concatenate([feat, jnp.zeros((8 - feats, feat.shape[1]), F32)], axis=0)
        extra = mm(feat.T.astype(BF16), feat_weight)
        add_sums(jnp.maximum(chunk - 1, 0), hidden_before)
        after = jnp.minimum(chunk + 1, chunks - 1)
        for first in range(0, group * block_edges, part_rows):
            gather(after, range(first, first + part_rows), target)
            half = rows_of(source, first, part_rows) + extra[first : first + part_rows]
            hidden[first : first + part_rows, :] = silu_half(half).astype(BF16)

    def edge_step(step, carry):
        work(2 * step, even_rows, odd_rows, even_hidden, odd_hidden)
        work(2 * step + 1, odd_rows, even_rows, odd_hidden, even_hidden)
        return carry

    odd_hidden[...] = jnp.zeros_like(odd_hidden)
    gather(0, range(group * block_edges), even_rows)
    lax.fori_loop(0, chunks // 2, edge_step, 0)
    add_sums(chunks - 1, odd_hidden)
    odd = place % 2 == 1
    below, above = total[:owned].astype(BF16), total[2 * owned :].astype(BF16)
    own_ref[...] = total[owned : 2 * owned]
    cross_ref[...] = jnp.where(odd, above, below)
    chip_ref[...] = jnp.where(odd, below, above)


def wanted_kernel(owned, slot_ref, send_ref, wanted_ref):
    nodes = slot_ref.shape[1]
    blocks, block_edges = send_ref.shape
    places = wanted_ref.shape[1]
    chunk = LANES
    per_chunk = chunk // owned * SEND_CAP
    row, column = iota((chunk, chunk), 0), iota((chunk, chunk), 1)
    before = ((row > column) & (row // owned == column // owned)).astype(F32).astype(BF16)
    local_owner = (iota((chunk, LANES), 0) // owned * SEND_CAP).astype(F32)

    def find(index, best):
        ids = ids_of_rows(slot_ref[...], index * chunk, chunk)
        hit = jnp.zeros((chunk, block_edges), F32)
        for b in range(blocks):
            hit = jnp.maximum(hit, (ids == send_ref[b : b + 1, :]).astype(F32))
        hit = jnp.broadcast_to(jnp.max(hit, axis=1, keepdims=True), (chunk, LANES))
        rank = mm(before, hit.astype(BF16)) + local_owner
        spot = jnp.where(hit > 0, rank.astype(I32) + index * per_chunk, -1)
        spot = jnp.concatenate([spot] * (places // LANES), axis=1)
        found = jnp.where(spot == iota((chunk, places), 1), ids, -1)
        return jnp.maximum(best, jnp.max(found, axis=0, keepdims=True))

    best = lax.fori_loop(0, nodes // chunk, find, jnp.full((1, places), -1, I32), unroll=2)
    best = best.astype(F32)
    for b in range(blocks):
        senders = jnp.broadcast_to(send_ref[b : b + 1, :].astype(F32), (block_edges, block_edges)).T
        senders = jnp.concatenate([senders] * (places // LANES), axis=1)
        wanted_ref[b * block_edges : (b + 1) * block_edges, :] = (
            (senders == best).astype(F32).astype(BF16)
        )


def supply_kernel(
    blocks,
    place_ref,
    slot_ref,
    request_ref,
    latent_ref,
    edge_out_ref,
    node_input_ref,
    node_bias_ref,
    supply_ref,
    upper_ref,
    lower_ref,
):
    width = latent_ref.shape[1]
    upper_ref[...] = mm(latent_ref[...], node_input_ref[:width]) + node_bias_ref[...]
    lower_ref[...] = mm(edge_out_ref[...], node_input_ref[width:]).astype(BF16)
    owned = supply_ref.shape[1]
    devices = supply_ref.shape[0] // SEND_CAP
    per_device = request_ref.shape[0] // devices
    ids = ids_of_rows(slot_ref[...], place_ref[0] * owned, owned)
    lane = iota((owned, LANES), 1)
    used = jnp.zeros((owned, LANES), F32)
    for d in range(devices):
        hit = jnp.zeros((owned, request_ref.shape[1]), F32)
        for b in range(blocks):
            at = d * per_device + b
            hit = jnp.maximum(hit, (ids == request_ref[at : at + 1, :]).astype(F32))
        used = jnp.where(lane == d, jnp.max(hit, axis=1, keepdims=True), used)
    before = (iota((owned, owned), 0) > iota((owned, owned), 1)).astype(F32).astype(BF16)
    rank = jnp.where(used > 0, mm(before, used.astype(BF16)), -1.0)
    rank = jnp.concatenate([rank, jnp.full((LANES - owned, LANES), -1.0, F32)], axis=0).T
    slots = iota((SEND_CAP, owned), 0).astype(F32)
    supply = jnp.concatenate(
        [(rank[d : d + 1, :owned] == slots).astype(F32) for d in range(devices)], axis=0
    )
    supply_ref[...] = supply.astype(BF16)


def node_kernel(
    own_ref,
    from_cross_ref,
    from_chip_ref,
    latent_ref,
    upper_ref,
    lower_ref,
    node_out_ref,
    node_gain_ref,
    mesh_sender_ref,
    supply_ref,
    encoded_ref,
    rows_ref,
):
    latent = latent_ref[...]
    node_sum = own_ref[...] + from_cross_ref[...].astype(F32) + from_chip_ref[...].astype(F32)
    hidden = silu(upper_ref[...] + mm(node_sum.astype(BF16), lower_ref[...])).astype(BF16)
    encoded = latent.astype(F32) + layer_norm(mm(hidden, node_out_ref[...])) * node_gain_ref[...]
    encoded = encoded.astype(BF16)
    encoded_ref[...] = encoded
    sender_code = mm(encoded, mesh_sender_ref[...]).astype(BF16)
    rows_ref[...] = mm(supply_ref[...], sender_code).astype(BF16)


def receiver_kernel(
    place_ref,
    slot_ref,
    recv_ref,
    encoded_ref,
    mesh_receiver_ref,
    message_bias_ref,
    message_out_ref,
    update_input_ref,
    update_bias_ref,
    incoming_ref,
    pick_ref,
    parts_ref,
    upper_ref,
    lower_ref,
):
    owned, width = encoded_ref.shape
    blocks = recv_ref.shape[0]
    ids = ids_of_rows(slot_ref[...], place_ref[0] * owned, owned)
    incoming = jnp.concatenate(
        [(ids == recv_ref[b : b + 1, :]).astype(F32) for b in range(blocks)], axis=1
    )
    pick = incoming.T.astype(BF16)
    pick_ref[...] = jnp.concatenate([pick, pick], axis=1)
    incoming_ref[...] = incoming.astype(BF16)
    encoded = encoded_ref[...]
    receiver = mm(encoded, mesh_receiver_ref[...]) + message_bias_ref[...]
    high = receiver.astype(BF16)
    parts_ref[:owned, :] = high
    parts_ref[owned:, :] = (receiver - high.astype(F32)).astype(BF16)
    upper_ref[...] = mm(encoded, update_input_ref[:width]) + update_bias_ref[...]
    lower_ref[...] = mm(message_out_ref[...], update_input_ref[width:]).astype(BF16)


def message_kernel(
    wanted_ref,
    piece_ref,
    incoming_ref,
    pick_ref,
    parts_ref,
    upper_ref,
    lower_ref,
    encoded_ref,
    update_out_ref,
    update_gain_ref,
    out_ref,
):
    chosen = jnp.concatenate([wanted_ref[...], pick_ref[...]], axis=1)
    codes = jnp.concatenate([piece_ref[...], parts_ref[...]], axis=0)
    message = silu(mm(chosen, codes)).astype(BF16)
    message_sum = mm(incoming_ref[...], message).astype(BF16)
    hidden = silu(upper_ref[...] + mm(message_sum, lower_ref[...])).astype(BF16)
    out = layer_norm(mm(hidden, update_out_ref[...])) * update_gain_ref[...]
    out_ref[...] = (encoded_ref[...].astype(F32) + out).astype(BF16)


def call(kernel, out_shape, spaces, scratch=(), flops=0, moved=0, vmem=8, out_space=VMEM):
    return pl.pallas_call(
        kernel,
        out_shape=out_shape,
        in_specs=[pl.BlockSpec(memory_space=space) for space in spaces],
        out_specs=jax.tree.map(lambda _: pl.BlockSpec(memory_space=out_space), out_shape),
        scratch_shapes=scratch,
        compiler_params=pltpu.CompilerParams(vmem_limit_bytes=vmem * MEBI),
        cost_estimate=pl.CostEstimate(flops=flops, bytes_accessed=moved, transcendentals=0),
    )


def hold(value):
    return value if value.size == 1 else pltpu.with_memory_space_constraint(value, HBM)


def shape(*sizes, kind=BF16):
    return jax.ShapeDtypeStruct(sizes, kind)


def per_device(
    grid_in,
    grid_first,
    grid_bias,
    grid_second,
    send_weight,
    edge_bias,
    feat_weight,
    edge_out,
    node_input,
    node_bias,
    node_out,
    node_gain,
    mesh_sender,
    mesh_receiver,
    message_bias,
    message_out,
    update_input,
    update_bias,
    update_out,
    update_gain,
    mesh_latent,
    g2m_send,
    g2m_recv,
    g2m_feat,
    g2m_count,
    mesh_slot,
    mesh_send,
    mesh_recv,
):
    devices = lax.axis_size("bulk")
    position = lax.axis_index("bulk")
    place = position.astype(I32).reshape(1)
    owned, width = mesh_latent.shape
    grid_rows = grid_in.shape[0]
    places = devices * SEND_CAP
    edges = mesh_send.size
    slot = mesh_slot.reshape(1, -1)
    row = lambda vector: vector.reshape(1, -1)

    asked = call(
        asking_kernel,
        shape(devices * mesh_send.shape[0], mesh_send.shape[1], kind=I32),
        [HBM],
        scratch=[pltpu.SemaphoreType.DMA((devices,))],
        moved=100_000,
        out_space=HBM,
    )(hold(mesh_send))
    asked, first_place = lax.optimization_barrier((asked, place))
    requests = lax.all_to_all(asked, "bulk", 0, 0, tiled=True)
    operands = (
        grid_first,
        grid_in.T,
        grid_second,
        send_weight,
        row(grid_bias),
        row(edge_bias),
        slot,
        feat_weight,
        g2m_send,
        g2m_recv,
        g2m_feat,
        g2m_count.reshape(1, 1),
    )
    own, cross, chip = call(
        edge_kernel,
        (shape(owned, width, kind=F32), shape(owned, width), shape(owned, width)),
        [SMEM] + [HBM] * len(operands),
        scratch=[VMEM(value.shape, value.dtype) for value in operands]
        + [
            SMEM(g2m_send.shape, I32),
            VMEM((grid_rows * (width // LANES), LANES), F32),
            VMEM((CHUNK_BLOCKS * g2m_send.shape[1] * (width // LANES), LANES), F32),
            VMEM((CHUNK_BLOCKS * g2m_send.shape[1] * (width // LANES), LANES), F32),
            VMEM((CHUNK_BLOCKS * g2m_send.shape[1], width), BF16),
            VMEM((CHUNK_BLOCKS * g2m_send.shape[1], width), BF16),
            VMEM((3 * owned, LANES), I32),
            VMEM((3 * owned, width), F32),
            pltpu.SemaphoreType.DMA((len(operands) + GRID_STEPS,)),
        ],
        flops=10_000_000_000,
        moved=4_000_000,
        vmem=32,
    )(first_place, *[hold(value) for value in operands])
    requests, _ = lax.optimization_barrier((requests, own))
    crossing = [(d, d + 1) for d in range(1, devices - 1, 2)]
    within = [(d, d + 1) for d in range(0, devices, 2)]
    both = lambda pairs: pairs + [(b, a) for a, b in pairs]
    from_cross = lax.ppermute(cross, "bulk", both(crossing))
    from_chip = lax.ppermute(chip, "bulk", both(within))
    supply, upper, lower = call(
        functools.partial(supply_kernel, mesh_send.shape[0]),
        (shape(places, owned), shape(owned, width, kind=F32), shape(width, width)),
        [SMEM] + [VMEM] * 6,
        flops=500_000_000,
        moved=500_000,
    )(place, slot, requests, mesh_latent, edge_out, node_input, row(node_bias))
    encoded, rows = call(
        node_kernel,
        (shape(owned, width), shape(places, width)),
        [VMEM] * 10,
        flops=500_000_000,
        moved=4_000_000,
    )(
        own,
        from_cross,
        from_chip,
        mesh_latent,
        upper,
        lower,
        node_out,
        row(node_gain),
        mesh_sender,
        supply,
    )
    piece = lax.all_to_all(rows, "bulk", 0, 0, tiled=True)
    mesh_send, _ = lax.optimization_barrier((mesh_send, encoded))
    wanted = call(
        functools.partial(wanted_kernel, owned),
        shape(edges, places),
        [VMEM] * 2,
        flops=1_000_000_000,
        moved=500_000,
    )(slot, mesh_send)
    incoming, pick, parts, upper, lower = call(
        receiver_kernel,
        (
            shape(owned, edges),
            shape(edges, 2 * owned),
            shape(2 * owned, width),
            shape(owned, width, kind=F32),
            shape(width, width),
        ),
        [SMEM] + [VMEM] * 8,
        flops=1_000_000_000,
        moved=4_000_000,
    )(
        place,
        slot,
        mesh_recv,
        encoded,
        mesh_receiver,
        row(message_bias),
        message_out,
        update_input,
        row(update_bias),
    )
    return call(
        message_kernel,
        shape(owned, width),
        [VMEM] * 10,
        flops=1_000_000_000,
        moved=4_000_000,
    )(
        wanted,
        piece,
        incoming,
        pick,
        parts,
        upper,
        lower,
        encoded,
        update_out,
        row(update_gain),
    )


def solution(mesh):
    split = {0: ("groups", "bulk"), 20: "bulk", 21: "bulk", 22: "bulk", 23: "bulk", 24: "bulk"}
    split.update({26: "bulk", 27: "bulk"})
    placed = tuple(P(split[at]) if at in split else P() for at in range(28))
    return jax.shard_map(
        per_device,
        mesh=mesh,
        in_specs=placed,
        out_specs=P(("groups", "bulk"), None),
        check_vma=False,
    )
```

```python
import functools
import math

import jax
import jax.numpy as jnp
from jax import lax
from jax.experimental import pallas as pl
from jax.experimental.pallas import tpu as pltpu
from jax.sharding import PartitionSpec as P

F32 = jnp.float32
BF16 = jnp.bfloat16
I32 = jnp.int32
SEND_CAP = 16
LANES = 128
VMEM = pltpu.VMEM
SMEM = pltpu.SMEM
HBM = pltpu.HBM
GRID_STEPS = 2
CHUNK_BLOCKS = 4
ROW_PITCH = 5
PIECE_PITCH = 2
MEBI = 1024 * 1024


def mm(left, right):
    return jnp.dot(left, right, preferred_element_type=F32)


def mm_nt(left, right):
    return lax.dot_general(left, right, (((1,), (1,)), ((), ())), preferred_element_type=F32)


def silu_half(half):
    return half + half * jnp.tanh(half)


def silu(value):
    return silu_half(0.5 * value)


def layer_norm(value):
    center = value - jnp.mean(value, axis=-1, keepdims=True)
    spread = jnp.mean(center * center, axis=-1, keepdims=True)
    return center * lax.rsqrt(spread + 1e-05)


def iota(shape, dim):
    return lax.broadcasted_iota(I32, shape, dim)


def one_hot(columns, rows):
    hit = columns.astype(jnp.int16) == lax.broadcasted_iota(jnp.int16, (rows, columns.shape[1]), 0)
    return jnp.where(hit, jnp.ones((), BF16), jnp.zeros((), BF16))


def ids_of_rows(slot, first, count):
    nodes = slot.shape[1]
    rows = iota((count, nodes), 0) + first
    return jnp.max(jnp.where(slot == rows, iota((count, nodes), 1), -1), axis=1, keepdims=True)


def edge_kernel(
    place_ref,
    first_hbm,
    grid_hbm,
    second_hbm,
    send_weight_hbm,
    grid_bias_hbm,
    edge_bias_hbm,
    slot_hbm,
    feat_weight_hbm,
    send_hbm,
    recv_hbm,
    feat_hbm,
    count_hbm,
    own_ref,
    cross_ref,
    chip_ref,
    first_ref,
    grid_ref,
    second_ref,
    send_weight_ref,
    grid_bias_ref,
    edge_bias_ref,
    slot_ref,
    feat_weight_ref,
    send_ref,
    recv_ref,
    feat_ref,
    count_ref,
    starts,
    table,
    even_rows,
    odd_rows,
    even_hidden,
    odd_hidden,
    ids_ref,
    total,
    sems,
):
    channels, grid_rows = grid_ref.shape
    width = second_ref.shape[1]
    pieces = width // LANES
    blocks, block_edges = send_ref.shape
    owned = own_ref.shape[0]
    feats = feat_ref.shape[1]
    step_rows = grid_rows // GRID_STEPS

    def grid_copy(step):
        part = pl.ds(pl.multiple_of(step * step_rows, step_rows), step_rows)
        return pltpu.make_async_copy(grid_hbm.at[:, part], grid_ref.at[:, part], sems.at[step])

    pairs = [
        (first_hbm, first_ref),
        (second_hbm, second_ref),
        (send_weight_hbm, send_weight_ref),
        (grid_bias_hbm, grid_bias_ref),
        (edge_bias_hbm, edge_bias_ref),
        (send_hbm, send_ref),
        (slot_hbm, slot_ref),
        (feat_weight_hbm, feat_weight_ref),
        (recv_hbm, recv_ref),
        (feat_hbm, feat_ref),
        (count_hbm, count_ref),
        (send_ref, starts),
    ]
    copies = [
        pltpu.make_async_copy(source, target, sems.at[GRID_STEPS + at])
        for at, (source, target) in enumerate(pairs)
    ]
    first_copy, second_copy, send_weight_copy, grid_bias_copy, edge_bias_copy, send_copy = copies[:6]
    slot_copy, starts_copy = copies[6], copies[-1]
    first_copy.start()
    grid_copy(0).start()
    for copy in copies[1:-1]:
        copy.start()
    for step in range(1, GRID_STEPS):
        grid_copy(step).start()
    send_copy.wait()
    senders = send_ref[...]
    send_ref[...] = senders * ROW_PITCH
    starts_copy.start()
    slot_copy.wait()
    place = place_ref[0]
    ids_ref[...] = jnp.broadcast_to(
        ids_of_rows(slot_ref[...], (place - 1) * owned, 3 * owned), ids_ref.shape
    )
    total[...] = jnp.zeros_like(total)
    first_copy.wait()
    first_ref[...] = first_ref[...] * 0.5
    second_copy.wait()
    send_weight_copy.wait()
    send_weight_ref[...] = send_weight_ref[...] * 0.5
    grid_bias_copy.wait()
    edge_bias_copy.wait()
    grid_bias = 0.5 * grid_bias_ref[...]
    edge_bias = 0.5 * edge_bias_ref[...]
    values = []
    for step in range(GRID_STEPS):
        grid_copy(step).wait()
        value = grid_ref[:, step * step_rows : (step + 1) * step_rows].T
        values.append(mm(value, first_ref[...]))
    values = [silu_half(value + grid_bias).astype(BF16) for value in values]
    values = [mm(value, second_ref[...]) for value in values]
    values = [layer_norm(value).astype(BF16) for value in values]
    values = [mm(value, send_weight_ref[...]) for value in values]
    for step, value in enumerate(values):
        row = (value + edge_bias).astype(BF16).astype(F32)
        for group in range(step_rows // 8):
            for piece in range(pieces):
                at = (step * step_rows + group * 8) * ROW_PITCH + piece * PIECE_PITCH
                table[pl.ds(at, 8, stride=ROW_PITCH), :] = row[
                    group * 8 : group * 8 + 8, piece * LANES : (piece + 1) * LANES
                ]
    for copy in copies[7:]:
        copy.wait()
    used = count_ref[...]
    feat_weight = 0.5 * feat_weight_ref[...].astype(F32)
    feat_weight = jnp.concatenate([feat_weight, jnp.zeros((8 - feats, width), F32)], axis=0)
    feat_weight = feat_weight.astype(BF16)
    group = CHUNK_BLOCKS
    chunks = blocks // group
    part_rows = 64

    def gather(chunk, edges, target):
        for edge in edges:
            start = starts[chunk * group + edge // block_edges, edge % block_edges]
            target[pl.ds(edge * ROW_PITCH, pieces, stride=PIECE_PITCH), :] = table[
                pl.ds(start, pieces, stride=PIECE_PITCH), :
            ]

    def rows_of(source, first, count):
        return jnp.concatenate(
            [
                jnp.concatenate(
                    [
                        source[pl.ds(at * 8 * ROW_PITCH + piece * PIECE_PITCH, 8, stride=ROW_PITCH), :]
                        for at in range(first // 8, (first + count) // 8)
                    ],
                    axis=0,
                )
                for piece in range(pieces)
            ],
            axis=1,
        )

    def add_sums(chunk, hidden):
        here = [chunk * group + b for b in range(group)]
        receivers = [jnp.where(b < used, recv_ref[pl.ds(b, 1), :], -2) for b in here]
        spread = jnp.concatenate([(ids_ref[...] == row).astype(F32) for row in receivers], axis=1)
        total[...] += mm(spread.astype(BF16), hidden[...])

    def work(chunk, source, target, hidden, hidden_before):
        here = [chunk * group + b for b in range(group)]
        feat = jnp.concatenate([feat_ref[b] for b in here], axis=1)
        feat = jnp.concatenate([feat, jnp.zeros((8 - feats, feat.shape[1]), F32)], axis=0)
        extra = mm(feat.T.astype(BF16), feat_weight)
        add_sums(jnp.maximum(chunk - 1, 0), hidden_before)
        after = jnp.minimum(chunk + 1, chunks - 1)
        for first in range(0, group * block_edges, part_rows):
            gather(after, range(first, first + part_rows), target)
            half = rows_of(source, first, part_rows) + extra[first : first + part_rows]
            hidden[first : first + part_rows, :] = silu_half(half).astype(BF16)

    def edge_step(step, carry):
        work(2 * step, even_rows, odd_rows, even_hidden, odd_hidden)
        work(2 * step + 1, odd_rows, even_rows, odd_hidden, even_hidden)
        return carry

    odd_hidden[...] = jnp.zeros_like(odd_hidden)
    gather(0, range(group * block_edges), even_rows)
    lax.fori_loop(0, chunks // 2, edge_step, 0)
    add_sums(chunks - 1, odd_hidden)
    odd = place % 2 == 1
    below, above = total[:owned].astype(BF16), total[2 * owned :].astype(BF16)
    own_ref[...] = total[owned : 2 * owned]
    cross_ref[...] = jnp.where(odd, above, below)
    chip_ref[...] = jnp.where(odd, below, above)


def wanted_kernel(owned, slot_ref, send_ref, wanted_ref):
    nodes = slot_ref.shape[1]
    blocks, block_edges = send_ref.shape
    places = wanted_ref.shape[1]
    chunk = LANES
    per_chunk = chunk // owned * SEND_CAP
    row, column = iota((chunk, chunk), 0), iota((chunk, chunk), 1)
    before = ((row > column) & (row // owned == column // owned)).astype(F32).astype(BF16)
    local_owner = (iota((chunk, LANES), 0) // owned * SEND_CAP).astype(F32)

    def find(index, best):
        ids = ids_of_rows(slot_ref[...], index * chunk, chunk)
        hit = jnp.zeros((chunk, block_edges), F32)
        for b in range(blocks):
            hit = jnp.maximum(hit, (ids == send_ref[b : b + 1, :]).astype(F32))
        hit = jnp.broadcast_to(jnp.max(hit, axis=1, keepdims=True), (chunk, LANES))
        rank = mm(before, hit.astype(BF16)) + local_owner
        spot = jnp.where(hit > 0, rank.astype(I32) + index * per_chunk, -1)
        spot = jnp.concatenate([spot] * (places // LANES), axis=1)
        found = jnp.where(spot == iota((chunk, places), 1), ids, -1)
        return jnp.maximum(best, jnp.max(found, axis=0, keepdims=True))

    best = lax.fori_loop(0, nodes // chunk, find, jnp.full((1, places), -1, I32), unroll=2)
    best = best.astype(F32)
    for b in range(blocks):
        senders = jnp.broadcast_to(send_ref[b : b + 1, :].astype(F32), (block_edges, block_edges)).T
        senders = jnp.concatenate([senders] * (places // LANES), axis=1)
        wanted_ref[b * block_edges : (b + 1) * block_edges, :] = (
            (senders == best).astype(F32).astype(BF16)
        )


def supply_kernel(
    blocks,
    place_ref,
    slot_ref,
    request_ref,
    latent_ref,
    edge_out_ref,
    node_input_ref,
    node_bias_ref,
    supply_ref,
    upper_ref,
    lower_ref,
):
    width = latent_ref.shape[1]
    upper_ref[...] = mm(latent_ref[...], node_input_ref[:width]) + node_bias_ref[...]
    lower_ref[...] = mm(edge_out_ref[...], node_input_ref[width:]).astype(BF16)
    owned = supply_ref.shape[1]
    devices = supply_ref.shape[0] // SEND_CAP
    per_device = request_ref.shape[0] // devices
    ids = ids_of_rows(slot_ref[...], place_ref[0] * owned, owned)
    lane = iota((owned, LANES), 1)
    used = jnp.zeros((owned, LANES), F32)
    for d in range(devices):
        hit = jnp.zeros((owned, request_ref.shape[1]), F32)
        for b in range(blocks):
            at = d * per_device + b
            hit = jnp.maximum(hit, (ids == request_ref[at : at + 1, :]).astype(F32))
        used = jnp.where(lane == d, jnp.max(hit, axis=1, keepdims=True), used)
    before = (iota((owned, owned), 0) > iota((owned, owned), 1)).astype(F32).astype(BF16)
    rank = jnp.where(used > 0, mm(before, used.astype(BF16)), -1.0)
    rank = jnp.concatenate([rank, jnp.full((LANES - owned, LANES), -1.0, F32)], axis=0).T
    slots = iota((SEND_CAP, owned), 0).astype(F32)
    supply = jnp.concatenate(
        [(rank[d : d + 1, :owned] == slots).astype(F32) for d in range(devices)], axis=0
    )
    supply_ref[...] = supply.astype(BF16)


def node_kernel(
    own_ref,
    from_cross_ref,
    from_chip_ref,
    latent_ref,
    upper_ref,
    lower_ref,
    node_out_ref,
    node_gain_ref,
    mesh_sender_ref,
    supply_ref,
    encoded_ref,
    rows_ref,
):
    latent = latent_ref[...]
    node_sum = own_ref[...] + from_cross_ref[...].astype(F32) + from_chip_ref[...].astype(F32)
    hidden = silu(upper_ref[...] + mm(node_sum.astype(BF16), lower_ref[...])).astype(BF16)
    encoded = latent.astype(F32) + layer_norm(mm(hidden, node_out_ref[...])) * node_gain_ref[...]
    encoded = encoded.astype(BF16)
    encoded_ref[...] = encoded
    sender_code = mm(encoded, mesh_sender_ref[...]).astype(BF16)
    rows_ref[...] = mm(supply_ref[...], sender_code).astype(BF16)


def receiver_kernel(
    place_ref,
    slot_ref,
    recv_ref,
    encoded_ref,
    mesh_receiver_ref,
    message_bias_ref,
    message_out_ref,
    update_input_ref,
    update_bias_ref,
    incoming_ref,
    pick_ref,
    parts_ref,
    upper_ref,
    lower_ref,
):
    owned, width = encoded_ref.shape
    blocks = recv_ref.shape[0]
    ids = ids_of_rows(slot_ref[...], place_ref[0] * owned, owned)
    incoming = jnp.concatenate(
        [(ids == recv_ref[b : b + 1, :]).astype(F32) for b in range(blocks)], axis=1
    )
    pick = incoming.T.astype(BF16)
    pick_ref[...] = jnp.concatenate([pick, pick], axis=1)
    incoming_ref[...] = incoming.astype(BF16)
    encoded = encoded_ref[...]
    receiver = mm(encoded, mesh_receiver_ref[...]) + message_bias_ref[...]
    high = receiver.astype(BF16)
    parts_ref[:owned, :] = high
    parts_ref[owned:, :] = (receiver - high.astype(F32)).astype(BF16)
    upper_ref[...] = mm(encoded, update_input_ref[:width]) + update_bias_ref[...]
    lower_ref[...] = mm(message_out_ref[...], update_input_ref[width:]).astype(BF16)


def message_kernel(
    wanted_ref,
    piece_ref,
    incoming_ref,
    pick_ref,
    parts_ref,
    upper_ref,
    lower_ref,
    encoded_ref,
    update_out_ref,
    update_gain_ref,
    out_ref,
):
    chosen = jnp.concatenate([wanted_ref[...], pick_ref[...]], axis=1)
    codes = jnp.concatenate([piece_ref[...], parts_ref[...]], axis=0)
    message = silu(mm(chosen, codes)).astype(BF16)
    message_sum = mm(incoming_ref[...], message).astype(BF16)
    hidden = silu(upper_ref[...] + mm(message_sum, lower_ref[...])).astype(BF16)
    out = layer_norm(mm(hidden, update_out_ref[...])) * update_gain_ref[...]
    out_ref[...] = (encoded_ref[...].astype(F32) + out).astype(BF16)


def call(kernel, out_shape, spaces, scratch=(), flops=0, moved=0, vmem=8):
    return pl.pallas_call(
        kernel,
        out_shape=out_shape,
        in_specs=[pl.BlockSpec(memory_space=space) for space in spaces],
        out_specs=jax.tree.map(lambda _: pl.BlockSpec(memory_space=VMEM), out_shape),
        scratch_shapes=scratch,
        compiler_params=pltpu.CompilerParams(vmem_limit_bytes=vmem * MEBI),
        cost_estimate=pl.CostEstimate(flops=flops, bytes_accessed=moved, transcendentals=0),
    )


def hold(value):
    return value if value.size == 1 else pltpu.with_memory_space_constraint(value, HBM)


def shape(*sizes, kind=BF16):
    return jax.ShapeDtypeStruct(sizes, kind)


def per_device(
    grid_in,
    grid_first,
    grid_bias,
    grid_second,
    send_weight,
    edge_bias,
    feat_weight,
    edge_out,
    node_input,
    node_bias,
    node_out,
    node_gain,
    mesh_sender,
    mesh_receiver,
    message_bias,
    message_out,
    update_input,
    update_bias,
    update_out,
    update_gain,
    mesh_latent,
    g2m_send,
    g2m_recv,
    g2m_feat,
    g2m_count,
    mesh_slot,
    mesh_send,
    mesh_recv,
):
    devices = lax.axis_size("bulk")
    position = lax.axis_index("bulk")
    place = position.astype(I32).reshape(1)
    owned, width = mesh_latent.shape
    grid_rows = grid_in.shape[0]
    places = devices * SEND_CAP
    edges = mesh_send.size
    slot = mesh_slot.reshape(1, -1)
    row = lambda vector: vector.reshape(1, -1)

    requests = lax.all_to_all(jnp.tile(mesh_send, (devices, 1)), "bulk", 0, 0, tiled=True)
    operands = (
        grid_first,
        grid_in.T,
        grid_second,
        send_weight,
        row(grid_bias),
        row(edge_bias),
        slot,
        feat_weight,
        g2m_send,
        g2m_recv,
        g2m_feat,
        g2m_count.reshape(1, 1),
    )
    own, cross, chip = call(
        edge_kernel,
        (shape(owned, width, kind=F32), shape(owned, width), shape(owned, width)),
        [SMEM] + [HBM] * len(operands),
        scratch=[VMEM(value.shape, value.dtype) for value in operands]
        + [
            SMEM(g2m_send.shape, I32),
            VMEM((grid_rows * ROW_PITCH + 8, LANES), F32),
            VMEM((CHUNK_BLOCKS * g2m_send.shape[1] * ROW_PITCH + 8, LANES), F32),
            VMEM((CHUNK_BLOCKS * g2m_send.shape[1] * ROW_PITCH + 8, LANES), F32),
            VMEM((CHUNK_BLOCKS * g2m_send.shape[1], width), BF16),
            VMEM((CHUNK_BLOCKS * g2m_send.shape[1], width), BF16),
            VMEM((3 * owned, LANES), I32),
            VMEM((3 * owned, width), F32),
            pltpu.SemaphoreType.DMA((len(operands) + GRID_STEPS,)),
        ],
        flops=10_000_000_000,
        moved=4_000_000,
        vmem=32,
    )(place, *[hold(value) for value in operands])
    requests, _ = lax.optimization_barrier((requests, own))
    crossing = [(d, d + 1) for d in range(1, devices - 1, 2)]
    within = [(d, d + 1) for d in range(0, devices, 2)]
    both = lambda pairs: pairs + [(b, a) for a, b in pairs]
    from_cross = lax.ppermute(cross, "bulk", both(crossing))
    from_chip = lax.ppermute(chip, "bulk", both(within))
    supply, upper, lower = call(
        functools.partial(supply_kernel, mesh_send.shape[0]),
        (shape(places, owned), shape(owned, width, kind=F32), shape(width, width)),
        [SMEM] + [VMEM] * 6,
        flops=500_000_000,
        moved=500_000,
    )(place, slot, requests, mesh_latent, edge_out, node_input, row(node_bias))
    encoded, rows = call(
        node_kernel,
        (shape(owned, width), shape(places, width)),
        [VMEM] * 10,
        flops=500_000_000,
        moved=4_000_000,
    )(
        own,
        from_cross,
        from_chip,
        mesh_latent,
        upper,
        lower,
        node_out,
        row(node_gain),
        mesh_sender,
        supply,
    )
    piece = lax.all_to_all(rows, "bulk", 0, 0, tiled=True)
    mesh_send, _ = lax.optimization_barrier((mesh_send, encoded))
    wanted = call(
        functools.partial(wanted_kernel, owned),
        shape(edges, places),
        [VMEM] * 2,
        flops=1_000_000_000,
        moved=500_000,
    )(slot, mesh_send)
    incoming, pick, parts, upper, lower = call(
        receiver_kernel,
        (
            shape(owned, edges),
            shape(edges, 2 * owned),
            shape(2 * owned, width),
            shape(owned, width, kind=F32),
            shape(width, width),
        ),
        [SMEM] + [VMEM] * 8,
        flops=1_000_000_000,
        moved=4_000_000,
    )(
        place,
        slot,
        mesh_recv,
        encoded,
        mesh_receiver,
        row(message_bias),
        message_out,
        update_input,
        row(update_bias),
    )
    return call(
        message_kernel,
        shape(owned, width),
        [VMEM] * 10,
        flops=1_000_000_000,
        moved=4_000_000,
    )(
        wanted,
        piece,
        incoming,
        pick,
        parts,
        upper,
        lower,
        encoded,
        update_out,
        row(update_gain),
    )


def solution(mesh):
    split = {0: ("groups", "bulk"), 20: "bulk", 21: "bulk", 22: "bulk", 23: "bulk", 24: "bulk"}
    split.update({26: "bulk", 27: "bulk"})
    placed = tuple(P(split[at]) if at in split else P() for at in range(28))
    return jax.shard_map(
        per_device,
        mesh=mesh,
        in_specs=placed,
        out_specs=P(("groups", "bulk"), None),
        check_vma=False,
    )
```

```python
import functools
import math

import jax
import jax.numpy as jnp
from jax import lax
from jax.experimental import pallas as pl
from jax.experimental.pallas import tpu as pltpu
from jax.sharding import PartitionSpec as P

F32 = jnp.float32
BF16 = jnp.bfloat16
I32 = jnp.int32
SEND_CAP = 16
LANES = 128
VMEM = pltpu.VMEM
SMEM = pltpu.SMEM
HBM = pltpu.HBM
GRID_STEPS = 2
CHUNK_BLOCKS = 4
PART_ROWS = 64
MEBI = 1024 * 1024


def mm(left, right):
    return jnp.dot(left, right, preferred_element_type=F32)


def mm_nt(left, right):
    return lax.dot_general(left, right, (((1,), (1,)), ((), ())), preferred_element_type=F32)


def silu_half(half):
    return half + half * jnp.tanh(half)


def silu(value):
    return silu_half(0.5 * value)


def layer_norm(value):
    center = value - jnp.mean(value, axis=-1, keepdims=True)
    spread = jnp.mean(center * center, axis=-1, keepdims=True)
    return center * lax.rsqrt(spread + 1e-05)


def iota(shape, dim):
    return lax.broadcasted_iota(I32, shape, dim)


def one_hot(columns, rows):
    hit = columns.astype(jnp.int16) == lax.broadcasted_iota(jnp.int16, (rows, columns.shape[1]), 0)
    return jnp.where(hit, jnp.ones((), BF16), jnp.zeros((), BF16))


def ids_of_rows(slot, first, count):
    nodes = slot.shape[1]
    rows = iota((count, nodes), 0) + first
    return jnp.max(jnp.where(slot == rows, iota((count, nodes), 1), -1), axis=1, keepdims=True)


def edge_kernel(
    place_ref,
    first_hbm,
    grid_hbm,
    second_hbm,
    send_weight_hbm,
    grid_bias_hbm,
    edge_bias_hbm,
    slot_hbm,
    feat_weight_hbm,
    send_hbm,
    recv_hbm,
    feat_hbm,
    count_hbm,
    own_ref,
    cross_ref,
    chip_ref,
    first_ref,
    grid_ref,
    second_ref,
    send_weight_ref,
    grid_bias_ref,
    edge_bias_ref,
    slot_ref,
    feat_weight_ref,
    send_ref,
    recv_ref,
    feat_ref,
    count_ref,
    starts,
    states,
    table,
    even_rows,
    odd_rows,
    even_hidden,
    odd_hidden,
    ids_ref,
    total,
    sems,
):
    channels, grid_rows = grid_ref.shape
    width = second_ref.shape[1]
    pieces = width // LANES
    blocks, block_edges = send_ref.shape
    owned = own_ref.shape[0]
    feats = feat_ref.shape[1]
    step_rows = grid_rows // GRID_STEPS

    def grid_copy(step):
        part = pl.ds(pl.multiple_of(step * step_rows, step_rows), step_rows)
        return pltpu.make_async_copy(grid_hbm.at[:, part], grid_ref.at[:, part], sems.at[step])

    pairs = [
        (first_hbm, first_ref),
        (second_hbm, second_ref),
        (send_weight_hbm, send_weight_ref),
        (grid_bias_hbm, grid_bias_ref),
        (edge_bias_hbm, edge_bias_ref),
        (send_hbm, send_ref),
        (slot_hbm, slot_ref),
        (feat_weight_hbm, feat_weight_ref),
        (recv_hbm, recv_ref),
        (feat_hbm, feat_ref),
        (count_hbm, count_ref),
        (send_ref, starts),
    ]
    copies = [
        pltpu.make_async_copy(source, target, sems.at[GRID_STEPS + at])
        for at, (source, target) in enumerate(pairs)
    ]
    first_copy, second_copy, send_weight_copy, grid_bias_copy, edge_bias_copy, send_copy = copies[:6]
    slot_copy, starts_copy = copies[6], copies[-1]
    first_copy.start()
    grid_copy(0).start()
    for copy in copies[1:-1]:
        copy.start()
    for step in range(1, GRID_STEPS):
        grid_copy(step).start()
    send_copy.wait()
    senders = send_ref[...]
    send_ref[...] = (senders // 8) * (8 * pieces) + senders % 8
    starts_copy.start()
    slot_copy.wait()
    place = place_ref[0]
    ids_ref[...] = jnp.broadcast_to(
        ids_of_rows(slot_ref[...], (place - 1) * owned, 3 * owned), ids_ref.shape
    )
    total[...] = jnp.zeros_like(total)
    first_copy.wait()
    first_ref[...] = first_ref[...] * 0.5
    second_copy.wait()
    send_weight_copy.wait()
    send_weight_ref[...] = send_weight_ref[...] * 0.5
    grid_bias_copy.wait()
    edge_bias_copy.wait()
    grid_bias = 0.5 * grid_bias_ref[...]
    edge_bias = 0.5 * edge_bias_ref[...]
    parts = [(step, first) for step in range(GRID_STEPS) for first in range(0, step_rows, PART_ROWS)]
    values = []
    for step in range(GRID_STEPS):
        grid_copy(step).wait()
        value = grid_ref[:, step * step_rows : (step + 1) * step_rows].T
        values.append(mm(value, first_ref[...]))
    for step, first in parts:
        half = values[step][first : first + PART_ROWS] + grid_bias
        states[step, first : first + PART_ROWS, :] = silu_half(half).astype(BF16)
    values = [mm(states[step], second_ref[...]) for step in range(GRID_STEPS)]
    for step, first in parts:
        code = layer_norm(values[step][first : first + PART_ROWS])
        states[step, first : first + PART_ROWS, :] = code.astype(BF16)
    values = [mm(states[step], send_weight_ref[...]) for step in range(GRID_STEPS)]
    for step, first in parts:
        rows = (values[step][first : first + PART_ROWS] + edge_bias).astype(BF16).astype(F32)
        base = (step * step_rows + first) * pieces + 8 * pieces
        for group in range(PART_ROWS // 8):
            for piece in range(pieces):
                at = base + (group * pieces + piece) * 8
                table[at : at + 8, :] = rows[
                    group * 8 : group * 8 + 8, piece * LANES : (piece + 1) * LANES
                ]
    for copy in copies[7:]:
        copy.wait()
    used = count_ref[...]
    feat_weight = 0.5 * feat_weight_ref[...].astype(F32)
    feat_weight = jnp.concatenate([feat_weight, jnp.zeros((8 - feats, width), F32)], axis=0)
    feat_weight = feat_weight.astype(BF16)
    group = CHUNK_BLOCKS
    chunks = blocks // group

    lower_half = iota((2 * pieces, LANES), 0) < pieces

    def gather(chunk, edges, target):
        for edge in edges[::2]:
            place = [starts[chunk * group + e // block_edges, e % block_edges] for e in (edge, edge + 1)]
            lower = table[pl.ds(place[0] + 8 * pieces, 2 * pieces, stride=8), :]
            upper = table[pl.ds(place[1], 2 * pieces, stride=8), :]
            target[edge * pieces : (edge + 2) * pieces, :] = jnp.where(lower_half, lower, upper)

    def rows_of(source, first, count):
        return jnp.concatenate(
            [
                jnp.concatenate(
                    [
                        source[pl.ds(at * pieces + piece, 8, stride=pieces), :]
                        for at in range(first, first + count, 8)
                    ],
                    axis=0,
                )
                for piece in range(pieces)
            ],
            axis=1,
        )

    def add_sums(chunk, hidden):
        here = [chunk * group + b for b in range(group)]
        receivers = [jnp.where(b < used, recv_ref[pl.ds(b, 1), :], -2) for b in here]
        spread = jnp.concatenate([(ids_ref[...] == row).astype(F32) for row in receivers], axis=1)
        total[...] += mm(spread.astype(BF16), hidden[...])

    def work(chunk, source, target, hidden, hidden_before):
        here = [chunk * group + b for b in range(group)]
        feat = jnp.concatenate([feat_ref[b] for b in here], axis=1)
        feat = jnp.concatenate([feat, jnp.zeros((8 - feats, feat.shape[1]), F32)], axis=0)
        feat = feat.T.astype(BF16)
        add_sums(jnp.maximum(chunk - 1, 0), hidden_before)
        after = jnp.minimum(chunk + 1, chunks - 1)
        for first in range(0, group * block_edges, PART_ROWS):
            part = slice(first, first + PART_ROWS)
            gather(after, range(first, first + PART_ROWS), target)
            half = rows_of(source, first, PART_ROWS) + mm(feat[part], feat_weight)
            hidden[part, :] = silu_half(half).astype(BF16)

    def edge_step(step, carry):
        work(2 * step, even_rows, odd_rows, even_hidden, odd_hidden)
        work(2 * step + 1, odd_rows, even_rows, odd_hidden, even_hidden)
        return carry

    odd_hidden[...] = jnp.zeros_like(odd_hidden)
    gather(0, range(group * block_edges), even_rows)
    lax.fori_loop(0, chunks // 2, edge_step, 0)
    add_sums(chunks - 1, odd_hidden)
    odd = place % 2 == 1
    below, above = total[:owned].astype(BF16), total[2 * owned :].astype(BF16)
    own_ref[...] = total[owned : 2 * owned]
    cross_ref[...] = jnp.where(odd, above, below)
    chip_ref[...] = jnp.where(odd, below, above)


def wanted_kernel(owned, slot_ref, send_ref, wanted_ref):
    nodes = slot_ref.shape[1]
    blocks, block_edges = send_ref.shape
    places = wanted_ref.shape[1]
    chunk = LANES
    per_chunk = chunk // owned * SEND_CAP
    row, column = iota((chunk, chunk), 0), iota((chunk, chunk), 1)
    before = ((row > column) & (row // owned == column // owned)).astype(F32).astype(BF16)
    local_owner = (iota((chunk, LANES), 0) // owned * SEND_CAP).astype(F32)

    def find(index, best):
        ids = ids_of_rows(slot_ref[...], index * chunk, chunk)
        hit = jnp.zeros((chunk, block_edges), F32)
        for b in range(blocks):
            hit = jnp.maximum(hit, (ids == send_ref[b : b + 1, :]).astype(F32))
        hit = jnp.broadcast_to(jnp.max(hit, axis=1, keepdims=True), (chunk, LANES))
        rank = mm(before, hit.astype(BF16)) + local_owner
        spot = jnp.where(hit > 0, rank.astype(I32) + index * per_chunk, -1)
        spot = jnp.concatenate([spot] * (places // LANES), axis=1)
        found = jnp.where(spot == iota((chunk, places), 1), ids, -1)
        return jnp.maximum(best, jnp.max(found, axis=0, keepdims=True))

    best = lax.fori_loop(0, nodes // chunk, find, jnp.full((1, places), -1, I32), unroll=2)
    best = best.astype(F32)
    for b in range(blocks):
        senders = jnp.broadcast_to(send_ref[b : b + 1, :].astype(F32), (block_edges, block_edges)).T
        senders = jnp.concatenate([senders] * (places // LANES), axis=1)
        wanted_ref[b * block_edges : (b + 1) * block_edges, :] = (
            (senders == best).astype(F32).astype(BF16)
        )


def supply_kernel(
    blocks,
    place_ref,
    slot_ref,
    request_ref,
    latent_ref,
    edge_out_ref,
    node_input_ref,
    node_bias_ref,
    supply_ref,
    upper_ref,
    lower_ref,
):
    width = latent_ref.shape[1]
    upper_ref[...] = mm(latent_ref[...], node_input_ref[:width]) + node_bias_ref[...]
    lower_ref[...] = mm(edge_out_ref[...], node_input_ref[width:]).astype(BF16)
    owned = supply_ref.shape[1]
    devices = supply_ref.shape[0] // SEND_CAP
    per_device = request_ref.shape[0] // devices
    ids = ids_of_rows(slot_ref[...], place_ref[0] * owned, owned)
    lane = iota((owned, LANES), 1)
    used = jnp.zeros((owned, LANES), F32)
    for d in range(devices):
        hit = jnp.zeros((owned, request_ref.shape[1]), F32)
        for b in range(blocks):
            at = d * per_device + b
            hit = jnp.maximum(hit, (ids == request_ref[at : at + 1, :]).astype(F32))
        used = jnp.where(lane == d, jnp.max(hit, axis=1, keepdims=True), used)
    before = (iota((owned, owned), 0) > iota((owned, owned), 1)).astype(F32).astype(BF16)
    rank = jnp.where(used > 0, mm(before, used.astype(BF16)), -1.0)
    rank = jnp.concatenate([rank, jnp.full((LANES - owned, LANES), -1.0, F32)], axis=0).T
    slots = iota((SEND_CAP, owned), 0).astype(F32)
    supply = jnp.concatenate(
        [(rank[d : d + 1, :owned] == slots).astype(F32) for d in range(devices)], axis=0
    )
    supply_ref[...] = supply.astype(BF16)


def node_kernel(
    own_ref,
    from_cross_ref,
    from_chip_ref,
    latent_ref,
    upper_ref,
    lower_ref,
    node_out_ref,
    node_gain_ref,
    mesh_sender_ref,
    supply_ref,
    encoded_ref,
    rows_ref,
):
    latent = latent_ref[...]
    node_sum = own_ref[...] + from_cross_ref[...].astype(F32) + from_chip_ref[...].astype(F32)
    hidden = silu(upper_ref[...] + mm(node_sum.astype(BF16), lower_ref[...])).astype(BF16)
    encoded = latent.astype(F32) + layer_norm(mm(hidden, node_out_ref[...])) * node_gain_ref[...]
    encoded = encoded.astype(BF16)
    encoded_ref[...] = encoded
    sender_code = mm(encoded, mesh_sender_ref[...]).astype(BF16)
    rows_ref[...] = mm(supply_ref[...], sender_code).astype(BF16)


def receiver_kernel(
    place_ref,
    slot_ref,
    recv_ref,
    encoded_ref,
    mesh_receiver_ref,
    message_bias_ref,
    message_out_ref,
    update_input_ref,
    update_bias_ref,
    incoming_ref,
    pick_ref,
    parts_ref,
    upper_ref,
    lower_ref,
):
    owned, width = encoded_ref.shape
    blocks = recv_ref.shape[0]
    ids = ids_of_rows(slot_ref[...], place_ref[0] * owned, owned)
    incoming = jnp.concatenate(
        [(ids == recv_ref[b : b + 1, :]).astype(F32) for b in range(blocks)], axis=1
    )
    pick = incoming.T.astype(BF16)
    pick_ref[...] = jnp.concatenate([pick, pick], axis=1)
    incoming_ref[...] = incoming.astype(BF16)
    encoded = encoded_ref[...]
    receiver = mm(encoded, mesh_receiver_ref[...]) + message_bias_ref[...]
    high = receiver.astype(BF16)
    parts_ref[:owned, :] = high
    parts_ref[owned:, :] = (receiver - high.astype(F32)).astype(BF16)
    upper_ref[...] = mm(encoded, update_input_ref[:width]) + update_bias_ref[...]
    lower_ref[...] = mm(message_out_ref[...], update_input_ref[width:]).astype(BF16)


def message_kernel(
    wanted_ref,
    piece_ref,
    incoming_ref,
    pick_ref,
    parts_ref,
    upper_ref,
    lower_ref,
    encoded_ref,
    update_out_ref,
    update_gain_ref,
    out_ref,
):
    chosen = jnp.concatenate([wanted_ref[...], pick_ref[...]], axis=1)
    codes = jnp.concatenate([piece_ref[...], parts_ref[...]], axis=0)
    message = silu(mm(chosen, codes)).astype(BF16)
    message_sum = mm(incoming_ref[...], message).astype(BF16)
    hidden = silu(upper_ref[...] + mm(message_sum, lower_ref[...])).astype(BF16)
    out = layer_norm(mm(hidden, update_out_ref[...])) * update_gain_ref[...]
    out_ref[...] = (encoded_ref[...].astype(F32) + out).astype(BF16)


def call(kernel, out_shape, spaces, scratch=(), flops=0, moved=0, vmem=8):
    return pl.pallas_call(
        kernel,
        out_shape=out_shape,
        in_specs=[pl.BlockSpec(memory_space=space) for space in spaces],
        out_specs=jax.tree.map(lambda _: pl.BlockSpec(memory_space=VMEM), out_shape),
        scratch_shapes=scratch,
        compiler_params=pltpu.CompilerParams(vmem_limit_bytes=vmem * MEBI),
        cost_estimate=pl.CostEstimate(flops=flops, bytes_accessed=moved, transcendentals=0),
    )


def hold(value):
    return value if value.size == 1 else pltpu.with_memory_space_constraint(value, HBM)


def shape(*sizes, kind=BF16):
    return jax.ShapeDtypeStruct(sizes, kind)


def per_device(
    grid_in,
    grid_first,
    grid_bias,
    grid_second,
    send_weight,
    edge_bias,
    feat_weight,
    edge_out,
    node_input,
    node_bias,
    node_out,
    node_gain,
    mesh_sender,
    mesh_receiver,
    message_bias,
    message_out,
    update_input,
    update_bias,
    update_out,
    update_gain,
    mesh_latent,
    g2m_send,
    g2m_recv,
    g2m_feat,
    g2m_count,
    mesh_slot,
    mesh_send,
    mesh_recv,
):
    devices = lax.axis_size("bulk")
    position = lax.axis_index("bulk")
    place = position.astype(I32).reshape(1)
    owned, width = mesh_latent.shape
    grid_rows = grid_in.shape[0]
    places = devices * SEND_CAP
    edges = mesh_send.size
    slot = mesh_slot.reshape(1, -1)
    row = lambda vector: vector.reshape(1, -1)

    requests = lax.all_to_all(jnp.tile(mesh_send, (devices, 1)), "bulk", 0, 0, tiled=True)
    operands = (
        grid_first,
        grid_in.T,
        grid_second,
        send_weight,
        row(grid_bias),
        row(edge_bias),
        slot,
        feat_weight,
        g2m_send,
        g2m_recv,
        g2m_feat,
        g2m_count.reshape(1, 1),
    )
    own, cross, chip = call(
        edge_kernel,
        (shape(owned, width, kind=F32), shape(owned, width), shape(owned, width)),
        [SMEM] + [HBM] * len(operands),
        scratch=[VMEM(value.shape, value.dtype) for value in operands]
        + [
            SMEM(g2m_send.shape, I32),
            VMEM((GRID_STEPS, grid_rows // GRID_STEPS, width), BF16),
            VMEM(((grid_rows + 16) * (width // LANES), LANES), F32),
            VMEM((CHUNK_BLOCKS * g2m_send.shape[1] * (width // LANES), LANES), F32),
            VMEM((CHUNK_BLOCKS * g2m_send.shape[1] * (width // LANES), LANES), F32),
            VMEM((CHUNK_BLOCKS * g2m_send.shape[1], width), BF16),
            VMEM((CHUNK_BLOCKS * g2m_send.shape[1], width), BF16),
            VMEM((3 * owned, LANES), I32),
            VMEM((3 * owned, width), F32),
            pltpu.SemaphoreType.DMA((len(operands) + GRID_STEPS,)),
        ],
        flops=10_000_000_000,
        moved=4_000_000,
        vmem=32,
    )(place, *[hold(value) for value in operands])
    requests, _ = lax.optimization_barrier((requests, own))
    crossing = [(d, d + 1) for d in range(1, devices - 1, 2)]
    within = [(d, d + 1) for d in range(0, devices, 2)]
    both = lambda pairs: pairs + [(b, a) for a, b in pairs]
    from_cross = lax.ppermute(cross, "bulk", both(crossing))
    from_chip = lax.ppermute(chip, "bulk", both(within))
    supply, upper, lower = call(
        functools.partial(supply_kernel, mesh_send.shape[0]),
        (shape(places, owned), shape(owned, width, kind=F32), shape(width, width)),
        [SMEM] + [VMEM] * 6,
        flops=500_000_000,
        moved=500_000,
    )(place, slot, requests, mesh_latent, edge_out, node_input, row(node_bias))
    encoded, rows = call(
        node_kernel,
        (shape(owned, width), shape(places, width)),
        [VMEM] * 10,
        flops=500_000_000,
        moved=4_000_000,
    )(
        own,
        from_cross,
        from_chip,
        mesh_latent,
        upper,
        lower,
        node_out,
        row(node_gain),
        mesh_sender,
        supply,
    )
    piece = lax.all_to_all(rows, "bulk", 0, 0, tiled=True)
    mesh_send, _ = lax.optimization_barrier((mesh_send, encoded))
    wanted = call(
        functools.partial(wanted_kernel, owned),
        shape(edges, places),
        [VMEM] * 2,
        flops=1_000_000_000,
        moved=500_000,
    )(slot, mesh_send)
    incoming, pick, parts, upper, lower = call(
        receiver_kernel,
        (
            shape(owned, edges),
            shape(edges, 2 * owned),
            shape(2 * owned, width),
            shape(owned, width, kind=F32),
            shape(width, width),
        ),
        [SMEM] + [VMEM] * 8,
        flops=1_000_000_000,
        moved=4_000_000,
    )(
        place,
        slot,
        mesh_recv,
        encoded,
        mesh_receiver,
        row(message_bias),
        message_out,
        update_input,
        row(update_bias),
    )
    return call(
        message_kernel,
        shape(owned, width),
        [VMEM] * 10,
        flops=1_000_000_000,
        moved=4_000_000,
    )(
        wanted,
        piece,
        incoming,
        pick,
        parts,
        upper,
        lower,
        encoded,
        update_out,
        row(update_gain),
    )


def solution(mesh):
    split = {0: ("groups", "bulk"), 20: "bulk", 21: "bulk", 22: "bulk", 23: "bulk", 24: "bulk"}
    split.update({26: "bulk", 27: "bulk"})
    placed = tuple(P(split[at]) if at in split else P() for at in range(28))
    return jax.shard_map(
        per_device,
        mesh=mesh,
        in_specs=placed,
        out_specs=P(("groups", "bulk"), None),
        check_vma=False,
    )
```

```python
import functools
import math

import jax
import jax.numpy as jnp
from jax import lax
from jax.experimental import pallas as pl
from jax.experimental.pallas import tpu as pltpu
from jax.sharding import PartitionSpec as P

F32 = jnp.float32
BF16 = jnp.bfloat16
I32 = jnp.int32
SEND_CAP = 16
LANES = 128
VMEM = pltpu.VMEM
SMEM = pltpu.SMEM
HBM = pltpu.HBM
GRID_STEPS = 2
CHUNK_BLOCKS = 4
PART_ROWS = 64
MEBI = 1024 * 1024


def mm(left, right):
    return jnp.dot(left, right, preferred_element_type=F32)


def mm_nt(left, right):
    return lax.dot_general(left, right, (((1,), (1,)), ((), ())), preferred_element_type=F32)


def silu_half(half):
    return half + half * jnp.tanh(half)


def silu(value):
    return silu_half(0.5 * value)


def layer_norm(value):
    center = value - jnp.mean(value, axis=-1, keepdims=True)
    spread = jnp.mean(center * center, axis=-1, keepdims=True)
    return center * lax.rsqrt(spread + 1e-05)


def iota(shape, dim):
    return lax.broadcasted_iota(I32, shape, dim)


def one_hot(columns, rows):
    hit = columns.astype(jnp.int16) == lax.broadcasted_iota(jnp.int16, (rows, columns.shape[1]), 0)
    return jnp.where(hit, jnp.ones((), BF16), jnp.zeros((), BF16))


def ids_of_rows(slot, first, count):
    nodes = slot.shape[1]
    rows = iota((count, nodes), 0) + first
    return jnp.max(jnp.where(slot == rows, iota((count, nodes), 1), -1), axis=1, keepdims=True)


def edge_kernel(
    place_ref,
    first_hbm,
    grid_hbm,
    second_hbm,
    send_weight_hbm,
    grid_bias_hbm,
    edge_bias_hbm,
    slot_hbm,
    feat_weight_hbm,
    send_hbm,
    recv_hbm,
    feat_hbm,
    count_hbm,
    own_ref,
    cross_ref,
    chip_ref,
    first_ref,
    grid_ref,
    second_ref,
    send_weight_ref,
    grid_bias_ref,
    edge_bias_ref,
    slot_ref,
    feat_weight_ref,
    send_ref,
    recv_ref,
    feat_ref,
    count_ref,
    starts,
    states,
    table,
    even_rows,
    odd_rows,
    even_hidden,
    odd_hidden,
    ids_ref,
    total,
    sems,
):
    channels, grid_rows = grid_ref.shape
    width = second_ref.shape[1]
    pieces = width // LANES
    blocks, block_edges = send_ref.shape
    owned = own_ref.shape[0]
    feats = feat_ref.shape[1]
    step_rows = grid_rows // GRID_STEPS

    def grid_copy(step):
        part = pl.ds(pl.multiple_of(step * step_rows, step_rows), step_rows)
        return pltpu.make_async_copy(grid_hbm.at[:, part], grid_ref.at[:, part], sems.at[step])

    pairs = [
        (first_hbm, first_ref),
        (second_hbm, second_ref),
        (send_weight_hbm, send_weight_ref),
        (grid_bias_hbm, grid_bias_ref),
        (edge_bias_hbm, edge_bias_ref),
        (send_hbm, send_ref),
        (slot_hbm, slot_ref),
        (feat_weight_hbm, feat_weight_ref),
        (recv_hbm, recv_ref),
        (feat_hbm, feat_ref),
        (count_hbm, count_ref),
        (send_ref, starts),
    ]
    copies = [
        pltpu.make_async_copy(source, target, sems.at[GRID_STEPS + at])
        for at, (source, target) in enumerate(pairs)
    ]
    first_copy, second_copy, send_weight_copy, grid_bias_copy, edge_bias_copy, send_copy = copies[:6]
    slot_copy, starts_copy = copies[6], copies[-1]
    first_copy.start()
    grid_copy(0).start()
    for copy in copies[1:-1]:
        copy.start()
    for step in range(1, GRID_STEPS):
        grid_copy(step).start()
    send_copy.wait()
    senders = send_ref[...]
    send_ref[...] = (senders // 8) * (8 * pieces) + senders % 8
    starts_copy.start()
    slot_copy.wait()
    place = place_ref[0]
    ids_ref[...] = jnp.broadcast_to(
        ids_of_rows(slot_ref[...], (place - 1) * owned, 3 * owned), ids_ref.shape
    )
    total[...] = jnp.zeros_like(total)
    first_copy.wait()
    first_ref[...] = first_ref[...] * 0.5
    second_copy.wait()
    send_weight_copy.wait()
    send_weight_ref[...] = send_weight_ref[...] * 0.5
    grid_bias_copy.wait()
    edge_bias_copy.wait()
    grid_bias = 0.5 * grid_bias_ref[...]
    edge_bias = 0.5 * edge_bias_ref[...]
    parts = [(step, first) for step in range(GRID_STEPS) for first in range(0, step_rows, PART_ROWS)]
    values = []
    for step in range(GRID_STEPS):
        grid_copy(step).wait()
        value = grid_ref[:, step * step_rows : (step + 1) * step_rows].T
        values.append(mm(value, first_ref[...]))
    for step, first in parts:
        half = values[step][first : first + PART_ROWS] + grid_bias
        states[step, first : first + PART_ROWS, :] = silu_half(half).astype(BF16)
    values = [mm(states[step], second_ref[...]) for step in range(GRID_STEPS)]
    for step, first in parts:
        code = layer_norm(values[step][first : first + PART_ROWS])
        states[step, first : first + PART_ROWS, :] = code.astype(BF16)
    values = [mm(states[step], send_weight_ref[...]) for step in range(GRID_STEPS)]
    for step, first in parts:
        rows = (values[step][first : first + PART_ROWS] + edge_bias).astype(BF16).astype(F32)
        base = (step * step_rows + first) * pieces
        for group in range(PART_ROWS // 8):
            for piece in range(pieces):
                at = base + (group * pieces + piece) * 8
                table[at : at + 8, :] = rows[
                    group * 8 : group * 8 + 8, piece * LANES : (piece + 1) * LANES
                ]
    for copy in copies[7:]:
        copy.wait()
    used = count_ref[...]
    feat_weight = 0.5 * feat_weight_ref[...].astype(F32)
    feat_weight = jnp.concatenate([feat_weight, jnp.zeros((8 - feats, width), F32)], axis=0)
    feat_weight = feat_weight.astype(BF16)
    group = CHUNK_BLOCKS
    chunks = blocks // group

    def gather(chunk, edges, target):
        for edge in edges:
            start = starts[chunk * group + edge // block_edges, edge % block_edges]
            target[pl.ds(edge // 8 * (8 * pieces) + edge % 8, pieces, stride=8), :] = table[
                pl.ds(start, pieces, stride=8), :
            ]

    def rows_of(source, first, count):
        return jnp.concatenate(
            [
                jnp.concatenate(
                    [
                        source[pl.ds((at * pieces + piece) * 8, 8), :]
                        for at in range(first // 8, (first + count) // 8)
                    ],
                    axis=0,
                )
                for piece in range(pieces)
            ],
            axis=1,
        )

    def add_sums(chunk, hidden):
        here = [chunk * group + b for b in range(group)]
        receivers = [jnp.where(b < used, recv_ref[pl.ds(b, 1), :], -2) for b in here]
        spread = jnp.concatenate([(ids_ref[...] == row).astype(F32) for row in receivers], axis=1)
        total[...] += mm(spread.astype(BF16), hidden[...])

    def work(chunk, source, target, hidden, hidden_before):
        here = [chunk * group + b for b in range(group)]
        feat = jnp.concatenate([feat_ref[b] for b in here], axis=1)
        feat = jnp.concatenate([feat, jnp.zeros((8 - feats, feat.shape[1]), F32)], axis=0)
        extra = mm(feat.T.astype(BF16), feat_weight)
        add_sums(jnp.maximum(chunk - 1, 0), hidden_before)
        after = jnp.minimum(chunk + 1, chunks - 1)
        for first in range(0, group * block_edges, PART_ROWS):
            gather(after, range(first, first + PART_ROWS), target)
            half = rows_of(source, first, PART_ROWS) + extra[first : first + PART_ROWS]
            hidden[first : first + PART_ROWS, :] = silu_half(half).astype(BF16)

    def edge_step(step, carry):
        work(2 * step, even_rows, odd_rows, even_hidden, odd_hidden)
        work(2 * step + 1, odd_rows, even_rows, odd_hidden, even_hidden)
        return carry

    odd_hidden[...] = jnp.zeros_like(odd_hidden)
    gather(0, range(group * block_edges), even_rows)
    lax.fori_loop(0, chunks // 2, edge_step, 0)
    add_sums(chunks - 1, odd_hidden)
    odd = place % 2 == 1
    below, above = total[:owned].astype(BF16), total[2 * owned :].astype(BF16)
    own_ref[...] = total[owned : 2 * owned]
    cross_ref[...] = jnp.where(odd, above, below)
    chip_ref[...] = jnp.where(odd, below, above)


def wanted_kernel(owned, slot_ref, send_ref, wanted_ref):
    nodes = slot_ref.shape[1]
    blocks, block_edges = send_ref.shape
    places = wanted_ref.shape[1]
    chunk = LANES
    per_chunk = chunk // owned * SEND_CAP
    row, column = iota((chunk, chunk), 0), iota((chunk, chunk), 1)
    before = ((row > column) & (row // owned == column // owned)).astype(F32).astype(BF16)
    local_owner = (iota((chunk, LANES), 0) // owned * SEND_CAP).astype(F32)

    def find(index, best):
        ids = ids_of_rows(slot_ref[...], index * chunk, chunk)
        hit = jnp.zeros((chunk, block_edges), F32)
        for b in range(blocks):
            hit = jnp.maximum(hit, (ids == send_ref[b : b + 1, :]).astype(F32))
        hit = jnp.broadcast_to(jnp.max(hit, axis=1, keepdims=True), (chunk, LANES))
        rank = mm(before, hit.astype(BF16)) + local_owner
        spot = jnp.where(hit > 0, rank.astype(I32) + index * per_chunk, -1)
        spot = jnp.concatenate([spot] * (places // LANES), axis=1)
        found = jnp.where(spot == iota((chunk, places), 1), ids, -1)
        return jnp.maximum(best, jnp.max(found, axis=0, keepdims=True))

    best = lax.fori_loop(0, nodes // chunk, find, jnp.full((1, places), -1, I32), unroll=2)
    best = best.astype(F32)
    for b in range(blocks):
        senders = jnp.broadcast_to(send_ref[b : b + 1, :].astype(F32), (block_edges, block_edges)).T
        senders = jnp.concatenate([senders] * (places // LANES), axis=1)
        wanted_ref[b * block_edges : (b + 1) * block_edges, :] = (
            (senders == best).astype(F32).astype(BF16)
        )


def supply_kernel(
    blocks,
    place_ref,
    slot_ref,
    request_ref,
    latent_ref,
    edge_out_ref,
    node_input_ref,
    node_bias_ref,
    supply_ref,
    upper_ref,
    lower_ref,
):
    width = latent_ref.shape[1]
    upper_ref[...] = mm(latent_ref[...], node_input_ref[:width]) + node_bias_ref[...]
    lower_ref[...] = mm(edge_out_ref[...], node_input_ref[width:]).astype(BF16)
    owned = supply_ref.shape[1]
    devices = supply_ref.shape[0] // SEND_CAP
    per_device = request_ref.shape[0] // devices
    ids = ids_of_rows(slot_ref[...], place_ref[0] * owned, owned)
    lane = iota((owned, LANES), 1)
    used = jnp.zeros((owned, LANES), F32)
    for d in range(devices):
        hit = jnp.zeros((owned, request_ref.shape[1]), F32)
        for b in range(blocks):
            at = d * per_device + b
            hit = jnp.maximum(hit, (ids == request_ref[at : at + 1, :]).astype(F32))
        used = jnp.where(lane == d, jnp.max(hit, axis=1, keepdims=True), used)
    before = (iota((owned, owned), 0) > iota((owned, owned), 1)).astype(F32).astype(BF16)
    rank = jnp.where(used > 0, mm(before, used.astype(BF16)), -1.0)
    rank = jnp.concatenate([rank, jnp.full((LANES - owned, LANES), -1.0, F32)], axis=0).T
    slots = iota((SEND_CAP, owned), 0).astype(F32)
    supply = jnp.concatenate(
        [(rank[d : d + 1, :owned] == slots).astype(F32) for d in range(devices)], axis=0
    )
    supply_ref[...] = supply.astype(BF16)


def node_kernel(
    own_ref,
    from_cross_ref,
    from_chip_ref,
    latent_ref,
    upper_ref,
    lower_ref,
    node_out_ref,
    node_gain_ref,
    mesh_sender_ref,
    supply_ref,
    encoded_ref,
    rows_ref,
):
    latent = latent_ref[...]
    node_sum = own_ref[...] + from_cross_ref[...].astype(F32) + from_chip_ref[...].astype(F32)
    hidden = silu(upper_ref[...] + mm(node_sum.astype(BF16), lower_ref[...])).astype(BF16)
    encoded = latent.astype(F32) + layer_norm(mm(hidden, node_out_ref[...])) * node_gain_ref[...]
    encoded = encoded.astype(BF16)
    encoded_ref[...] = encoded
    sender_code = mm(encoded, mesh_sender_ref[...]).astype(BF16)
    rows_ref[...] = mm(supply_ref[...], sender_code).astype(BF16)


def receiver_kernel(
    place_ref,
    slot_ref,
    recv_ref,
    encoded_ref,
    mesh_receiver_ref,
    message_bias_ref,
    message_out_ref,
    update_input_ref,
    update_bias_ref,
    incoming_ref,
    pick_ref,
    parts_ref,
    upper_ref,
    lower_ref,
):
    owned, width = encoded_ref.shape
    blocks = recv_ref.shape[0]
    ids = ids_of_rows(slot_ref[...], place_ref[0] * owned, owned)
    incoming = jnp.concatenate(
        [(ids == recv_ref[b : b + 1, :]).astype(F32) for b in range(blocks)], axis=1
    )
    pick = incoming.T.astype(BF16)
    pick_ref[...] = jnp.concatenate([pick, pick], axis=1)
    incoming_ref[...] = incoming.astype(BF16)
    encoded = encoded_ref[...]
    receiver = mm(encoded, mesh_receiver_ref[...]) + message_bias_ref[...]
    high = receiver.astype(BF16)
    parts_ref[:owned, :] = high
    parts_ref[owned:, :] = (receiver - high.astype(F32)).astype(BF16)
    upper_ref[...] = mm(encoded, update_input_ref[:width]) + update_bias_ref[...]
    lower_ref[...] = mm(message_out_ref[...], update_input_ref[width:]).astype(BF16)


def message_kernel(
    wanted_ref,
    piece_ref,
    incoming_ref,
    pick_ref,
    parts_ref,
    upper_ref,
    lower_ref,
    encoded_ref,
    update_out_ref,
    update_gain_ref,
    out_ref,
):
    chosen = jnp.concatenate([wanted_ref[...], pick_ref[...]], axis=1)
    codes = jnp.concatenate([piece_ref[...], parts_ref[...]], axis=0)
    message = silu(mm(chosen, codes)).astype(BF16)
    message_sum = mm(incoming_ref[...], message).astype(BF16)
    hidden = silu(upper_ref[...] + mm(message_sum, lower_ref[...])).astype(BF16)
    out = layer_norm(mm(hidden, update_out_ref[...])) * update_gain_ref[...]
    out_ref[...] = (encoded_ref[...].astype(F32) + out).astype(BF16)


def call(kernel, out_shape, spaces, scratch=(), flops=0, moved=0, vmem=8):
    return pl.pallas_call(
        kernel,
        out_shape=out_shape,
        in_specs=[pl.BlockSpec(memory_space=space) for space in spaces],
        out_specs=jax.tree.map(lambda _: pl.BlockSpec(memory_space=VMEM), out_shape),
        scratch_shapes=scratch,
        compiler_params=pltpu.CompilerParams(vmem_limit_bytes=vmem * MEBI),
        cost_estimate=pl.CostEstimate(flops=flops, bytes_accessed=moved, transcendentals=0),
    )


def hold(value):
    return value if value.size == 1 else pltpu.with_memory_space_constraint(value, HBM)


def shape(*sizes, kind=BF16):
    return jax.ShapeDtypeStruct(sizes, kind)


def per_device(
    grid_in,
    grid_first,
    grid_bias,
    grid_second,
    send_weight,
    edge_bias,
    feat_weight,
    edge_out,
    node_input,
    node_bias,
    node_out,
    node_gain,
    mesh_sender,
    mesh_receiver,
    message_bias,
    message_out,
    update_input,
    update_bias,
    update_out,
    update_gain,
    mesh_latent,
    g2m_send,
    g2m_recv,
    g2m_feat,
    g2m_count,
    mesh_slot,
    mesh_send,
    mesh_recv,
):
    devices = lax.axis_size("bulk")
    position = lax.axis_index("bulk")
    place = position.astype(I32).reshape(1)
    owned, width = mesh_latent.shape
    grid_rows = grid_in.shape[0]
    places = devices * SEND_CAP
    edges = mesh_send.size
    slot = mesh_slot.reshape(1, -1)
    row = lambda vector: vector.reshape(1, -1)

    requests = lax.all_to_all(jnp.tile(mesh_send, (devices, 1)), "bulk", 0, 0, tiled=True)
    operands = (
        grid_first,
        grid_in.T,
        grid_second,
        send_weight,
        row(grid_bias),
        row(edge_bias),
        slot,
        feat_weight,
        g2m_send,
        g2m_recv,
        g2m_feat,
        g2m_count.reshape(1, 1),
    )
    own, cross, chip = call(
        edge_kernel,
        (shape(owned, width, kind=F32), shape(owned, width), shape(owned, width)),
        [SMEM] + [HBM] * len(operands),
        scratch=[VMEM(value.shape, value.dtype) for value in operands]
        + [
            SMEM(g2m_send.shape, I32),
            VMEM((GRID_STEPS, grid_rows // GRID_STEPS, width), BF16),
            VMEM((grid_rows * (width // LANES), LANES), F32),
            VMEM((CHUNK_BLOCKS * g2m_send.shape[1] * (width // LANES), LANES), F32),
            VMEM((CHUNK_BLOCKS * g2m_send.shape[1] * (width // LANES), LANES), F32),
            VMEM((CHUNK_BLOCKS * g2m_send.shape[1], width), BF16),
            VMEM((CHUNK_BLOCKS * g2m_send.shape[1], width), BF16),
            VMEM((3 * owned, LANES), I32),
            VMEM((3 * owned, width), F32),
            pltpu.SemaphoreType.DMA((len(operands) + GRID_STEPS,)),
        ],
        flops=10_000_000_000,
        moved=4_000_000,
        vmem=32,
    )(place, *[hold(value) for value in operands])
    requests, _ = lax.optimization_barrier((requests, own))
    crossing = [(d, d + 1) for d in range(1, devices - 1, 2)]
    within = [(d, d + 1) for d in range(0, devices, 2)]
    both = lambda pairs: pairs + [(b, a) for a, b in pairs]
    from_cross = lax.ppermute(cross, "bulk", both(crossing))
    from_chip = lax.ppermute(chip, "bulk", both(within))
    supply, upper, lower = call(
        functools.partial(supply_kernel, mesh_send.shape[0]),
        (shape(places, owned), shape(owned, width, kind=F32), shape(width, width)),
        [SMEM] + [VMEM] * 6,
        flops=500_000_000,
        moved=500_000,
    )(place, slot, requests, mesh_latent, edge_out, node_input, row(node_bias))
    encoded, rows = call(
        node_kernel,
        (shape(owned, width), shape(places, width)),
        [VMEM] * 10,
        flops=500_000_000,
        moved=4_000_000,
    )(
        own,
        from_cross,
        from_chip,
        mesh_latent,
        upper,
        lower,
        node_out,
        row(node_gain),
        mesh_sender,
        supply,
    )
    piece = lax.all_to_all(rows, "bulk", 0, 0, tiled=True)
    mesh_send, _ = lax.optimization_barrier((mesh_send, encoded))
    wanted = call(
        functools.partial(wanted_kernel, owned),
        shape(edges, places),
        [VMEM] * 2,
        flops=1_000_000_000,
        moved=500_000,
    )(slot, mesh_send)
    incoming, pick, parts, upper, lower = call(
        receiver_kernel,
        (
            shape(owned, edges),
            shape(edges, 2 * owned),
            shape(2 * owned, width),
            shape(owned, width, kind=F32),
            shape(width, width),
        ),
        [SMEM] + [VMEM] * 8,
        flops=1_000_000_000,
        moved=4_000_000,
    )(
        place,
        slot,
        mesh_recv,
        encoded,
        mesh_receiver,
        row(message_bias),
        message_out,
        update_input,
        row(update_bias),
    )
    return call(
        message_kernel,
        shape(owned, width),
        [VMEM] * 10,
        flops=1_000_000_000,
        moved=4_000_000,
    )(
        wanted,
        piece,
        incoming,
        pick,
        parts,
        upper,
        lower,
        encoded,
        update_out,
        row(update_gain),
    )


def solution(mesh):
    split = {0: ("groups", "bulk"), 20: "bulk", 21: "bulk", 22: "bulk", 23: "bulk", 24: "bulk"}
    split.update({26: "bulk", 27: "bulk"})
    placed = tuple(P(split[at]) if at in split else P() for at in range(28))
    return jax.shard_map(
        per_device,
        mesh=mesh,
        in_specs=placed,
        out_specs=P(("groups", "bulk"), None),
        check_vma=False,
    )
```

```python
import functools
import math

import jax
import jax.numpy as jnp
from jax import lax
from jax.experimental import pallas as pl
from jax.experimental.pallas import tpu as pltpu
from jax.sharding import PartitionSpec as P

F32 = jnp.float32
BF16 = jnp.bfloat16
I32 = jnp.int32
SEND_CAP = 16
LANES = 128
VMEM = pltpu.VMEM
SMEM = pltpu.SMEM
HBM = pltpu.HBM
GRID_STEPS = 4
CHUNK_BLOCKS = 4
MEBI = 1024 * 1024


def mm(left, right):
    return jnp.dot(left, right, preferred_element_type=F32)


def mm_nt(left, right):
    return lax.dot_general(left, right, (((1,), (1,)), ((), ())), preferred_element_type=F32)


def silu_half(half):
    return half + half * jnp.tanh(half)


def silu(value):
    return silu_half(0.5 * value)


def layer_norm(value):
    center = value - jnp.mean(value, axis=-1, keepdims=True)
    spread = jnp.mean(center * center, axis=-1, keepdims=True)
    return center * lax.rsqrt(spread + 1e-05)


def iota(shape, dim):
    return lax.broadcasted_iota(I32, shape, dim)


def one_hot(columns, rows):
    hit = columns.astype(jnp.int16) == lax.broadcasted_iota(jnp.int16, (rows, columns.shape[1]), 0)
    return jnp.where(hit, jnp.ones((), BF16), jnp.zeros((), BF16))


def ids_of_rows(slot, first, count):
    nodes = slot.shape[1]
    rows = iota((count, nodes), 0) + first
    return jnp.max(jnp.where(slot == rows, iota((count, nodes), 1), -1), axis=1, keepdims=True)


def edge_kernel(
    place_ref,
    first_hbm,
    grid_hbm,
    second_hbm,
    send_weight_hbm,
    grid_bias_hbm,
    edge_bias_hbm,
    slot_hbm,
    feat_weight_hbm,
    send_hbm,
    recv_hbm,
    feat_hbm,
    count_hbm,
    own_ref,
    cross_ref,
    chip_ref,
    first_ref,
    grid_ref,
    second_ref,
    send_weight_ref,
    grid_bias_ref,
    edge_bias_ref,
    slot_ref,
    feat_weight_ref,
    send_ref,
    recv_ref,
    feat_ref,
    count_ref,
    starts,
    table,
    even_rows,
    odd_rows,
    even_hidden,
    odd_hidden,
    ids_ref,
    total,
    sems,
):
    channels, grid_rows = grid_ref.shape
    width = second_ref.shape[1]
    pieces = width // LANES
    blocks, block_edges = send_ref.shape
    owned = own_ref.shape[0]
    feats = feat_ref.shape[1]
    step_rows = grid_rows // GRID_STEPS

    def grid_copy(step):
        part = pl.ds(pl.multiple_of(step * step_rows, step_rows), step_rows)
        return pltpu.make_async_copy(grid_hbm.at[:, part], grid_ref.at[:, part], sems.at[step])

    pairs = [
        (first_hbm, first_ref),
        (second_hbm, second_ref),
        (send_weight_hbm, send_weight_ref),
        (grid_bias_hbm, grid_bias_ref),
        (edge_bias_hbm, edge_bias_ref),
        (send_hbm, send_ref),
        (slot_hbm, slot_ref),
        (feat_weight_hbm, feat_weight_ref),
        (recv_hbm, recv_ref),
        (feat_hbm, feat_ref),
        (count_hbm, count_ref),
        (send_ref, starts),
    ]
    copies = [
        pltpu.make_async_copy(source, target, sems.at[GRID_STEPS + at])
        for at, (source, target) in enumerate(pairs)
    ]
    first_copy, second_copy, send_weight_copy, grid_bias_copy, edge_bias_copy, send_copy = copies[:6]
    slot_copy, starts_copy = copies[6], copies[-1]
    first_copy.start()
    grid_copy(0).start()
    for copy in copies[1:-1]:
        copy.start()
    for step in range(1, GRID_STEPS):
        grid_copy(step).start()
    send_copy.wait()
    senders = send_ref[...]
    send_ref[...] = (senders // 8) * (8 * pieces) + senders % 8
    starts_copy.start()
    slot_copy.wait()
    place = place_ref[0]
    ids_ref[...] = jnp.broadcast_to(
        ids_of_rows(slot_ref[...], (place - 1) * owned, 3 * owned), ids_ref.shape
    )
    total[...] = jnp.zeros_like(total)
    first_copy.wait()
    first_ref[...] = first_ref[...] * 0.5
    second_copy.wait()
    send_weight_copy.wait()
    send_weight_ref[...] = send_weight_ref[...] * 0.5
    grid_bias_copy.wait()
    edge_bias_copy.wait()
    grid_bias = 0.5 * grid_bias_ref[...]
    edge_bias = 0.5 * edge_bias_ref[...]
    def turn(step):
        return grid_ref[:, step * step_rows : (step + 1) * step_rows].T

    def store(step, value):
        rows = (value + edge_bias).astype(BF16).astype(F32)
        for group in range(step_rows // 8):
            for piece in range(pieces):
                at = ((step * step_rows // 8 + group) * pieces + piece) * 8
                table[at : at + 8, :] = rows[
                    group * 8 : group * 8 + 8, piece * LANES : (piece + 1) * LANES
                ]

    grid_copy(0).wait()
    first, second, third = {}, {}, {}
    first[0] = mm(turn(0), first_ref[...])
    for step in range(1, GRID_STEPS):
        grid_copy(step).wait()
    for step in range(1, GRID_STEPS + 3):
        turned = turn(step) if step < GRID_STEPS else None
        if step - 3 in third:
            store(step - 3, third.pop(step - 3))
        if step - 2 in second:
            code = layer_norm(second.pop(step - 2)).astype(BF16)
        else:
            code = None
        if step - 1 in first:
            hidden = silu_half(first.pop(step - 1) + grid_bias).astype(BF16)
        else:
            hidden = None
        if code is not None:
            third[step - 2] = mm(code, send_weight_ref[...])
        if hidden is not None:
            second[step - 1] = mm(hidden, second_ref[...])
        if turned is not None:
            first[step] = mm(turned, first_ref[...])
    for copy in copies[7:]:
        copy.wait()
    used = count_ref[...]
    feat_weight = 0.5 * feat_weight_ref[...].astype(F32)
    feat_weight = jnp.concatenate([feat_weight, jnp.zeros((8 - feats, width), F32)], axis=0)
    feat_weight = feat_weight.astype(BF16)
    group = CHUNK_BLOCKS
    chunks = blocks // group
    part_rows = 64

    def gather(chunk, edges, target):
        for edge in edges:
            start = starts[chunk * group + edge // block_edges, edge % block_edges]
            target[pl.ds(edge // 8 * (8 * pieces) + edge % 8, pieces, stride=8), :] = table[
                pl.ds(start, pieces, stride=8), :
            ]

    def rows_of(source, first, count):
        return jnp.concatenate(
            [
                jnp.concatenate(
                    [
                        source[pl.ds((at * pieces + piece) * 8, 8), :]
                        for at in range(first // 8, (first + count) // 8)
                    ],
                    axis=0,
                )
                for piece in range(pieces)
            ],
            axis=1,
        )

    def add_sums(chunk, hidden):
        here = [chunk * group + b for b in range(group)]
        receivers = [jnp.where(b < used, recv_ref[pl.ds(b, 1), :], -2) for b in here]
        spread = jnp.concatenate([(ids_ref[...] == row).astype(F32) for row in receivers], axis=1)
        total[...] += mm(spread.astype(BF16), hidden[...])

    def work(chunk, source, target, hidden, hidden_before):
        here = [chunk * group + b for b in range(group)]
        feat = jnp.concatenate([feat_ref[b] for b in here], axis=1)
        feat = jnp.concatenate([feat, jnp.zeros((8 - feats, feat.shape[1]), F32)], axis=0)
        extra = mm(feat.T.astype(BF16), feat_weight)
        add_sums(jnp.maximum(chunk - 1, 0), hidden_before)
        after = jnp.minimum(chunk + 1, chunks - 1)
        for first in range(0, group * block_edges, part_rows):
            gather(after, range(first, first + part_rows), target)
            half = rows_of(source, first, part_rows) + extra[first : first + part_rows]
            hidden[first : first + part_rows, :] = silu_half(half).astype(BF16)

    def edge_step(step, carry):
        work(2 * step, even_rows, odd_rows, even_hidden, odd_hidden)
        work(2 * step + 1, odd_rows, even_rows, odd_hidden, even_hidden)
        return carry

    odd_hidden[...] = jnp.zeros_like(odd_hidden)
    gather(0, range(group * block_edges), even_rows)
    lax.fori_loop(0, chunks // 2, edge_step, 0)
    add_sums(chunks - 1, odd_hidden)
    odd = place % 2 == 1
    below, above = total[:owned].astype(BF16), total[2 * owned :].astype(BF16)
    own_ref[...] = total[owned : 2 * owned]
    cross_ref[...] = jnp.where(odd, above, below)
    chip_ref[...] = jnp.where(odd, below, above)


def wanted_kernel(owned, slot_ref, send_ref, wanted_ref):
    nodes = slot_ref.shape[1]
    blocks, block_edges = send_ref.shape
    places = wanted_ref.shape[1]
    chunk = LANES
    per_chunk = chunk // owned * SEND_CAP
    row, column = iota((chunk, chunk), 0), iota((chunk, chunk), 1)
    before = ((row > column) & (row // owned == column // owned)).astype(F32).astype(BF16)
    local_owner = (iota((chunk, LANES), 0) // owned * SEND_CAP).astype(F32)

    def find(index, best):
        ids = ids_of_rows(slot_ref[...], index * chunk, chunk)
        hit = jnp.zeros((chunk, block_edges), F32)
        for b in range(blocks):
            hit = jnp.maximum(hit, (ids == send_ref[b : b + 1, :]).astype(F32))
        hit = jnp.broadcast_to(jnp.max(hit, axis=1, keepdims=True), (chunk, LANES))
        rank = mm(before, hit.astype(BF16)) + local_owner
        spot = jnp.where(hit > 0, rank.astype(I32) + index * per_chunk, -1)
        spot = jnp.concatenate([spot] * (places // LANES), axis=1)
        found = jnp.where(spot == iota((chunk, places), 1), ids, -1)
        return jnp.maximum(best, jnp.max(found, axis=0, keepdims=True))

    best = lax.fori_loop(0, nodes // chunk, find, jnp.full((1, places), -1, I32), unroll=2)
    best = best.astype(F32)
    for b in range(blocks):
        senders = jnp.broadcast_to(send_ref[b : b + 1, :].astype(F32), (block_edges, block_edges)).T
        senders = jnp.concatenate([senders] * (places // LANES), axis=1)
        wanted_ref[b * block_edges : (b + 1) * block_edges, :] = (
            (senders == best).astype(F32).astype(BF16)
        )


def supply_kernel(
    blocks,
    place_ref,
    slot_ref,
    request_ref,
    latent_ref,
    edge_out_ref,
    node_input_ref,
    node_bias_ref,
    supply_ref,
    upper_ref,
    lower_ref,
):
    width = latent_ref.shape[1]
    upper_ref[...] = mm(latent_ref[...], node_input_ref[:width]) + node_bias_ref[...]
    lower_ref[...] = mm(edge_out_ref[...], node_input_ref[width:]).astype(BF16)
    owned = supply_ref.shape[1]
    devices = supply_ref.shape[0] // SEND_CAP
    per_device = request_ref.shape[0] // devices
    ids = ids_of_rows(slot_ref[...], place_ref[0] * owned, owned)
    lane = iota((owned, LANES), 1)
    used = jnp.zeros((owned, LANES), F32)
    for d in range(devices):
        hit = jnp.zeros((owned, request_ref.shape[1]), F32)
        for b in range(blocks):
            at = d * per_device + b
            hit = jnp.maximum(hit, (ids == request_ref[at : at + 1, :]).astype(F32))
        used = jnp.where(lane == d, jnp.max(hit, axis=1, keepdims=True), used)
    before = (iota((owned, owned), 0) > iota((owned, owned), 1)).astype(F32).astype(BF16)
    rank = jnp.where(used > 0, mm(before, used.astype(BF16)), -1.0)
    rank = jnp.concatenate([rank, jnp.full((LANES - owned, LANES), -1.0, F32)], axis=0).T
    slots = iota((SEND_CAP, owned), 0).astype(F32)
    supply = jnp.concatenate(
        [(rank[d : d + 1, :owned] == slots).astype(F32) for d in range(devices)], axis=0
    )
    supply_ref[...] = supply.astype(BF16)


def node_kernel(
    own_ref,
    from_cross_ref,
    from_chip_ref,
    latent_ref,
    upper_ref,
    lower_ref,
    node_out_ref,
    node_gain_ref,
    mesh_sender_ref,
    supply_ref,
    encoded_ref,
    rows_ref,
):
    latent = latent_ref[...]
    node_sum = own_ref[...] + from_cross_ref[...].astype(F32) + from_chip_ref[...].astype(F32)
    hidden = silu(upper_ref[...] + mm(node_sum.astype(BF16), lower_ref[...])).astype(BF16)
    encoded = latent.astype(F32) + layer_norm(mm(hidden, node_out_ref[...])) * node_gain_ref[...]
    encoded = encoded.astype(BF16)
    encoded_ref[...] = encoded
    sender_code = mm(encoded, mesh_sender_ref[...]).astype(BF16)
    rows_ref[...] = mm(supply_ref[...], sender_code).astype(BF16)


def receiver_kernel(
    place_ref,
    slot_ref,
    recv_ref,
    encoded_ref,
    mesh_receiver_ref,
    message_bias_ref,
    message_out_ref,
    update_input_ref,
    update_bias_ref,
    incoming_ref,
    pick_ref,
    parts_ref,
    upper_ref,
    lower_ref,
):
    owned, width = encoded_ref.shape
    blocks = recv_ref.shape[0]
    ids = ids_of_rows(slot_ref[...], place_ref[0] * owned, owned)
    incoming = jnp.concatenate(
        [(ids == recv_ref[b : b + 1, :]).astype(F32) for b in range(blocks)], axis=1
    )
    pick = incoming.T.astype(BF16)
    pick_ref[...] = jnp.concatenate([pick, pick], axis=1)
    incoming_ref[...] = incoming.astype(BF16)
    encoded = encoded_ref[...]
    receiver = mm(encoded, mesh_receiver_ref[...]) + message_bias_ref[...]
    high = receiver.astype(BF16)
    parts_ref[:owned, :] = high
    parts_ref[owned:, :] = (receiver - high.astype(F32)).astype(BF16)
    upper_ref[...] = mm(encoded, update_input_ref[:width]) + update_bias_ref[...]
    lower_ref[...] = mm(message_out_ref[...], update_input_ref[width:]).astype(BF16)


def message_kernel(
    wanted_ref,
    piece_ref,
    incoming_ref,
    pick_ref,
    parts_ref,
    upper_ref,
    lower_ref,
    encoded_ref,
    update_out_ref,
    update_gain_ref,
    out_ref,
):
    chosen = jnp.concatenate([wanted_ref[...], pick_ref[...]], axis=1)
    codes = jnp.concatenate([piece_ref[...], parts_ref[...]], axis=0)
    message = silu(mm(chosen, codes)).astype(BF16)
    message_sum = mm(incoming_ref[...], message).astype(BF16)
    hidden = silu(upper_ref[...] + mm(message_sum, lower_ref[...])).astype(BF16)
    out = layer_norm(mm(hidden, update_out_ref[...])) * update_gain_ref[...]
    out_ref[...] = (encoded_ref[...].astype(F32) + out).astype(BF16)


def call(kernel, out_shape, spaces, scratch=(), flops=0, moved=0, vmem=8):
    return pl.pallas_call(
        kernel,
        out_shape=out_shape,
        in_specs=[pl.BlockSpec(memory_space=space) for space in spaces],
        out_specs=jax.tree.map(lambda _: pl.BlockSpec(memory_space=VMEM), out_shape),
        scratch_shapes=scratch,
        compiler_params=pltpu.CompilerParams(vmem_limit_bytes=vmem * MEBI),
        cost_estimate=pl.CostEstimate(flops=flops, bytes_accessed=moved, transcendentals=0),
    )


def hold(value):
    return value if value.size == 1 else pltpu.with_memory_space_constraint(value, HBM)


def shape(*sizes, kind=BF16):
    return jax.ShapeDtypeStruct(sizes, kind)


def per_device(
    grid_in,
    grid_first,
    grid_bias,
    grid_second,
    send_weight,
    edge_bias,
    feat_weight,
    edge_out,
    node_input,
    node_bias,
    node_out,
    node_gain,
    mesh_sender,
    mesh_receiver,
    message_bias,
    message_out,
    update_input,
    update_bias,
    update_out,
    update_gain,
    mesh_latent,
    g2m_send,
    g2m_recv,
    g2m_feat,
    g2m_count,
    mesh_slot,
    mesh_send,
    mesh_recv,
):
    devices = lax.axis_size("bulk")
    position = lax.axis_index("bulk")
    place = position.astype(I32).reshape(1)
    owned, width = mesh_latent.shape
    grid_rows = grid_in.shape[0]
    places = devices * SEND_CAP
    edges = mesh_send.size
    slot = mesh_slot.reshape(1, -1)
    row = lambda vector: vector.reshape(1, -1)

    requests = lax.all_to_all(jnp.tile(mesh_send, (devices, 1)), "bulk", 0, 0, tiled=True)
    operands = (
        grid_first,
        grid_in.T,
        grid_second,
        send_weight,
        row(grid_bias),
        row(edge_bias),
        slot,
        feat_weight,
        g2m_send,
        g2m_recv,
        g2m_feat,
        g2m_count.reshape(1, 1),
    )
    own, cross, chip = call(
        edge_kernel,
        (shape(owned, width, kind=F32), shape(owned, width), shape(owned, width)),
        [SMEM] + [HBM] * len(operands),
        scratch=[VMEM(value.shape, value.dtype) for value in operands]
        + [
            SMEM(g2m_send.shape, I32),
            VMEM((grid_rows * (width // LANES), LANES), F32),
            VMEM((CHUNK_BLOCKS * g2m_send.shape[1] * (width // LANES), LANES), F32),
            VMEM((CHUNK_BLOCKS * g2m_send.shape[1] * (width // LANES), LANES), F32),
            VMEM((CHUNK_BLOCKS * g2m_send.shape[1], width), BF16),
            VMEM((CHUNK_BLOCKS * g2m_send.shape[1], width), BF16),
            VMEM((3 * owned, LANES), I32),
            VMEM((3 * owned, width), F32),
            pltpu.SemaphoreType.DMA((len(operands) + GRID_STEPS,)),
        ],
        flops=10_000_000_000,
        moved=4_000_000,
        vmem=32,
    )(place, *[hold(value) for value in operands])
    requests, _ = lax.optimization_barrier((requests, own))
    crossing = [(d, d + 1) for d in range(1, devices - 1, 2)]
    within = [(d, d + 1) for d in range(0, devices, 2)]
    both = lambda pairs: pairs + [(b, a) for a, b in pairs]
    from_cross = lax.ppermute(cross, "bulk", both(crossing))
    from_chip = lax.ppermute(chip, "bulk", both(within))
    supply, upper, lower = call(
        functools.partial(supply_kernel, mesh_send.shape[0]),
        (shape(places, owned), shape(owned, width, kind=F32), shape(width, width)),
        [SMEM] + [VMEM] * 6,
        flops=500_000_000,
        moved=500_000,
    )(place, slot, requests, mesh_latent, edge_out, node_input, row(node_bias))
    encoded, rows = call(
        node_kernel,
        (shape(owned, width), shape(places, width)),
        [VMEM] * 10,
        flops=500_000_000,
        moved=4_000_000,
    )(
        own,
        from_cross,
        from_chip,
        mesh_latent,
        upper,
        lower,
        node_out,
        row(node_gain),
        mesh_sender,
        supply,
    )
    piece = lax.all_to_all(rows, "bulk", 0, 0, tiled=True)
    mesh_send, _ = lax.optimization_barrier((mesh_send, encoded))
    wanted = call(
        functools.partial(wanted_kernel, owned),
        shape(edges, places),
        [VMEM] * 2,
        flops=1_000_000_000,
        moved=500_000,
    )(slot, mesh_send)
    incoming, pick, parts, upper, lower = call(
        receiver_kernel,
        (
            shape(owned, edges),
            shape(edges, 2 * owned),
            shape(2 * owned, width),
            shape(owned, width, kind=F32),
            shape(width, width),
        ),
        [SMEM] + [VMEM] * 8,
        flops=1_000_000_000,
        moved=4_000_000,
    )(
        place,
        slot,
        mesh_recv,
        encoded,
        mesh_receiver,
        row(message_bias),
        message_out,
        update_input,
        row(update_bias),
    )
    return call(
        message_kernel,
        shape(owned, width),
        [VMEM] * 10,
        flops=1_000_000_000,
        moved=4_000_000,
    )(
        wanted,
        piece,
        incoming,
        pick,
        parts,
        upper,
        lower,
        encoded,
        update_out,
        row(update_gain),
    )


def solution(mesh):
    split = {0: ("groups", "bulk"), 20: "bulk", 21: "bulk", 22: "bulk", 23: "bulk", 24: "bulk"}
    split.update({26: "bulk", 27: "bulk"})
    placed = tuple(P(split[at]) if at in split else P() for at in range(28))
    return jax.shard_map(
        per_device,
        mesh=mesh,
        in_specs=placed,
        out_specs=P(("groups", "bulk"), None),
        check_vma=False,
    )
```

```python
import functools
import math

import jax
import jax.numpy as jnp
from jax import lax
from jax.experimental import pallas as pl
from jax.experimental.pallas import tpu as pltpu
from jax.sharding import PartitionSpec as P

F32 = jnp.float32
BF16 = jnp.bfloat16
I32 = jnp.int32
SEND_CAP = 16
LANES = 128
VMEM = pltpu.VMEM
SMEM = pltpu.SMEM
HBM = pltpu.HBM
GRID_STEPS = 4
CHUNK_BLOCKS = 6
MEBI = 1024 * 1024


def mm(left, right):
    return jnp.dot(left, right, preferred_element_type=F32)


def mm_nt(left, right):
    return lax.dot_general(left, right, (((1,), (1,)), ((), ())), preferred_element_type=F32)


def silu_half(half):
    return half + half * jnp.tanh(half)


def silu(value):
    return silu_half(0.5 * value)


def layer_norm(value):
    center = value - jnp.mean(value, axis=-1, keepdims=True)
    spread = jnp.mean(center * center, axis=-1, keepdims=True)
    return center * lax.rsqrt(spread + 1e-05)


def iota(shape, dim):
    return lax.broadcasted_iota(I32, shape, dim)


def one_hot(columns, rows):
    hit = columns.astype(jnp.int16) == lax.broadcasted_iota(jnp.int16, (rows, columns.shape[1]), 0)
    return jnp.where(hit, jnp.ones((), BF16), jnp.zeros((), BF16))


def ids_of_rows(slot, first, count):
    nodes = slot.shape[1]
    rows = iota((count, nodes), 0) + first
    return jnp.max(jnp.where(slot == rows, iota((count, nodes), 1), -1), axis=1, keepdims=True)


def edge_kernel(
    place_ref,
    first_hbm,
    grid_hbm,
    second_hbm,
    send_weight_hbm,
    grid_bias_hbm,
    edge_bias_hbm,
    slot_hbm,
    feat_weight_hbm,
    send_hbm,
    recv_hbm,
    feat_hbm,
    count_hbm,
    own_ref,
    cross_ref,
    chip_ref,
    first_ref,
    grid_ref,
    second_ref,
    send_weight_ref,
    grid_bias_ref,
    edge_bias_ref,
    slot_ref,
    feat_weight_ref,
    send_ref,
    recv_ref,
    feat_ref,
    count_ref,
    starts,
    table,
    even_rows,
    odd_rows,
    even_hidden,
    odd_hidden,
    ids_ref,
    total,
    sems,
):
    channels, grid_rows = grid_ref.shape
    width = second_ref.shape[1]
    pieces = width // LANES
    blocks, block_edges = send_ref.shape
    owned = own_ref.shape[0]
    feats = feat_ref.shape[1]
    step_rows = grid_rows // GRID_STEPS

    def grid_copy(step):
        part = pl.ds(pl.multiple_of(step * step_rows, step_rows), step_rows)
        return pltpu.make_async_copy(grid_hbm.at[:, part], grid_ref.at[:, part], sems.at[step])

    pairs = [
        (first_hbm, first_ref),
        (second_hbm, second_ref),
        (send_weight_hbm, send_weight_ref),
        (grid_bias_hbm, grid_bias_ref),
        (edge_bias_hbm, edge_bias_ref),
        (send_hbm, send_ref),
        (slot_hbm, slot_ref),
        (feat_weight_hbm, feat_weight_ref),
        (recv_hbm, recv_ref),
        (feat_hbm, feat_ref),
        (count_hbm, count_ref),
        (send_ref, starts),
    ]
    copies = [
        pltpu.make_async_copy(source, target, sems.at[GRID_STEPS + at])
        for at, (source, target) in enumerate(pairs)
    ]
    first_copy, second_copy, send_weight_copy, grid_bias_copy, edge_bias_copy, send_copy = copies[:6]
    slot_copy, starts_copy = copies[6], copies[-1]
    first_copy.start()
    grid_copy(0).start()
    for copy in copies[1:-1]:
        copy.start()
    for step in range(1, GRID_STEPS):
        grid_copy(step).start()
    send_copy.wait()
    senders = send_ref[...]
    send_ref[...] = (senders // 8) * (8 * pieces) + senders % 8
    starts_copy.start()
    slot_copy.wait()
    place = place_ref[0]
    ids_ref[...] = jnp.broadcast_to(
        ids_of_rows(slot_ref[...], (place - 1) * owned, 3 * owned), ids_ref.shape
    )
    total[...] = jnp.zeros_like(total)
    first_copy.wait()
    first_ref[...] = first_ref[...] * 0.5
    second_copy.wait()
    send_weight_copy.wait()
    send_weight_ref[...] = send_weight_ref[...] * 0.5
    grid_bias_copy.wait()
    edge_bias_copy.wait()
    grid_bias = 0.5 * grid_bias_ref[...]
    edge_bias = 0.5 * edge_bias_ref[...]
    def turn(step):
        return grid_ref[:, step * step_rows : (step + 1) * step_rows].T

    def store(step, value):
        rows = (value + edge_bias).astype(BF16).astype(F32)
        for group in range(step_rows // 8):
            for piece in range(pieces):
                at = ((step * step_rows // 8 + group) * pieces + piece) * 8
                table[at : at + 8, :] = rows[
                    group * 8 : group * 8 + 8, piece * LANES : (piece + 1) * LANES
                ]

    grid_copy(0).wait()
    first, second, third = {}, {}, {}
    first[0] = mm(turn(0), first_ref[...])
    for step in range(1, GRID_STEPS):
        grid_copy(step).wait()
    for step in range(1, GRID_STEPS + 3):
        turned = turn(step) if step < GRID_STEPS else None
        if step - 3 in third:
            store(step - 3, third.pop(step - 3))
        if step - 2 in second:
            code = layer_norm(second.pop(step - 2)).astype(BF16)
        else:
            code = None
        if step - 1 in first:
            hidden = silu_half(first.pop(step - 1) + grid_bias).astype(BF16)
        else:
            hidden = None
        if code is not None:
            third[step - 2] = mm(code, send_weight_ref[...])
        if hidden is not None:
            second[step - 1] = mm(hidden, second_ref[...])
        if turned is not None:
            first[step] = mm(turned, first_ref[...])
    for copy in copies[7:]:
        copy.wait()
    used = count_ref[...]
    feat_weight = 0.5 * feat_weight_ref[...].astype(F32)
    feat_weight = jnp.concatenate([feat_weight, jnp.zeros((8 - feats, width), F32)], axis=0)
    feat_weight = feat_weight.astype(BF16)
    group = CHUNK_BLOCKS
    chunks = blocks // group
    part_rows = 64

    def gather(chunk, edges, target):
        for edge in edges:
            start = starts[chunk * group + edge // block_edges, edge % block_edges]
            target[pl.ds(edge // 8 * (8 * pieces) + edge % 8, pieces, stride=8), :] = table[
                pl.ds(start, pieces, stride=8), :
            ]

    def rows_of(source, first, count):
        return jnp.concatenate(
            [
                jnp.concatenate(
                    [
                        source[pl.ds((at * pieces + piece) * 8, 8), :]
                        for at in range(first // 8, (first + count) // 8)
                    ],
                    axis=0,
                )
                for piece in range(pieces)
            ],
            axis=1,
        )

    def add_sums(chunk, hidden):
        here = [chunk * group + b for b in range(group)]
        receivers = [jnp.where(b < used, recv_ref[pl.ds(b, 1), :], -2) for b in here]
        spread = jnp.concatenate([(ids_ref[...] == row).astype(F32) for row in receivers], axis=1)
        total[...] += mm(spread.astype(BF16), hidden[...])

    def work(chunk, source, target, hidden, hidden_before):
        here = [chunk * group + b for b in range(group)]
        feat = jnp.concatenate([feat_ref[b] for b in here], axis=1)
        feat = jnp.concatenate([feat, jnp.zeros((8 - feats, feat.shape[1]), F32)], axis=0)
        extra = mm(feat.T.astype(BF16), feat_weight)
        add_sums(jnp.maximum(chunk - 1, 0), hidden_before)
        after = jnp.minimum(chunk + 1, chunks - 1)
        for first in range(0, group * block_edges, part_rows):
            gather(after, range(first, first + part_rows), target)
            half = rows_of(source, first, part_rows) + extra[first : first + part_rows]
            hidden[first : first + part_rows, :] = silu_half(half).astype(BF16)

    def edge_step(step, carry):
        work(2 * step, even_rows, odd_rows, even_hidden, odd_hidden)
        work(2 * step + 1, odd_rows, even_rows, odd_hidden, even_hidden)
        return carry

    odd_hidden[...] = jnp.zeros_like(odd_hidden)
    gather(0, range(group * block_edges), even_rows)
    lax.fori_loop(0, chunks // 2, edge_step, 0)
    add_sums(chunks - 1, odd_hidden)
    odd = place % 2 == 1
    below, above = total[:owned].astype(BF16), total[2 * owned :].astype(BF16)
    own_ref[...] = total[owned : 2 * owned]
    cross_ref[...] = jnp.where(odd, above, below)
    chip_ref[...] = jnp.where(odd, below, above)


def wanted_kernel(owned, slot_ref, send_ref, wanted_ref):
    nodes = slot_ref.shape[1]
    blocks, block_edges = send_ref.shape
    places = wanted_ref.shape[1]
    chunk = LANES
    per_chunk = chunk // owned * SEND_CAP
    row, column = iota((chunk, chunk), 0), iota((chunk, chunk), 1)
    before = ((row > column) & (row // owned == column // owned)).astype(F32).astype(BF16)
    local_owner = (iota((chunk, LANES), 0) // owned * SEND_CAP).astype(F32)

    def find(index, best):
        ids = ids_of_rows(slot_ref[...], index * chunk, chunk)
        hit = jnp.zeros((chunk, block_edges), F32)
        for b in range(blocks):
            hit = jnp.maximum(hit, (ids == send_ref[b : b + 1, :]).astype(F32))
        hit = jnp.broadcast_to(jnp.max(hit, axis=1, keepdims=True), (chunk, LANES))
        rank = mm(before, hit.astype(BF16)) + local_owner
        spot = jnp.where(hit > 0, rank.astype(I32) + index * per_chunk, -1)
        spot = jnp.concatenate([spot] * (places // LANES), axis=1)
        found = jnp.where(spot == iota((chunk, places), 1), ids, -1)
        return jnp.maximum(best, jnp.max(found, axis=0, keepdims=True))

    best = lax.fori_loop(0, nodes // chunk, find, jnp.full((1, places), -1, I32), unroll=2)
    best = best.astype(F32)
    for b in range(blocks):
        senders = jnp.broadcast_to(send_ref[b : b + 1, :].astype(F32), (block_edges, block_edges)).T
        senders = jnp.concatenate([senders] * (places // LANES), axis=1)
        wanted_ref[b * block_edges : (b + 1) * block_edges, :] = (
            (senders == best).astype(F32).astype(BF16)
        )


def supply_kernel(
    blocks,
    place_ref,
    slot_ref,
    request_ref,
    latent_ref,
    edge_out_ref,
    node_input_ref,
    node_bias_ref,
    supply_ref,
    upper_ref,
    lower_ref,
):
    width = latent_ref.shape[1]
    upper_ref[...] = mm(latent_ref[...], node_input_ref[:width]) + node_bias_ref[...]
    lower_ref[...] = mm(edge_out_ref[...], node_input_ref[width:]).astype(BF16)
    owned = supply_ref.shape[1]
    devices = supply_ref.shape[0] // SEND_CAP
    per_device = request_ref.shape[0] // devices
    ids = ids_of_rows(slot_ref[...], place_ref[0] * owned, owned)
    lane = iota((owned, LANES), 1)
    used = jnp.zeros((owned, LANES), F32)
    for d in range(devices):
        hit = jnp.zeros((owned, request_ref.shape[1]), F32)
        for b in range(blocks):
            at = d * per_device + b
            hit = jnp.maximum(hit, (ids == request_ref[at : at + 1, :]).astype(F32))
        used = jnp.where(lane == d, jnp.max(hit, axis=1, keepdims=True), used)
    before = (iota((owned, owned), 0) > iota((owned, owned), 1)).astype(F32).astype(BF16)
    rank = jnp.where(used > 0, mm(before, used.astype(BF16)), -1.0)
    rank = jnp.concatenate([rank, jnp.full((LANES - owned, LANES), -1.0, F32)], axis=0).T
    slots = iota((SEND_CAP, owned), 0).astype(F32)
    supply = jnp.concatenate(
        [(rank[d : d + 1, :owned] == slots).astype(F32) for d in range(devices)], axis=0
    )
    supply_ref[...] = supply.astype(BF16)


def node_kernel(
    own_ref,
    from_cross_ref,
    from_chip_ref,
    latent_ref,
    upper_ref,
    lower_ref,
    node_out_ref,
    node_gain_ref,
    mesh_sender_ref,
    supply_ref,
    encoded_ref,
    rows_ref,
):
    latent = latent_ref[...]
    node_sum = own_ref[...] + from_cross_ref[...].astype(F32) + from_chip_ref[...].astype(F32)
    hidden = silu(upper_ref[...] + mm(node_sum.astype(BF16), lower_ref[...])).astype(BF16)
    encoded = latent.astype(F32) + layer_norm(mm(hidden, node_out_ref[...])) * node_gain_ref[...]
    encoded = encoded.astype(BF16)
    encoded_ref[...] = encoded
    sender_code = mm(encoded, mesh_sender_ref[...]).astype(BF16)
    rows_ref[...] = mm(supply_ref[...], sender_code).astype(BF16)


def receiver_kernel(
    place_ref,
    slot_ref,
    recv_ref,
    encoded_ref,
    mesh_receiver_ref,
    message_bias_ref,
    message_out_ref,
    update_input_ref,
    update_bias_ref,
    incoming_ref,
    pick_ref,
    parts_ref,
    upper_ref,
    lower_ref,
):
    owned, width = encoded_ref.shape
    blocks = recv_ref.shape[0]
    ids = ids_of_rows(slot_ref[...], place_ref[0] * owned, owned)
    incoming = jnp.concatenate(
        [(ids == recv_ref[b : b + 1, :]).astype(F32) for b in range(blocks)], axis=1
    )
    pick = incoming.T.astype(BF16)
    pick_ref[...] = jnp.concatenate([pick, pick], axis=1)
    incoming_ref[...] = incoming.astype(BF16)
    encoded = encoded_ref[...]
    receiver = mm(encoded, mesh_receiver_ref[...]) + message_bias_ref[...]
    high = receiver.astype(BF16)
    parts_ref[:owned, :] = high
    parts_ref[owned:, :] = (receiver - high.astype(F32)).astype(BF16)
    upper_ref[...] = mm(encoded, update_input_ref[:width]) + update_bias_ref[...]
    lower_ref[...] = mm(message_out_ref[...], update_input_ref[width:]).astype(BF16)


def message_kernel(
    wanted_ref,
    piece_ref,
    incoming_ref,
    pick_ref,
    parts_ref,
    upper_ref,
    lower_ref,
    encoded_ref,
    update_out_ref,
    update_gain_ref,
    out_ref,
):
    chosen = jnp.concatenate([wanted_ref[...], pick_ref[...]], axis=1)
    codes = jnp.concatenate([piece_ref[...], parts_ref[...]], axis=0)
    message = silu(mm(chosen, codes)).astype(BF16)
    message_sum = mm(incoming_ref[...], message).astype(BF16)
    hidden = silu(upper_ref[...] + mm(message_sum, lower_ref[...])).astype(BF16)
    out = layer_norm(mm(hidden, update_out_ref[...])) * update_gain_ref[...]
    out_ref[...] = (encoded_ref[...].astype(F32) + out).astype(BF16)


def call(kernel, out_shape, spaces, scratch=(), flops=0, moved=0, vmem=8):
    return pl.pallas_call(
        kernel,
        out_shape=out_shape,
        in_specs=[pl.BlockSpec(memory_space=space) for space in spaces],
        out_specs=jax.tree.map(lambda _: pl.BlockSpec(memory_space=VMEM), out_shape),
        scratch_shapes=scratch,
        compiler_params=pltpu.CompilerParams(vmem_limit_bytes=vmem * MEBI),
        cost_estimate=pl.CostEstimate(flops=flops, bytes_accessed=moved, transcendentals=0),
    )


def hold(value):
    return value if value.size == 1 else pltpu.with_memory_space_constraint(value, HBM)


def shape(*sizes, kind=BF16):
    return jax.ShapeDtypeStruct(sizes, kind)


def per_device(
    grid_in,
    grid_first,
    grid_bias,
    grid_second,
    send_weight,
    edge_bias,
    feat_weight,
    edge_out,
    node_input,
    node_bias,
    node_out,
    node_gain,
    mesh_sender,
    mesh_receiver,
    message_bias,
    message_out,
    update_input,
    update_bias,
    update_out,
    update_gain,
    mesh_latent,
    g2m_send,
    g2m_recv,
    g2m_feat,
    g2m_count,
    mesh_slot,
    mesh_send,
    mesh_recv,
):
    devices = lax.axis_size("bulk")
    position = lax.axis_index("bulk")
    place = position.astype(I32).reshape(1)
    owned, width = mesh_latent.shape
    grid_rows = grid_in.shape[0]
    places = devices * SEND_CAP
    edges = mesh_send.size
    slot = mesh_slot.reshape(1, -1)
    row = lambda vector: vector.reshape(1, -1)

    requests = lax.all_to_all(jnp.tile(mesh_send, (devices, 1)), "bulk", 0, 0, tiled=True)
    operands = (
        grid_first,
        grid_in.T,
        grid_second,
        send_weight,
        row(grid_bias),
        row(edge_bias),
        slot,
        feat_weight,
        g2m_send,
        g2m_recv,
        g2m_feat,
        g2m_count.reshape(1, 1),
    )
    own, cross, chip = call(
        edge_kernel,
        (shape(owned, width, kind=F32), shape(owned, width), shape(owned, width)),
        [SMEM] + [HBM] * len(operands),
        scratch=[VMEM(value.shape, value.dtype) for value in operands]
        + [
            SMEM(g2m_send.shape, I32),
            VMEM((grid_rows * (width // LANES), LANES), F32),
            VMEM((CHUNK_BLOCKS * g2m_send.shape[1] * (width // LANES), LANES), F32),
            VMEM((CHUNK_BLOCKS * g2m_send.shape[1] * (width // LANES), LANES), F32),
            VMEM((CHUNK_BLOCKS * g2m_send.shape[1], width), BF16),
            VMEM((CHUNK_BLOCKS * g2m_send.shape[1], width), BF16),
            VMEM((3 * owned, LANES), I32),
            VMEM((3 * owned, width), F32),
            pltpu.SemaphoreType.DMA((len(operands) + GRID_STEPS,)),
        ],
        flops=10_000_000_000,
        moved=4_000_000,
        vmem=32,
    )(place, *[hold(value) for value in operands])
    requests, _ = lax.optimization_barrier((requests, own))
    crossing = [(d, d + 1) for d in range(1, devices - 1, 2)]
    within = [(d, d + 1) for d in range(0, devices, 2)]
    both = lambda pairs: pairs + [(b, a) for a, b in pairs]
    from_cross = lax.ppermute(cross, "bulk", both(crossing))
    from_chip = lax.ppermute(chip, "bulk", both(within))
    supply, upper, lower = call(
        functools.partial(supply_kernel, mesh_send.shape[0]),
        (shape(places, owned), shape(owned, width, kind=F32), shape(width, width)),
        [SMEM] + [VMEM] * 6,
        flops=500_000_000,
        moved=500_000,
    )(place, slot, requests, mesh_latent, edge_out, node_input, row(node_bias))
    encoded, rows = call(
        node_kernel,
        (shape(owned, width), shape(places, width)),
        [VMEM] * 10,
        flops=500_000_000,
        moved=4_000_000,
    )(
        own,
        from_cross,
        from_chip,
        mesh_latent,
        upper,
        lower,
        node_out,
        row(node_gain),
        mesh_sender,
        supply,
    )
    piece = lax.all_to_all(rows, "bulk", 0, 0, tiled=True)
    mesh_send, _ = lax.optimization_barrier((mesh_send, encoded))
    wanted = call(
        functools.partial(wanted_kernel, owned),
        shape(edges, places),
        [VMEM] * 2,
        flops=1_000_000_000,
        moved=500_000,
    )(slot, mesh_send)
    incoming, pick, parts, upper, lower = call(
        receiver_kernel,
        (
            shape(owned, edges),
            shape(edges, 2 * owned),
            shape(2 * owned, width),
            shape(owned, width, kind=F32),
            shape(width, width),
        ),
        [SMEM] + [VMEM] * 8,
        flops=1_000_000_000,
        moved=4_000_000,
    )(
        place,
        slot,
        mesh_recv,
        encoded,
        mesh_receiver,
        row(message_bias),
        message_out,
        update_input,
        row(update_bias),
    )
    return call(
        message_kernel,
        shape(owned, width),
        [VMEM] * 10,
        flops=1_000_000_000,
        moved=4_000_000,
    )(
        wanted,
        piece,
        incoming,
        pick,
        parts,
        upper,
        lower,
        encoded,
        update_out,
        row(update_gain),
    )


def solution(mesh):
    split = {0: ("groups", "bulk"), 20: "bulk", 21: "bulk", 22: "bulk", 23: "bulk", 24: "bulk"}
    split.update({26: "bulk", 27: "bulk"})
    placed = tuple(P(split[at]) if at in split else P() for at in range(28))
    return jax.shard_map(
        per_device,
        mesh=mesh,
        in_specs=placed,
        out_specs=P(("groups", "bulk"), None),
        check_vma=False,
    )
```

```python
import functools
import math

import jax
import jax.numpy as jnp
from jax import lax
from jax.experimental import pallas as pl
from jax.experimental.pallas import tpu as pltpu
from jax.sharding import PartitionSpec as P

F32 = jnp.float32
BF16 = jnp.bfloat16
I32 = jnp.int32
SEND_CAP = 16
LANES = 128
VMEM = pltpu.VMEM
SMEM = pltpu.SMEM
HBM = pltpu.HBM
GRID_STEPS = 4
CHUNK_BLOCKS = 4
MEBI = 1024 * 1024


def mm(left, right):
    return jnp.dot(left, right, preferred_element_type=F32)


def mm_nt(left, right):
    return lax.dot_general(left, right, (((1,), (1,)), ((), ())), preferred_element_type=F32)


def silu_half(half):
    return half + half * jnp.tanh(half)


def silu(value):
    return silu_half(0.5 * value)


def layer_norm(value):
    center = value - jnp.mean(value, axis=-1, keepdims=True)
    spread = jnp.mean(center * center, axis=-1, keepdims=True)
    return center * lax.rsqrt(spread + 1e-05)


def iota(shape, dim):
    return lax.broadcasted_iota(I32, shape, dim)


def one_hot(columns, rows):
    hit = columns.astype(jnp.int16) == lax.broadcasted_iota(jnp.int16, (rows, columns.shape[1]), 0)
    return jnp.where(hit, jnp.ones((), BF16), jnp.zeros((), BF16))


def ids_of_rows(slot, first, count):
    nodes = slot.shape[1]
    rows = iota((count, nodes), 0) + first
    return jnp.max(jnp.where(slot == rows, iota((count, nodes), 1), -1), axis=1, keepdims=True)


def edge_kernel(
    place_ref,
    first_hbm,
    grid_hbm,
    second_hbm,
    send_weight_hbm,
    grid_bias_hbm,
    edge_bias_hbm,
    slot_hbm,
    feat_weight_hbm,
    send_hbm,
    recv_hbm,
    feat_hbm,
    count_hbm,
    own_ref,
    cross_ref,
    chip_ref,
    first_ref,
    grid_ref,
    second_ref,
    send_weight_ref,
    grid_bias_ref,
    edge_bias_ref,
    slot_ref,
    feat_weight_ref,
    send_ref,
    recv_ref,
    feat_ref,
    count_ref,
    starts,
    table,
    even_rows,
    odd_rows,
    even_hidden,
    odd_hidden,
    ids_ref,
    total,
    sems,
):
    channels, grid_rows = grid_ref.shape
    width = second_ref.shape[1]
    pieces = width // LANES
    blocks, block_edges = send_ref.shape
    owned = own_ref.shape[0]
    feats = feat_ref.shape[1]
    step_rows = grid_rows // GRID_STEPS

    def grid_copy(step):
        part = pl.ds(pl.multiple_of(step * step_rows, step_rows), step_rows)
        return pltpu.make_async_copy(grid_hbm.at[:, part], grid_ref.at[:, part], sems.at[step])

    pairs = [
        (first_hbm, first_ref),
        (second_hbm, second_ref),
        (send_weight_hbm, send_weight_ref),
        (grid_bias_hbm, grid_bias_ref),
        (edge_bias_hbm, edge_bias_ref),
        (send_hbm, send_ref),
        (slot_hbm, slot_ref),
        (feat_weight_hbm, feat_weight_ref),
        (recv_hbm, recv_ref),
        (feat_hbm, feat_ref),
        (count_hbm, count_ref),
        (send_ref, starts),
    ]
    copies = [
        pltpu.make_async_copy(source, target, sems.at[GRID_STEPS + at])
        for at, (source, target) in enumerate(pairs)
    ]
    first_copy, second_copy, send_weight_copy, grid_bias_copy, edge_bias_copy, send_copy = copies[:6]
    slot_copy, starts_copy = copies[6], copies[-1]
    for copy in (send_copy, slot_copy, grid_copy(0), first_copy, grid_bias_copy, second_copy):
        copy.start()
    for copy in (edge_bias_copy, send_weight_copy):
        copy.start()
    for step in range(1, GRID_STEPS):
        grid_copy(step).start()
    for copy in copies[7:-1]:
        copy.start()
    send_copy.wait()
    senders = send_ref[...]
    send_ref[...] = (senders // 8) * (8 * pieces) + senders % 8
    starts_copy.start()
    slot_copy.wait()
    place = place_ref[0]
    ids_ref[...] = jnp.broadcast_to(
        ids_of_rows(slot_ref[...], (place - 1) * owned, 3 * owned), ids_ref.shape
    )
    total[...] = jnp.zeros_like(total)

    def turn(step):
        return grid_ref[:, step * step_rows : (step + 1) * step_rows].T

    def store(step, value):
        rows = (value + edge_bias).astype(BF16).astype(F32)
        for group in range(step_rows // 8):
            for piece in range(pieces):
                at = ((step * step_rows // 8 + group) * pieces + piece) * 8
                table[at : at + 8, :] = rows[
                    group * 8 : group * 8 + 8, piece * LANES : (piece + 1) * LANES
                ]

    grid_copy(0).wait()
    turned = turn(0)
    first_copy.wait()
    first_ref[...] = first_ref[...] * 0.5
    first, second, third = {0: mm(turned, first_ref[...])}, {}, {}
    for copy in (grid_bias_copy, second_copy, edge_bias_copy, send_weight_copy):
        copy.wait()
    grid_bias = 0.5 * grid_bias_ref[...]
    edge_bias = 0.5 * edge_bias_ref[...]
    send_weight_ref[...] = send_weight_ref[...] * 0.5
    for step in range(1, GRID_STEPS):
        grid_copy(step).wait()
    for step in range(1, GRID_STEPS + 3):
        turned = turn(step) if step < GRID_STEPS else None
        if step - 3 in third:
            store(step - 3, third.pop(step - 3))
        if step - 2 in second:
            code = layer_norm(second.pop(step - 2)).astype(BF16)
        else:
            code = None
        if step - 1 in first:
            hidden = silu_half(first.pop(step - 1) + grid_bias).astype(BF16)
        else:
            hidden = None
        if code is not None:
            third[step - 2] = mm(code, send_weight_ref[...])
        if hidden is not None:
            second[step - 1] = mm(hidden, second_ref[...])
        if turned is not None:
            first[step] = mm(turned, first_ref[...])
    for copy in copies[7:]:
        copy.wait()
    used = count_ref[...]
    feat_weight = 0.5 * feat_weight_ref[...].astype(F32)
    feat_weight = jnp.concatenate([feat_weight, jnp.zeros((8 - feats, width), F32)], axis=0)
    feat_weight = feat_weight.astype(BF16)
    group = CHUNK_BLOCKS
    chunks = blocks // group
    part_rows = 64

    def gather(chunk, edges, target):
        for edge in edges:
            start = starts[chunk * group + edge // block_edges, edge % block_edges]
            target[pl.ds(edge // 8 * (8 * pieces) + edge % 8, pieces, stride=8), :] = table[
                pl.ds(start, pieces, stride=8), :
            ]

    def rows_of(source, first, count):
        return jnp.concatenate(
            [
                jnp.concatenate(
                    [
                        source[pl.ds((at * pieces + piece) * 8, 8), :]
                        for at in range(first // 8, (first + count) // 8)
                    ],
                    axis=0,
                )
                for piece in range(pieces)
            ],
            axis=1,
        )

    def add_sums(chunk, hidden):
        here = [chunk * group + b for b in range(group)]
        receivers = [jnp.where(b < used, recv_ref[pl.ds(b, 1), :], -2) for b in here]
        spread = jnp.concatenate([(ids_ref[...] == row).astype(F32) for row in receivers], axis=1)
        total[...] += mm(spread.astype(BF16), hidden[...])

    def work(chunk, source, target, hidden, hidden_before):
        here = [chunk * group + b for b in range(group)]
        feat = jnp.concatenate([feat_ref[b] for b in here], axis=1)
        feat = jnp.concatenate([feat, jnp.zeros((8 - feats, feat.shape[1]), F32)], axis=0)
        extra = mm(feat.T.astype(BF16), feat_weight)
        add_sums(jnp.maximum(chunk - 1, 0), hidden_before)
        after = jnp.minimum(chunk + 1, chunks - 1)
        for first in range(0, group * block_edges, part_rows):
            gather(after, range(first, first + part_rows), target)
            half = rows_of(source, first, part_rows) + extra[first : first + part_rows]
            hidden[first : first + part_rows, :] = silu_half(half).astype(BF16)

    def edge_step(step, carry):
        work(2 * step, even_rows, odd_rows, even_hidden, odd_hidden)
        work(2 * step + 1, odd_rows, even_rows, odd_hidden, even_hidden)
        return carry

    odd_hidden[...] = jnp.zeros_like(odd_hidden)
    gather(0, range(group * block_edges), even_rows)
    lax.fori_loop(0, chunks // 2, edge_step, 0)
    add_sums(chunks - 1, odd_hidden)
    odd = place % 2 == 1
    below, above = total[:owned].astype(BF16), total[2 * owned :].astype(BF16)
    own_ref[...] = total[owned : 2 * owned]
    cross_ref[...] = jnp.where(odd, above, below)
    chip_ref[...] = jnp.where(odd, below, above)


def wanted_kernel(owned, slot_ref, send_ref, wanted_ref):
    nodes = slot_ref.shape[1]
    blocks, block_edges = send_ref.shape
    places = wanted_ref.shape[1]
    chunk = LANES
    per_chunk = chunk // owned * SEND_CAP
    row, column = iota((chunk, chunk), 0), iota((chunk, chunk), 1)
    before = ((row > column) & (row // owned == column // owned)).astype(F32).astype(BF16)
    local_owner = (iota((chunk, LANES), 0) // owned * SEND_CAP).astype(F32)

    def find(index, best):
        ids = ids_of_rows(slot_ref[...], index * chunk, chunk)
        hit = jnp.zeros((chunk, block_edges), F32)
        for b in range(blocks):
            hit = jnp.maximum(hit, (ids == send_ref[b : b + 1, :]).astype(F32))
        hit = jnp.broadcast_to(jnp.max(hit, axis=1, keepdims=True), (chunk, LANES))
        rank = mm(before, hit.astype(BF16)) + local_owner
        spot = jnp.where(hit > 0, rank.astype(I32) + index * per_chunk, -1)
        spot = jnp.concatenate([spot] * (places // LANES), axis=1)
        found = jnp.where(spot == iota((chunk, places), 1), ids, -1)
        return jnp.maximum(best, jnp.max(found, axis=0, keepdims=True))

    best = lax.fori_loop(0, nodes // chunk, find, jnp.full((1, places), -1, I32), unroll=2)
    best = best.astype(F32)
    for b in range(blocks):
        senders = jnp.broadcast_to(send_ref[b : b + 1, :].astype(F32), (block_edges, block_edges)).T
        senders = jnp.concatenate([senders] * (places // LANES), axis=1)
        wanted_ref[b * block_edges : (b + 1) * block_edges, :] = (
            (senders == best).astype(F32).astype(BF16)
        )


def supply_kernel(
    blocks,
    place_ref,
    slot_ref,
    request_ref,
    latent_ref,
    edge_out_ref,
    node_input_ref,
    node_bias_ref,
    supply_ref,
    upper_ref,
    lower_ref,
):
    width = latent_ref.shape[1]
    upper_ref[...] = mm(latent_ref[...], node_input_ref[:width]) + node_bias_ref[...]
    lower_ref[...] = mm(edge_out_ref[...], node_input_ref[width:]).astype(BF16)
    owned = supply_ref.shape[1]
    devices = supply_ref.shape[0] // SEND_CAP
    per_device = request_ref.shape[0] // devices
    ids = ids_of_rows(slot_ref[...], place_ref[0] * owned, owned)
    lane = iota((owned, LANES), 1)
    used = jnp.zeros((owned, LANES), F32)
    for d in range(devices):
        hit = jnp.zeros((owned, request_ref.shape[1]), F32)
        for b in range(blocks):
            at = d * per_device + b
            hit = jnp.maximum(hit, (ids == request_ref[at : at + 1, :]).astype(F32))
        used = jnp.where(lane == d, jnp.max(hit, axis=1, keepdims=True), used)
    before = (iota((owned, owned), 0) > iota((owned, owned), 1)).astype(F32).astype(BF16)
    rank = jnp.where(used > 0, mm(before, used.astype(BF16)), -1.0)
    rank = jnp.concatenate([rank, jnp.full((LANES - owned, LANES), -1.0, F32)], axis=0).T
    slots = iota((SEND_CAP, owned), 0).astype(F32)
    supply = jnp.concatenate(
        [(rank[d : d + 1, :owned] == slots).astype(F32) for d in range(devices)], axis=0
    )
    supply_ref[...] = supply.astype(BF16)


def node_kernel(
    own_ref,
    from_cross_ref,
    from_chip_ref,
    latent_ref,
    upper_ref,
    lower_ref,
    node_out_ref,
    node_gain_ref,
    mesh_sender_ref,
    supply_ref,
    encoded_ref,
    rows_ref,
):
    latent = latent_ref[...]
    node_sum = own_ref[...] + from_cross_ref[...].astype(F32) + from_chip_ref[...].astype(F32)
    hidden = silu(upper_ref[...] + mm(node_sum.astype(BF16), lower_ref[...])).astype(BF16)
    encoded = latent.astype(F32) + layer_norm(mm(hidden, node_out_ref[...])) * node_gain_ref[...]
    encoded = encoded.astype(BF16)
    encoded_ref[...] = encoded
    sender_code = mm(encoded, mesh_sender_ref[...]).astype(BF16)
    rows_ref[...] = mm(supply_ref[...], sender_code).astype(BF16)


def receiver_kernel(
    place_ref,
    slot_ref,
    recv_ref,
    encoded_ref,
    mesh_receiver_ref,
    message_bias_ref,
    message_out_ref,
    update_input_ref,
    update_bias_ref,
    incoming_ref,
    pick_ref,
    parts_ref,
    upper_ref,
    lower_ref,
):
    owned, width = encoded_ref.shape
    blocks = recv_ref.shape[0]
    ids = ids_of_rows(slot_ref[...], place_ref[0] * owned, owned)
    incoming = jnp.concatenate(
        [(ids == recv_ref[b : b + 1, :]).astype(F32) for b in range(blocks)], axis=1
    )
    pick = incoming.T.astype(BF16)
    pick_ref[...] = jnp.concatenate([pick, pick], axis=1)
    incoming_ref[...] = incoming.astype(BF16)
    encoded = encoded_ref[...]
    receiver = mm(encoded, mesh_receiver_ref[...]) + message_bias_ref[...]
    high = receiver.astype(BF16)
    parts_ref[:owned, :] = high
    parts_ref[owned:, :] = (receiver - high.astype(F32)).astype(BF16)
    upper_ref[...] = mm(encoded, update_input_ref[:width]) + update_bias_ref[...]
    lower_ref[...] = mm(message_out_ref[...], update_input_ref[width:]).astype(BF16)


def message_kernel(
    wanted_ref,
    piece_ref,
    incoming_ref,
    pick_ref,
    parts_ref,
    upper_ref,
    lower_ref,
    encoded_ref,
    update_out_ref,
    update_gain_ref,
    out_ref,
):
    chosen = jnp.concatenate([wanted_ref[...], pick_ref[...]], axis=1)
    codes = jnp.concatenate([piece_ref[...], parts_ref[...]], axis=0)
    message = silu(mm(chosen, codes)).astype(BF16)
    message_sum = mm(incoming_ref[...], message).astype(BF16)
    hidden = silu(upper_ref[...] + mm(message_sum, lower_ref[...])).astype(BF16)
    out = layer_norm(mm(hidden, update_out_ref[...])) * update_gain_ref[...]
    out_ref[...] = (encoded_ref[...].astype(F32) + out).astype(BF16)


def call(kernel, out_shape, spaces, scratch=(), flops=0, moved=0, vmem=8):
    return pl.pallas_call(
        kernel,
        out_shape=out_shape,
        in_specs=[pl.BlockSpec(memory_space=space) for space in spaces],
        out_specs=jax.tree.map(lambda _: pl.BlockSpec(memory_space=VMEM), out_shape),
        scratch_shapes=scratch,
        compiler_params=pltpu.CompilerParams(vmem_limit_bytes=vmem * MEBI),
        cost_estimate=pl.CostEstimate(flops=flops, bytes_accessed=moved, transcendentals=0),
    )


def hold(value):
    return value if value.size == 1 else pltpu.with_memory_space_constraint(value, HBM)


def shape(*sizes, kind=BF16):
    return jax.ShapeDtypeStruct(sizes, kind)


def per_device(
    grid_in,
    grid_first,
    grid_bias,
    grid_second,
    send_weight,
    edge_bias,
    feat_weight,
    edge_out,
    node_input,
    node_bias,
    node_out,
    node_gain,
    mesh_sender,
    mesh_receiver,
    message_bias,
    message_out,
    update_input,
    update_bias,
    update_out,
    update_gain,
    mesh_latent,
    g2m_send,
    g2m_recv,
    g2m_feat,
    g2m_count,
    mesh_slot,
    mesh_send,
    mesh_recv,
):
    devices = lax.axis_size("bulk")
    position = lax.axis_index("bulk")
    place = position.astype(I32).reshape(1)
    owned, width = mesh_latent.shape
    grid_rows = grid_in.shape[0]
    places = devices * SEND_CAP
    edges = mesh_send.size
    slot = mesh_slot.reshape(1, -1)
    row = lambda vector: vector.reshape(1, -1)

    requests = lax.all_to_all(jnp.tile(mesh_send, (devices, 1)), "bulk", 0, 0, tiled=True)
    operands = (
        grid_first,
        grid_in.T,
        grid_second,
        send_weight,
        row(grid_bias),
        row(edge_bias),
        slot,
        feat_weight,
        g2m_send,
        g2m_recv,
        g2m_feat,
        g2m_count.reshape(1, 1),
    )
    own, cross, chip = call(
        edge_kernel,
        (shape(owned, width, kind=F32), shape(owned, width), shape(owned, width)),
        [SMEM] + [HBM] * len(operands),
        scratch=[VMEM(value.shape, value.dtype) for value in operands]
        + [
            SMEM(g2m_send.shape, I32),
            VMEM((grid_rows * (width // LANES), LANES), F32),
            VMEM((CHUNK_BLOCKS * g2m_send.shape[1] * (width // LANES), LANES), F32),
            VMEM((CHUNK_BLOCKS * g2m_send.shape[1] * (width // LANES), LANES), F32),
            VMEM((CHUNK_BLOCKS * g2m_send.shape[1], width), BF16),
            VMEM((CHUNK_BLOCKS * g2m_send.shape[1], width), BF16),
            VMEM((3 * owned, LANES), I32),
            VMEM((3 * owned, width), F32),
            pltpu.SemaphoreType.DMA((len(operands) + GRID_STEPS,)),
        ],
        flops=10_000_000_000,
        moved=4_000_000,
        vmem=32,
    )(place, *[hold(value) for value in operands])
    requests, _ = lax.optimization_barrier((requests, own))
    crossing = [(d, d + 1) for d in range(1, devices - 1, 2)]
    within = [(d, d + 1) for d in range(0, devices, 2)]
    both = lambda pairs: pairs + [(b, a) for a, b in pairs]
    from_cross = lax.ppermute(cross, "bulk", both(crossing))
    from_chip = lax.ppermute(chip, "bulk", both(within))
    supply, upper, lower = call(
        functools.partial(supply_kernel, mesh_send.shape[0]),
        (shape(places, owned), shape(owned, width, kind=F32), shape(width, width)),
        [SMEM] + [VMEM] * 6,
        flops=500_000_000,
        moved=500_000,
    )(place, slot, requests, mesh_latent, edge_out, node_input, row(node_bias))
    encoded, rows = call(
        node_kernel,
        (shape(owned, width), shape(places, width)),
        [VMEM] * 10,
        flops=500_000_000,
        moved=4_000_000,
    )(
        own,
        from_cross,
        from_chip,
        mesh_latent,
        upper,
        lower,
        node_out,
        row(node_gain),
        mesh_sender,
        supply,
    )
    piece = lax.all_to_all(rows, "bulk", 0, 0, tiled=True)
    mesh_send, _ = lax.optimization_barrier((mesh_send, encoded))
    wanted = call(
        functools.partial(wanted_kernel, owned),
        shape(edges, places),
        [VMEM] * 2,
        flops=1_000_000_000,
        moved=500_000,
    )(slot, mesh_send)
    incoming, pick, parts, upper, lower = call(
        receiver_kernel,
        (
            shape(owned, edges),
            shape(edges, 2 * owned),
            shape(2 * owned, width),
            shape(owned, width, kind=F32),
            shape(width, width),
        ),
        [SMEM] + [VMEM] * 8,
        flops=1_000_000_000,
        moved=4_000_000,
    )(
        place,
        slot,
        mesh_recv,
        encoded,
        mesh_receiver,
        row(message_bias),
        message_out,
        update_input,
        row(update_bias),
    )
    return call(
        message_kernel,
        shape(owned, width),
        [VMEM] * 10,
        flops=1_000_000_000,
        moved=4_000_000,
    )(
        wanted,
        piece,
        incoming,
        pick,
        parts,
        upper,
        lower,
        encoded,
        update_out,
        row(update_gain),
    )


def solution(mesh):
    split = {0: ("groups", "bulk"), 20: "bulk", 21: "bulk", 22: "bulk", 23: "bulk", 24: "bulk"}
    split.update({26: "bulk", 27: "bulk"})
    placed = tuple(P(split[at]) if at in split else P() for at in range(28))
    return jax.shard_map(
        per_device,
        mesh=mesh,
        in_specs=placed,
        out_specs=P(("groups", "bulk"), None),
        check_vma=False,
    )
```

```python
import functools
import math

import jax
import jax.numpy as jnp
from jax import lax
from jax.experimental import pallas as pl
from jax.experimental.pallas import tpu as pltpu
from jax.sharding import PartitionSpec as P

F32 = jnp.float32
BF16 = jnp.bfloat16
I32 = jnp.int32
SEND_CAP = 16
LANES = 128
VMEM = pltpu.VMEM
SMEM = pltpu.SMEM
HBM = pltpu.HBM
GRID_STEPS = 4
CHUNK_BLOCKS = 4
MEBI = 1024 * 1024


def mm(left, right):
    return jnp.dot(left, right, preferred_element_type=F32)


def mm_nt(left, right):
    return lax.dot_general(left, right, (((1,), (1,)), ((), ())), preferred_element_type=F32)


def silu_half(half):
    return half + half * jnp.tanh(half)


def silu(value):
    return silu_half(0.5 * value)


def layer_norm(value):
    center = value - jnp.mean(value, axis=-1, keepdims=True)
    spread = jnp.mean(center * center, axis=-1, keepdims=True)
    return center * lax.rsqrt(spread + 1e-05)


def lane_mean(value):
    width = value.shape[1]
    sums = sum(value[:, at : at + LANES] for at in range(0, width, LANES))
    high = sums.astype(BF16)
    low = (sums - high.astype(F32)).astype(BF16)
    weight = jnp.full((2 * LANES, LANES), 1.0 / width, BF16)
    return mm(jnp.concatenate([high, low], axis=1), weight)


def wide_layer_norm(value):
    wide = lambda mean: jnp.concatenate([mean] * (value.shape[1] // LANES), axis=1)
    center = value - wide(lane_mean(value))
    return center * wide(lax.rsqrt(lane_mean(center * center) + 1e-05))


def iota(shape, dim):
    return lax.broadcasted_iota(I32, shape, dim)


def one_hot(columns, rows):
    hit = columns.astype(jnp.int16) == lax.broadcasted_iota(jnp.int16, (rows, columns.shape[1]), 0)
    return jnp.where(hit, jnp.ones((), BF16), jnp.zeros((), BF16))


def ids_of_rows(slot, first, count):
    nodes = slot.shape[1]
    rows = iota((count, nodes), 0) + first
    return jnp.max(jnp.where(slot == rows, iota((count, nodes), 1), -1), axis=1, keepdims=True)


def edge_kernel(
    place_ref,
    first_hbm,
    grid_hbm,
    second_hbm,
    send_weight_hbm,
    grid_bias_hbm,
    edge_bias_hbm,
    slot_hbm,
    feat_weight_hbm,
    send_hbm,
    recv_hbm,
    feat_hbm,
    count_hbm,
    own_ref,
    cross_ref,
    chip_ref,
    first_ref,
    grid_ref,
    second_ref,
    send_weight_ref,
    grid_bias_ref,
    edge_bias_ref,
    slot_ref,
    feat_weight_ref,
    send_ref,
    recv_ref,
    feat_ref,
    count_ref,
    starts,
    table,
    even_rows,
    odd_rows,
    even_hidden,
    odd_hidden,
    ids_ref,
    total,
    sems,
):
    channels, grid_rows = grid_ref.shape
    width = second_ref.shape[1]
    pieces = width // LANES
    blocks, block_edges = send_ref.shape
    owned = own_ref.shape[0]
    feats = feat_ref.shape[1]
    step_rows = grid_rows // GRID_STEPS

    def grid_copy(step):
        part = pl.ds(pl.multiple_of(step * step_rows, step_rows), step_rows)
        return pltpu.make_async_copy(grid_hbm.at[:, part], grid_ref.at[:, part], sems.at[step])

    pairs = [
        (first_hbm, first_ref),
        (second_hbm, second_ref),
        (send_weight_hbm, send_weight_ref),
        (grid_bias_hbm, grid_bias_ref),
        (edge_bias_hbm, edge_bias_ref),
        (send_hbm, send_ref),
        (slot_hbm, slot_ref),
        (feat_weight_hbm, feat_weight_ref),
        (recv_hbm, recv_ref),
        (feat_hbm, feat_ref),
        (count_hbm, count_ref),
        (send_ref, starts),
    ]
    copies = [
        pltpu.make_async_copy(source, target, sems.at[GRID_STEPS + at])
        for at, (source, target) in enumerate(pairs)
    ]
    first_copy, second_copy, send_weight_copy, grid_bias_copy, edge_bias_copy, send_copy = copies[:6]
    slot_copy, starts_copy = copies[6], copies[-1]
    first_copy.start()
    grid_copy(0).start()
    for copy in copies[1:-1]:
        copy.start()
    for step in range(1, GRID_STEPS):
        grid_copy(step).start()
    send_copy.wait()
    senders = send_ref[...]
    send_ref[...] = (senders // 8) * (8 * pieces) + senders % 8
    starts_copy.start()
    slot_copy.wait()
    place = place_ref[0]
    ids_ref[...] = jnp.broadcast_to(
        ids_of_rows(slot_ref[...], (place - 1) * owned, 3 * owned), ids_ref.shape
    )
    total[...] = jnp.zeros_like(total)
    first_copy.wait()
    first_ref[...] = first_ref[...] * 0.5
    second_copy.wait()
    send_weight_copy.wait()
    send_weight_ref[...] = send_weight_ref[...] * 0.5
    grid_bias_copy.wait()
    edge_bias_copy.wait()
    grid_bias = 0.5 * grid_bias_ref[...]
    edge_bias = 0.5 * edge_bias_ref[...]
    def turn(step):
        return grid_ref[:, step * step_rows : (step + 1) * step_rows].T

    def store(step, value):
        rows = (value + edge_bias).astype(BF16).astype(F32)
        for group in range(step_rows // 8):
            for piece in range(pieces):
                at = ((step * step_rows // 8 + group) * pieces + piece) * 8
                table[at : at + 8, :] = rows[
                    group * 8 : group * 8 + 8, piece * LANES : (piece + 1) * LANES
                ]

    grid_copy(0).wait()
    first, second, third = {}, {}, {}
    first[0] = mm(turn(0), first_ref[...])
    for step in range(1, GRID_STEPS):
        grid_copy(step).wait()
    for step in range(1, GRID_STEPS + 3):
        turned = turn(step) if step < GRID_STEPS else None
        if step - 3 in third:
            store(step - 3, third.pop(step - 3))
        if step - 2 in second:
            code = wide_layer_norm(second.pop(step - 2)).astype(BF16)
        else:
            code = None
        if step - 1 in first:
            hidden = silu_half(first.pop(step - 1) + grid_bias).astype(BF16)
        else:
            hidden = None
        if code is not None:
            third[step - 2] = mm(code, send_weight_ref[...])
        if hidden is not None:
            second[step - 1] = mm(hidden, second_ref[...])
        if turned is not None:
            first[step] = mm(turned, first_ref[...])
    for copy in copies[7:]:
        copy.wait()
    used = count_ref[...]
    feat_weight = 0.5 * feat_weight_ref[...].astype(F32)
    feat_weight = jnp.concatenate([feat_weight, jnp.zeros((8 - feats, width), F32)], axis=0)
    feat_weight = feat_weight.astype(BF16)
    group = CHUNK_BLOCKS
    chunks = blocks // group
    part_rows = 64

    def gather(chunk, edges, target):
        for edge in edges:
            start = starts[chunk * group + edge // block_edges, edge % block_edges]
            target[pl.ds(edge // 8 * (8 * pieces) + edge % 8, pieces, stride=8), :] = table[
                pl.ds(start, pieces, stride=8), :
            ]

    def rows_of(source, first, count):
        return jnp.concatenate(
            [
                jnp.concatenate(
                    [
                        source[pl.ds((at * pieces + piece) * 8, 8), :]
                        for at in range(first // 8, (first + count) // 8)
                    ],
                    axis=0,
                )
                for piece in range(pieces)
            ],
            axis=1,
        )

    def add_sums(chunk, hidden):
        here = [chunk * group + b for b in range(group)]
        receivers = [jnp.where(b < used, recv_ref[pl.ds(b, 1), :], -2) for b in here]
        spread = jnp.concatenate([(ids_ref[...] == row).astype(F32) for row in receivers], axis=1)
        total[...] += mm(spread.astype(BF16), hidden[...])

    def work(chunk, source, target, hidden, hidden_before):
        here = [chunk * group + b for b in range(group)]
        feat = jnp.concatenate([feat_ref[b] for b in here], axis=1)
        feat = jnp.concatenate([feat, jnp.zeros((8 - feats, feat.shape[1]), F32)], axis=0)
        extra = mm(feat.T.astype(BF16), feat_weight)
        add_sums(jnp.maximum(chunk - 1, 0), hidden_before)
        after = jnp.minimum(chunk + 1, chunks - 1)
        for first in range(0, group * block_edges, part_rows):
            gather(after, range(first, first + part_rows), target)
            half = rows_of(source, first, part_rows) + extra[first : first + part_rows]
            hidden[first : first + part_rows, :] = silu_half(half).astype(BF16)

    def edge_step(step, carry):
        work(2 * step, even_rows, odd_rows, even_hidden, odd_hidden)
        work(2 * step + 1, odd_rows, even_rows, odd_hidden, even_hidden)
        return carry

    odd_hidden[...] = jnp.zeros_like(odd_hidden)
    gather(0, range(group * block_edges), even_rows)
    lax.fori_loop(0, chunks // 2, edge_step, 0)
    add_sums(chunks - 1, odd_hidden)
    odd = place % 2 == 1
    below, above = total[:owned].astype(BF16), total[2 * owned :].astype(BF16)
    own_ref[...] = total[owned : 2 * owned]
    cross_ref[...] = jnp.where(odd, above, below)
    chip_ref[...] = jnp.where(odd, below, above)


def wanted_kernel(owned, slot_ref, send_ref, wanted_ref):
    nodes = slot_ref.shape[1]
    blocks, block_edges = send_ref.shape
    places = wanted_ref.shape[1]
    chunk = LANES
    per_chunk = chunk // owned * SEND_CAP
    row, column = iota((chunk, chunk), 0), iota((chunk, chunk), 1)
    before = ((row > column) & (row // owned == column // owned)).astype(F32).astype(BF16)
    local_owner = (iota((chunk, LANES), 0) // owned * SEND_CAP).astype(F32)

    def find(index, best):
        ids = ids_of_rows(slot_ref[...], index * chunk, chunk)
        hit = jnp.zeros((chunk, block_edges), F32)
        for b in range(blocks):
            hit = jnp.maximum(hit, (ids == send_ref[b : b + 1, :]).astype(F32))
        hit = jnp.broadcast_to(jnp.max(hit, axis=1, keepdims=True), (chunk, LANES))
        rank = mm(before, hit.astype(BF16)) + local_owner
        spot = jnp.where(hit > 0, rank.astype(I32) + index * per_chunk, -1)
        spot = jnp.concatenate([spot] * (places // LANES), axis=1)
        found = jnp.where(spot == iota((chunk, places), 1), ids, -1)
        return jnp.maximum(best, jnp.max(found, axis=0, keepdims=True))

    best = lax.fori_loop(0, nodes // chunk, find, jnp.full((1, places), -1, I32), unroll=2)
    best = best.astype(F32)
    for b in range(blocks):
        senders = jnp.broadcast_to(send_ref[b : b + 1, :].astype(F32), (block_edges, block_edges)).T
        senders = jnp.concatenate([senders] * (places // LANES), axis=1)
        wanted_ref[b * block_edges : (b + 1) * block_edges, :] = (
            (senders == best).astype(F32).astype(BF16)
        )


def supply_kernel(
    blocks,
    place_ref,
    slot_ref,
    request_ref,
    latent_ref,
    edge_out_ref,
    node_input_ref,
    node_bias_ref,
    supply_ref,
    upper_ref,
    lower_ref,
):
    width = latent_ref.shape[1]
    upper_ref[...] = mm(latent_ref[...], node_input_ref[:width]) + node_bias_ref[...]
    lower_ref[...] = mm(edge_out_ref[...], node_input_ref[width:]).astype(BF16)
    owned = supply_ref.shape[1]
    devices = supply_ref.shape[0] // SEND_CAP
    per_device = request_ref.shape[0] // devices
    ids = ids_of_rows(slot_ref[...], place_ref[0] * owned, owned)
    lane = iota((owned, LANES), 1)
    used = jnp.zeros((owned, LANES), F32)
    for d in range(devices):
        hit = jnp.zeros((owned, request_ref.shape[1]), F32)
        for b in range(blocks):
            at = d * per_device + b
            hit = jnp.maximum(hit, (ids == request_ref[at : at + 1, :]).astype(F32))
        used = jnp.where(lane == d, jnp.max(hit, axis=1, keepdims=True), used)
    before = (iota((owned, owned), 0) > iota((owned, owned), 1)).astype(F32).astype(BF16)
    rank = jnp.where(used > 0, mm(before, used.astype(BF16)), -1.0)
    rank = jnp.concatenate([rank, jnp.full((LANES - owned, LANES), -1.0, F32)], axis=0).T
    slots = iota((SEND_CAP, owned), 0).astype(F32)
    supply = jnp.concatenate(
        [(rank[d : d + 1, :owned] == slots).astype(F32) for d in range(devices)], axis=0
    )
    supply_ref[...] = supply.astype(BF16)


def node_kernel(
    own_ref,
    from_cross_ref,
    from_chip_ref,
    latent_ref,
    upper_ref,
    lower_ref,
    node_out_ref,
    node_gain_ref,
    mesh_sender_ref,
    supply_ref,
    encoded_ref,
    rows_ref,
):
    latent = latent_ref[...]
    node_sum = own_ref[...] + from_cross_ref[...].astype(F32) + from_chip_ref[...].astype(F32)
    hidden = silu(upper_ref[...] + mm(node_sum.astype(BF16), lower_ref[...])).astype(BF16)
    encoded = latent.astype(F32) + layer_norm(mm(hidden, node_out_ref[...])) * node_gain_ref[...]
    encoded = encoded.astype(BF16)
    encoded_ref[...] = encoded
    sender_code = mm(encoded, mesh_sender_ref[...]).astype(BF16)
    rows_ref[...] = mm(supply_ref[...], sender_code).astype(BF16)


def receiver_kernel(
    place_ref,
    slot_ref,
    recv_ref,
    encoded_ref,
    mesh_receiver_ref,
    message_bias_ref,
    message_out_ref,
    update_input_ref,
    update_bias_ref,
    incoming_ref,
    pick_ref,
    parts_ref,
    upper_ref,
    lower_ref,
):
    owned, width = encoded_ref.shape
    blocks = recv_ref.shape[0]
    ids = ids_of_rows(slot_ref[...], place_ref[0] * owned, owned)
    incoming = jnp.concatenate(
        [(ids == recv_ref[b : b + 1, :]).astype(F32) for b in range(blocks)], axis=1
    )
    pick = incoming.T.astype(BF16)
    pick_ref[...] = jnp.concatenate([pick, pick], axis=1)
    incoming_ref[...] = incoming.astype(BF16)
    encoded = encoded_ref[...]
    receiver = mm(encoded, mesh_receiver_ref[...]) + message_bias_ref[...]
    high = receiver.astype(BF16)
    parts_ref[:owned, :] = high
    parts_ref[owned:, :] = (receiver - high.astype(F32)).astype(BF16)
    upper_ref[...] = mm(encoded, update_input_ref[:width]) + update_bias_ref[...]
    lower_ref[...] = mm(message_out_ref[...], update_input_ref[width:]).astype(BF16)


def message_kernel(
    wanted_ref,
    piece_ref,
    incoming_ref,
    pick_ref,
    parts_ref,
    upper_ref,
    lower_ref,
    encoded_ref,
    update_out_ref,
    update_gain_ref,
    out_ref,
):
    chosen = jnp.concatenate([wanted_ref[...], pick_ref[...]], axis=1)
    codes = jnp.concatenate([piece_ref[...], parts_ref[...]], axis=0)
    message = silu(mm(chosen, codes)).astype(BF16)
    message_sum = mm(incoming_ref[...], message).astype(BF16)
    hidden = silu(upper_ref[...] + mm(message_sum, lower_ref[...])).astype(BF16)
    out = layer_norm(mm(hidden, update_out_ref[...])) * update_gain_ref[...]
    out_ref[...] = (encoded_ref[...].astype(F32) + out).astype(BF16)


def call(kernel, out_shape, spaces, scratch=(), flops=0, moved=0, vmem=8):
    return pl.pallas_call(
        kernel,
        out_shape=out_shape,
        in_specs=[pl.BlockSpec(memory_space=space) for space in spaces],
        out_specs=jax.tree.map(lambda _: pl.BlockSpec(memory_space=VMEM), out_shape),
        scratch_shapes=scratch,
        compiler_params=pltpu.CompilerParams(vmem_limit_bytes=vmem * MEBI),
        cost_estimate=pl.CostEstimate(flops=flops, bytes_accessed=moved, transcendentals=0),
    )


def hold(value):
    return value if value.size == 1 else pltpu.with_memory_space_constraint(value, HBM)


def shape(*sizes, kind=BF16):
    return jax.ShapeDtypeStruct(sizes, kind)


def per_device(
    grid_in,
    grid_first,
    grid_bias,
    grid_second,
    send_weight,
    edge_bias,
    feat_weight,
    edge_out,
    node_input,
    node_bias,
    node_out,
    node_gain,
    mesh_sender,
    mesh_receiver,
    message_bias,
    message_out,
    update_input,
    update_bias,
    update_out,
    update_gain,
    mesh_latent,
    g2m_send,
    g2m_recv,
    g2m_feat,
    g2m_count,
    mesh_slot,
    mesh_send,
    mesh_recv,
):
    devices = lax.axis_size("bulk")
    position = lax.axis_index("bulk")
    place = position.astype(I32).reshape(1)
    owned, width = mesh_latent.shape
    grid_rows = grid_in.shape[0]
    places = devices * SEND_CAP
    edges = mesh_send.size
    slot = mesh_slot.reshape(1, -1)
    row = lambda vector: vector.reshape(1, -1)

    requests = lax.all_to_all(jnp.tile(mesh_send, (devices, 1)), "bulk", 0, 0, tiled=True)
    operands = (
        grid_first,
        grid_in.T,
        grid_second,
        send_weight,
        row(grid_bias),
        row(edge_bias),
        slot,
        feat_weight,
        g2m_send,
        g2m_recv,
        g2m_feat,
        g2m_count.reshape(1, 1),
    )
    own, cross, chip = call(
        edge_kernel,
        (shape(owned, width, kind=F32), shape(owned, width), shape(owned, width)),
        [SMEM] + [HBM] * len(operands),
        scratch=[VMEM(value.shape, value.dtype) for value in operands]
        + [
            SMEM(g2m_send.shape, I32),
            VMEM((grid_rows * (width // LANES), LANES), F32),
            VMEM((CHUNK_BLOCKS * g2m_send.shape[1] * (width // LANES), LANES), F32),
            VMEM((CHUNK_BLOCKS * g2m_send.shape[1] * (width // LANES), LANES), F32),
            VMEM((CHUNK_BLOCKS * g2m_send.shape[1], width), BF16),
            VMEM((CHUNK_BLOCKS * g2m_send.shape[1], width), BF16),
            VMEM((3 * owned, LANES), I32),
            VMEM((3 * owned, width), F32),
            pltpu.SemaphoreType.DMA((len(operands) + GRID_STEPS,)),
        ],
        flops=10_000_000_000,
        moved=4_000_000,
        vmem=32,
    )(place, *[hold(value) for value in operands])
    requests, _ = lax.optimization_barrier((requests, own))
    crossing = [(d, d + 1) for d in range(1, devices - 1, 2)]
    within = [(d, d + 1) for d in range(0, devices, 2)]
    both = lambda pairs: pairs + [(b, a) for a, b in pairs]
    from_cross = lax.ppermute(cross, "bulk", both(crossing))
    from_chip = lax.ppermute(chip, "bulk", both(within))
    supply, upper, lower = call(
        functools.partial(supply_kernel, mesh_send.shape[0]),
        (shape(places, owned), shape(owned, width, kind=F32), shape(width, width)),
        [SMEM] + [VMEM] * 6,
        flops=500_000_000,
        moved=500_000,
    )(place, slot, requests, mesh_latent, edge_out, node_input, row(node_bias))
    encoded, rows = call(
        node_kernel,
        (shape(owned, width), shape(places, width)),
        [VMEM] * 10,
        flops=500_000_000,
        moved=4_000_000,
    )(
        own,
        from_cross,
        from_chip,
        mesh_latent,
        upper,
        lower,
        node_out,
        row(node_gain),
        mesh_sender,
        supply,
    )
    piece = lax.all_to_all(rows, "bulk", 0, 0, tiled=True)
    mesh_send, _ = lax.optimization_barrier((mesh_send, encoded))
    wanted = call(
        functools.partial(wanted_kernel, owned),
        shape(edges, places),
        [VMEM] * 2,
        flops=1_000_000_000,
        moved=500_000,
    )(slot, mesh_send)
    incoming, pick, parts, upper, lower = call(
        receiver_kernel,
        (
            shape(owned, edges),
            shape(edges, 2 * owned),
            shape(2 * owned, width),
            shape(owned, width, kind=F32),
            shape(width, width),
        ),
        [SMEM] + [VMEM] * 8,
        flops=1_000_000_000,
        moved=4_000_000,
    )(
        place,
        slot,
        mesh_recv,
        encoded,
        mesh_receiver,
        row(message_bias),
        message_out,
        update_input,
        row(update_bias),
    )
    return call(
        message_kernel,
        shape(owned, width),
        [VMEM] * 10,
        flops=1_000_000_000,
        moved=4_000_000,
    )(
        wanted,
        piece,
        incoming,
        pick,
        parts,
        upper,
        lower,
        encoded,
        update_out,
        row(update_gain),
    )


def solution(mesh):
    split = {0: ("groups", "bulk"), 20: "bulk", 21: "bulk", 22: "bulk", 23: "bulk", 24: "bulk"}
    split.update({26: "bulk", 27: "bulk"})
    placed = tuple(P(split[at]) if at in split else P() for at in range(28))
    return jax.shard_map(
        per_device,
        mesh=mesh,
        in_specs=placed,
        out_specs=P(("groups", "bulk"), None),
        check_vma=False,
    )
```

```python
import functools
import math

import jax
import jax.numpy as jnp
from jax import lax
from jax.experimental import pallas as pl
from jax.experimental.pallas import tpu as pltpu
from jax.sharding import PartitionSpec as P

F32 = jnp.float32
BF16 = jnp.bfloat16
I32 = jnp.int32
SEND_CAP = 16
LANES = 128
VMEM = pltpu.VMEM
SMEM = pltpu.SMEM
HBM = pltpu.HBM
GRID_STEPS = 4
CHUNK_BLOCKS = 2
MEBI = 1024 * 1024


def mm(left, right):
    return jnp.dot(left, right, preferred_element_type=F32)


def mm_nt(left, right):
    return lax.dot_general(left, right, (((1,), (1,)), ((), ())), preferred_element_type=F32)


def silu_half(half):
    return half + half * jnp.tanh(half)


def silu(value):
    return silu_half(0.5 * value)


def layer_norm(value):
    center = value - jnp.mean(value, axis=-1, keepdims=True)
    spread = jnp.mean(center * center, axis=-1, keepdims=True)
    return center * lax.rsqrt(spread + 1e-05)


def iota(shape, dim):
    return lax.broadcasted_iota(I32, shape, dim)


def one_hot(columns, rows):
    hit = columns.astype(jnp.int16) == lax.broadcasted_iota(jnp.int16, (rows, columns.shape[1]), 0)
    return jnp.where(hit, jnp.ones((), BF16), jnp.zeros((), BF16))


def ids_of_rows(slot, first, count):
    nodes = slot.shape[1]
    rows = iota((count, nodes), 0) + first
    return jnp.max(jnp.where(slot == rows, iota((count, nodes), 1), -1), axis=1, keepdims=True)


def edge_kernel(
    place_ref,
    first_hbm,
    grid_hbm,
    second_hbm,
    send_weight_hbm,
    grid_bias_hbm,
    edge_bias_hbm,
    slot_hbm,
    feat_weight_hbm,
    send_hbm,
    recv_hbm,
    feat_hbm,
    count_hbm,
    own_ref,
    cross_ref,
    chip_ref,
    first_ref,
    grid_ref,
    second_ref,
    send_weight_ref,
    grid_bias_ref,
    edge_bias_ref,
    slot_ref,
    feat_weight_ref,
    send_ref,
    recv_ref,
    feat_ref,
    count_ref,
    starts,
    table,
    even_rows,
    odd_rows,
    even_hidden,
    odd_hidden,
    ids_ref,
    total,
    sems,
):
    channels, grid_rows = grid_ref.shape
    width = second_ref.shape[1]
    pieces = width // LANES
    blocks, block_edges = send_ref.shape
    owned = own_ref.shape[0]
    feats = feat_ref.shape[1]
    step_rows = grid_rows // GRID_STEPS

    def grid_copy(step):
        part = pl.ds(pl.multiple_of(step * step_rows, step_rows), step_rows)
        return pltpu.make_async_copy(grid_hbm.at[:, part], grid_ref.at[:, part], sems.at[step])

    pairs = [
        (first_hbm, first_ref),
        (second_hbm, second_ref),
        (send_weight_hbm, send_weight_ref),
        (grid_bias_hbm, grid_bias_ref),
        (edge_bias_hbm, edge_bias_ref),
        (send_hbm, send_ref),
        (slot_hbm, slot_ref),
        (feat_weight_hbm, feat_weight_ref),
        (recv_hbm, recv_ref),
        (feat_hbm, feat_ref),
        (count_hbm, count_ref),
        (send_ref, starts),
    ]
    copies = [
        pltpu.make_async_copy(source, target, sems.at[GRID_STEPS + at])
        for at, (source, target) in enumerate(pairs)
    ]
    first_copy, second_copy, send_weight_copy, grid_bias_copy, edge_bias_copy, send_copy = copies[:6]
    slot_copy, starts_copy = copies[6], copies[-1]
    first_copy.start()
    grid_copy(0).start()
    for copy in copies[1:-1]:
        copy.start()
    for step in range(1, GRID_STEPS):
        grid_copy(step).start()
    send_copy.wait()
    senders = send_ref[...]
    send_ref[...] = (senders // 8) * (8 * pieces) + senders % 8
    starts_copy.start()
    slot_copy.wait()
    place = place_ref[0]
    ids_ref[...] = jnp.broadcast_to(
        ids_of_rows(slot_ref[...], (place - 1) * owned, 3 * owned), ids_ref.shape
    )
    total[...] = jnp.zeros_like(total)
    first_copy.wait()
    first_ref[...] = first_ref[...] * 0.5
    second_copy.wait()
    send_weight_copy.wait()
    send_weight_ref[...] = send_weight_ref[...] * 0.5
    grid_bias_copy.wait()
    edge_bias_copy.wait()
    grid_bias = 0.5 * grid_bias_ref[...]
    edge_bias = 0.5 * edge_bias_ref[...]
    def turn(step):
        return grid_ref[:, step * step_rows : (step + 1) * step_rows].T

    def store(step, value):
        rows = (value + edge_bias).astype(BF16).astype(F32)
        for group in range(step_rows // 8):
            for piece in range(pieces):
                at = ((step * step_rows // 8 + group) * pieces + piece) * 8
                table[at : at + 8, :] = rows[
                    group * 8 : group * 8 + 8, piece * LANES : (piece + 1) * LANES
                ]

    grid_copy(0).wait()
    first, second, third = {}, {}, {}
    first[0] = mm(turn(0), first_ref[...])
    for step in range(1, GRID_STEPS):
        grid_copy(step).wait()
    for step in range(1, GRID_STEPS + 3):
        turned = turn(step) if step < GRID_STEPS else None
        if step - 3 in third:
            store(step - 3, third.pop(step - 3))
        if step - 2 in second:
            code = layer_norm(second.pop(step - 2)).astype(BF16)
        else:
            code = None
        if step - 1 in first:
            hidden = silu_half(first.pop(step - 1) + grid_bias).astype(BF16)
        else:
            hidden = None
        if code is not None:
            third[step - 2] = mm(code, send_weight_ref[...])
        if hidden is not None:
            second[step - 1] = mm(hidden, second_ref[...])
        if turned is not None:
            first[step] = mm(turned, first_ref[...])
    for copy in copies[7:]:
        copy.wait()
    used = count_ref[...]
    feat_weight = 0.5 * feat_weight_ref[...].astype(F32)
    feat_weight = jnp.concatenate([feat_weight, jnp.zeros((8 - feats, width), F32)], axis=0)
    feat_weight = feat_weight.astype(BF16)
    group = CHUNK_BLOCKS
    chunks = blocks // group
    part_rows = 64

    def gather(chunk, edges, target):
        for edge in edges:
            start = starts[chunk * group + edge // block_edges, edge % block_edges]
            target[pl.ds(edge // 8 * (8 * pieces) + edge % 8, pieces, stride=8), :] = table[
                pl.ds(start, pieces, stride=8), :
            ]

    def rows_of(source, first, count):
        return jnp.concatenate(
            [
                jnp.concatenate(
                    [
                        source[pl.ds((at * pieces + piece) * 8, 8), :]
                        for at in range(first // 8, (first + count) // 8)
                    ],
                    axis=0,
                )
                for piece in range(pieces)
            ],
            axis=1,
        )

    def add_sums(chunk, hidden):
        here = [chunk * group + b for b in range(group)]
        receivers = [jnp.where(b < used, recv_ref[pl.ds(b, 1), :], -2) for b in here]
        spread = jnp.concatenate([(ids_ref[...] == row).astype(F32) for row in receivers], axis=1)
        total[...] += mm(spread.astype(BF16), hidden[...])

    def work(chunk, source, target, hidden, hidden_before):
        here = [chunk * group + b for b in range(group)]
        feat = jnp.concatenate([feat_ref[b] for b in here], axis=1)
        feat = jnp.concatenate([feat, jnp.zeros((8 - feats, feat.shape[1]), F32)], axis=0)
        extra = mm(feat.T.astype(BF16), feat_weight)
        add_sums(jnp.maximum(chunk - 1, 0), hidden_before)
        after = jnp.minimum(chunk + 1, chunks - 1)
        for first in range(0, group * block_edges, part_rows):
            gather(after, range(first, first + part_rows), target)
            half = rows_of(source, first, part_rows) + extra[first : first + part_rows]
            hidden[first : first + part_rows, :] = silu_half(half).astype(BF16)

    def edge_step(step, carry):
        work(2 * step, even_rows, odd_rows, even_hidden, odd_hidden)
        work(2 * step + 1, odd_rows, even_rows, odd_hidden, even_hidden)
        return carry

    odd_hidden[...] = jnp.zeros_like(odd_hidden)
    gather(0, range(group * block_edges), even_rows)
    lax.fori_loop(0, chunks // 2, edge_step, 0)
    add_sums(chunks - 1, odd_hidden)
    odd = place % 2 == 1
    below, above = total[:owned].astype(BF16), total[2 * owned :].astype(BF16)
    own_ref[...] = total[owned : 2 * owned]
    cross_ref[...] = jnp.where(odd, above, below)
    chip_ref[...] = jnp.where(odd, below, above)


def wanted_kernel(owned, slot_ref, send_ref, wanted_ref):
    nodes = slot_ref.shape[1]
    blocks, block_edges = send_ref.shape
    places = wanted_ref.shape[1]
    chunk = LANES
    per_chunk = chunk // owned * SEND_CAP
    row, column = iota((chunk, chunk), 0), iota((chunk, chunk), 1)
    before = ((row > column) & (row // owned == column // owned)).astype(F32).astype(BF16)
    local_owner = (iota((chunk, LANES), 0) // owned * SEND_CAP).astype(F32)

    def find(index, best):
        ids = ids_of_rows(slot_ref[...], index * chunk, chunk)
        hit = jnp.zeros((chunk, block_edges), F32)
        for b in range(blocks):
            hit = jnp.maximum(hit, (ids == send_ref[b : b + 1, :]).astype(F32))
        hit = jnp.broadcast_to(jnp.max(hit, axis=1, keepdims=True), (chunk, LANES))
        rank = mm(before, hit.astype(BF16)) + local_owner
        spot = jnp.where(hit > 0, rank.astype(I32) + index * per_chunk, -1)
        spot = jnp.concatenate([spot] * (places // LANES), axis=1)
        found = jnp.where(spot == iota((chunk, places), 1), ids, -1)
        return jnp.maximum(best, jnp.max(found, axis=0, keepdims=True))

    best = lax.fori_loop(0, nodes // chunk, find, jnp.full((1, places), -1, I32), unroll=2)
    best = best.astype(F32)
    for b in range(blocks):
        senders = jnp.broadcast_to(send_ref[b : b + 1, :].astype(F32), (block_edges, block_edges)).T
        senders = jnp.concatenate([senders] * (places // LANES), axis=1)
        wanted_ref[b * block_edges : (b + 1) * block_edges, :] = (
            (senders == best).astype(F32).astype(BF16)
        )


def supply_kernel(
    blocks,
    place_ref,
    slot_ref,
    request_ref,
    latent_ref,
    edge_out_ref,
    node_input_ref,
    node_bias_ref,
    supply_ref,
    upper_ref,
    lower_ref,
):
    width = latent_ref.shape[1]
    upper_ref[...] = mm(latent_ref[...], node_input_ref[:width]) + node_bias_ref[...]
    lower_ref[...] = mm(edge_out_ref[...], node_input_ref[width:]).astype(BF16)
    owned = supply_ref.shape[1]
    devices = supply_ref.shape[0] // SEND_CAP
    per_device = request_ref.shape[0] // devices
    ids = ids_of_rows(slot_ref[...], place_ref[0] * owned, owned)
    lane = iota((owned, LANES), 1)
    used = jnp.zeros((owned, LANES), F32)
    for d in range(devices):
        hit = jnp.zeros((owned, request_ref.shape[1]), F32)
        for b in range(blocks):
            at = d * per_device + b
            hit = jnp.maximum(hit, (ids == request_ref[at : at + 1, :]).astype(F32))
        used = jnp.where(lane == d, jnp.max(hit, axis=1, keepdims=True), used)
    before = (iota((owned, owned), 0) > iota((owned, owned), 1)).astype(F32).astype(BF16)
    rank = jnp.where(used > 0, mm(before, used.astype(BF16)), -1.0)
    rank = jnp.concatenate([rank, jnp.full((LANES - owned, LANES), -1.0, F32)], axis=0).T
    slots = iota((SEND_CAP, owned), 0).astype(F32)
    supply = jnp.concatenate(
        [(rank[d : d + 1, :owned] == slots).astype(F32) for d in range(devices)], axis=0
    )
    supply_ref[...] = supply.astype(BF16)


def node_kernel(
    own_ref,
    from_cross_ref,
    from_chip_ref,
    latent_ref,
    upper_ref,
    lower_ref,
    node_out_ref,
    node_gain_ref,
    mesh_sender_ref,
    supply_ref,
    encoded_ref,
    rows_ref,
):
    latent = latent_ref[...]
    node_sum = own_ref[...] + from_cross_ref[...].astype(F32) + from_chip_ref[...].astype(F32)
    hidden = silu(upper_ref[...] + mm(node_sum.astype(BF16), lower_ref[...])).astype(BF16)
    encoded = latent.astype(F32) + layer_norm(mm(hidden, node_out_ref[...])) * node_gain_ref[...]
    encoded = encoded.astype(BF16)
    encoded_ref[...] = encoded
    sender_code = mm(encoded, mesh_sender_ref[...]).astype(BF16)
    rows_ref[...] = mm(supply_ref[...], sender_code).astype(BF16)


def receiver_kernel(
    place_ref,
    slot_ref,
    recv_ref,
    encoded_ref,
    mesh_receiver_ref,
    message_bias_ref,
    message_out_ref,
    update_input_ref,
    update_bias_ref,
    incoming_ref,
    pick_ref,
    parts_ref,
    upper_ref,
    lower_ref,
):
    owned, width = encoded_ref.shape
    blocks = recv_ref.shape[0]
    ids = ids_of_rows(slot_ref[...], place_ref[0] * owned, owned)
    incoming = jnp.concatenate(
        [(ids == recv_ref[b : b + 1, :]).astype(F32) for b in range(blocks)], axis=1
    )
    pick = incoming.T.astype(BF16)
    pick_ref[...] = jnp.concatenate([pick, pick], axis=1)
    incoming_ref[...] = incoming.astype(BF16)
    encoded = encoded_ref[...]
    receiver = mm(encoded, mesh_receiver_ref[...]) + message_bias_ref[...]
    high = receiver.astype(BF16)
    parts_ref[:owned, :] = high
    parts_ref[owned:, :] = (receiver - high.astype(F32)).astype(BF16)
    upper_ref[...] = mm(encoded, update_input_ref[:width]) + update_bias_ref[...]
    lower_ref[...] = mm(message_out_ref[...], update_input_ref[width:]).astype(BF16)


def message_kernel(
    wanted_ref,
    piece_ref,
    incoming_ref,
    pick_ref,
    parts_ref,
    upper_ref,
    lower_ref,
    encoded_ref,
    update_out_ref,
    update_gain_ref,
    out_ref,
):
    chosen = jnp.concatenate([wanted_ref[...], pick_ref[...]], axis=1)
    codes = jnp.concatenate([piece_ref[...], parts_ref[...]], axis=0)
    message = silu(mm(chosen, codes)).astype(BF16)
    message_sum = mm(incoming_ref[...], message).astype(BF16)
    hidden = silu(upper_ref[...] + mm(message_sum, lower_ref[...])).astype(BF16)
    out = layer_norm(mm(hidden, update_out_ref[...])) * update_gain_ref[...]
    out_ref[...] = (encoded_ref[...].astype(F32) + out).astype(BF16)


def call(kernel, out_shape, spaces, scratch=(), flops=0, moved=0, vmem=8):
    return pl.pallas_call(
        kernel,
        out_shape=out_shape,
        in_specs=[pl.BlockSpec(memory_space=space) for space in spaces],
        out_specs=jax.tree.map(lambda _: pl.BlockSpec(memory_space=VMEM), out_shape),
        scratch_shapes=scratch,
        compiler_params=pltpu.CompilerParams(vmem_limit_bytes=vmem * MEBI),
        cost_estimate=pl.CostEstimate(flops=flops, bytes_accessed=moved, transcendentals=0),
    )


def hold(value):
    return value if value.size == 1 else pltpu.with_memory_space_constraint(value, HBM)


def shape(*sizes, kind=BF16):
    return jax.ShapeDtypeStruct(sizes, kind)


def per_device(
    grid_in,
    grid_first,
    grid_bias,
    grid_second,
    send_weight,
    edge_bias,
    feat_weight,
    edge_out,
    node_input,
    node_bias,
    node_out,
    node_gain,
    mesh_sender,
    mesh_receiver,
    message_bias,
    message_out,
    update_input,
    update_bias,
    update_out,
    update_gain,
    mesh_latent,
    g2m_send,
    g2m_recv,
    g2m_feat,
    g2m_count,
    mesh_slot,
    mesh_send,
    mesh_recv,
):
    devices = lax.axis_size("bulk")
    position = lax.axis_index("bulk")
    place = position.astype(I32).reshape(1)
    owned, width = mesh_latent.shape
    grid_rows = grid_in.shape[0]
    places = devices * SEND_CAP
    edges = mesh_send.size
    slot = mesh_slot.reshape(1, -1)
    row = lambda vector: vector.reshape(1, -1)

    requests = lax.all_to_all(jnp.tile(mesh_send, (devices, 1)), "bulk", 0, 0, tiled=True)
    operands = (
        grid_first,
        grid_in.T,
        grid_second,
        send_weight,
        row(grid_bias),
        row(edge_bias),
        slot,
        feat_weight,
        g2m_send,
        g2m_recv,
        g2m_feat,
        g2m_count.reshape(1, 1),
    )
    own, cross, chip = call(
        edge_kernel,
        (shape(owned, width, kind=F32), shape(owned, width), shape(owned, width)),
        [SMEM] + [HBM] * len(operands),
        scratch=[VMEM(value.shape, value.dtype) for value in operands]
        + [
            SMEM(g2m_send.shape, I32),
            VMEM((grid_rows * (width // LANES), LANES), F32),
            VMEM((CHUNK_BLOCKS * g2m_send.shape[1] * (width // LANES), LANES), F32),
            VMEM((CHUNK_BLOCKS * g2m_send.shape[1] * (width // LANES), LANES), F32),
            VMEM((CHUNK_BLOCKS * g2m_send.shape[1], width), BF16),
            VMEM((CHUNK_BLOCKS * g2m_send.shape[1], width), BF16),
            VMEM((3 * owned, LANES), I32),
            VMEM((3 * owned, width), F32),
            pltpu.SemaphoreType.DMA((len(operands) + GRID_STEPS,)),
        ],
        flops=10_000_000_000,
        moved=4_000_000,
        vmem=32,
    )(place, *[hold(value) for value in operands])
    requests, _ = lax.optimization_barrier((requests, own))
    crossing = [(d, d + 1) for d in range(1, devices - 1, 2)]
    within = [(d, d + 1) for d in range(0, devices, 2)]
    both = lambda pairs: pairs + [(b, a) for a, b in pairs]
    from_cross = lax.ppermute(cross, "bulk", both(crossing))
    from_chip = lax.ppermute(chip, "bulk", both(within))
    supply, upper, lower = call(
        functools.partial(supply_kernel, mesh_send.shape[0]),
        (shape(places, owned), shape(owned, width, kind=F32), shape(width, width)),
        [SMEM] + [VMEM] * 6,
        flops=500_000_000,
        moved=500_000,
    )(place, slot, requests, mesh_latent, edge_out, node_input, row(node_bias))
    encoded, rows = call(
        node_kernel,
        (shape(owned, width), shape(places, width)),
        [VMEM] * 10,
        flops=500_000_000,
        moved=4_000_000,
    )(
        own,
        from_cross,
        from_chip,
        mesh_latent,
        upper,
        lower,
        node_out,
        row(node_gain),
        mesh_sender,
        supply,
    )
    piece = lax.all_to_all(rows, "bulk", 0, 0, tiled=True)
    mesh_send, _ = lax.optimization_barrier((mesh_send, encoded))
    wanted = call(
        functools.partial(wanted_kernel, owned),
        shape(edges, places),
        [VMEM] * 2,
        flops=1_000_000_000,
        moved=500_000,
    )(slot, mesh_send)
    incoming, pick, parts, upper, lower = call(
        receiver_kernel,
        (
            shape(owned, edges),
            shape(edges, 2 * owned),
            shape(2 * owned, width),
            shape(owned, width, kind=F32),
            shape(width, width),
        ),
        [SMEM] + [VMEM] * 8,
        flops=1_000_000_000,
        moved=4_000_000,
    )(
        place,
        slot,
        mesh_recv,
        encoded,
        mesh_receiver,
        row(message_bias),
        message_out,
        update_input,
        row(update_bias),
    )
    return call(
        message_kernel,
        shape(owned, width),
        [VMEM] * 10,
        flops=1_000_000_000,
        moved=4_000_000,
    )(
        wanted,
        piece,
        incoming,
        pick,
        parts,
        upper,
        lower,
        encoded,
        update_out,
        row(update_gain),
    )


def solution(mesh):
    split = {0: ("groups", "bulk"), 20: "bulk", 21: "bulk", 22: "bulk", 23: "bulk", 24: "bulk"}
    split.update({26: "bulk", 27: "bulk"})
    placed = tuple(P(split[at]) if at in split else P() for at in range(28))
    return jax.shard_map(
        per_device,
        mesh=mesh,
        in_specs=placed,
        out_specs=P(("groups", "bulk"), None),
        check_vma=False,
    )
```

```python
import functools
import math

import jax
import jax.numpy as jnp
from jax import lax
from jax.experimental import pallas as pl
from jax.experimental.pallas import tpu as pltpu
from jax.sharding import PartitionSpec as P

F32 = jnp.float32
BF16 = jnp.bfloat16
I32 = jnp.int32
SEND_CAP = 16
LANES = 128
VMEM = pltpu.VMEM
SMEM = pltpu.SMEM
HBM = pltpu.HBM
GRID_STEPS = 4
CHUNK_BLOCKS = 4
MEBI = 1024 * 1024


def mm(left, right):
    return jnp.dot(left, right, preferred_element_type=F32)


def mm_nt(left, right):
    return lax.dot_general(left, right, (((1,), (1,)), ((), ())), preferred_element_type=F32)


def silu_half(half):
    return half + half * jnp.tanh(half)


def silu(value):
    return silu_half(0.5 * value)


def layer_norm(value):
    center = value - jnp.mean(value, axis=-1, keepdims=True)
    spread = jnp.mean(center * center, axis=-1, keepdims=True)
    return center * lax.rsqrt(spread + 1e-05)


def iota(shape, dim):
    return lax.broadcasted_iota(I32, shape, dim)


def one_hot(places, columns):
    count = places.shape[1]
    places = jnp.broadcast_to(places.astype(F32), (LANES, count)).T.astype(I32).astype(jnp.int16)
    places = jnp.concatenate([places] * (columns // LANES), axis=1)
    hit = places == lax.broadcasted_iota(jnp.int16, (count, columns), 1)
    return jnp.where(hit, jnp.ones((), BF16), jnp.zeros((), BF16))


def ids_of_rows(slot, first, count):
    nodes = slot.shape[1]
    rows = iota((count, nodes), 0) + first
    return jnp.max(jnp.where(slot == rows, iota((count, nodes), 1), -1), axis=1, keepdims=True)


def edge_kernel(
    place_ref,
    first_hbm,
    grid_hbm,
    second_hbm,
    send_weight_hbm,
    grid_bias_hbm,
    edge_bias_hbm,
    slot_hbm,
    feat_weight_hbm,
    send_hbm,
    recv_hbm,
    feat_hbm,
    count_hbm,
    own_ref,
    cross_ref,
    chip_ref,
    first_ref,
    grid_ref,
    second_ref,
    send_weight_ref,
    grid_bias_ref,
    edge_bias_ref,
    slot_ref,
    feat_weight_ref,
    send_ref,
    recv_ref,
    feat_ref,
    count_ref,
    starts,
    senders_ref,
    flat,
    table,
    even_rows,
    odd_rows,
    even_hidden,
    odd_hidden,
    ids_ref,
    total,
    sems,
):
    channels, grid_rows = grid_ref.shape
    width = second_ref.shape[1]
    pieces = width // LANES
    blocks, block_edges = send_ref.shape
    owned = own_ref.shape[0]
    feats = feat_ref.shape[1]
    step_rows = grid_rows // GRID_STEPS

    def grid_copy(step):
        part = pl.ds(pl.multiple_of(step * step_rows, step_rows), step_rows)
        return pltpu.make_async_copy(grid_hbm.at[:, part], grid_ref.at[:, part], sems.at[step])

    pairs = [
        (first_hbm, first_ref),
        (second_hbm, second_ref),
        (send_weight_hbm, send_weight_ref),
        (grid_bias_hbm, grid_bias_ref),
        (edge_bias_hbm, edge_bias_ref),
        (send_hbm, send_ref),
        (slot_hbm, slot_ref),
        (feat_weight_hbm, feat_weight_ref),
        (recv_hbm, recv_ref),
        (feat_hbm, feat_ref),
        (count_hbm, count_ref),
        (send_ref, starts),
    ]
    copies = [
        pltpu.make_async_copy(source, target, sems.at[GRID_STEPS + at])
        for at, (source, target) in enumerate(pairs)
    ]
    first_copy, second_copy, send_weight_copy, grid_bias_copy, edge_bias_copy, send_copy = copies[:6]
    slot_copy, starts_copy = copies[6], copies[-1]
    first_copy.start()
    grid_copy(0).start()
    for copy in copies[1:-1]:
        copy.start()
    for step in range(1, GRID_STEPS):
        grid_copy(step).start()
    send_copy.wait()
    senders = send_ref[...]
    senders_ref[...] = senders
    send_ref[...] = (senders // 8) * (8 * pieces) + senders % 8
    starts_copy.start()
    slot_copy.wait()
    place = place_ref[0]
    ids_ref[...] = jnp.broadcast_to(
        ids_of_rows(slot_ref[...], (place - 1) * owned, 3 * owned), ids_ref.shape
    )
    total[...] = jnp.zeros_like(total)
    first_copy.wait()
    first_ref[...] = first_ref[...] * 0.5
    second_copy.wait()
    send_weight_copy.wait()
    send_weight_ref[...] = send_weight_ref[...] * 0.5
    grid_bias_copy.wait()
    edge_bias_copy.wait()
    grid_bias = 0.5 * grid_bias_ref[...]
    edge_bias = 0.5 * edge_bias_ref[...]
    def turn(step):
        return grid_ref[:, step * step_rows : (step + 1) * step_rows].T

    def store(step, value):
        rows = (value + edge_bias).astype(BF16)
        flat[step * step_rows : (step + 1) * step_rows, :] = rows
        rows = rows.astype(F32)
        for group in range(step_rows // 8):
            for piece in range(pieces):
                at = ((step * step_rows // 8 + group) * pieces + piece) * 8
                table[at : at + 8, :] = rows[
                    group * 8 : group * 8 + 8, piece * LANES : (piece + 1) * LANES
                ]

    grid_copy(0).wait()
    first, second, third = {}, {}, {}
    first[0] = mm(turn(0), first_ref[...])
    for step in range(1, GRID_STEPS):
        grid_copy(step).wait()
    for step in range(1, GRID_STEPS + 3):
        turned = turn(step) if step < GRID_STEPS else None
        if step - 3 in third:
            store(step - 3, third.pop(step - 3))
        if step - 2 in second:
            code = layer_norm(second.pop(step - 2)).astype(BF16)
        else:
            code = None
        if step - 1 in first:
            hidden = silu_half(first.pop(step - 1) + grid_bias).astype(BF16)
        else:
            hidden = None
        if code is not None:
            third[step - 2] = mm(code, send_weight_ref[...])
        if hidden is not None:
            second[step - 1] = mm(hidden, second_ref[...])
        if turned is not None:
            first[step] = mm(turned, first_ref[...])
    for copy in copies[7:]:
        copy.wait()
    used = count_ref[...]
    feat_weight = 0.5 * feat_weight_ref[...].astype(F32)
    feat_weight = jnp.concatenate([feat_weight, jnp.zeros((8 - feats, width), F32)], axis=0)
    feat_weight = feat_weight.astype(BF16)
    group = CHUNK_BLOCKS
    chunks = blocks // group
    part_rows = 64

    def gather(chunk, edges, target):
        for edge in edges:
            start = starts[chunk * group + edge // block_edges, edge % block_edges]
            target[pl.ds(edge // 8 * (8 * pieces) + edge % 8, pieces, stride=8), :] = table[
                pl.ds(start, pieces, stride=8), :
            ]

    def rows_of(source, first, count):
        return jnp.concatenate(
            [
                jnp.concatenate(
                    [
                        source[pl.ds((at * pieces + piece) * 8, 8), :]
                        for at in range(first // 8, (first + count) // 8)
                    ],
                    axis=0,
                )
                for piece in range(pieces)
            ],
            axis=1,
        )

    def add_sums(chunk, hidden):
        here = [chunk * group + b for b in range(group)]
        receivers = [jnp.where(b < used, recv_ref[pl.ds(b, 1), :], -2) for b in here]
        spread = jnp.concatenate([(ids_ref[...] == row).astype(F32) for row in receivers], axis=1)
        total[...] += mm(spread.astype(BF16), hidden[...])

    def work(chunk, source, target, hidden, hidden_before):
        here = [chunk * group + b for b in range(group)]
        feat = jnp.concatenate([feat_ref[b] for b in here], axis=1)
        feat = jnp.concatenate([feat, jnp.zeros((8 - feats, feat.shape[1]), F32)], axis=0)
        extra = mm(feat.T.astype(BF16), feat_weight)
        picker = one_hot(senders_ref[pl.ds(here[-1], 1), :], grid_rows)
        chosen = mm(picker, flat[...])
        add_sums(jnp.maximum(chunk - 1, 0), hidden_before)
        after = jnp.minimum(chunk + 1, chunks - 1)
        loaded = (group - 1) * block_edges
        each = loaded // (group * block_edges // part_rows)
        for at, first in enumerate(range(0, group * block_edges, part_rows)):
            gather(after, range(at * each, (at + 1) * each), target)
            if first < loaded:
                half = rows_of(source, first, part_rows)
            else:
                half = chosen[first - loaded : first - loaded + part_rows]
            half = half + extra[first : first + part_rows]
            hidden[first : first + part_rows, :] = silu_half(half).astype(BF16)

    def edge_step(step, carry):
        work(2 * step, even_rows, odd_rows, even_hidden, odd_hidden)
        work(2 * step + 1, odd_rows, even_rows, odd_hidden, even_hidden)
        return carry

    odd_hidden[...] = jnp.zeros_like(odd_hidden)
    gather(0, range((group - 1) * block_edges), even_rows)
    lax.fori_loop(0, chunks // 2, edge_step, 0)
    add_sums(chunks - 1, odd_hidden)
    odd = place % 2 == 1
    below, above = total[:owned].astype(BF16), total[2 * owned :].astype(BF16)
    own_ref[...] = total[owned : 2 * owned]
    cross_ref[...] = jnp.where(odd, above, below)
    chip_ref[...] = jnp.where(odd, below, above)


def wanted_kernel(owned, slot_ref, send_ref, wanted_ref):
    nodes = slot_ref.shape[1]
    blocks, block_edges = send_ref.shape
    places = wanted_ref.shape[1]
    chunk = LANES
    per_chunk = chunk // owned * SEND_CAP
    row, column = iota((chunk, chunk), 0), iota((chunk, chunk), 1)
    before = ((row > column) & (row // owned == column // owned)).astype(F32).astype(BF16)
    local_owner = (iota((chunk, LANES), 0) // owned * SEND_CAP).astype(F32)

    def find(index, best):
        ids = ids_of_rows(slot_ref[...], index * chunk, chunk)
        hit = jnp.zeros((chunk, block_edges), F32)
        for b in range(blocks):
            hit = jnp.maximum(hit, (ids == send_ref[b : b + 1, :]).astype(F32))
        hit = jnp.broadcast_to(jnp.max(hit, axis=1, keepdims=True), (chunk, LANES))
        rank = mm(before, hit.astype(BF16)) + local_owner
        spot = jnp.where(hit > 0, rank.astype(I32) + index * per_chunk, -1)
        spot = jnp.concatenate([spot] * (places // LANES), axis=1)
        found = jnp.where(spot == iota((chunk, places), 1), ids, -1)
        return jnp.maximum(best, jnp.max(found, axis=0, keepdims=True))

    best = lax.fori_loop(0, nodes // chunk, find, jnp.full((1, places), -1, I32), unroll=2)
    best = best.astype(F32)
    for b in range(blocks):
        senders = jnp.broadcast_to(send_ref[b : b + 1, :].astype(F32), (block_edges, block_edges)).T
        senders = jnp.concatenate([senders] * (places // LANES), axis=1)
        wanted_ref[b * block_edges : (b + 1) * block_edges, :] = (
            (senders == best).astype(F32).astype(BF16)
        )


def supply_kernel(
    blocks,
    place_ref,
    slot_ref,
    request_ref,
    latent_ref,
    edge_out_ref,
    node_input_ref,
    node_bias_ref,
    supply_ref,
    upper_ref,
    lower_ref,
):
    width = latent_ref.shape[1]
    upper_ref[...] = mm(latent_ref[...], node_input_ref[:width]) + node_bias_ref[...]
    lower_ref[...] = mm(edge_out_ref[...], node_input_ref[width:]).astype(BF16)
    owned = supply_ref.shape[1]
    devices = supply_ref.shape[0] // SEND_CAP
    per_device = request_ref.shape[0] // devices
    ids = ids_of_rows(slot_ref[...], place_ref[0] * owned, owned)
    lane = iota((owned, LANES), 1)
    used = jnp.zeros((owned, LANES), F32)
    for d in range(devices):
        hit = jnp.zeros((owned, request_ref.shape[1]), F32)
        for b in range(blocks):
            at = d * per_device + b
            hit = jnp.maximum(hit, (ids == request_ref[at : at + 1, :]).astype(F32))
        used = jnp.where(lane == d, jnp.max(hit, axis=1, keepdims=True), used)
    before = (iota((owned, owned), 0) > iota((owned, owned), 1)).astype(F32).astype(BF16)
    rank = jnp.where(used > 0, mm(before, used.astype(BF16)), -1.0)
    rank = jnp.concatenate([rank, jnp.full((LANES - owned, LANES), -1.0, F32)], axis=0).T
    slots = iota((SEND_CAP, owned), 0).astype(F32)
    supply = jnp.concatenate(
        [(rank[d : d + 1, :owned] == slots).astype(F32) for d in range(devices)], axis=0
    )
    supply_ref[...] = supply.astype(BF16)


def node_kernel(
    own_ref,
    from_cross_ref,
    from_chip_ref,
    latent_ref,
    upper_ref,
    lower_ref,
    node_out_ref,
    node_gain_ref,
    mesh_sender_ref,
    supply_ref,
    encoded_ref,
    rows_ref,
):
    latent = latent_ref[...]
    node_sum = own_ref[...] + from_cross_ref[...].astype(F32) + from_chip_ref[...].astype(F32)
    hidden = silu(upper_ref[...] + mm(node_sum.astype(BF16), lower_ref[...])).astype(BF16)
    encoded = latent.astype(F32) + layer_norm(mm(hidden, node_out_ref[...])) * node_gain_ref[...]
    encoded = encoded.astype(BF16)
    encoded_ref[...] = encoded
    sender_code = mm(encoded, mesh_sender_ref[...]).astype(BF16)
    rows_ref[...] = mm(supply_ref[...], sender_code).astype(BF16)


def receiver_kernel(
    place_ref,
    slot_ref,
    recv_ref,
    encoded_ref,
    mesh_receiver_ref,
    message_bias_ref,
    message_out_ref,
    update_input_ref,
    update_bias_ref,
    incoming_ref,
    pick_ref,
    parts_ref,
    upper_ref,
    lower_ref,
):
    owned, width = encoded_ref.shape
    blocks = recv_ref.shape[0]
    ids = ids_of_rows(slot_ref[...], place_ref[0] * owned, owned)
    incoming = jnp.concatenate(
        [(ids == recv_ref[b : b + 1, :]).astype(F32) for b in range(blocks)], axis=1
    )
    pick = incoming.T.astype(BF16)
    pick_ref[...] = jnp.concatenate([pick, pick], axis=1)
    incoming_ref[...] = incoming.astype(BF16)
    encoded = encoded_ref[...]
    receiver = mm(encoded, mesh_receiver_ref[...]) + message_bias_ref[...]
    high = receiver.astype(BF16)
    parts_ref[:owned, :] = high
    parts_ref[owned:, :] = (receiver - high.astype(F32)).astype(BF16)
    upper_ref[...] = mm(encoded, update_input_ref[:width]) + update_bias_ref[...]
    lower_ref[...] = mm(message_out_ref[...], update_input_ref[width:]).astype(BF16)


def message_kernel(
    wanted_ref,
    piece_ref,
    incoming_ref,
    pick_ref,
    parts_ref,
    upper_ref,
    lower_ref,
    encoded_ref,
    update_out_ref,
    update_gain_ref,
    out_ref,
):
    chosen = jnp.concatenate([wanted_ref[...], pick_ref[...]], axis=1)
    codes = jnp.concatenate([piece_ref[...], parts_ref[...]], axis=0)
    message = silu(mm(chosen, codes)).astype(BF16)
    message_sum = mm(incoming_ref[...], message).astype(BF16)
    hidden = silu(upper_ref[...] + mm(message_sum, lower_ref[...])).astype(BF16)
    out = layer_norm(mm(hidden, update_out_ref[...])) * update_gain_ref[...]
    out_ref[...] = (encoded_ref[...].astype(F32) + out).astype(BF16)


def call(kernel, out_shape, spaces, scratch=(), flops=0, moved=0, vmem=8):
    return pl.pallas_call(
        kernel,
        out_shape=out_shape,
        in_specs=[pl.BlockSpec(memory_space=space) for space in spaces],
        out_specs=jax.tree.map(lambda _: pl.BlockSpec(memory_space=VMEM), out_shape),
        scratch_shapes=scratch,
        compiler_params=pltpu.CompilerParams(vmem_limit_bytes=vmem * MEBI),
        cost_estimate=pl.CostEstimate(flops=flops, bytes_accessed=moved, transcendentals=0),
    )


def hold(value):
    return value if value.size == 1 else pltpu.with_memory_space_constraint(value, HBM)


def shape(*sizes, kind=BF16):
    return jax.ShapeDtypeStruct(sizes, kind)


def per_device(
    grid_in,
    grid_first,
    grid_bias,
    grid_second,
    send_weight,
    edge_bias,
    feat_weight,
    edge_out,
    node_input,
    node_bias,
    node_out,
    node_gain,
    mesh_sender,
    mesh_receiver,
    message_bias,
    message_out,
    update_input,
    update_bias,
    update_out,
    update_gain,
    mesh_latent,
    g2m_send,
    g2m_recv,
    g2m_feat,
    g2m_count,
    mesh_slot,
    mesh_send,
    mesh_recv,
):
    devices = lax.axis_size("bulk")
    position = lax.axis_index("bulk")
    place = position.astype(I32).reshape(1)
    owned, width = mesh_latent.shape
    grid_rows = grid_in.shape[0]
    places = devices * SEND_CAP
    edges = mesh_send.size
    slot = mesh_slot.reshape(1, -1)
    row = lambda vector: vector.reshape(1, -1)

    requests = lax.all_to_all(jnp.tile(mesh_send, (devices, 1)), "bulk", 0, 0, tiled=True)
    operands = (
        grid_first,
        grid_in.T,
        grid_second,
        send_weight,
        row(grid_bias),
        row(edge_bias),
        slot,
        feat_weight,
        g2m_send,
        g2m_recv,
        g2m_feat,
        g2m_count.reshape(1, 1),
    )
    own, cross, chip = call(
        edge_kernel,
        (shape(owned, width, kind=F32), shape(owned, width), shape(owned, width)),
        [SMEM] + [HBM] * len(operands),
        scratch=[VMEM(value.shape, value.dtype) for value in operands]
        + [
            SMEM(g2m_send.shape, I32),
            VMEM(g2m_send.shape, I32),
            VMEM((grid_rows, width), BF16),
            VMEM((grid_rows * (width // LANES), LANES), F32),
            VMEM((CHUNK_BLOCKS * g2m_send.shape[1] * (width // LANES), LANES), F32),
            VMEM((CHUNK_BLOCKS * g2m_send.shape[1] * (width // LANES), LANES), F32),
            VMEM((CHUNK_BLOCKS * g2m_send.shape[1], width), BF16),
            VMEM((CHUNK_BLOCKS * g2m_send.shape[1], width), BF16),
            VMEM((3 * owned, LANES), I32),
            VMEM((3 * owned, width), F32),
            pltpu.SemaphoreType.DMA((len(operands) + GRID_STEPS,)),
        ],
        flops=10_000_000_000,
        moved=4_000_000,
        vmem=32,
    )(place, *[hold(value) for value in operands])
    requests, _ = lax.optimization_barrier((requests, own))
    crossing = [(d, d + 1) for d in range(1, devices - 1, 2)]
    within = [(d, d + 1) for d in range(0, devices, 2)]
    both = lambda pairs: pairs + [(b, a) for a, b in pairs]
    from_cross = lax.ppermute(cross, "bulk", both(crossing))
    from_chip = lax.ppermute(chip, "bulk", both(within))
    supply, upper, lower = call(
        functools.partial(supply_kernel, mesh_send.shape[0]),
        (shape(places, owned), shape(owned, width, kind=F32), shape(width, width)),
        [SMEM] + [VMEM] * 6,
        flops=500_000_000,
        moved=500_000,
    )(place, slot, requests, mesh_latent, edge_out, node_input, row(node_bias))
    encoded, rows = call(
        node_kernel,
        (shape(owned, width), shape(places, width)),
        [VMEM] * 10,
        flops=500_000_000,
        moved=4_000_000,
    )(
        own,
        from_cross,
        from_chip,
        mesh_latent,
        upper,
        lower,
        node_out,
        row(node_gain),
        mesh_sender,
        supply,
    )
    piece = lax.all_to_all(rows, "bulk", 0, 0, tiled=True)
    mesh_send, _ = lax.optimization_barrier((mesh_send, encoded))
    wanted = call(
        functools.partial(wanted_kernel, owned),
        shape(edges, places),
        [VMEM] * 2,
        flops=1_000_000_000,
        moved=500_000,
    )(slot, mesh_send)
    incoming, pick, parts, upper, lower = call(
        receiver_kernel,
        (
            shape(owned, edges),
            shape(edges, 2 * owned),
            shape(2 * owned, width),
            shape(owned, width, kind=F32),
            shape(width, width),
        ),
        [SMEM] + [VMEM] * 8,
        flops=1_000_000_000,
        moved=4_000_000,
    )(
        place,
        slot,
        mesh_recv,
        encoded,
        mesh_receiver,
        row(message_bias),
        message_out,
        update_input,
        row(update_bias),
    )
    return call(
        message_kernel,
        shape(owned, width),
        [VMEM] * 10,
        flops=1_000_000_000,
        moved=4_000_000,
    )(
        wanted,
        piece,
        incoming,
        pick,
        parts,
        upper,
        lower,
        encoded,
        update_out,
        row(update_gain),
    )


def solution(mesh):
    split = {0: ("groups", "bulk"), 20: "bulk", 21: "bulk", 22: "bulk", 23: "bulk", 24: "bulk"}
    split.update({26: "bulk", 27: "bulk"})
    placed = tuple(P(split[at]) if at in split else P() for at in range(28))
    return jax.shard_map(
        per_device,
        mesh=mesh,
        in_specs=placed,
        out_specs=P(("groups", "bulk"), None),
        check_vma=False,
    )
```

```python
import functools
import math

import jax
import jax.numpy as jnp
from jax import lax
from jax.experimental import pallas as pl
from jax.experimental.pallas import tpu as pltpu
from jax.sharding import PartitionSpec as P

F32 = jnp.float32
BF16 = jnp.bfloat16
I32 = jnp.int32
SEND_CAP = 16
LANES = 128
VMEM = pltpu.VMEM
SMEM = pltpu.SMEM
HBM = pltpu.HBM
GRID_STEPS = 4
CHUNK_BLOCKS = 4
MEBI = 1024 * 1024


def mm(left, right):
    return jnp.dot(left, right, preferred_element_type=F32)


def mm_nt(left, right):
    return lax.dot_general(left, right, (((1,), (1,)), ((), ())), preferred_element_type=F32)


def silu_half(half):
    return half + half * jnp.tanh(half)


def silu(value):
    return silu_half(0.5 * value)


def layer_norm(value):
    center = value - jnp.mean(value, axis=-1, keepdims=True)
    spread = jnp.mean(center * center, axis=-1, keepdims=True)
    return center * lax.rsqrt(spread + 1e-05)


def iota(shape, dim):
    return lax.broadcasted_iota(I32, shape, dim)


def one_hot(columns, rows):
    hit = columns.astype(jnp.int16) == lax.broadcasted_iota(jnp.int16, (rows, columns.shape[1]), 0)
    return jnp.where(hit, jnp.ones((), BF16), jnp.zeros((), BF16))


def ids_of_rows(slot, first, count):
    nodes = slot.shape[1]
    rows = iota((count, nodes), 0) + first
    return jnp.max(jnp.where(slot == rows, iota((count, nodes), 1), -1), axis=1, keepdims=True)


def edge_kernel(
    place_ref,
    first_hbm,
    grid_hbm,
    second_hbm,
    send_weight_hbm,
    grid_bias_hbm,
    edge_bias_hbm,
    slot_hbm,
    feat_weight_hbm,
    send_hbm,
    recv_hbm,
    feat_hbm,
    count_hbm,
    own_ref,
    cross_ref,
    chip_ref,
    first_ref,
    grid_ref,
    second_ref,
    send_weight_ref,
    grid_bias_ref,
    edge_bias_ref,
    slot_ref,
    feat_weight_ref,
    send_ref,
    recv_ref,
    feat_ref,
    count_ref,
    starts,
    table,
    even_rows,
    odd_rows,
    even_hidden,
    odd_hidden,
    ids_ref,
    total,
    sems,
):
    channels, grid_rows = grid_ref.shape
    width = second_ref.shape[1]
    pieces = width // LANES
    blocks, block_edges = send_ref.shape
    owned = own_ref.shape[0]
    feats = feat_ref.shape[1]
    step_rows = grid_rows // GRID_STEPS

    def grid_copy(step):
        part = pl.ds(pl.multiple_of(step * step_rows, step_rows), step_rows)
        return pltpu.make_async_copy(grid_hbm.at[:, part], grid_ref.at[:, part], sems.at[step])

    pairs = [
        (first_hbm, first_ref),
        (second_hbm, second_ref),
        (send_weight_hbm, send_weight_ref),
        (grid_bias_hbm, grid_bias_ref),
        (edge_bias_hbm, edge_bias_ref),
        (send_hbm, send_ref),
        (slot_hbm, slot_ref),
        (feat_weight_hbm, feat_weight_ref),
        (recv_hbm, recv_ref),
        (feat_hbm, feat_ref),
        (count_hbm, count_ref),
        (send_ref, starts),
    ]
    copies = [
        pltpu.make_async_copy(source, target, sems.at[GRID_STEPS + at])
        for at, (source, target) in enumerate(pairs)
    ]
    first_copy, second_copy, send_weight_copy, grid_bias_copy, edge_bias_copy, send_copy = copies[:6]
    slot_copy, starts_copy = copies[6], copies[-1]
    first_copy.start()
    grid_copy(0).start()
    for copy in copies[1:-1]:
        copy.start()
    for step in range(1, GRID_STEPS):
        grid_copy(step).start()
    send_copy.wait()
    senders = send_ref[...]
    send_ref[...] = (senders // 8) * (8 * pieces) + senders % 8
    starts_copy.start()
    slot_copy.wait()
    place = place_ref[0]
    ids_ref[...] = jnp.broadcast_to(
        ids_of_rows(slot_ref[...], (place - 1) * owned, 3 * owned), ids_ref.shape
    )
    total[...] = jnp.zeros_like(total)
    first_copy.wait()
    first_ref[...] = first_ref[...] * 0.5
    second_copy.wait()
    send_weight_copy.wait()
    send_weight_ref[...] = send_weight_ref[...] * 0.5
    grid_bias_copy.wait()
    edge_bias_copy.wait()
    grid_bias = 0.5 * grid_bias_ref[...]
    edge_bias = 0.5 * edge_bias_ref[...]
    def turn(step):
        return grid_ref[:, step * step_rows : (step + 1) * step_rows].T

    def store(step, value):
        rows = (value + edge_bias).astype(BF16).astype(F32)
        for group in range(step_rows // 8):
            for piece in range(pieces):
                at = ((step * step_rows // 8 + group) * pieces + piece) * 8
                table[at : at + 8, :] = rows[
                    group * 8 : group * 8 + 8, piece * LANES : (piece + 1) * LANES
                ]

    grid_copy(0).wait()
    first, second, third = {}, {}, {}
    first[0] = mm(turn(0), first_ref[...])
    for step in range(1, GRID_STEPS):
        grid_copy(step).wait()
    for step in range(1, GRID_STEPS + 3):
        turned = turn(step) if step < GRID_STEPS else None
        if step - 3 in third:
            store(step - 3, third.pop(step - 3))
        if step - 2 in second:
            code = layer_norm(second.pop(step - 2)).astype(BF16)
        else:
            code = None
        if step - 1 in first:
            hidden = silu_half(first.pop(step - 1) + grid_bias).astype(BF16)
        else:
            hidden = None
        if code is not None:
            third[step - 2] = mm(code, send_weight_ref[...])
        if hidden is not None:
            second[step - 1] = mm(hidden, second_ref[...])
        if turned is not None:
            first[step] = mm(turned, first_ref[...])
    for copy in copies[7:]:
        copy.wait()
    used = count_ref[...]
    feat_weight = 0.5 * feat_weight_ref[...].astype(F32)
    feat_weight = jnp.concatenate([feat_weight, jnp.zeros((8 - feats, width), F32)], axis=0)
    feat_weight = feat_weight.astype(BF16)
    group = CHUNK_BLOCKS
    chunks = blocks // group
    part_rows = 128

    def gather(chunk, edges, target):
        for edge in edges:
            start = starts[chunk * group + edge // block_edges, edge % block_edges]
            target[pl.ds(edge // 8 * (8 * pieces) + edge % 8, pieces, stride=8), :] = table[
                pl.ds(start, pieces, stride=8), :
            ]

    def rows_of(source, first, count):
        return jnp.concatenate(
            [
                jnp.concatenate(
                    [
                        source[pl.ds((at * pieces + piece) * 8, 8), :]
                        for at in range(first // 8, (first + count) // 8)
                    ],
                    axis=0,
                )
                for piece in range(pieces)
            ],
            axis=1,
        )

    def add_sums(chunk, hidden):
        here = [chunk * group + b for b in range(group)]
        receivers = [jnp.where(b < used, recv_ref[pl.ds(b, 1), :], -2) for b in here]
        spread = jnp.concatenate([(ids_ref[...] == row).astype(F32) for row in receivers], axis=1)
        total[...] += mm(spread.astype(BF16), hidden[...])

    def work(chunk, source, target, hidden, hidden_before):
        here = [chunk * group + b for b in range(group)]
        feat = jnp.concatenate([feat_ref[b] for b in here], axis=1)
        feat = jnp.concatenate([feat, jnp.zeros((8 - feats, feat.shape[1]), F32)], axis=0)
        extra = mm(feat.T.astype(BF16), feat_weight)
        add_sums(jnp.maximum(chunk - 1, 0), hidden_before)
        after = jnp.minimum(chunk + 1, chunks - 1)
        for first in range(0, group * block_edges, part_rows):
            gather(after, range(first, first + part_rows), target)
            half = rows_of(source, first, part_rows) + extra[first : first + part_rows]
            hidden[first : first + part_rows, :] = silu_half(half).astype(BF16)

    def edge_step(step, carry):
        work(2 * step, even_rows, odd_rows, even_hidden, odd_hidden)
        work(2 * step + 1, odd_rows, even_rows, odd_hidden, even_hidden)
        return carry

    odd_hidden[...] = jnp.zeros_like(odd_hidden)
    gather(0, range(group * block_edges), even_rows)
    lax.fori_loop(0, chunks // 2, edge_step, 0)
    add_sums(chunks - 1, odd_hidden)
    odd = place % 2 == 1
    below, above = total[:owned].astype(BF16), total[2 * owned :].astype(BF16)
    own_ref[...] = total[owned : 2 * owned]
    cross_ref[...] = jnp.where(odd, above, below)
    chip_ref[...] = jnp.where(odd, below, above)


def wanted_kernel(owned, slot_ref, send_ref, wanted_ref):
    nodes = slot_ref.shape[1]
    blocks, block_edges = send_ref.shape
    places = wanted_ref.shape[1]
    chunk = LANES
    per_chunk = chunk // owned * SEND_CAP
    row, column = iota((chunk, chunk), 0), iota((chunk, chunk), 1)
    before = ((row > column) & (row // owned == column // owned)).astype(F32).astype(BF16)
    local_owner = (iota((chunk, LANES), 0) // owned * SEND_CAP).astype(F32)

    def find(index, best):
        ids = ids_of_rows(slot_ref[...], index * chunk, chunk)
        hit = jnp.zeros((chunk, block_edges), F32)
        for b in range(blocks):
            hit = jnp.maximum(hit, (ids == send_ref[b : b + 1, :]).astype(F32))
        hit = jnp.broadcast_to(jnp.max(hit, axis=1, keepdims=True), (chunk, LANES))
        rank = mm(before, hit.astype(BF16)) + local_owner
        spot = jnp.where(hit > 0, rank.astype(I32) + index * per_chunk, -1)
        spot = jnp.concatenate([spot] * (places // LANES), axis=1)
        found = jnp.where(spot == iota((chunk, places), 1), ids, -1)
        return jnp.maximum(best, jnp.max(found, axis=0, keepdims=True))

    best = lax.fori_loop(0, nodes // chunk, find, jnp.full((1, places), -1, I32), unroll=2)
    best = best.astype(F32)
    for b in range(blocks):
        senders = jnp.broadcast_to(send_ref[b : b + 1, :].astype(F32), (block_edges, block_edges)).T
        senders = jnp.concatenate([senders] * (places // LANES), axis=1)
        wanted_ref[b * block_edges : (b + 1) * block_edges, :] = (
            (senders == best).astype(F32).astype(BF16)
        )


def supply_kernel(
    blocks,
    place_ref,
    slot_ref,
    request_ref,
    latent_ref,
    edge_out_ref,
    node_input_ref,
    node_bias_ref,
    supply_ref,
    upper_ref,
    lower_ref,
):
    width = latent_ref.shape[1]
    upper_ref[...] = mm(latent_ref[...], node_input_ref[:width]) + node_bias_ref[...]
    lower_ref[...] = mm(edge_out_ref[...], node_input_ref[width:]).astype(BF16)
    owned = supply_ref.shape[1]
    devices = supply_ref.shape[0] // SEND_CAP
    per_device = request_ref.shape[0] // devices
    ids = ids_of_rows(slot_ref[...], place_ref[0] * owned, owned)
    lane = iota((owned, LANES), 1)
    used = jnp.zeros((owned, LANES), F32)
    for d in range(devices):
        hit = jnp.zeros((owned, request_ref.shape[1]), F32)
        for b in range(blocks):
            at = d * per_device + b
            hit = jnp.maximum(hit, (ids == request_ref[at : at + 1, :]).astype(F32))
        used = jnp.where(lane == d, jnp.max(hit, axis=1, keepdims=True), used)
    before = (iota((owned, owned), 0) > iota((owned, owned), 1)).astype(F32).astype(BF16)
    rank = jnp.where(used > 0, mm(before, used.astype(BF16)), -1.0)
    rank = jnp.concatenate([rank, jnp.full((LANES - owned, LANES), -1.0, F32)], axis=0).T
    slots = iota((SEND_CAP, owned), 0).astype(F32)
    supply = jnp.concatenate(
        [(rank[d : d + 1, :owned] == slots).astype(F32) for d in range(devices)], axis=0
    )
    supply_ref[...] = supply.astype(BF16)


def node_kernel(
    own_ref,
    from_cross_ref,
    from_chip_ref,
    latent_ref,
    upper_ref,
    lower_ref,
    node_out_ref,
    node_gain_ref,
    mesh_sender_ref,
    supply_ref,
    encoded_ref,
    rows_ref,
):
    latent = latent_ref[...]
    node_sum = own_ref[...] + from_cross_ref[...].astype(F32) + from_chip_ref[...].astype(F32)
    hidden = silu(upper_ref[...] + mm(node_sum.astype(BF16), lower_ref[...])).astype(BF16)
    encoded = latent.astype(F32) + layer_norm(mm(hidden, node_out_ref[...])) * node_gain_ref[...]
    encoded = encoded.astype(BF16)
    encoded_ref[...] = encoded
    sender_code = mm(encoded, mesh_sender_ref[...]).astype(BF16)
    rows_ref[...] = mm(supply_ref[...], sender_code).astype(BF16)


def receiver_kernel(
    place_ref,
    slot_ref,
    recv_ref,
    encoded_ref,
    mesh_receiver_ref,
    message_bias_ref,
    message_out_ref,
    update_input_ref,
    update_bias_ref,
    incoming_ref,
    pick_ref,
    parts_ref,
    upper_ref,
    lower_ref,
):
    owned, width = encoded_ref.shape
    blocks = recv_ref.shape[0]
    ids = ids_of_rows(slot_ref[...], place_ref[0] * owned, owned)
    incoming = jnp.concatenate(
        [(ids == recv_ref[b : b + 1, :]).astype(F32) for b in range(blocks)], axis=1
    )
    pick = incoming.T.astype(BF16)
    pick_ref[...] = jnp.concatenate([pick, pick], axis=1)
    incoming_ref[...] = incoming.astype(BF16)
    encoded = encoded_ref[...]
    receiver = mm(encoded, mesh_receiver_ref[...]) + message_bias_ref[...]
    high = receiver.astype(BF16)
    parts_ref[:owned, :] = high
    parts_ref[owned:, :] = (receiver - high.astype(F32)).astype(BF16)
    upper_ref[...] = mm(encoded, update_input_ref[:width]) + update_bias_ref[...]
    lower_ref[...] = mm(message_out_ref[...], update_input_ref[width:]).astype(BF16)


def message_kernel(
    wanted_ref,
    piece_ref,
    incoming_ref,
    pick_ref,
    parts_ref,
    upper_ref,
    lower_ref,
    encoded_ref,
    update_out_ref,
    update_gain_ref,
    out_ref,
):
    chosen = jnp.concatenate([wanted_ref[...], pick_ref[...]], axis=1)
    codes = jnp.concatenate([piece_ref[...], parts_ref[...]], axis=0)
    message = silu(mm(chosen, codes)).astype(BF16)
    message_sum = mm(incoming_ref[...], message).astype(BF16)
    hidden = silu(upper_ref[...] + mm(message_sum, lower_ref[...])).astype(BF16)
    out = layer_norm(mm(hidden, update_out_ref[...])) * update_gain_ref[...]
    out_ref[...] = (encoded_ref[...].astype(F32) + out).astype(BF16)


def call(kernel, out_shape, spaces, scratch=(), flops=0, moved=0, vmem=8):
    return pl.pallas_call(
        kernel,
        out_shape=out_shape,
        in_specs=[pl.BlockSpec(memory_space=space) for space in spaces],
        out_specs=jax.tree.map(lambda _: pl.BlockSpec(memory_space=VMEM), out_shape),
        scratch_shapes=scratch,
        compiler_params=pltpu.CompilerParams(vmem_limit_bytes=vmem * MEBI),
        cost_estimate=pl.CostEstimate(flops=flops, bytes_accessed=moved, transcendentals=0),
    )


def hold(value):
    return value if value.size == 1 else pltpu.with_memory_space_constraint(value, HBM)


def shape(*sizes, kind=BF16):
    return jax.ShapeDtypeStruct(sizes, kind)


def per_device(
    grid_in,
    grid_first,
    grid_bias,
    grid_second,
    send_weight,
    edge_bias,
    feat_weight,
    edge_out,
    node_input,
    node_bias,
    node_out,
    node_gain,
    mesh_sender,
    mesh_receiver,
    message_bias,
    message_out,
    update_input,
    update_bias,
    update_out,
    update_gain,
    mesh_latent,
    g2m_send,
    g2m_recv,
    g2m_feat,
    g2m_count,
    mesh_slot,
    mesh_send,
    mesh_recv,
):
    devices = lax.axis_size("bulk")
    position = lax.axis_index("bulk")
    place = position.astype(I32).reshape(1)
    owned, width = mesh_latent.shape
    grid_rows = grid_in.shape[0]
    places = devices * SEND_CAP
    edges = mesh_send.size
    slot = mesh_slot.reshape(1, -1)
    row = lambda vector: vector.reshape(1, -1)

    requests = lax.all_to_all(jnp.tile(mesh_send, (devices, 1)), "bulk", 0, 0, tiled=True)
    operands = (
        grid_first,
        grid_in.T,
        grid_second,
        send_weight,
        row(grid_bias),
        row(edge_bias),
        slot,
        feat_weight,
        g2m_send,
        g2m_recv,
        g2m_feat,
        g2m_count.reshape(1, 1),
    )
    own, cross, chip = call(
        edge_kernel,
        (shape(owned, width, kind=F32), shape(owned, width), shape(owned, width)),
        [SMEM] + [HBM] * len(operands),
        scratch=[VMEM(value.shape, value.dtype) for value in operands]
        + [
            SMEM(g2m_send.shape, I32),
            VMEM((grid_rows * (width // LANES), LANES), F32),
            VMEM((CHUNK_BLOCKS * g2m_send.shape[1] * (width // LANES), LANES), F32),
            VMEM((CHUNK_BLOCKS * g2m_send.shape[1] * (width // LANES), LANES), F32),
            VMEM((CHUNK_BLOCKS * g2m_send.shape[1], width), BF16),
            VMEM((CHUNK_BLOCKS * g2m_send.shape[1], width), BF16),
            VMEM((3 * owned, LANES), I32),
            VMEM((3 * owned, width), F32),
            pltpu.SemaphoreType.DMA((len(operands) + GRID_STEPS,)),
        ],
        flops=10_000_000_000,
        moved=4_000_000,
        vmem=32,
    )(place, *[hold(value) for value in operands])
    requests, _ = lax.optimization_barrier((requests, own))
    crossing = [(d, d + 1) for d in range(1, devices - 1, 2)]
    within = [(d, d + 1) for d in range(0, devices, 2)]
    both = lambda pairs: pairs + [(b, a) for a, b in pairs]
    from_cross = lax.ppermute(cross, "bulk", both(crossing))
    from_chip = lax.ppermute(chip, "bulk", both(within))
    supply, upper, lower = call(
        functools.partial(supply_kernel, mesh_send.shape[0]),
        (shape(places, owned), shape(owned, width, kind=F32), shape(width, width)),
        [SMEM] + [VMEM] * 6,
        flops=500_000_000,
        moved=500_000,
    )(place, slot, requests, mesh_latent, edge_out, node_input, row(node_bias))
    encoded, rows = call(
        node_kernel,
        (shape(owned, width), shape(places, width)),
        [VMEM] * 10,
        flops=500_000_000,
        moved=4_000_000,
    )(
        own,
        from_cross,
        from_chip,
        mesh_latent,
        upper,
        lower,
        node_out,
        row(node_gain),
        mesh_sender,
        supply,
    )
    piece = lax.all_to_all(rows, "bulk", 0, 0, tiled=True)
    mesh_send, _ = lax.optimization_barrier((mesh_send, encoded))
    wanted = call(
        functools.partial(wanted_kernel, owned),
        shape(edges, places),
        [VMEM] * 2,
        flops=1_000_000_000,
        moved=500_000,
    )(slot, mesh_send)
    incoming, pick, parts, upper, lower = call(
        receiver_kernel,
        (
            shape(owned, edges),
            shape(edges, 2 * owned),
            shape(2 * owned, width),
            shape(owned, width, kind=F32),
            shape(width, width),
        ),
        [SMEM] + [VMEM] * 8,
        flops=1_000_000_000,
        moved=4_000_000,
    )(
        place,
        slot,
        mesh_recv,
        encoded,
        mesh_receiver,
        row(message_bias),
        message_out,
        update_input,
        row(update_bias),
    )
    return call(
        message_kernel,
        shape(owned, width),
        [VMEM] * 10,
        flops=1_000_000_000,
        moved=4_000_000,
    )(
        wanted,
        piece,
        incoming,
        pick,
        parts,
        upper,
        lower,
        encoded,
        update_out,
        row(update_gain),
    )


def solution(mesh):
    split = {0: ("groups", "bulk"), 20: "bulk", 21: "bulk", 22: "bulk", 23: "bulk", 24: "bulk"}
    split.update({26: "bulk", 27: "bulk"})
    placed = tuple(P(split[at]) if at in split else P() for at in range(28))
    return jax.shard_map(
        per_device,
        mesh=mesh,
        in_specs=placed,
        out_specs=P(("groups", "bulk"), None),
        check_vma=False,
    )
```
